32 devices in a mesh: groups: 2 (over y), tiles: 16 (over z, x, core).
Axes of the slice: x: 2, y: 2, z: 4, core: 2. Of those that a mesh axis runs over, the one named last changes fastest.
Arguments:
- hidden: bfloat16 [6144, 3072], P(('groups', 'tiles')), parts along dimension 0, may hold values from -6 to 6
- queries: bfloat16 [6144, 1536], P(('groups', 'tiles')), parts along dimension 0, may hold values from -5 to 5
- keys: bfloat16 [6144, 1536], P(('groups', 'tiles')), parts along dimension 0, may hold values from -5 to 5
- values: bfloat16 [6144, 1536], P(('groups', 'tiles')), parts along dimension 0, may hold values from -6 to 6
- control: bfloat16 [6144, 3072], P(('groups', 'tiles')), parts along dimension 0, may hold values from -6 to 6
- out_weight: bfloat16 [1536, 3072], P('tiles'), may hold values from -2 to 2
- pattern: int32 [32, 6], P(('groups', 'tiles')), parts along dimension 0, may hold values 0 or 1
Outputs:
- block_out: bfloat16 [6144, 3072], P(('groups', 'tiles')), parts along dimension 0
The draws below stay inside these ranges and needn't reach their ends.
There are 2 independent parts, one for each index of `groups`. The reference program is written for one: setup_inputs(seed, part) draws one part's arguments, and reference() takes and returns one part's arrays. A program takes and returns all parts, laid end to end along the dimension named above; an argument that names none is the same for every part. Nothing has to cross between parts.
All inputs are finite; a program needn't handle non-finite values. No bound on the sum of `pattern` on one device may be relied on, other than what follows from the above.
Results may differ from the reference program's by a relative error of at most 0.0055.
Values may be sent and summed in bfloat16 or wider, within the bound.
No kernel may reach another device: no remote copies, remote signals or barrier semaphores. Data moves between devices by JAX's collectives and lax.ppermute only.
A program may use at most 128 MiB of HBM per device.

```python
import jax
import jax.numpy as jnp
from jax import lax

D = 3072
HEAD_DIM = 128
HEADS = 12
TILE_F = 3
TILE_H = 8
TILE_W = 8
GRID_W = 4
GRID_H = 2
TILE = 192
INNER = 1536
FRAME_TILES = 2
TOKENS = 3072
N_TILES = 16


def draw_queries(key, part):
    key = jax.random.fold_in(key, 11)
    matrix = jnp.clip(jax.random.normal(key, (TOKENS, INNER), jnp.float32), -5.0, 5.0)
    return matrix.astype(jnp.bfloat16)


def draw_keys(key, part):
    key = jax.random.fold_in(key, 12)
    matrix = jnp.clip(jax.random.normal(key, (TOKENS, INNER), jnp.float32), -5.0, 5.0)
    return matrix.astype(jnp.bfloat16)


def touch_ends(values, key, smallest, top_value):
    spot = [jax.random.randint(jax.random.fold_in(key, axis), (), 0, length) for axis, length in enumerate(values.shape)]
    longest = values.shape.index(max(values.shape))
    beside = spot[:longest] + [(spot[longest] + 1) % values.shape[longest]] + spot[longest + 1:]
    return values.at[tuple(spot)].set(smallest).at[tuple(beside)].set(top_value)


def block_levels(own_key, shape, split, smallest, high):
    level, own = 1.0, jax.random.fold_in(own_key, 6)
    for position, blocks in split:
        heights = jnp.exp(jax.random.uniform(jax.random.fold_in(own, position), (blocks,), jnp.float32, smallest / len(split), high / len(split)))
        level = level * jnp.repeat(heights, shape[position] // blocks).reshape([-1 if axis == position else 1 for axis in range(len(shape))])
    return level


def noise(own_key, extent, spread, bound, cuts=(), held_as=jnp.bfloat16):
    factor_of = block_levels(own_key, extent, cuts, -0.22, 0.18) if cuts else 1.0
    values = jax.random.normal(own_key, extent, jnp.float32) * spread * factor_of
    return jnp.minimum(jnp.maximum(values, -bound), bound).astype(held_as)


def setup_inputs(seed: int = 0, part: int = 0) -> dict:
    seeds = jax.random.split(jax.random.key(seed), 8)
    own_keys = jax.random.split(jax.random.fold_in(seeds[7], part), 8)
    hidden = noise(own_keys[0], (TOKENS, D), 1.0, 6.0, ((0, 16),))
    queries = draw_queries(jax.random.fold_in(jax.random.fold_in(seeds[7], part), 71), part)
    keys = draw_keys(jax.random.fold_in(jax.random.fold_in(seeds[7], part), 71), part)
    values = noise(own_keys[3], (TOKENS, INNER), 1.0, 6.0, ((0, 16),))
    control = noise(own_keys[4], (TOKENS, D), 1.0, 6.0, ((0, 16),))
    out_weight = noise(seeds[5], (INNER, D), 0.3, 2.0, ((0, 16),))
    pattern = touch_ends((jax.random.randint(own_keys[6], (N_TILES, 6), 0, 4) < 3).astype(jnp.int32), jax.random.fold_in(own_keys[6], 1), 0, 1)
    return {"hidden": hidden, "queries": queries, "keys": keys, "values": values, "control": control, "out_weight": out_weight, "pattern": pattern}


def pair_terms(query_tile, key_tile, value_tile):
    scores = jnp.einsum('qhd,khd->hqk', query_tile.astype(jnp.float32), key_tile.astype(jnp.float32)) * (HEAD_DIM ** -0.5)
    peak_rows = jnp.max(scores, axis=-1)
    weights = jnp.exp(scores - peak_rows[:, :, None]).astype(jnp.bfloat16)
    total = jnp.sum(weights.astype(jnp.float32), axis=-1)
    output = jnp.einsum('hqk,khd->qhd', weights.astype(jnp.float32), value_tile.astype(jnp.float32))
    return output, peak_rows, total


def combine(partials, active_list):
    peak_stack = jnp.stack([jnp.where(active, item[1], -1e30) for item, active in zip(partials, active_list)])
    largest = jnp.max(peak_stack, axis=0)
    factors = jnp.exp(peak_stack - largest[None])
    numerator = jnp.zeros_like(partials[0][0])
    denominator = jnp.zeros_like(partials[0][2])
    for number in range(len(partials)):
        numerator = numerator + factors[number].T[:, :, None] * partials[number][0]
        denominator = denominator + factors[number] * partials[number][2]
    result = numerator / denominator.T[:, :, None]
    return result.reshape(result.shape[0], -1).astype(jnp.bfloat16)


def reference(hidden, queries, keys, values, control, out_weight, pattern):
    query_all = queries.reshape(N_TILES, TILE, HEADS, HEAD_DIM)
    key_all = keys.reshape(N_TILES, TILE, HEADS, HEAD_DIM)
    value_all = values.reshape(N_TILES, TILE, HEADS, HEAD_DIM)
    layer = GRID_W * GRID_H
    offsets = (-layer, layer, -GRID_W, GRID_W, -1, 1)

    def one_tile(tile_index):
        frame_tile = tile_index // layer
        row_tile = (tile_index // GRID_W) % GRID_H
        across = tile_index % GRID_W
        limits = (frame_tile >= 1, frame_tile <= FRAME_TILES - 2, row_tile >= 1, row_tile <= GRID_H - 2, across >= 1, across <= GRID_W - 2)
        partials = [pair_terms(query_all[tile_index], key_all[tile_index], value_all[tile_index])]
        active_list = [jnp.array(True)]
        for direction in range(6):
            neighbour = jnp.clip(tile_index + offsets[direction], 0, N_TILES - 1).astype(jnp.int32)
            partials.append(pair_terms(query_all[tile_index], key_all[neighbour], value_all[neighbour]))
            active_list.append(limits[direction] & (pattern[tile_index, direction] == 1))
        return combine(partials, active_list)

    attention = lax.map(one_tile, jnp.arange(N_TILES, dtype=jnp.int32)).reshape(TOKENS, INNER)
    control_tiles = control.reshape(FRAME_TILES, GRID_H, TILE_F, TILE_H, GRID_W, TILE_W, D)
    control_tiles = control_tiles.transpose(0, 1, 4, 2, 3, 5, 6).reshape(TOKENS, D)
    projected = jnp.dot(attention, out_weight, preferred_element_type=jnp.float32)
    block_out = hidden.astype(jnp.float32) + projected + control_tiles.astype(jnp.float32)
    return block_out.astype(jnp.bfloat16)
```

```python
import functools
import math

import jax
import jax.numpy as jnp
from jax import lax
from jax.experimental import pallas as pl
from jax.experimental.pallas import tpu as pltpu
from jax.sharding import Mesh
from jax.sharding import PartitionSpec as P

HEAD_DIM = 128
TILE_W = 8
SCALE = HEAD_DIM**-0.5 * math.log2(math.e)
TILES = ("outer", "pair", "core")
VMEM_LIMIT = 40 * 1024 * 1024


def head_part(q, k, v):
    scores = lax.dot_general(q, k, (((1,), (1,)), ((), ())), preferred_element_type=jnp.float32)
    peak = jnp.max(scores, axis=1, keepdims=True)
    weights = jnp.exp2((scores - peak) * SCALE).astype(jnp.bfloat16)
    ones = jnp.ones((v.shape[0], HEAD_DIM), jnp.bfloat16)
    both = jnp.dot(weights, jnp.concatenate([v, ones], axis=1), preferred_element_type=jnp.float32)
    return both[:, :HEAD_DIM], both[:, HEAD_DIM:], jnp.broadcast_to(peak, v.shape)


def merge(old, new):
    part, total, peak = old
    part_new, total_new, peak_new = new
    top = jnp.maximum(peak, peak_new)
    f_old = jnp.exp2((peak - top) * SCALE)
    f_new = jnp.exp2((peak_new - top) * SCALE)
    return f_old * part + f_new * part_new, f_old * total + f_new * total_new, top


def attend_kernel(slots, first, active, q, *refs):
    kv = refs[: 2 * slots]
    refs = refs[2 * slots :]
    if not first:
        state_in, refs = refs[:3], refs[3:]
    state = refs[:3]
    heads = q.shape[1] // HEAD_DIM
    for h in range(heads):
        at = pl.ds(h * HEAD_DIM, HEAD_DIM)
        if first:
            now = head_part(q[:, at], kv[0][:, at], kv[1][:, at])
        else:
            now = tuple(r[:, at] for r in state_in)
        for r, x in zip(state, now):
            r[:, at] = x
    for slot in range(1 if first else 0, slots):

        @pl.when(active[slot] == 1)
        def _():
            for h in range(heads):
                at = pl.ds(h * HEAD_DIM, HEAD_DIM)
                new = head_part(q[:, at], kv[2 * slot][:, at], kv[2 * slot + 1][:, at])
                for r, x in zip(state, merge(tuple(r[:, at] for r in state), new)):
                    r[:, at] = x


def attend(active, q, kv, state):
    slots = len(kv) // 2
    rows, inner = q.shape
    shape = jax.ShapeDtypeStruct((rows, inner), jnp.float32)
    first = state is None
    return pl.pallas_call(
        functools.partial(attend_kernel, slots, first),
        out_shape=[shape] * 3,
        in_specs=[pl.BlockSpec(memory_space=pltpu.SMEM)]
        + [pl.BlockSpec(memory_space=pltpu.VMEM)] * (1 + 2 * slots + (0 if first else 3)),
        out_specs=[pl.BlockSpec(memory_space=pltpu.VMEM)] * 3,
        compiler_params=pltpu.CompilerParams(vmem_limit_bytes=VMEM_LIMIT),
        cost_estimate=pl.CostEstimate(
            flops=slots * 6 * rows * rows * inner, bytes_accessed=rows * inner * (2 + 4 * slots + 12), transcendentals=0
        ),
        name="attend",
    )(active, q, *kv, *([] if first else state))


def finish_kernel(moves, info, q, k, v, part, total, peak, hidden, control, *refs):
    pieces = len({m[0] for m in moves})
    weight = refs[:pieces]
    out, attention, held, hidden_v, control_v, sems, res_sems = refs[pieces:]
    copies = []
    for number, (piece, index, group, start, share) in enumerate(moves):
        count = weight[piece].shape[-2]
        if share:
            side = info[1] if share > 0 else 1 - info[1]
            start = pl.multiple_of(start + side * count, count)
        copies.append(
            pltpu.make_async_copy(
                weight[piece].at[index], held.at[group, pl.ds(start, count), :], sems.at[number]
            )
        )
    residual = [
        pltpu.make_async_copy(hidden, hidden_v, res_sems.at[0]),
        pltpu.make_async_copy(control, control_v, res_sems.at[1]),
    ]
    for copy in copies + residual:
        copy.start()
    heads = q.shape[1] // HEAD_DIM

    def normal(state, at):
        attention[:, at] = (state[0] / state[1]).astype(jnp.bfloat16)

    @pl.when(info[0] == 1)
    def _():
        for h in range(heads):
            at = pl.ds(h * HEAD_DIM, HEAD_DIM)
            new = head_part(q[:, at], k[:, at], v[:, at])
            normal(merge((part[:, at], total[:, at], peak[:, at]), new), at)

    @pl.when(info[0] != 1)
    def _():
        for h in range(heads):
            at = pl.ds(h * HEAD_DIM, HEAD_DIM)
            normal((part[:, at], total[:, at]), at)

    for copy in copies + residual:
        copy.wait()
    groups, _, columns = held.shape
    step = 512 if columns % 512 == 0 else columns
    for group in range(groups):
        for j in range(columns // step):
            at = pl.ds(group * columns + j * step, step)
            projected = jnp.dot(
                attention[...], held[group, :, pl.ds(j * step, step)], preferred_element_type=jnp.float32
            )
            out[:, at] = (
                hidden_v[:, at].astype(jnp.float32) + projected + control_v[:, at].astype(jnp.float32)
            ).astype(jnp.bfloat16)


def finish(info, q, kv, state, hidden, control, weight, moves):
    rows, inner = q.shape
    width = hidden.shape[1]
    groups = len({m[2] for m in moves})
    any_space = pl.BlockSpec(memory_space=pl.ANY)
    vmem = pl.BlockSpec(memory_space=pltpu.VMEM)
    return pl.pallas_call(
        functools.partial(finish_kernel, moves),
        out_shape=jax.ShapeDtypeStruct((rows, width), jnp.bfloat16),
        in_specs=[pl.BlockSpec(memory_space=pltpu.SMEM)] + [vmem] * 6 + [any_space] * (2 + len(weight)),
        out_specs=vmem,
        scratch_shapes=[
            pltpu.VMEM((rows, inner), jnp.bfloat16),
            pltpu.VMEM((groups, inner, width // groups), jnp.bfloat16),
            pltpu.VMEM((rows, width), jnp.bfloat16),
            pltpu.VMEM((rows, width), jnp.bfloat16),
            pltpu.SemaphoreType.DMA((len(moves),)),
            pltpu.SemaphoreType.DMA((2,)),
        ],
        compiler_params=pltpu.CompilerParams(vmem_limit_bytes=VMEM_LIMIT),
        cost_estimate=pl.CostEstimate(
            flops=2 * rows * inner * width, bytes_accessed=2 * inner * width + 6 * rows * width, transcendentals=0
        ),
        name="finish",
    )(info, q, *kv, *state, hidden, control, *weight)


def swapped(block, axis, distance):
    count = lax.axis_size(axis)
    route = []
    for low in range(count):
        high = low | 1 << distance
        if high != low and high < count:
            route += [(low, high), (high, low)]
    return lax.ppermute(block, axis, route)


def relay_control(control, across, grid_width):
    rows, width = control.shape
    slab_lines = rows // (grid_width * TILE_W)
    slab_blocks = control.reshape(slab_lines, grid_width, TILE_W, width).transpose(1, 0, 2, 3)
    slab_blocks = slab_blocks.reshape(grid_width, rows // grid_width, width)
    positions = jnp.arange(grid_width, dtype=jnp.int32)
    order = jnp.bitwise_xor(across, positions)
    buffer = jnp.take(slab_blocks, order, axis=0)
    for bit in range(grid_width.bit_length() - 1):
        low = 1 << bit
        shaped = buffer.reshape(grid_width // (2 * low), 2, low, rows // grid_width, width)
        incoming = swapped(shaped[:, 1], TILES, bit)
        buffer = jnp.stack([shaped[:, 0], incoming], axis=1).reshape(
            grid_width, rows // grid_width, width
        )
    arranged = jnp.take(buffer, order, axis=0)
    return arranged.reshape(rows, width)


def gather_weight(out_weight):
    groups = lax.axis_size("groups")
    outer, pair, cores = (lax.axis_size(a) for a in TILES)
    rows, width = out_weight.shape
    columns = width // groups
    share = lax.dynamic_slice(out_weight, (0, lax.axis_index("groups") * columns), (rows, columns))
    line = lax.all_gather(share, "outer")
    mine = lax.all_gather(line, ("groups", "pair")).reshape(groups, pair, outer, rows, columns)
    other = lax.ppermute(mine, "core", [(0, 1), (1, 0)])
    if rows % 16 == 0:
        moves = tuple(
            (piece, (g, p, o), g, (o * pair + p) * cores * rows, 1 - 2 * piece)
            for g in range(groups)
            for p in range(pair)
            for o in range(outer)
            for piece in range(2)
        )
        return (mine, other), moves
    first = lax.axis_index("core") == 0
    both = jnp.stack([jnp.where(first, mine, other), jnp.where(first, other, mine)], axis=3)
    whole = both.transpose(0, 2, 1, 3, 4, 5).reshape(groups, outer * pair * cores * rows, columns)
    return (whole,), tuple((0, (g,), g, 0, 0) for g in range(groups))


def neighbour_slots(tile_count, strides, counts):
    slots = []
    for axis, (stride, count) in enumerate(zip(strides, counts)):
        for odd in range(2):
            route = []
            for t in range(tile_count):
                place = t // stride % count
                if place % 2 == odd and place + 1 < count:
                    route += [(t, t + stride), (t + stride, t)]
            if route:
                slots.append((axis, odd, route))
    return slots


def on_device(hidden, queries, keys, values, control, out_weight, pattern):
    sizes = [lax.axis_size(a) for a in TILES]
    tile_count = math.prod(sizes)
    grid_width = min(8, tile_count // 4)
    grid_height = min(4, tile_count // 8)
    layer = grid_width * grid_height
    strides = (layer, grid_width, 1)
    counts = (tile_count // layer, grid_height, grid_width)
    position = lax.axis_index(TILES)
    weight, moves = gather_weight(out_weight)
    slots = neighbour_slots(tile_count, strides, counts)
    slots = [s for s in slots if s[0] == 2] + [s for s in slots if s[0] == 0] + [s for s in slots if s[0] == 1]
    active, near = [], []
    for axis, odd, route in slots:
        place = position // strides[axis] % counts[axis]
        up = (place % 2 == odd).astype(jnp.int32)
        valid = jnp.where(up == 1, place + 1 < counts[axis], place >= 1)
        active.append((valid & (pattern[0, 2 * axis + up] == 1)).astype(jnp.int32))
        near.append(tuple(lax.ppermute(x, TILES, route) for x in (keys, values)))
    control_tiles = relay_control(control, position % grid_width, grid_width)
    early = len([s for s in slots if s[0] == 2])
    flags = jnp.stack([jnp.ones((), jnp.int32)] + active[:early])
    state = attend(flags, queries, [keys, values] + [x for kv in near[:early] for x in kv], None)
    for number in range(early, len(slots) - 1):
        state = attend(active[number][None], queries, list(near[number]), state)
    info = jnp.stack([active[-1], lax.axis_index("core").astype(jnp.int32)])
    return finish(info, queries, near[-1], state, hidden, control_tiles, weight, moves)


def solution(mesh):
    groups = mesh.shape["groups"]
    tiles = mesh.shape["tiles"]
    split = Mesh(mesh.devices.reshape(groups, tiles // 4, 2, 2), ("groups",) + TILES)
    rows = P(("groups",) + TILES, None)
    placed = (rows, rows, rows, rows, rows, P(TILES, None), rows)
    return jax.shard_map(
        on_device,
        mesh=split,
        in_specs=placed,
        out_specs=rows,
        check_vma=False,
    )
```

```python
import functools
import math

import jax
import jax.numpy as jnp
from jax import lax
from jax.experimental import pallas as pl
from jax.experimental.pallas import tpu as pltpu
from jax.sharding import Mesh
from jax.sharding import PartitionSpec as P

HEAD_DIM = 128
TILE_W = 8
HALVES = 2
SCALE = HEAD_DIM**-0.5 * math.log2(math.e)
TILES = ("outer", "pair", "core")
VMEM_LIMIT = 40 * 1024 * 1024
VMEM = pl.BlockSpec(memory_space=pltpu.VMEM)
SMEM = pl.BlockSpec(memory_space=pltpu.SMEM)
ANY = pl.BlockSpec(memory_space=pl.ANY)


def after(x, *others):
    return lax.optimization_barrier((x, *others))[0]


def head_part(q, k, v):
    scores = lax.dot_general(q, k, (((1,), (1,)), ((), ())), preferred_element_type=jnp.float32)
    peak = jnp.max(scores, axis=1, keepdims=True)
    weights = jnp.exp2((scores - peak) * SCALE).astype(jnp.bfloat16)
    ones = jnp.ones((v.shape[0], HEAD_DIM), jnp.bfloat16)
    both = jnp.dot(weights, jnp.concatenate([v, ones], axis=1), preferred_element_type=jnp.float32)
    return both[:, :HEAD_DIM], both[:, HEAD_DIM:], jnp.broadcast_to(peak, v.shape)


def merge(old, new):
    part, total, peak = old
    part_new, total_new, peak_new = new
    top = jnp.maximum(peak, peak_new)
    f_old = jnp.exp2((peak - top) * SCALE)
    f_new = jnp.exp2((peak_new - top) * SCALE)
    return f_old * part + f_new * part_new, f_old * total + f_new * total_new, top


def fold(state, active, slot, q, first_head, kv):
    columns = kv.shape[1] // 2

    @pl.when(active[slot] == 1)
    def _():
        for h in range(columns // HEAD_DIM):
            at = pl.ds(h * HEAD_DIM, HEAD_DIM)
            new = head_part(
                q[:, pl.ds((first_head + h) * HEAD_DIM, HEAD_DIM)],
                kv[:, at],
                kv[:, pl.ds(columns + h * HEAD_DIM, HEAD_DIM)],
            )
            for r, x in zip(state, merge(tuple(r[:, at] for r in state), new)):
                r[:, at] = x


def attend_kernel(slots, first_head, active, q, own, *refs):
    near, state = refs[:slots], refs[slots:]
    columns = own.shape[1] // 2
    for h in range(columns // HEAD_DIM):
        at = pl.ds(h * HEAD_DIM, HEAD_DIM)
        new = head_part(
            q[:, pl.ds((first_head + h) * HEAD_DIM, HEAD_DIM)],
            own[:, at],
            own[:, pl.ds(columns + h * HEAD_DIM, HEAD_DIM)],
        )
        for r, x in zip(state, new):
            r[:, at] = x
    for slot in range(slots):
        fold(state, active, slot, q, first_head, near[slot])


def attend(active, q, first_head, own, near):
    rows, columns = own.shape[0], own.shape[1] // 2
    shape = jax.ShapeDtypeStruct((rows, columns), jnp.float32)
    return pl.pallas_call(
        functools.partial(attend_kernel, len(near), first_head),
        out_shape=[shape] * 3,
        in_specs=[SMEM] + [VMEM] * (2 + len(near)),
        out_specs=[VMEM] * 3,
        compiler_params=pltpu.CompilerParams(vmem_limit_bytes=VMEM_LIMIT),
        cost_estimate=pl.CostEstimate(
            flops=(1 + len(near)) * 6 * rows * rows * columns,
            bytes_accessed=rows * columns * (4 + 4 * len(near) + 12),
            transcendentals=0,
        ),
        name="attend",
    )(active, q, own, *near)


def close_kernel(slots, first_head, active, q, part, total, peak, *refs):
    near, out, state = refs[:slots], refs[slots], refs[slots + 1 :]
    for r, x in zip(state, (part, total, peak)):
        r[...] = x[...]
    for slot in range(slots):
        fold(state, active, slot, q, first_head, near[slot])
    out[...] = (state[0][...] / state[1][...]).astype(jnp.bfloat16)


def close(active, q, first_head, state, near):
    rows, columns = state[0].shape
    return pl.pallas_call(
        functools.partial(close_kernel, len(near), first_head),
        out_shape=jax.ShapeDtypeStruct((rows, columns), jnp.bfloat16),
        in_specs=[SMEM] + [VMEM] * (4 + len(near)),
        out_specs=VMEM,
        scratch_shapes=[pltpu.VMEM((rows, columns), jnp.float32)] * 3,
        compiler_params=pltpu.CompilerParams(vmem_limit_bytes=VMEM_LIMIT),
        cost_estimate=pl.CostEstimate(
            flops=len(near) * 6 * rows * rows * columns,
            bytes_accessed=rows * columns * (4 * len(near) + 16),
            transcendentals=0,
        ),
        name="close",
    )(active, q, *state, *near)


def finish_kernel(slots, blocks, moves, control_rows, place, active, q, ready, part, total, peak, *refs):
    near, refs = refs[:slots], refs[slots:]
    hidden, refs = refs[0], refs[1:]
    control, refs = refs[:blocks], refs[blocks:]
    pieces = len({m[0] for m in moves})
    weight, refs = refs[:pieces], refs[pieces:]
    out, attention, held, hidden_v, control_v, *state, sems, res_sems = refs
    copies = []
    for number, (piece, index, flips) in enumerate(moves):
        source = weight[piece].at[index] if index else weight[piece]
        if flips is None:
            target = held
        else:
            count = source.shape[0]
            (group, pair), outer_flip, core_flip = flips
            outer, core = place[1] ^ outer_flip, place[3] ^ core_flip
            start = pl.multiple_of(((outer * 2 + pair) * 2 + core) * count, count)
            target = held.at[group, pl.ds(start, count), :]
        copies.append(pltpu.make_async_copy(source, target, sems.at[number]))
    copies.append(pltpu.make_async_copy(hidden, hidden_v, res_sems.at[blocks]))
    for d in range(blocks):
        start = pl.multiple_of((place[4] ^ d) * control_rows, control_rows) if blocks > 1 else 0
        copies.append(
            pltpu.make_async_copy(control[d], control_v.at[pl.ds(start, control_rows), :], res_sems.at[d])
        )
    for copy in copies:
        copy.start()
    rows, done = ready.shape
    for r, x in zip(state, (part, total, peak)):
        r[...] = x[...]
    for slot in range(slots):
        fold(state, active, slot, q, done // HEAD_DIM, near[slot])
    attention[:, pl.ds(0, done)] = ready[...]
    attention[:, pl.ds(done, part.shape[1])] = (state[0][...] / state[1][...]).astype(jnp.bfloat16)
    for copy in copies:
        copy.wait()
    groups, _, columns = held.shape
    step = 512 if columns % 512 == 0 else columns
    for group in range(groups):
        for j in range(columns // step):
            at = pl.ds(group * columns + j * step, step)
            projected = jnp.dot(
                attention[...], held[group, :, pl.ds(j * step, step)], preferred_element_type=jnp.float32
            )
            out[:, at] = (
                hidden_v[:, at].astype(jnp.float32) + projected + control_v[:, at].astype(jnp.float32)
            ).astype(jnp.bfloat16)


def finish(place, active, q, ready, state, near, hidden, control, weight, moves):
    rows, inner = q.shape
    width = hidden.shape[1]
    groups = lax.axis_size("groups")
    control_rows = control[0].shape[0]
    columns = state[0].shape[1]
    return pl.pallas_call(
        functools.partial(finish_kernel, len(near), len(control), moves, control_rows),
        out_shape=jax.ShapeDtypeStruct((rows, width), jnp.bfloat16),
        in_specs=[SMEM] * 2 + [VMEM] * (5 + len(near)) + [ANY] * (1 + len(control) + len(weight)),
        out_specs=VMEM,
        scratch_shapes=[
            pltpu.VMEM((rows, inner), jnp.bfloat16),
            pltpu.VMEM((groups, inner, width // groups), jnp.bfloat16),
            pltpu.VMEM((rows, width), jnp.bfloat16),
            pltpu.VMEM((rows, width), jnp.bfloat16),
        ]
        + [pltpu.VMEM((rows, columns), jnp.float32)] * 3
        + [
            pltpu.SemaphoreType.DMA((len(moves),)),
            pltpu.SemaphoreType.DMA((len(control) + 1,)),
        ],
        compiler_params=pltpu.CompilerParams(vmem_limit_bytes=VMEM_LIMIT),
        cost_estimate=pl.CostEstimate(
            flops=2 * rows * inner * width, bytes_accessed=2 * inner * width + 6 * rows * width, transcendentals=0
        ),
        name="finish",
    )(place, active, q, ready, *state, *near, hidden, *control, *weight)


def flipped(block, axis, flip):
    return lax.ppermute(block, axis, [(i, i ^ flip) for i in range(lax.axis_size(axis))])


def control_blocks(control, across, grid_width, wait_for):
    rows, width = control.shape
    block = rows // grid_width
    lines = control.reshape(block // TILE_W, grid_width, TILE_W, width)
    blocks = []
    for d in range(grid_width):
        mine = lax.dynamic_index_in_dim(lines, across ^ d, 1, keepdims=False).reshape(block, width)
        blocks.append(flipped(after(mine, *wait_for) if d > 1 else mine, TILES, d) if d else mine)
    if block % 16 == 0:
        return blocks
    order = jnp.arange(grid_width, dtype=jnp.int32) ^ across
    return [jnp.take(jnp.stack(blocks), order, axis=0).reshape(rows, width)]


def gather_weight(out_weight):
    groups = lax.axis_size("groups")
    outer, pair, cores = (lax.axis_size(a) for a in TILES)
    rows, width = out_weight.shape
    columns = width // groups
    share = lax.dynamic_slice(out_weight, (0, lax.axis_index("groups") * columns), (rows, columns))
    line = share[None]
    flip = outer // 2
    while flip > 2:
        line = jnp.concatenate([line, flipped(line, "outer", flip)])
        flip //= 2
    far = flipped(line, "outer", 2)
    near = flipped(line, "outer", 1)
    last = flipped(far, "outer", 1)
    steps = [line, jnp.concatenate([far, near, last])]
    flips = [sum(((outer // 2) >> b) * (i >> b & 1) for b in range(outer.bit_length() - 1)) for i in range(outer // 4)]
    flips = [flips, [f ^ x for x in (2, 1, 3) for f in flips]]
    mine = [lax.all_gather(x, ("groups", "pair")) for x in steps]
    other = [flipped(x, "core", 1) for x in mine]
    if rows % 16 == 0:
        moves = tuple(
            (2 * step + core, (g * pair + p, i), ((g, p), f, core))
            for step in range(2)
            for core in range(2)
            for g in range(groups)
            for p in range(pair)
            for i, f in enumerate(flips[step])
        )
        return [x for pair_of in zip(mine, other) for x in pair_of], moves, far, last
    whole = [jnp.concatenate(x, axis=1) for x in (mine, other)]
    order = jnp.array([flips_all.index(f) for flips_all in [flips[0] + flips[1]] for f in range(outer)], jnp.int32)
    whole = [jnp.take(x, order[jnp.arange(outer) ^ lax.axis_index("outer")], axis=1) for x in whole]
    first = lax.axis_index("core") == 0
    both = jnp.stack([jnp.where(first, whole[0], whole[1]), jnp.where(first, whole[1], whole[0])], axis=2)
    both = both.reshape(groups, pair, outer, cores, rows, columns).transpose(0, 2, 1, 3, 4, 5)
    whole = both.reshape(groups, outer * pair * cores * rows, columns)
    return [whole], ((0, None, None),), far, last


def neighbour_slots(tile_count, strides, counts):
    slots = []
    for axis, (stride, count) in enumerate(zip(strides, counts)):
        for odd in range(2):
            route = []
            for t in range(tile_count):
                place = t // stride % count
                if place % 2 == odd and place + 1 < count:
                    route += [(t, t + stride), (t + stride, t)]
            if route:
                slots.append((axis, odd, route))
    return slots


def on_device(hidden, queries, keys, values, control, out_weight, pattern):
    sizes = [lax.axis_size(a) for a in TILES]
    tile_count = math.prod(sizes)
    grid_width = min(8, tile_count // 4)
    grid_height = min(4, tile_count // 8)
    layer = grid_width * grid_height
    strides = (layer, grid_width, 1)
    counts = (tile_count // layer, grid_height, grid_width)
    position = lax.axis_index(TILES)
    across = position % grid_width
    weight, moves, far, last = gather_weight(out_weight)
    columns = queries.shape[1] // HALVES
    kv = [
        jnp.concatenate([x[:, half * columns : (half + 1) * columns] for x in (keys, values)], axis=1)
        for half in range(HALVES)
    ]
    slots = neighbour_slots(tile_count, strides, counts)
    early = [s for s in slots if s[0] == 2]
    late = [s for s in slots if s[0] != 2]

    def flags(chosen):
        active = []
        for axis, odd, _ in chosen:
            place = position // strides[axis] % counts[axis]
            up = (place % 2 == odd).astype(jnp.int32)
            valid = jnp.where(up == 1, place + 1 < counts[axis], place >= 1)
            active.append((valid & (pattern[0, 2 * axis + up] == 1)).astype(jnp.int32))
        return jnp.stack(active)

    early_active, late_active = flags(early), flags(late)
    early_near, late_near = [], []
    for half in range(HALVES):
        early_near.append([])
        for axis, odd, route in early:
            block = kv[half] if odd == 0 else after(kv[half], far)
            early_near[half].append(lax.ppermute(block, TILES, route))
        waits = [far, last] if half == 0 else late_near[-1]
        late_near.append(
            [lax.ppermute(after(kv[half], waits[i % 2]), TILES, route) for i, (_, _, route) in enumerate(late)]
        )
    control_parts = control_blocks(control, across, grid_width, (far,))
    heads = columns // HEAD_DIM
    states = [attend(early_active, queries, half * heads, kv[half], early_near[half]) for half in range(HALVES)]
    ready = [close(late_active, queries, half * heads, states[half], late_near[half]) for half in range(HALVES - 1)]
    ready = ready[0] if len(ready) == 1 else jnp.concatenate(ready, axis=1)
    place = jnp.stack([lax.axis_index(a) for a in ("groups",) + TILES] + [across]).astype(jnp.int32)
    return finish(
        place, late_active, queries, ready, states[-1], late_near[-1], hidden, control_parts, weight, moves
    )


def solution(mesh):
    groups = mesh.shape["groups"]
    tiles = mesh.shape["tiles"]
    split = Mesh(mesh.devices.reshape(groups, tiles // 4, 2, 2), ("groups",) + TILES)
    rows = P(("groups",) + TILES, None)
    placed = (rows, rows, rows, rows, rows, P(TILES, None), rows)
    return jax.shard_map(
        on_device,
        mesh=split,
        in_specs=placed,
        out_specs=rows,
        check_vma=False,
    )
```

```python
import functools
import math

import jax
import jax.numpy as jnp
from jax import lax
from jax.experimental import pallas as pl
from jax.experimental.pallas import tpu as pltpu
from jax.sharding import Mesh
from jax.sharding import PartitionSpec as P

HEAD_DIM = 128
TILE_W = 8
HALVES = 2
SCALE = HEAD_DIM**-0.5 * math.log2(math.e)
TILES = ("outer", "pair", "core")
VMEM_LIMIT = 40 * 1024 * 1024
VMEM = pl.BlockSpec(memory_space=pltpu.VMEM)
SMEM = pl.BlockSpec(memory_space=pltpu.SMEM)
ANY = pl.BlockSpec(memory_space=pl.ANY)


def after(x, *others):
    return lax.optimization_barrier((x, *others))[0]


def head_part(q, k, v):
    scores = lax.dot_general(q, k, (((1,), (1,)), ((), ())), preferred_element_type=jnp.float32)
    peak = jnp.max(scores, axis=1, keepdims=True)
    weights = jnp.exp2((scores - peak) * SCALE).astype(jnp.bfloat16)
    ones = jnp.ones((v.shape[0], HEAD_DIM), jnp.bfloat16)
    both = jnp.dot(weights, jnp.concatenate([v, ones], axis=1), preferred_element_type=jnp.float32)
    return both[:, :HEAD_DIM], both[:, HEAD_DIM:], jnp.broadcast_to(peak, v.shape)


def merge(old, new):
    part, total, peak = old
    part_new, total_new, peak_new = new
    top = jnp.maximum(peak, peak_new)
    f_old = jnp.exp2((peak - top) * SCALE)
    f_new = jnp.exp2((peak_new - top) * SCALE)
    return f_old * part + f_new * part_new, f_old * total + f_new * total_new, top


def fold(state, active, slot, q, first_head, kv):
    columns = kv.shape[1] // 2

    @pl.when(active[slot] == 1)
    def _():
        for h in range(columns // HEAD_DIM):
            at = pl.ds(h * HEAD_DIM, HEAD_DIM)
            new = head_part(
                q[:, pl.ds((first_head + h) * HEAD_DIM, HEAD_DIM)],
                kv[:, at],
                kv[:, pl.ds(columns + h * HEAD_DIM, HEAD_DIM)],
            )
            for r, x in zip(state, merge(tuple(r[:, at] for r in state), new)):
                r[:, at] = x


def attend_kernel(slots, first_head, active, q, own, *refs):
    near, state = refs[:slots], refs[slots:]
    columns = own.shape[1] // 2
    for h in range(columns // HEAD_DIM):
        at = pl.ds(h * HEAD_DIM, HEAD_DIM)
        new = head_part(
            q[:, pl.ds((first_head + h) * HEAD_DIM, HEAD_DIM)],
            own[:, at],
            own[:, pl.ds(columns + h * HEAD_DIM, HEAD_DIM)],
        )
        for r, x in zip(state, new):
            r[:, at] = x
    for slot in range(slots):
        fold(state, active, slot, q, first_head, near[slot])


def attend(active, q, first_head, own, near):
    rows, columns = own.shape[0], own.shape[1] // 2
    shape = jax.ShapeDtypeStruct((rows, columns), jnp.float32)
    return pl.pallas_call(
        functools.partial(attend_kernel, len(near), first_head),
        out_shape=[shape] * 3,
        in_specs=[SMEM] + [VMEM] * (2 + len(near)),
        out_specs=[VMEM] * 3,
        compiler_params=pltpu.CompilerParams(vmem_limit_bytes=VMEM_LIMIT),
        cost_estimate=pl.CostEstimate(
            flops=(1 + len(near)) * 6 * rows * rows * columns,
            bytes_accessed=rows * columns * (4 + 4 * len(near) + 12),
            transcendentals=0,
        ),
        name="attend",
    )(active, q, own, *near)


def close_kernel(slots, first_head, active, q, part, total, peak, *refs):
    near, out, state = refs[:slots], refs[slots], refs[slots + 1 :]
    for r, x in zip(state, (part, total, peak)):
        r[...] = x[...]
    for slot in range(slots):
        fold(state, active, slot, q, first_head, near[slot])
    out[...] = (state[0][...] / state[1][...]).astype(jnp.bfloat16)


def close(active, q, first_head, state, near):
    rows, columns = state[0].shape
    return pl.pallas_call(
        functools.partial(close_kernel, len(near), first_head),
        out_shape=jax.ShapeDtypeStruct((rows, columns), jnp.bfloat16),
        in_specs=[SMEM] + [VMEM] * (4 + len(near)),
        out_specs=VMEM,
        scratch_shapes=[pltpu.VMEM((rows, columns), jnp.float32)] * 3,
        compiler_params=pltpu.CompilerParams(vmem_limit_bytes=VMEM_LIMIT),
        cost_estimate=pl.CostEstimate(
            flops=len(near) * 6 * rows * rows * columns,
            bytes_accessed=rows * columns * (4 * len(near) + 16),
            transcendentals=0,
        ),
        name="close",
    )(active, q, *state, *near)


def finish_kernel(slots, blocks, moves, control_rows, place, active, q, ready, part, total, peak, *refs):
    near, refs = refs[:slots], refs[slots:]
    hidden, refs = refs[0], refs[1:]
    control, refs = refs[:blocks], refs[blocks:]
    pieces = len({m[0] for m in moves})
    weight, refs = refs[:pieces], refs[pieces:]
    out, attention, held, hidden_v, control_v, *state, sems, res_sems = refs
    copies = []
    for number, (piece, index, flips) in enumerate(moves):
        source = weight[piece].at[index] if flips else weight[piece]
        if flips is None:
            target = held
        else:
            count = source.shape[0]
            group, outer, pair, core = (place[i] ^ flip for i, flip in enumerate(flips))
            start = pl.multiple_of(((outer * 2 + pair) * 2 + core) * count, count)
            target = held.at[group, pl.ds(start, count), :]
        copies.append(pltpu.make_async_copy(source, target, sems.at[number]))
    copies.append(pltpu.make_async_copy(hidden, hidden_v, res_sems.at[blocks]))
    for d in range(blocks):
        start = pl.multiple_of((place[4] ^ d) * control_rows, control_rows) if blocks > 1 else 0
        copies.append(
            pltpu.make_async_copy(control[d], control_v.at[pl.ds(start, control_rows), :], res_sems.at[d])
        )
    for copy in copies:
        copy.start()
    rows, done = ready.shape
    for r, x in zip(state, (part, total, peak)):
        r[...] = x[...]
    for slot in range(slots):
        fold(state, active, slot, q, done // HEAD_DIM, near[slot])
    attention[:, pl.ds(0, done)] = ready[...]
    attention[:, pl.ds(done, part.shape[1])] = (state[0][...] / state[1][...]).astype(jnp.bfloat16)
    for copy in copies:
        copy.wait()
    groups, _, columns = held.shape
    step = 512 if columns % 512 == 0 else columns
    for group in range(groups):
        for j in range(columns // step):
            at = pl.ds(group * columns + j * step, step)
            projected = jnp.dot(
                attention[...], held[group, :, pl.ds(j * step, step)], preferred_element_type=jnp.float32
            )
            out[:, at] = (
                hidden_v[:, at].astype(jnp.float32) + projected + control_v[:, at].astype(jnp.float32)
            ).astype(jnp.bfloat16)


def finish(place, active, q, ready, state, near, hidden, control, weight, moves):
    rows, inner = q.shape
    width = hidden.shape[1]
    groups = lax.axis_size("groups")
    control_rows = control[0].shape[0]
    columns = state[0].shape[1]
    return pl.pallas_call(
        functools.partial(finish_kernel, len(near), len(control), moves, control_rows),
        out_shape=jax.ShapeDtypeStruct((rows, width), jnp.bfloat16),
        in_specs=[SMEM] * 2 + [VMEM] * (5 + len(near)) + [ANY] * (1 + len(control) + len(weight)),
        out_specs=VMEM,
        scratch_shapes=[
            pltpu.VMEM((rows, inner), jnp.bfloat16),
            pltpu.VMEM((groups, inner, width // groups), jnp.bfloat16),
            pltpu.VMEM((rows, width), jnp.bfloat16),
            pltpu.VMEM((rows, width), jnp.bfloat16),
        ]
        + [pltpu.VMEM((rows, columns), jnp.float32)] * 3
        + [
            pltpu.SemaphoreType.DMA((len(moves),)),
            pltpu.SemaphoreType.DMA((len(control) + 1,)),
        ],
        compiler_params=pltpu.CompilerParams(vmem_limit_bytes=VMEM_LIMIT),
        cost_estimate=pl.CostEstimate(
            flops=2 * rows * inner * width, bytes_accessed=2 * inner * width + 6 * rows * width, transcendentals=0
        ),
        name="finish",
    )(place, active, q, ready, *state, *near, hidden, *control, *weight)


def flipped(block, axis, flip):
    return lax.ppermute(block, axis, [(i, i ^ flip) for i in range(lax.axis_size(axis))])


class Lane:
    def __init__(self):
        self.last = None

    def __call__(self, send, block, *others):
        waits = [x for x in (self.last, *others) if x is not None]
        self.last = send(after(block, *waits) if waits else block)
        return self.last


def swap(axis, flip):
    return lambda block: flipped(block, axis, flip)


def route_of(route):
    return lambda block: lax.ppermute(block, TILES, route)


def copy_kernel(count, moves, start, *refs):
    sources, targets, sems = refs[:count], refs[count:-1], refs[-1]
    copies = []
    for number, (source, source_at, target, target_at) in enumerate(moves):
        column, columns, times = source_at
        column = pl.multiple_of(start[0] * columns, 128) if times else column
        from_ref = sources[source].at[..., pl.ds(column, columns)]
        copies.append(pltpu.make_async_copy(from_ref, targets[target].at[target_at], sems.at[number]))
    for copy in copies:
        copy.start()
    for copy in copies:
        copy.wait()


def copied(start, arrays, shapes, moves, name):
    return pl.pallas_call(
        functools.partial(copy_kernel, len(arrays), moves),
        out_shape=[jax.ShapeDtypeStruct(shape, jnp.bfloat16) for shape in shapes],
        in_specs=[SMEM] + [ANY] * len(arrays),
        out_specs=[ANY] * len(shapes),
        scratch_shapes=[pltpu.SemaphoreType.DMA((len(moves),))],
        cost_estimate=pl.CostEstimate(
            flops=0, bytes_accessed=4 * sum(math.prod(shape) for shape in shapes), transcendentals=0
        ),
        name=name,
    )(start, *arrays)


def stacked(a, b):
    if a.shape[1] % 16:
        return jnp.concatenate([a, b])
    n, rows, columns = a.shape
    whole = (0, columns, False)
    moves = ((0, whole, 0, pl.ds(0, n)), (1, whole, 0, pl.ds(n, n)))
    return copied(jnp.zeros(1, jnp.int32), (a, b), [(2 * n, rows, columns)], moves, "stacked")[0]


def neighbour_slots(tile_count, strides, counts):
    slots = []
    for axis, (stride, count) in enumerate(zip(strides, counts)):
        for odd in range(2):
            route = []
            for t in range(tile_count):
                place = t // stride % count
                if place % 2 == odd and place + 1 < count:
                    route += [(t, t + stride), (t + stride, t)]
            if route:
                slots.append((axis, odd, route))
    return slots


def on_device(hidden, queries, keys, values, control, out_weight, pattern):
    groups = lax.axis_size("groups")
    outer, pair, cores = (lax.axis_size(a) for a in TILES)
    tile_count = outer * pair * cores
    grid_width = min(8, tile_count // 4)
    grid_height = min(4, tile_count // 8)
    layer = grid_width * grid_height
    strides = (layer, grid_width, 1)
    counts = (tile_count // layer, grid_height, grid_width)
    position = lax.axis_index(TILES)
    across = position % grid_width
    rows, inner = queries.shape
    width = hidden.shape[1]
    columns = inner // HALVES
    heads = columns // HEAD_DIM
    slots = neighbour_slots(tile_count, strides, counts)
    early = [s for s in slots if s[0] == 2]
    late = [s for s in slots if s[0] != 2]

    def flags(chosen):
        active = []
        for axis, odd, _ in chosen:
            place = position // strides[axis] % counts[axis]
            up = (place % 2 == odd).astype(jnp.int32)
            valid = jnp.where(up == 1, place + 1 < counts[axis], place >= 1)
            active.append((valid & (pattern[0, 2 * axis + up] == 1)).astype(jnp.int32))
        return jnp.stack(active)

    early_active, late_active = flags(early), flags(late)
    far_lane, near_lane, x_lane, y_lane, core_lane = (Lane() for _ in range(5))

    shard, share = out_weight.shape[0], width // groups
    group = lax.axis_index("groups").astype(jnp.int32)
    line = copied(
        group[None], (out_weight,), [(1, shard, share)], ((0, (0, share, True), 0, 0),), "share"
    )[0]
    line_flips = [0]
    flip = outer // 2
    while flip > 2:
        line = jnp.concatenate([line, flipped(line, "outer", flip)])
        line_flips += [f ^ flip for f in line_flips]
        flip //= 2
    far = far_lane(swap("outer", 2), line)
    near = near_lane(swap("outer", 1), line)
    last = near_lane(swap("outer", 1), far)
    parts = [(line, 0), (far, 2), (near, 1), (last, 3)]

    halves = copied(
        group[None],
        (keys, values),
        [(rows, 2 * columns)] * HALVES,
        tuple(
            (source, (half * columns, columns, False), half, (slice(None), pl.ds(source * columns, columns)))
            for half in range(HALVES)
            for source in range(2)
        ),
        "halves",
    )
    block = rows // grid_width
    lines = control.reshape(block // TILE_W, grid_width, TILE_W, width)
    control_sent = [
        lax.dynamic_index_in_dim(lines, across ^ d, 1, keepdims=False).reshape(block, width) for d in range(grid_width)
    ]
    control_parts = [control_sent[0]] + [None] * (grid_width - 1)
    control_parts[1] = core_lane(swap(TILES, 1), control_sent[1])
    early_near = [[None] * len(early) for _ in range(HALVES)]
    for half in range(HALVES):
        early_near[half][0] = core_lane(route_of(early[0][2]), halves[half])

    held = []
    for piece, _ in parts:
        beside = x_lane(swap("pair", 1), piece)
        plane = stacked(piece, beside)
        held.append((plane, y_lane(swap("groups", 1), plane)))
    order = [(0, 0), (0, 1), (1, 0), (2, 0), (1, 1), (3, 0), (2, 1), (3, 1)]
    crossed = {at: core_lane(swap("core", 1), held[at[0]][at[1]]) for at in order}
    weight, moves = [], []
    for number, (_, outer_flip) in enumerate(parts):
        for y_flip in range(2):
            for core_flip in range(2):
                n = len(line_flips)
                moves += [
                    (len(weight), i, (y_flip, line_flips[i % n] ^ outer_flip, i // n, core_flip)) for i in range(2 * n)
                ]
                weight.append(crossed[number, y_flip] if core_flip else held[number][y_flip])

    late_near = []
    lanes = [far_lane, near_lane]
    for half in range(HALVES):
        late_near.append([lanes[i % 2](route_of(route), halves[half]) for i, (_, _, route) in enumerate(late)])
    for half in range(HALVES):
        for i in range(1, len(early)):
            early_near[half][i] = x_lane(route_of(early[i][2]), halves[half])
        for d in range(2 + half, grid_width, HALVES):
            control_parts[d] = x_lane(swap(TILES, d), control_sent[d])

    states = [attend(early_active, queries, half * heads, halves[half], early_near[half]) for half in range(HALVES)]
    ready = [close(late_active, queries, half * heads, states[half], late_near[half]) for half in range(HALVES - 1)]
    ready = ready[0] if len(ready) == 1 else jnp.concatenate(ready, axis=1)
    if block % 16:
        control_parts = [
            jnp.take(
                jnp.stack(control_parts), jnp.arange(grid_width, dtype=jnp.int32) ^ across, axis=0
            ).reshape(rows, width)
        ]
    place = jnp.stack([lax.axis_index(a) for a in ("groups",) + TILES] + [across]).astype(jnp.int32)
    if shard % 16:
        weight, moves = [in_order(weight, moves, place, (groups, outer, pair, cores))], [(0, None, None)]
    return finish(
        place,
        late_active,
        queries,
        ready,
        states[-1],
        late_near[-1],
        hidden,
        control_parts,
        weight,
        tuple(moves),
    )


def in_order(weight, moves, place, sizes):
    blocks = {flips: weight[piece][index] for piece, index, flips in moves}
    whole = jnp.stack([blocks[flips] for flips in sorted(blocks)])
    shard, columns = whole.shape[1:]
    whole = whole.reshape(sizes + (shard, columns))
    for axis, size in enumerate(sizes):
        whole = jnp.take(whole, jnp.arange(size, dtype=jnp.int32) ^ place[axis], axis=axis)
    return whole.reshape(sizes[0], -1, columns)


def solution(mesh):
    groups = mesh.shape["groups"]
    tiles = mesh.shape["tiles"]
    split = Mesh(mesh.devices.reshape(groups, tiles // 4, 2, 2), ("groups",) + TILES)
    rows = P(("groups",) + TILES, None)
    placed = (rows, rows, rows, rows, rows, P(TILES, None), rows)
    return jax.shard_map(
        on_device,
        mesh=split,
        in_specs=placed,
        out_specs=rows,
        check_vma=False,
    )
```

```python
import functools
import math

import jax
import jax.numpy as jnp
from jax import lax
from jax.experimental import pallas as pl
from jax.experimental.pallas import tpu as pltpu
from jax.sharding import Mesh
from jax.sharding import PartitionSpec as P

HEAD_DIM = 128
TILE_W = 8
HALVES = 2
SCALE = HEAD_DIM**-0.5 * math.log2(math.e)
TILES = ("outer", "pair", "core")
VMEM_LIMIT = 40 * 1024 * 1024
VMEM = pl.BlockSpec(memory_space=pltpu.VMEM)
SMEM = pl.BlockSpec(memory_space=pltpu.SMEM)
ANY = pl.BlockSpec(memory_space=pl.ANY)


def after(x, *others):
    return lax.optimization_barrier((x, *others))[0]


def head_part(q, k, v):
    scores = lax.dot_general(q, k, (((1,), (1,)), ((), ())), preferred_element_type=jnp.float32)
    peak = jnp.max(scores, axis=1, keepdims=True)
    weights = jnp.exp2((scores - peak) * SCALE).astype(jnp.bfloat16)
    ones = jnp.ones((v.shape[0], HEAD_DIM), jnp.bfloat16)
    both = jnp.dot(weights, jnp.concatenate([v, ones], axis=1), preferred_element_type=jnp.float32)
    return both[:, :HEAD_DIM], both[:, HEAD_DIM:], jnp.broadcast_to(peak, v.shape)


def merge(old, new):
    part, total, peak = old
    part_new, total_new, peak_new = new
    top = jnp.maximum(peak, peak_new)
    f_old = jnp.exp2((peak - top) * SCALE)
    f_new = jnp.exp2((peak_new - top) * SCALE)
    return f_old * part + f_new * part_new, f_old * total + f_new * total_new, top


def fold(state, active, slot, q, first_head, kv):
    columns = kv.shape[1] // 2

    @pl.when(active[slot] == 1)
    def _():
        for h in range(columns // HEAD_DIM):
            at = pl.ds(h * HEAD_DIM, HEAD_DIM)
            new = head_part(
                q[:, pl.ds((first_head + h) * HEAD_DIM, HEAD_DIM)],
                kv[:, at],
                kv[:, pl.ds(columns + h * HEAD_DIM, HEAD_DIM)],
            )
            for r, x in zip(state, merge(tuple(r[:, at] for r in state), new)):
                r[:, at] = x


def attend_kernel(slots, first_head, active, q, own, *refs):
    near, state = refs[:slots], refs[slots:]
    columns = own.shape[1] // 2
    for h in range(columns // HEAD_DIM):
        at = pl.ds(h * HEAD_DIM, HEAD_DIM)
        new = head_part(
            q[:, pl.ds((first_head + h) * HEAD_DIM, HEAD_DIM)],
            own[:, at],
            own[:, pl.ds(columns + h * HEAD_DIM, HEAD_DIM)],
        )
        for r, x in zip(state, new):
            r[:, at] = x
    for slot in range(slots):
        fold(state, active, slot, q, first_head, near[slot])


def attend(active, q, first_head, own, near):
    rows, columns = own.shape[0], own.shape[1] // 2
    shape = jax.ShapeDtypeStruct((rows, columns), jnp.float32)
    return pl.pallas_call(
        functools.partial(attend_kernel, len(near), first_head),
        out_shape=[shape] * 3,
        in_specs=[SMEM] + [VMEM] * (2 + len(near)),
        out_specs=[VMEM] * 3,
        compiler_params=pltpu.CompilerParams(vmem_limit_bytes=VMEM_LIMIT),
        cost_estimate=pl.CostEstimate(
            flops=(1 + len(near)) * 6 * rows * rows * columns,
            bytes_accessed=rows * columns * (4 + 4 * len(near) + 12),
            transcendentals=0,
        ),
        name="attend",
    )(active, q, own, *near)


def close_kernel(slots, first_head, active, q, part, total, peak, *refs):
    near, out, state = refs[:slots], refs[slots], refs[slots + 1 :]
    for r, x in zip(state, (part, total, peak)):
        r[...] = x[...]
    for slot in range(slots):
        fold(state, active, slot, q, first_head, near[slot])
    out[...] = (state[0][...] / state[1][...]).astype(jnp.bfloat16)


def close(active, q, first_head, state, near):
    rows, columns = state[0].shape
    return pl.pallas_call(
        functools.partial(close_kernel, len(near), first_head),
        out_shape=jax.ShapeDtypeStruct((rows, columns), jnp.bfloat16),
        in_specs=[SMEM] + [VMEM] * (4 + len(near)),
        out_specs=VMEM,
        scratch_shapes=[pltpu.VMEM((rows, columns), jnp.float32)] * 3,
        compiler_params=pltpu.CompilerParams(vmem_limit_bytes=VMEM_LIMIT),
        cost_estimate=pl.CostEstimate(
            flops=len(near) * 6 * rows * rows * columns,
            bytes_accessed=rows * columns * (4 * len(near) + 16),
            transcendentals=0,
        ),
        name="close",
    )(active, q, *state, *near)


def finish_kernel(slots, blocks, moves, control_rows, place, active, q, ready, part, total, peak, *refs):
    near, refs = refs[:slots], refs[slots:]
    hidden, refs = refs[0], refs[1:]
    control, refs = refs[:blocks], refs[blocks:]
    pieces = len({m[0] for m in moves})
    weight, refs = refs[:pieces], refs[pieces:]
    out, attention, held, hidden_v, control_v, *state, sems, res_sems = refs
    copies = []
    for number, (piece, index, flips) in enumerate(moves):
        source = weight[piece].at[index] if flips else weight[piece]
        if flips is None:
            target = held
        else:
            count = source.shape[0]
            group, pair, core, flip = flips
            outer = place[1] ^ flip
            start = pl.multiple_of(((outer * 2 + pair) * 2 + core) * count, count)
            target = held.at[group, pl.ds(start, count), :]
        copies.append(pltpu.make_async_copy(source, target, sems.at[number]))
    copies.append(pltpu.make_async_copy(hidden, hidden_v, res_sems.at[blocks]))
    for d in range(blocks):
        start = pl.multiple_of((place[4] ^ d) * control_rows, control_rows) if blocks > 1 else 0
        copies.append(
            pltpu.make_async_copy(control[d], control_v.at[pl.ds(start, control_rows), :], res_sems.at[d])
        )
    for copy in copies:
        copy.start()
    rows, done = ready.shape
    for r, x in zip(state, (part, total, peak)):
        r[...] = x[...]
    for slot in range(slots):
        fold(state, active, slot, q, done // HEAD_DIM, near[slot])
    attention[:, pl.ds(0, done)] = ready[...]
    attention[:, pl.ds(done, part.shape[1])] = (state[0][...] / state[1][...]).astype(jnp.bfloat16)
    for copy in copies:
        copy.wait()
    groups, _, columns = held.shape
    step = 512 if columns % 512 == 0 else columns
    for group in range(groups):
        for j in range(columns // step):
            at = pl.ds(group * columns + j * step, step)
            projected = jnp.dot(
                attention[...], held[group, :, pl.ds(j * step, step)], preferred_element_type=jnp.float32
            )
            out[:, at] = (
                hidden_v[:, at].astype(jnp.float32) + projected + control_v[:, at].astype(jnp.float32)
            ).astype(jnp.bfloat16)


def finish(place, active, q, ready, state, near, hidden, control, weight, moves):
    rows, inner = q.shape
    width = hidden.shape[1]
    groups = lax.axis_size("groups")
    control_rows = control[0].shape[0]
    columns = state[0].shape[1]
    return pl.pallas_call(
        functools.partial(finish_kernel, len(near), len(control), moves, control_rows),
        out_shape=jax.ShapeDtypeStruct((rows, width), jnp.bfloat16),
        in_specs=[SMEM] * 2 + [VMEM] * (5 + len(near)) + [ANY] * (1 + len(control) + len(weight)),
        out_specs=VMEM,
        scratch_shapes=[
            pltpu.VMEM((rows, inner), jnp.bfloat16),
            pltpu.VMEM((groups, inner, width // groups), jnp.bfloat16),
            pltpu.VMEM((rows, width), jnp.bfloat16),
            pltpu.VMEM((rows, width), jnp.bfloat16),
        ]
        + [pltpu.VMEM((rows, columns), jnp.float32)] * 3
        + [
            pltpu.SemaphoreType.DMA((len(moves),)),
            pltpu.SemaphoreType.DMA((len(control) + 1,)),
        ],
        compiler_params=pltpu.CompilerParams(vmem_limit_bytes=VMEM_LIMIT),
        cost_estimate=pl.CostEstimate(
            flops=2 * rows * inner * width, bytes_accessed=2 * inner * width + 6 * rows * width, transcendentals=0
        ),
        name="finish",
    )(place, active, q, ready, *state, *near, hidden, *control, *weight)


def flipped(block, axis, flip):
    return lax.ppermute(block, axis, [(i, i ^ flip) for i in range(lax.axis_size(axis))])


class Lane:
    def __init__(self):
        self.last = None

    def __call__(self, send, block, *others):
        waits = [x for x in (self.last, *others) if x is not None]
        self.last = send(after(block, *waits) if waits else block)
        return self.last


def swap(axis, flip):
    return lambda block: flipped(block, axis, flip)


def route_of(route):
    return lambda block: lax.ppermute(block, TILES, route)


def neighbour_slots(tile_count, strides, counts):
    slots = []
    for axis, (stride, count) in enumerate(zip(strides, counts)):
        for odd in range(2):
            route = []
            for t in range(tile_count):
                place = t // stride % count
                if place % 2 == odd and place + 1 < count:
                    route += [(t, t + stride), (t + stride, t)]
            if route:
                slots.append((axis, odd, route))
    return slots


def on_device(hidden, queries, keys, values, control, out_weight, pattern):
    groups = lax.axis_size("groups")
    outer, pair, cores = (lax.axis_size(a) for a in TILES)
    tile_count = outer * pair * cores
    grid_width = min(8, tile_count // 4)
    grid_height = min(4, tile_count // 8)
    layer = grid_width * grid_height
    strides = (layer, grid_width, 1)
    counts = (tile_count // layer, grid_height, grid_width)
    position = lax.axis_index(TILES)
    across = position % grid_width
    rows, inner = queries.shape
    width = hidden.shape[1]
    columns = inner // HALVES
    heads = columns // HEAD_DIM
    slots = neighbour_slots(tile_count, strides, counts)
    early = [s for s in slots if s[0] == 2]
    late = [s for s in slots if s[0] != 2]

    def flags(chosen):
        active = []
        for axis, odd, _ in chosen:
            place = position // strides[axis] % counts[axis]
            up = (place % 2 == odd).astype(jnp.int32)
            valid = jnp.where(up == 1, place + 1 < counts[axis], place >= 1)
            active.append((valid & (pattern[0, 2 * axis + up] == 1)).astype(jnp.int32))
        return jnp.stack(active)

    early_active, late_active = flags(early), flags(late)
    far_lane, near_lane, x_lane, y_lane, core_lane = (Lane() for _ in range(5))

    shard, share = out_weight.shape[0], width // groups
    line = lax.dynamic_slice(out_weight, (0, lax.axis_index("groups") * share), (shard, share))[None]
    line_flips = [0]
    flip = outer // 2
    while flip > 2:
        line = jnp.concatenate([line, flipped(line, "outer", flip)])
        line_flips += [f ^ flip for f in line_flips]
        flip //= 2
    far = far_lane(swap("outer", 2), line)
    near = near_lane(swap("outer", 1), line)

    halves = [
        jnp.concatenate([x[:, half * columns : (half + 1) * columns] for x in (keys, values)], axis=1)
        for half in range(HALVES)
    ]
    block = rows // grid_width
    lines = control.reshape(block // TILE_W, grid_width, TILE_W, width)
    control_sent = [
        lax.dynamic_index_in_dim(lines, across ^ d, 1, keepdims=False).reshape(block, width) for d in range(grid_width)
    ]
    control_parts = [control_sent[0]] + [None] * (grid_width - 1)
    control_parts[1] = core_lane(swap(TILES, 1), control_sent[1])
    early_near = [[None] * len(early) for _ in range(HALVES)]
    x_done = [[] for _ in range(HALVES)]
    for half in range(HALVES):
        early_near[half][0] = core_lane(route_of(early[0][2]), halves[half], far, near)
        for i in range(1, len(early)):
            early_near[half][i] = x_lane(route_of(early[i][2]), halves[half])
            x_done[half].append(early_near[half][i])
        for d in range(2 + half, grid_width, HALVES):
            control_parts[d] = x_lane(swap(TILES, d), control_sent[d])
            x_done[half].append(control_parts[d])
    last = near_lane(swap("outer", 1), far)

    late_near = []
    lanes = [far_lane, near_lane]
    for half in range(HALVES):
        late_near.append(
            [
                lanes[i % 2](route_of(route), halves[half], *(x_done[1] if half else []))
                for i, (_, _, route) in enumerate(late)
            ]
        )

    def plane(piece, *others):
        return lax.all_gather(after(piece, *others) if others else piece, ("groups", "pair", "core"))

    weight = [plane(line)]
    weight.append(plane(jnp.concatenate([far, near, last]), weight[0], *x_done[0]))
    steps = [line_flips, [f ^ x for x in (2, 1, 3) for f in line_flips]]
    moves = [
        (number, ((g * pair + p) * cores + c, i), (g, p, c, flip))
        for number, flips in enumerate(steps)
        for g in range(groups)
        for p in range(pair)
        for c in range(cores)
        for i, flip in enumerate(flips)
    ]

    states = [attend(early_active, queries, half * heads, halves[half], early_near[half]) for half in range(HALVES)]
    ready = [close(late_active, queries, half * heads, states[half], late_near[half]) for half in range(HALVES - 1)]
    ready = ready[0] if len(ready) == 1 else jnp.concatenate(ready, axis=1)
    if block % 16:
        control_parts = [
            jnp.take(
                jnp.stack(control_parts), jnp.arange(grid_width, dtype=jnp.int32) ^ across, axis=0
            ).reshape(rows, width)
        ]
    place = jnp.stack([lax.axis_index(a) for a in ("groups",) + TILES] + [across]).astype(jnp.int32)
    if shard % 16:
        weight, moves = [in_order(weight, moves, place, (groups, outer, pair, cores))], [(0, None, None)]
    return finish(
        place,
        late_active,
        queries,
        ready,
        states[-1],
        late_near[-1],
        hidden,
        control_parts,
        weight,
        tuple(moves),
    )


def in_order(weight, moves, place, sizes):
    blocks = {(g, flip, p, c): weight[piece][index] for piece, index, (g, p, c, flip) in moves}
    whole = jnp.stack([blocks[at] for at in sorted(blocks)])
    shard, columns = whole.shape[1:]
    whole = whole.reshape(sizes + (shard, columns))
    whole = jnp.take(whole, jnp.arange(sizes[1], dtype=jnp.int32) ^ place[1], axis=1)
    return whole.reshape(sizes[0], -1, columns)


def solution(mesh):
    groups = mesh.shape["groups"]
    tiles = mesh.shape["tiles"]
    split = Mesh(mesh.devices.reshape(groups, tiles // 4, 2, 2), ("groups",) + TILES)
    rows = P(("groups",) + TILES, None)
    placed = (rows, rows, rows, rows, rows, P(TILES, None), rows)
    return jax.shard_map(
        on_device,
        mesh=split,
        in_specs=placed,
        out_specs=rows,
        check_vma=False,
    )
```

```python
import functools
import math

import jax
import jax.numpy as jnp
from jax import lax
from jax.experimental import pallas as pl
from jax.experimental.pallas import tpu as pltpu
from jax.sharding import Mesh
from jax.sharding import PartitionSpec as P

HEAD_DIM = 128
TILE_W = 8
CHUNKS = (2, 5, 3, 2)
SCALE = HEAD_DIM**-0.5 * math.log2(math.e)
TILES = ("outer", "pair", "core")
VMEM_LIMIT = 24 * 1024 * 1024
SMEM = pl.BlockSpec(memory_space=pltpu.SMEM)
ANY = pl.BlockSpec(memory_space=pl.ANY)


def after(x, *others):
    return lax.optimization_barrier((x, *others))[0] if others else x


def head_part(q, k, v):
    scores = lax.dot_general(q, k, (((1,), (1,)), ((), ())), preferred_element_type=jnp.float32)
    peak = jnp.max(scores, axis=1, keepdims=True)
    weights = jnp.exp2((scores - peak) * SCALE).astype(jnp.bfloat16)
    ones = jnp.ones((v.shape[0], HEAD_DIM), jnp.bfloat16)
    both = jnp.dot(weights, jnp.concatenate([v, ones], axis=1), preferred_element_type=jnp.float32)
    return both[:, :HEAD_DIM], both[:, HEAD_DIM:], jnp.broadcast_to(peak, v.shape)


def merge(old, new):
    part, total, peak = old
    part_new, total_new, peak_new = new
    top = jnp.maximum(peak, peak_new)
    f_old = jnp.exp2((peak - top) * SCALE)
    f_new = jnp.exp2((peak_new - top) * SCALE)
    return f_old * part + f_new * part_new, f_old * total + f_new * total_new, top


def columns_of(h):
    return pl.ds(h * HEAD_DIM, HEAD_DIM)


def fold(state, active, q, k, v):
    @pl.when(active == 1)
    def _():
        for h in range(q.shape[1] // HEAD_DIM):
            at = columns_of(h)
            new = head_part(q[:, at], k[:, at], v[:, at])
            for r, x in zip(state, merge(tuple(r[:, at] for r in state), new)):
                r[:, at] = x


class Fetch:
    def __init__(self, sems):
        self.sems, self.count = sems, 0

    def __call__(self, source, target):
        copy = pltpu.make_async_copy(source, target, self.sems.at[self.count])
        self.count += 1
        copy.start()
        return copy


def attend_kernel(first, slots, active, q, *refs):
    kv, (part, stats), scratch = refs[: 2 * slots + 2], refs[2 * slots + 2 : 2 * slots + 4], refs[2 * slots + 4 :]
    q_v, kv_v, total_v, peak_v, part_v, stats_v, sems = (*scratch[:1], scratch[1 : 2 * slots + 3], *scratch[2 * slots + 3 :])
    fetch = Fetch(sems)
    at = pl.ds(first * HEAD_DIM, q_v.shape[1])
    copies = [fetch(source.at[:, at], target) for source, target in zip((q, *kv), (q_v, *kv_v))]
    for copy in copies[:3]:
        copy.wait()
    state = (part_v, total_v, peak_v)
    heads = q_v.shape[1] // HEAD_DIM
    for h in range(heads):
        at = columns_of(h)
        for r, x in zip(state, head_part(q_v[:, at], kv_v[0][:, at], kv_v[1][:, at])):
            r[:, at] = x
    for slot in range(slots):
        for copy in copies[3 + 2 * slot : 5 + 2 * slot]:
            copy.wait()
        fold(state, active[slot], q_v, kv_v[2 * slot + 2], kv_v[2 * slot + 3])
    lane = lax.broadcasted_iota(jnp.int32, stats_v.shape, 1)
    packed = jnp.zeros(stats_v.shape, jnp.float32)
    for h in range(heads):
        packed = jnp.where(lane == h, total_v[:, columns_of(h)], packed)
        packed = jnp.where(lane == HEAD_DIM // 2 + h, peak_v[:, columns_of(h)], packed)
    stats_v[...] = packed
    copies = [fetch(part_v, part), fetch(stats_v, stats)]
    for copy in copies:
        copy.wait()


def attend(active, q, kv, first, heads):
    rows, columns, slots = q.shape[0], heads * HEAD_DIM, len(kv) // 2 - 1
    return pl.pallas_call(
        functools.partial(attend_kernel, first, slots),
        out_shape=[
            jax.ShapeDtypeStruct((rows, columns), jnp.float32),
            jax.ShapeDtypeStruct((rows, HEAD_DIM), jnp.float32),
        ],
        in_specs=[SMEM] + [ANY] * (1 + len(kv)),
        out_specs=[ANY] * 2,
        scratch_shapes=[pltpu.VMEM((rows, columns), jnp.bfloat16)] * (1 + len(kv))
        + [pltpu.VMEM((rows, columns), jnp.float32)] * 3
        + [pltpu.VMEM((rows, HEAD_DIM), jnp.float32), pltpu.SemaphoreType.DMA((3 + len(kv),))],
        compiler_params=pltpu.CompilerParams(vmem_limit_bytes=VMEM_LIMIT),
        cost_estimate=pl.CostEstimate(
            flops=(1 + slots) * 6 * rows * rows * columns,
            bytes_accessed=rows * columns * (10 + 4 * slots),
            transcendentals=0,
        ),
        name="attend",
    )(active, q, *kv)


def close_heads(fetch, first, active, q, part, stats, near, q_v, near_v, state, stats_v, out, out_at):
    columns = state[0].shape[1]
    copies = [
        fetch(q.at[:, pl.ds(first * HEAD_DIM, columns)], q_v),
        fetch(part, state[0]),
        fetch(stats, stats_v),
    ] + [fetch(source, target) for source, target in zip(near, near_v)]
    for copy in copies[:3]:
        copy.wait()
    stats_now = stats_v[...]
    for h in range(columns // HEAD_DIM):
        for r, lane in zip(state[1:], (h, HEAD_DIM // 2 + h)):
            r[:, columns_of(h)] = jnp.broadcast_to(stats_now[:, lane : lane + 1], stats_now.shape)
    for slot, kv in enumerate(near_v):
        copies[3 + slot].wait()
        fold(state, active[slot], q_v, kv.at[:, pl.ds(0, columns)], kv.at[:, pl.ds(columns, columns)])
    out[:, out_at] = (state[0][...] / state[1][...]).astype(jnp.bfloat16)


def close_scratch(rows, columns, slots):
    return (
        [pltpu.VMEM((rows, columns), jnp.bfloat16)]
        + [pltpu.VMEM((rows, 2 * columns), jnp.bfloat16)] * slots
        + [pltpu.VMEM((rows, columns), jnp.float32)] * 3
        + [pltpu.VMEM((rows, HEAD_DIM), jnp.float32), pltpu.SemaphoreType.DMA((4 + slots,))]
    )


def close_kernel(first, slots, active, q, part, stats, *refs):
    near, out = refs[:slots], refs[slots]
    q_v, near_v, (*state, stats_v, sems, out_v) = refs[slots + 1], refs[slots + 2 : 2 * slots + 2], refs[2 * slots + 2 :]
    fetch = Fetch(sems)
    close_heads(fetch, first, active, q, part, stats, near, q_v, near_v, state, stats_v, out_v, slice(None))
    fetch(out_v, out).wait()


def close(active, q, state, near, first):
    rows, columns = state[0].shape
    return pl.pallas_call(
        functools.partial(close_kernel, first, len(near)),
        out_shape=jax.ShapeDtypeStruct((rows, columns), jnp.bfloat16),
        in_specs=[SMEM] + [ANY] * (3 + len(near)),
        out_specs=ANY,
        scratch_shapes=close_scratch(rows, columns, len(near)) + [pltpu.VMEM((rows, columns), jnp.bfloat16)],
        compiler_params=pltpu.CompilerParams(vmem_limit_bytes=VMEM_LIMIT),
        cost_estimate=pl.CostEstimate(
            flops=len(near) * 6 * rows * rows * columns,
            bytes_accessed=rows * columns * (4 * len(near) + 8),
            transcendentals=0,
        ),
        name="close",
    )(active, q, *state, *near)


def finish_kernel(counts, moves, control_rows, place, active, q, part, stats, *refs):
    groups_of = []
    for count in counts:
        groups_of.append(refs[:count])
        refs = refs[count:]
    near, ready, weight, control = groups_of
    slots, blocks = len(near), len(control)
    hidden, out, refs = refs[0], refs[1], refs[2:]
    q_v, near_v, refs = refs[0], refs[1 : slots + 1], refs[slots + 1 :]
    *state, stats_v, sems, attention, held, hidden_v, control_v, out_v, late_sems = refs
    fetch, late_fetch = Fetch(sems), Fetch(late_sems)
    late = []
    done = 0
    for block in ready:
        late.append(late_fetch(block, attention.at[:, pl.ds(done, block.shape[1])]))
        done += block.shape[1]

    def fetch_late():
        for piece, index, at in moves:
            source = weight[piece] if at is None else weight[piece].at[index]
            if at is None:
                target = held
            else:
                flip, group, outer, pair, core = at
                count = source.shape[0]
                outer = place[1] ^ outer
                if flip:
                    group, pair, core = place[0] ^ group, place[2] ^ pair, place[3] ^ core
                start = pl.multiple_of(((outer * 2 + pair) * 2 + core) * count, count)
                target = held.at[group, pl.ds(start, count), :]
            late.append(late_fetch(source, target))
        late.append(late_fetch(hidden, hidden_v))
        for d in range(blocks):
            start = pl.multiple_of((place[4] ^ d) * control_rows, control_rows) if blocks > 1 else 0
            late.append(late_fetch(control[d], control_v.at[pl.ds(start, control_rows), :]))

    fetch_late()
    close_heads(
        fetch,
        done // HEAD_DIM,
        active,
        q,
        part,
        stats,
        near,
        q_v,
        near_v,
        state,
        stats_v,
        attention,
        pl.ds(done, part.shape[1]),
    )
    for copy in late:
        copy.wait()
    groups, _, columns = held.shape
    step = 512 if columns % 512 == 0 else columns
    stores = []
    for group in range(groups):
        for j in range(columns // step):
            at = pl.ds(group * columns + j * step, step)
            projected = jnp.dot(
                attention[...], held[group, :, pl.ds(j * step, step)], preferred_element_type=jnp.float32
            )
            out_v[:, at] = (
                hidden_v[:, at].astype(jnp.float32) + projected + control_v[:, at].astype(jnp.float32)
            ).astype(jnp.bfloat16)
            stores.append(late_fetch(out_v.at[:, at], out.at[:, at]))
    for copy in stores:
        copy.wait()


def finish(place, active, q, state, near, ready, weight, control, hidden, moves):
    rows, inner = q.shape
    width = hidden.shape[1]
    groups = lax.axis_size("groups")
    control_rows = control[0].shape[0]
    columns = state[0].shape[1]
    share = width // groups
    lists = (near, ready, weight, control)
    counts = tuple(len(x) for x in lists)
    step = 512 if share % 512 == 0 else share
    return pl.pallas_call(
        functools.partial(finish_kernel, counts, moves, control_rows),
        out_shape=jax.ShapeDtypeStruct((rows, width), jnp.bfloat16),
        in_specs=[SMEM] * 2 + [ANY] * (4 + sum(counts)),
        out_specs=ANY,
        scratch_shapes=close_scratch(rows, columns, len(near))
        + [
            pltpu.VMEM((rows, inner), jnp.bfloat16),
            pltpu.VMEM((groups, inner, share), jnp.bfloat16),
            pltpu.VMEM((rows, width), jnp.bfloat16),
            pltpu.VMEM((rows, width), jnp.bfloat16),
            pltpu.VMEM((rows, width), jnp.bfloat16),
            pltpu.SemaphoreType.DMA((len(ready) + len(moves) + 1 + len(control) + width // step,)),
        ],
        compiler_params=pltpu.CompilerParams(vmem_limit_bytes=VMEM_LIMIT),
        cost_estimate=pl.CostEstimate(
            flops=2 * rows * inner * width, bytes_accessed=2 * inner * width + 6 * rows * width, transcendentals=0
        ),
        name="finish",
    )(place, active, q, *state, *near, *ready, *weight, *control, hidden)


def tied_kernel(x, other, out):
    del x, other, out


def tied(x, other):
    return pl.pallas_call(
        tied_kernel,
        out_shape=jax.ShapeDtypeStruct(x.shape, x.dtype),
        in_specs=[ANY, ANY],
        out_specs=ANY,
        input_output_aliases={0: 0},
        cost_estimate=pl.CostEstimate(flops=0, bytes_accessed=0, transcendentals=0),
        name="tied",
    )(x, other)


def flipped(block, axis, flip):
    return lax.ppermute(block, axis, [(i, i ^ flip) for i in range(lax.axis_size(axis))])


class Lane:
    def __init__(self):
        self.last = ()

    def __call__(self, send, block, *others):
        self.last = (send(after(block, *self.last, *others)),)
        return self.last[0]


def swap(axis, flip):
    return lambda block: flipped(block, axis, flip)


def route_of(route):
    return lambda block: lax.ppermute(block, TILES, route)


def neighbour_slots(tile_count, strides, counts):
    slots = []
    for axis, (stride, count) in enumerate(zip(strides, counts)):
        for odd in range(2):
            route = []
            for t in range(tile_count):
                place = t // stride % count
                if place % 2 == odd and place + 1 < count:
                    route += [(t, t + stride), (t + stride, t)]
            if route:
                slots.append((axis, odd, route))
    return slots


def on_device(hidden, queries, keys, values, control, out_weight, pattern):
    groups = lax.axis_size("groups")
    outer, pair, cores = (lax.axis_size(a) for a in TILES)
    tile_count = outer * pair * cores
    grid_width = min(8, tile_count // 4)
    grid_height = min(4, tile_count // 8)
    layer = grid_width * grid_height
    strides = (layer, grid_width, 1)
    counts = (tile_count // layer, grid_height, grid_width)
    position = lax.axis_index(TILES)
    across = position % grid_width
    rows = queries.shape[0]
    width = hidden.shape[1]
    slots = neighbour_slots(tile_count, strides, counts)
    early = [s for s in slots if s[0] == 2]
    late = [s for s in slots if s[0] != 2]

    def flags(chosen):
        active = []
        for axis, odd, _ in chosen:
            place = position // strides[axis] % counts[axis]
            up = (place % 2 == odd).astype(jnp.int32)
            valid = jnp.where(up == 1, place + 1 < counts[axis], place >= 1)
            active.append((valid & (pattern[0, 2 * axis + up] == 1)).astype(jnp.int32))
        return jnp.stack(active)

    early_active, late_active = flags(early), flags(late)
    far_lane, near_lane, x_lane, y_lane, core_lane = (Lane() for _ in range(5))

    shard, share = out_weight.shape[0], width // groups
    line = out_weight[:, :share]
    for g in range(1, groups):
        line = jnp.where(lax.axis_index("groups") == g, out_weight[:, g * share : (g + 1) * share], line)
    line = lax.optimization_barrier(line)[None]
    line_flips = [0]
    flip = outer // 2
    while flip > 2:
        line = jnp.concatenate([line, flipped(line, "outer", flip)])
        line_flips += [f ^ flip for f in line_flips]
        flip //= 2
    own = lax.all_gather(line, ("groups", "pair", "core"))
    far = far_lane(swap("outer", 2), line)
    near = near_lane(swap("outer", 1), line)
    last = near_lane(swap("outer", 1), far)

    firsts = [sum(CHUNKS[:i]) for i in range(len(CHUNKS))]
    chunks = [
        jnp.concatenate([x[:, f * HEAD_DIM : (f + n) * HEAD_DIM] for x in (keys, values)], axis=1)
        for f, n in zip(firsts, CHUNKS)
    ]
    block = rows // grid_width
    lines = after(control, line).reshape(block // TILE_W, grid_width, TILE_W, width)
    control_sent = [
        lax.dynamic_index_in_dim(lines, across ^ d, 1, keepdims=False).reshape(block, width) for d in range(grid_width)
    ]
    control_parts = [control_sent[0]] + [None] * (grid_width - 1)
    control_parts[1] = swap(TILES, 1)(control_sent[1])
    early_near = [[None, None] for _ in early]
    for i, x in enumerate((keys, values)):
        early_near[0][i] = core_lane(route_of(early[0][2]), x)

    def early_along_x(i):
        for slot in range(1, len(early)):
            early_near[slot][i] = x_lane(route_of(early[slot][2]), (keys, values)[i])

    late_near = []

    def along_z(number, *others):
        lanes = (far_lane, near_lane)
        others = others or ((), ())
        late_near.append(
            [lanes[i % 2](route_of(route), chunks[number], *others[i % 2]) for i, (_, _, route) in enumerate(late)]
        )

    x_lane.last = (line,)
    early_along_x(0)
    for d in range(2, grid_width - 1):
        control_parts[d] = swap(TILES, d)(control_sent[d])
    first = [far, near] + control_parts[2:-1]
    along_z(0)
    far_x, near_x = (x_lane(swap("pair", 1), x, *first) for x in (far, near))
    last_x = x_lane(swap("pair", 1), last)
    early_along_x(1)
    control_parts[-1] = x_lane(swap(TILES, grid_width - 1), tied(control_sent[-1], own))
    plane = jnp.concatenate([far, near, far_x, near_x])
    plane_y = y_lane(swap("groups", 1), plane, *late_near[0])
    along_z(1, (), (last_x,))
    plane_last = jnp.concatenate([last, last_x])
    plane_last_y = y_lane(swap("groups", 1), plane_last, *late_near[1])
    along_z(2)
    along_z(3)
    held = [plane, plane_y, plane_last, plane_last_y]
    gates = [(), late_near[1] + [control_parts[-1]], (), late_near[2]]
    crossed = [core_lane(swap("core", 1), x, *gate) for x, gate in zip(held, gates)]
    n = len(line_flips)
    moves = [
        (0, ((g * pair + p) * cores + c, i), (False, g, f, p, c))
        for g in range(groups)
        for p in range(pair)
        for c in range(cores)
        for i, f in enumerate(line_flips)
    ]
    weight = [own]
    for number, flips in enumerate(((2, 1), (2, 1), (3,), (3,))):
        for core_flip, pieces in enumerate((held, crossed)):
            moves += [
                (len(weight), ((p * len(flips) + i) * n + j,), (True, number % 2, f ^ at, p, core_flip))
                for p in range(pair)
                for i, at in enumerate(flips)
                for j, f in enumerate(line_flips)
            ]
            weight.append(pieces[number])

    early_kv = [keys, values] + [x for kv in early_near for x in kv]
    states = [attend(early_active, queries, early_kv, f, n) for f, n in zip(firsts, CHUNKS)]
    ready = [close(late_active, queries, states[i], late_near[i], firsts[i]) for i in range(len(CHUNKS) - 1)]
    if block % 16:
        control_parts = [
            jnp.take(
                jnp.stack(control_parts), jnp.arange(grid_width, dtype=jnp.int32) ^ across, axis=0
            ).reshape(rows, width)
        ]
    place = jnp.stack([lax.axis_index(a) for a in ("groups",) + TILES] + [across]).astype(jnp.int32)
    if shard % 16:
        weight, moves = [in_order(weight, moves, place, (groups, outer, pair, cores))], [(0, None, None)]
    return finish(
        place,
        late_active,
        queries,
        states[-1],
        late_near[-1],
        ready,
        weight,
        control_parts,
        hidden,
        tuple(moves),
    )


def in_order(weight, moves, place, sizes):
    groups, outer, pair, cores = sizes
    shard, columns = weight[0].shape[-2:]
    own = weight[0].reshape(groups, pair, cores, -1, shard, columns)
    for axis, at in enumerate((0, 2, 3)):
        own = jnp.take(own, jnp.arange(sizes[at], dtype=jnp.int32) ^ place[at], axis=axis)
    weight = [own.reshape(weight[0].shape)] + weight[1:]
    blocks = {at[1:]: weight[piece][index] for piece, index, at in moves}
    whole = jnp.stack([blocks[at] for at in sorted(blocks)]).reshape(sizes + (shard, columns))
    for axis, size in enumerate(sizes):
        whole = jnp.take(whole, jnp.arange(size, dtype=jnp.int32) ^ place[axis], axis=axis)
    return whole.reshape(groups, -1, columns)


def solution(mesh):
    groups = mesh.shape["groups"]
    tiles = mesh.shape["tiles"]
    split = Mesh(mesh.devices.reshape(groups, tiles // 4, 2, 2), ("groups",) + TILES)
    rows = P(("groups",) + TILES, None)
    placed = (rows, rows, rows, rows, rows, P(TILES, None), rows)
    return jax.shard_map(
        on_device,
        mesh=split,
        in_specs=placed,
        out_specs=rows,
        check_vma=False,
    )
```

```python
import functools
import math

import jax
import jax.numpy as jnp
from jax import lax
from jax.experimental import pallas as pl
from jax.experimental.pallas import tpu as pltpu
from jax.sharding import Mesh
from jax.sharding import PartitionSpec as P

HEAD_DIM = 128
TILE_W = 8
CHUNKS = (2, 6, 4)
SCALE = HEAD_DIM**-0.5 * math.log2(math.e)
TILES = ("outer", "pair", "core")
VMEM_LIMIT = 24 * 1024 * 1024
SMEM = pl.BlockSpec(memory_space=pltpu.SMEM)
ANY = pl.BlockSpec(memory_space=pl.ANY)
HBM = pl.BlockSpec(memory_space=pltpu.HBM)


def after(x, *others):
    return lax.optimization_barrier((x, *others))[0] if others else x


def head_part(q, k, v):
    scores = lax.dot_general(q, k, (((1,), (1,)), ((), ())), preferred_element_type=jnp.float32)
    peak = jnp.max(scores, axis=1, keepdims=True)
    weights = jnp.exp2((scores - peak) * SCALE).astype(jnp.bfloat16)
    ones = jnp.ones((v.shape[0], HEAD_DIM), jnp.bfloat16)
    both = jnp.dot(weights, jnp.concatenate([v, ones], axis=1), preferred_element_type=jnp.float32)
    return both[:, :HEAD_DIM], both[:, HEAD_DIM:], jnp.broadcast_to(peak, v.shape)


def merge(old, new):
    part, total, peak = old
    part_new, total_new, peak_new = new
    top = jnp.maximum(peak, peak_new)
    f_old = jnp.exp2((peak - top) * SCALE)
    f_new = jnp.exp2((peak_new - top) * SCALE)
    return f_old * part + f_new * part_new, f_old * total + f_new * total_new, top


def columns_of(h):
    return pl.ds(h * HEAD_DIM, HEAD_DIM)


def fold(state, active, q, k, v):
    @pl.when(active == 1)
    def _():
        for h in range(q.shape[1] // HEAD_DIM):
            at = columns_of(h)
            new = head_part(q[:, at], k[:, at], v[:, at])
            for r, x in zip(state, merge(tuple(r[:, at] for r in state), new)):
                r[:, at] = x


class Fetch:
    def __init__(self, sems):
        self.sems, self.count = sems, 0

    def __call__(self, source, target):
        copy = pltpu.make_async_copy(source, target, self.sems.at[self.count])
        self.count += 1
        copy.start()
        return copy


def attend_kernel(slots, active, q, *refs):
    kv, (part, stats), scratch = refs[: 2 * slots + 2], refs[2 * slots + 2 : 2 * slots + 4], refs[2 * slots + 4 :]
    q_v, kv_v, (part_v, total_v, peak_v, stats_v, sems) = scratch[0], scratch[1 : 2 * slots + 3], scratch[2 * slots + 3 :]
    fetch = Fetch(sems)
    copies = [fetch(source, target) for source, target in zip((q, *kv), (q_v, *kv_v))]
    for copy in copies[:3]:
        copy.wait()
    state = (part_v, total_v, peak_v)
    heads = q_v.shape[1] // HEAD_DIM
    for h in range(heads):
        at = columns_of(h)
        for r, x in zip(state, head_part(q_v[:, at], kv_v[0][:, at], kv_v[1][:, at])):
            r[:, at] = x
    for slot in range(slots):
        for copy in copies[3 + 2 * slot : 5 + 2 * slot]:
            copy.wait()
        fold(state, active[slot], q_v, kv_v[2 * slot + 2], kv_v[2 * slot + 3])
    lane = lax.broadcasted_iota(jnp.int32, stats_v.shape, 1)
    packed = jnp.zeros(stats_v.shape, jnp.float32)
    for h in range(heads):
        packed = jnp.where(lane == h, total_v[:, columns_of(h)], packed)
        packed = jnp.where(lane == HEAD_DIM // 2 + h, peak_v[:, columns_of(h)], packed)
    stats_v[...] = packed
    copies = [fetch(part_v, part), fetch(stats_v, stats)]
    for copy in copies:
        copy.wait()


def attend(active, q, kv):
    rows, columns = q.shape
    slots = len(kv) // 2 - 1
    return pl.pallas_call(
        functools.partial(attend_kernel, slots),
        out_shape=[
            jax.ShapeDtypeStruct((rows, columns), jnp.float32),
            jax.ShapeDtypeStruct((rows, HEAD_DIM), jnp.float32),
        ],
        in_specs=[SMEM] + [ANY] * (1 + len(kv)),
        out_specs=[ANY] * 2,
        scratch_shapes=[pltpu.VMEM((rows, columns), jnp.bfloat16)] * (1 + len(kv))
        + [pltpu.VMEM((rows, columns), jnp.float32)] * 3
        + [pltpu.VMEM((rows, HEAD_DIM), jnp.float32), pltpu.SemaphoreType.DMA((3 + len(kv),))],
        compiler_params=pltpu.CompilerParams(vmem_limit_bytes=VMEM_LIMIT),
        cost_estimate=pl.CostEstimate(
            flops=(1 + slots) * 6 * rows * rows * columns,
            bytes_accessed=rows * columns * (10 + 4 * slots),
            transcendentals=0,
        ),
        name="attend",
    )(active, q, *kv)


def close_heads(fetch, first, active, q, part, stats, near, q_v, near_v, state, stats_v, out, out_at):
    columns = state[0].shape[1]
    copies = [
        fetch(q.at[:, pl.ds(first * HEAD_DIM, columns)], q_v),
        fetch(part.at[:, pl.ds(first * HEAD_DIM, columns)], state[0]),
        fetch(stats, stats_v),
    ] + [fetch(source, target) for source, target in zip(near, near_v)]
    for copy in copies[:3]:
        copy.wait()
    stats_now = stats_v[...]
    for h in range(columns // HEAD_DIM):
        for r, lane in zip(state[1:], (first + h, HEAD_DIM // 2 + first + h)):
            r[:, columns_of(h)] = jnp.broadcast_to(stats_now[:, lane : lane + 1], stats_now.shape)
    for slot, kv in enumerate(near_v):
        copies[3 + slot].wait()
        fold(state, active[slot], q_v, kv.at[:, pl.ds(0, columns)], kv.at[:, pl.ds(columns, columns)])
    out[:, out_at] = (state[0][...] / state[1][...]).astype(jnp.bfloat16)


def close_scratch(rows, columns, slots):
    return (
        [pltpu.VMEM((rows, columns), jnp.bfloat16)]
        + [pltpu.VMEM((rows, 2 * columns), jnp.bfloat16)] * slots
        + [pltpu.VMEM((rows, columns), jnp.float32)] * 3
        + [pltpu.VMEM((rows, HEAD_DIM), jnp.float32), pltpu.SemaphoreType.DMA((4 + slots,))]
    )


def close_kernel(first, slots, active, q, part, stats, *refs):
    near, out = refs[:slots], refs[slots]
    q_v, near_v, (*state, stats_v, sems, out_v) = refs[slots + 1], refs[slots + 2 : 2 * slots + 2], refs[2 * slots + 2 :]
    fetch = Fetch(sems)
    close_heads(fetch, first, active, q, part, stats, near, q_v, near_v, state, stats_v, out_v, slice(None))
    fetch(out_v, out).wait()


def close(active, q, state, near, first):
    rows, columns = q.shape[0], near[0].shape[1] // 2
    return pl.pallas_call(
        functools.partial(close_kernel, first, len(near)),
        out_shape=jax.ShapeDtypeStruct((rows, columns), jnp.bfloat16),
        in_specs=[SMEM] + [ANY] * (3 + len(near)),
        out_specs=ANY,
        scratch_shapes=close_scratch(rows, columns, len(near)) + [pltpu.VMEM((rows, columns), jnp.bfloat16)],
        compiler_params=pltpu.CompilerParams(vmem_limit_bytes=VMEM_LIMIT),
        cost_estimate=pl.CostEstimate(
            flops=len(near) * 6 * rows * rows * columns,
            bytes_accessed=rows * columns * (4 * len(near) + 8),
            transcendentals=0,
        ),
        name="close",
    )(active, q, *state, *near)


def finish_kernel(counts, moves, control_rows, place, active, q, part, stats, *refs):
    groups_of = []
    for count in counts:
        groups_of.append(refs[:count])
        refs = refs[count:]
    near, ready, weight, control = groups_of
    slots, blocks = len(near), len(control)
    hidden, out, refs = refs[0], refs[1], refs[2:]
    q_v, near_v, refs = refs[0], refs[1 : slots + 1], refs[slots + 1 :]
    *state, stats_v, sems, attention, held, hidden_v, control_v, out_v, late_sems = refs
    fetch, late_fetch = Fetch(sems), Fetch(late_sems)
    late = []
    done = 0
    for block in ready:
        late.append(late_fetch(block, attention.at[:, pl.ds(done, block.shape[1])]))
        done += block.shape[1]

    def fetch_late():
        for piece, index, at in moves:
            source = weight[piece] if at is None else weight[piece].at[index]
            if at is None:
                target = held
            else:
                flip, group, outer, pair, core = at
                count = source.shape[0]
                outer = place[1] ^ outer
                if flip:
                    group, pair, core = place[0] ^ group, place[2] ^ pair, place[3] ^ core
                start = pl.multiple_of(((outer * 2 + pair) * 2 + core) * count, count)
                target = held.at[group, pl.ds(start, count), :]
            late.append(late_fetch(source, target))
        late.append(late_fetch(hidden, hidden_v))
        for d in range(blocks):
            start = pl.multiple_of((place[4] ^ d) * control_rows, control_rows) if blocks > 1 else 0
            late.append(late_fetch(control[d], control_v.at[pl.ds(start, control_rows), :]))

    fetch_late()
    close_heads(
        fetch,
        done // HEAD_DIM,
        active,
        q,
        part,
        stats,
        near,
        q_v,
        near_v,
        state,
        stats_v,
        attention,
        pl.ds(done, q_v.shape[1]),
    )
    for copy in late[len(ready) + len(moves) :] + late[: len(ready)]:
        copy.wait()
    groups, _, columns = held.shape
    step = 256 if columns % 256 == 0 else columns
    stores = []
    for group in range(groups):
        for number, (_, _, at) in enumerate(moves):
            known = at is not None and not at[0]
            if (at[1] == group) if known else group == 0:
                late[len(ready) + number].wait()
        for j in range(columns // step):
            at = pl.ds(group * columns + j * step, step)
            projected = jnp.dot(
                attention[...], held[group, :, pl.ds(j * step, step)], preferred_element_type=jnp.float32
            )
            out_v[:, at] = (
                hidden_v[:, at].astype(jnp.float32) + projected + control_v[:, at].astype(jnp.float32)
            ).astype(jnp.bfloat16)
            stores.append(late_fetch(out_v.at[:, at], out.at[:, at]))
    for copy in stores:
        copy.wait()


def finish(place, active, q, state, near, ready, weight, control, hidden, moves):
    rows, inner = q.shape
    width = hidden.shape[1]
    groups = lax.axis_size("groups")
    control_rows = control[0].shape[0]
    columns = near[0].shape[1] // 2
    share = width // groups
    lists = (near, ready, weight, control)
    counts = tuple(len(x) for x in lists)
    step = 256 if share % 256 == 0 else share
    return pl.pallas_call(
        functools.partial(finish_kernel, counts, moves, control_rows),
        out_shape=jax.ShapeDtypeStruct((rows, width), jnp.bfloat16),
        in_specs=[SMEM] * 2
        + [HBM]
        + [ANY] * (2 + len(near) + len(ready))
        + [HBM]
        + [ANY] * (len(weight) - 1 + len(control))
        + [HBM],
        out_specs=ANY,
        scratch_shapes=close_scratch(rows, columns, len(near))
        + [
            pltpu.VMEM((rows, inner), jnp.bfloat16),
            pltpu.VMEM((groups, inner, share), jnp.bfloat16),
            pltpu.VMEM((rows, width), jnp.bfloat16),
            pltpu.VMEM((rows, width), jnp.bfloat16),
            pltpu.VMEM((rows, width), jnp.bfloat16),
            pltpu.SemaphoreType.DMA((len(ready) + len(moves) + 1 + len(control) + width // step,)),
        ],
        compiler_params=pltpu.CompilerParams(vmem_limit_bytes=VMEM_LIMIT),
        cost_estimate=pl.CostEstimate(
            flops=2 * rows * inner * width, bytes_accessed=2 * inner * width + 6 * rows * width, transcendentals=0
        ),
        name="finish",
    )(place, active, q, *state, *near, *ready, *weight, *control, hidden)


def flipped(block, axis, flip):
    return lax.ppermute(block, axis, [(i, i ^ flip) for i in range(lax.axis_size(axis))])


class Lane:
    def __init__(self):
        self.last = ()

    def __call__(self, send, block, *others):
        self.last = (send(after(block, *self.last, *others)),)
        return self.last[0]


def swap(axis, flip):
    return lambda block: flipped(block, axis, flip)


def route_of(route):
    return lambda block: lax.ppermute(block, TILES, route)


def neighbour_slots(tile_count, strides, counts):
    slots = []
    for axis, (stride, count) in enumerate(zip(strides, counts)):
        for odd in range(2):
            route = []
            for t in range(tile_count):
                place = t // stride % count
                if place % 2 == odd and place + 1 < count:
                    route += [(t, t + stride), (t + stride, t)]
            if route:
                slots.append((axis, odd, route))
    return slots


def on_device(hidden, queries, keys, values, control, out_weight, pattern):
    groups = lax.axis_size("groups")
    outer, pair, cores = (lax.axis_size(a) for a in TILES)
    tile_count = outer * pair * cores
    grid_width = min(8, tile_count // 4)
    grid_height = min(4, tile_count // 8)
    layer = grid_width * grid_height
    strides = (layer, grid_width, 1)
    counts = (tile_count // layer, grid_height, grid_width)
    position = lax.axis_index(TILES)
    across = position % grid_width
    rows = queries.shape[0]
    width = hidden.shape[1]
    slots = neighbour_slots(tile_count, strides, counts)
    early = [s for s in slots if s[0] == 2]
    late = [s for s in slots if s[0] != 2]

    def flags(chosen):
        active = []
        for axis, odd, _ in chosen:
            place = position // strides[axis] % counts[axis]
            up = (place % 2 == odd).astype(jnp.int32)
            valid = jnp.where(up == 1, place + 1 < counts[axis], place >= 1)
            active.append((valid & (pattern[0, 2 * axis + up] == 1)).astype(jnp.int32))
        return jnp.stack(active)

    early_active, late_active = flags(early), flags(late)
    far_lane, near_lane = Lane(), Lane()

    shard, share = out_weight.shape[0], width // groups
    line = out_weight[:, :share]
    for g in range(1, groups):
        line = jnp.where(lax.axis_index("groups") == g, out_weight[:, g * share : (g + 1) * share], line)
    line = lax.optimization_barrier(line)[None]
    line_flips = [0]
    flip = outer // 2
    while flip > 2:
        line = jnp.concatenate([line, flipped(line, "outer", flip)])
        line_flips += [f ^ flip for f in line_flips]
        flip //= 2
    far = far_lane(swap("outer", 2), line)
    near = near_lane(swap("outer", 1), line)
    last = swap("outer", 1)(far)

    firsts = [sum(CHUNKS[:i]) for i in range(len(CHUNKS))]
    chunks = [
        jnp.concatenate([x[:, f * HEAD_DIM : (f + n) * HEAD_DIM] for x in (keys, values)], axis=1)
        for f, n in zip(firsts, CHUNKS)
    ]
    block = rows // grid_width
    lines = after(control, line).reshape(block // TILE_W, grid_width, TILE_W, width)
    control_sent = [
        lax.dynamic_index_in_dim(lines, across ^ d, 1, keepdims=False).reshape(block, width) for d in range(grid_width)
    ]
    control_parts = [control_sent[0]] + [swap(TILES, d)(control_sent[d]) for d in range(1, grid_width)]
    early_near = [tuple(lax.ppermute(x, TILES, route) for x in (keys, values)) for _, _, route in early]
    early_kv = [keys, values] + [x for kv in early_near for x in kv]
    state = attend(early_active, queries, early_kv)
    first = [kv[0] for kv in early_near[1:]] + control_parts[2:-1]
    second = [kv[1] for kv in early_near[1:]] + control_parts[-1:]

    late_near = []

    def along_z(number, *others):
        lanes = (far_lane, near_lane)
        late_near.append(
            [lanes[i % 2](route_of(route), chunks[number], *others) for i, (_, _, route) in enumerate(late)]
        )

    along_z(0)
    along_z(1)
    along_z(2)
    most = lax.all_gather(
        after(jnp.concatenate([line, far, near]), *first), ("groups", "pair", "core")
    )
    last_x = swap("pair", 1)(after(last, *late_near[0]))
    plane = jnp.concatenate([last, last_x])
    held = [plane, swap("groups", 1)(after(plane, *second))]
    crossed = [swap("core", 1)(after(x, *late_near[1])) for x in held]
    n = len(line_flips)
    moves = [
        (0, ((g * pair + p) * cores + c, i * n + j), (False, g, f ^ at, p, c))
        for g in range(groups)
        for p in range(pair)
        for c in range(cores)
        for i, at in enumerate((0, 2, 1))
        for j, f in enumerate(line_flips)
    ]
    weight = [most]
    for group_flip in range(2):
        for core_flip, pieces in enumerate((held, crossed)):
            moves += [
                (len(weight), (p * n + j,), (True, group_flip, f ^ 3, p, core_flip))
                for p in range(pair)
                for j, f in enumerate(line_flips)
            ]
            weight.append(pieces[group_flip])

    ready = [close(late_active, queries, state, late_near[i], firsts[i]) for i in range(len(CHUNKS) - 1)]
    if block % 16:
        control_parts = [
            jnp.take(
                jnp.stack(control_parts), jnp.arange(grid_width, dtype=jnp.int32) ^ across, axis=0
            ).reshape(rows, width)
        ]
    place = jnp.stack([lax.axis_index(a) for a in ("groups",) + TILES] + [across]).astype(jnp.int32)
    if shard % 16:
        weight, moves = [in_order(weight, moves, place, (groups, outer, pair, cores))], [(0, None, None)]
    return finish(
        place,
        late_active,
        queries,
        state,
        late_near[-1],
        ready,
        weight,
        control_parts,
        hidden,
        tuple(moves),
    )


def in_order(weight, moves, place, sizes):
    groups, outer, pair, cores = sizes
    shard, columns = weight[0].shape[-2:]
    own = weight[0].reshape(groups, pair, cores, -1, shard, columns)
    for axis, at in enumerate((0, 2, 3)):
        own = jnp.take(own, jnp.arange(sizes[at], dtype=jnp.int32) ^ place[at], axis=axis)
    weight = [own.reshape(weight[0].shape)] + weight[1:]
    blocks = {at[1:]: weight[piece][index] for piece, index, at in moves}
    whole = jnp.stack([blocks[at] for at in sorted(blocks)]).reshape(sizes + (shard, columns))
    for axis, size in enumerate(sizes):
        whole = jnp.take(whole, jnp.arange(size, dtype=jnp.int32) ^ place[axis], axis=axis)
    return whole.reshape(groups, -1, columns)


def solution(mesh):
    groups = mesh.shape["groups"]
    tiles = mesh.shape["tiles"]
    split = Mesh(mesh.devices.reshape(groups, tiles // 4, 2, 2), ("groups",) + TILES)
    rows = P(("groups",) + TILES, None)
    placed = (rows, rows, rows, rows, rows, P(TILES, None), rows)
    return jax.shard_map(
        on_device,
        mesh=split,
        in_specs=placed,
        out_specs=rows,
        check_vma=False,
    )
```

```python
import functools
import math

import jax
import jax.numpy as jnp
from jax import lax
from jax.experimental import pallas as pl
from jax.experimental.pallas import tpu as pltpu
from jax.sharding import Mesh
from jax.sharding import PartitionSpec as P

HEAD_DIM = 128
TILE_W = 8
CHUNKS = (6, 6)
SCALE = HEAD_DIM**-0.5 * math.log2(math.e)
TILES = ("outer", "pair", "core")
VMEM_LIMIT = 60 * 1024 * 1024
SMEM = pl.BlockSpec(memory_space=pltpu.SMEM)
ANY = pl.BlockSpec(memory_space=pl.ANY)


def after(x, *others):
    return lax.optimization_barrier((x, *others))[0] if others else x


def head_part(q, k, v):
    scores = lax.dot_general(q, k, (((1,), (1,)), ((), ())), preferred_element_type=jnp.float32)
    peak = jnp.max(scores, axis=1, keepdims=True)
    weights = jnp.exp2((scores - peak) * SCALE).astype(jnp.bfloat16)
    ones = jnp.ones((v.shape[0], HEAD_DIM), jnp.bfloat16)
    both = jnp.dot(weights, jnp.concatenate([v, ones], axis=1), preferred_element_type=jnp.float32)
    return both[:, :HEAD_DIM], both[:, HEAD_DIM:], jnp.broadcast_to(peak, v.shape)


def merge(old, new):
    part, total, peak = old
    part_new, total_new, peak_new = new
    top = jnp.maximum(peak, peak_new)
    f_old = jnp.exp2((peak - top) * SCALE)
    f_new = jnp.exp2((peak_new - top) * SCALE)
    return f_old * part + f_new * part_new, f_old * total + f_new * total_new, top


def columns_of(h):
    return pl.ds(h * HEAD_DIM, HEAD_DIM)


def fold(state, active, q, k, v):
    @pl.when(active == 1)
    def _():
        for h in range(q.shape[1] // HEAD_DIM):
            at = columns_of(h)
            new = head_part(q[:, at], k[:, at], v[:, at])
            for r, x in zip(state, merge(tuple(r[:, at] for r in state), new)):
                r[:, at] = x


class Fetch:
    def __init__(self, sems):
        self.sems, self.count = sems, 0

    def __call__(self, source, target):
        copy = pltpu.make_async_copy(source, target, self.sems.at[self.count])
        self.count += 1
        copy.start()
        return copy


def attend_kernel(slots, active, q, *refs):
    kv, (part, stats), scratch = refs[: 2 * slots + 2], refs[2 * slots + 2 : 2 * slots + 4], refs[2 * slots + 4 :]
    q_v, kv_v, (part_v, total_v, peak_v, stats_v, sems) = scratch[0], scratch[1 : 2 * slots + 3], scratch[2 * slots + 3 :]
    fetch = Fetch(sems)
    copies = [fetch(source, target) for source, target in zip((q, *kv), (q_v, *kv_v))]
    for copy in copies[:3]:
        copy.wait()
    state = (part_v, total_v, peak_v)
    heads = q_v.shape[1] // HEAD_DIM
    for h in range(heads):
        at = columns_of(h)
        for r, x in zip(state, head_part(q_v[:, at], kv_v[0][:, at], kv_v[1][:, at])):
            r[:, at] = x
    for slot in range(slots):
        for copy in copies[3 + 2 * slot : 5 + 2 * slot]:
            copy.wait()
        fold(state, active[slot], q_v, kv_v[2 * slot + 2], kv_v[2 * slot + 3])
    lane = lax.broadcasted_iota(jnp.int32, stats_v.shape, 1)
    packed = jnp.zeros(stats_v.shape, jnp.float32)
    for h in range(heads):
        packed = jnp.where(lane == h, total_v[:, columns_of(h)], packed)
        packed = jnp.where(lane == HEAD_DIM // 2 + h, peak_v[:, columns_of(h)], packed)
    stats_v[...] = packed
    copies = [fetch(part_v, part), fetch(stats_v, stats)]
    for copy in copies:
        copy.wait()


def attend(active, q, kv):
    rows, columns = q.shape
    slots = len(kv) // 2 - 1
    return pl.pallas_call(
        functools.partial(attend_kernel, slots),
        out_shape=[
            jax.ShapeDtypeStruct((rows, columns), jnp.float32),
            jax.ShapeDtypeStruct((rows, HEAD_DIM), jnp.float32),
        ],
        in_specs=[SMEM] + [ANY] * (1 + len(kv)),
        out_specs=[ANY] * 2,
        scratch_shapes=[pltpu.VMEM((rows, columns), jnp.bfloat16)] * (1 + len(kv))
        + [pltpu.VMEM((rows, columns), jnp.float32)] * 3
        + [pltpu.VMEM((rows, HEAD_DIM), jnp.float32), pltpu.SemaphoreType.DMA((3 + len(kv),))],
        compiler_params=pltpu.CompilerParams(vmem_limit_bytes=VMEM_LIMIT),
        cost_estimate=pl.CostEstimate(
            flops=(1 + slots) * 6 * rows * rows * columns,
            bytes_accessed=rows * columns * (10 + 4 * slots),
            transcendentals=0,
        ),
        name="attend",
    )(active, q, *kv)


def close_heads(fetch, first, active, q, part, stats, near, q_v, near_v, state, stats_v, out, out_at):
    columns = state[0].shape[1]
    copies = [
        fetch(q.at[:, pl.ds(first * HEAD_DIM, columns)], q_v),
        fetch(part.at[:, pl.ds(first * HEAD_DIM, columns)], state[0]),
        fetch(stats, stats_v),
    ] + [fetch(source, target) for source, target in zip(near, near_v)]
    for copy in copies[:3]:
        copy.wait()
    stats_now = stats_v[...]
    for h in range(columns // HEAD_DIM):
        for r, lane in zip(state[1:], (first + h, HEAD_DIM // 2 + first + h)):
            r[:, columns_of(h)] = jnp.broadcast_to(stats_now[:, lane : lane + 1], stats_now.shape)
    for slot, kv in enumerate(near_v):
        copies[3 + slot].wait()
        fold(state, active[slot], q_v, kv.at[:, pl.ds(0, columns)], kv.at[:, pl.ds(columns, columns)])
    out[:, out_at] = (state[0][...] / state[1][...]).astype(jnp.bfloat16)


def close_scratch(rows, columns, slots):
    return (
        [pltpu.VMEM((rows, columns), jnp.bfloat16)]
        + [pltpu.VMEM((rows, 2 * columns), jnp.bfloat16)] * slots
        + [pltpu.VMEM((rows, columns), jnp.float32)] * 3
        + [pltpu.VMEM((rows, HEAD_DIM), jnp.float32), pltpu.SemaphoreType.DMA((4 + slots,))]
    )


def close_kernel(first, slots, active, q, part, stats, *refs):
    near, out = refs[:slots], refs[slots]
    q_v, near_v, (*state, stats_v, sems, out_v) = refs[slots + 1], refs[slots + 2 : 2 * slots + 2], refs[2 * slots + 2 :]
    fetch = Fetch(sems)
    close_heads(fetch, first, active, q, part, stats, near, q_v, near_v, state, stats_v, out_v, slice(None))
    fetch(out_v, out).wait()


def close(active, q, state, near, first):
    rows, columns = q.shape[0], near[0].shape[1] // 2
    return pl.pallas_call(
        functools.partial(close_kernel, first, len(near)),
        out_shape=jax.ShapeDtypeStruct((rows, columns), jnp.bfloat16),
        in_specs=[SMEM] + [ANY] * (3 + len(near)),
        out_specs=ANY,
        scratch_shapes=close_scratch(rows, columns, len(near)) + [pltpu.VMEM((rows, columns), jnp.bfloat16)],
        compiler_params=pltpu.CompilerParams(vmem_limit_bytes=VMEM_LIMIT),
        cost_estimate=pl.CostEstimate(
            flops=len(near) * 6 * rows * rows * columns,
            bytes_accessed=rows * columns * (4 * len(near) + 8),
            transcendentals=0,
        ),
        name="close",
    )(active, q, *state, *near)


def finish_kernel(counts, moves, control_rows, place, active, q, part, stats, *refs):
    groups_of = []
    for count in counts:
        groups_of.append(refs[:count])
        refs = refs[count:]
    near, ready, weight, control = groups_of
    slots, blocks = len(near), len(control)
    hidden, out, refs = refs[0], refs[1], refs[2:]
    q_v, near_v, refs = refs[0], refs[1 : slots + 1], refs[slots + 1 :]
    *state, stats_v, sems, attention, held, hidden_v, control_v, out_v, late_sems = refs
    fetch, late_fetch = Fetch(sems), Fetch(late_sems)
    late = []
    done = 0
    for block in ready:
        late.append(late_fetch(block, attention.at[:, pl.ds(done, block.shape[1])]))
        done += block.shape[1]

    def fetch_late():
        for piece, index, at in moves:
            source = weight[piece] if at is None else weight[piece].at[index]
            if at is None:
                target = held
            else:
                group, outer, pair, core = at
                count = source.shape[0]
                outer = place[1] ^ outer
                start = pl.multiple_of(((outer * 2 + pair) * 2 + core) * count, count)
                target = held.at[group, pl.ds(start, count), :]
            late.append(late_fetch(source, target))
        late.append(late_fetch(hidden, hidden_v))
        for d in range(blocks):
            start = pl.multiple_of((place[4] ^ d) * control_rows, control_rows) if blocks > 1 else 0
            late.append(late_fetch(control[d], control_v.at[pl.ds(start, control_rows), :]))

    fetch_late()
    close_heads(
        fetch,
        done // HEAD_DIM,
        active,
        q,
        part,
        stats,
        near,
        q_v,
        near_v,
        state,
        stats_v,
        attention,
        pl.ds(done, q_v.shape[1]),
    )
    for copy in late[len(ready) + len(moves) :] + late[: len(ready)]:
        copy.wait()
    groups, _, columns = held.shape
    step = 256 if columns % 256 == 0 else columns
    stores = []
    for group in range(groups):
        for number, (_, _, at) in enumerate(moves):
            if group == (at[0] if at else 0):
                late[len(ready) + number].wait()
        for j in range(columns // step):
            at = pl.ds(group * columns + j * step, step)
            projected = jnp.dot(
                attention[...], held[group, :, pl.ds(j * step, step)], preferred_element_type=jnp.float32
            )
            out_v[:, at] = (
                hidden_v[:, at].astype(jnp.float32) + projected + control_v[:, at].astype(jnp.float32)
            ).astype(jnp.bfloat16)
            stores.append(late_fetch(out_v.at[:, at], out.at[:, at]))
    for copy in stores:
        copy.wait()


def finish(place, active, q, state, near, ready, weight, control, hidden, moves):
    rows, inner = q.shape
    width = hidden.shape[1]
    groups = lax.axis_size("groups")
    control_rows = control[0].shape[0]
    columns = near[0].shape[1] // 2
    share = width // groups
    lists = (near, ready, weight, control)
    counts = tuple(len(x) for x in lists)
    step = 256 if share % 256 == 0 else share
    return pl.pallas_call(
        functools.partial(finish_kernel, counts, moves, control_rows),
        out_shape=jax.ShapeDtypeStruct((rows, width), jnp.bfloat16),
        in_specs=[SMEM] * 2 + [ANY] * (4 + sum(counts)),
        out_specs=ANY,
        scratch_shapes=close_scratch(rows, columns, len(near))
        + [
            pltpu.VMEM((rows, inner), jnp.bfloat16),
            pltpu.VMEM((groups, inner, share), jnp.bfloat16),
            pltpu.VMEM((rows, width), jnp.bfloat16),
            pltpu.VMEM((rows, width), jnp.bfloat16),
            pltpu.VMEM((rows, width), jnp.bfloat16),
            pltpu.SemaphoreType.DMA((len(ready) + len(moves) + 1 + len(control) + width // step,)),
        ],
        compiler_params=pltpu.CompilerParams(vmem_limit_bytes=VMEM_LIMIT),
        cost_estimate=pl.CostEstimate(
            flops=2 * rows * inner * width, bytes_accessed=2 * inner * width + 6 * rows * width, transcendentals=0
        ),
        name="finish",
    )(place, active, q, *state, *near, *ready, *weight, *control, hidden)


def flipped(block, axis, flip):
    return lax.ppermute(block, axis, [(i, i ^ flip) for i in range(lax.axis_size(axis))])


class Lane:
    def __init__(self):
        self.last = ()

    def __call__(self, send, block, *others):
        self.last = (send(after(block, *self.last, *others)),)
        return self.last[0]


def swap(axis, flip):
    return lambda block: flipped(block, axis, flip)


def route_of(route):
    return lambda block: lax.ppermute(block, TILES, route)


def neighbour_slots(tile_count, strides, counts):
    slots = []
    for axis, (stride, count) in enumerate(zip(strides, counts)):
        for odd in range(2):
            route = []
            for t in range(tile_count):
                place = t // stride % count
                if place % 2 == odd and place + 1 < count:
                    route += [(t, t + stride), (t + stride, t)]
            if route:
                slots.append((axis, odd, route))
    return slots


def on_device(hidden, queries, keys, values, control, out_weight, pattern):
    groups = lax.axis_size("groups")
    outer, pair, cores = (lax.axis_size(a) for a in TILES)
    tile_count = outer * pair * cores
    grid_width = min(8, tile_count // 4)
    grid_height = min(4, tile_count // 8)
    layer = grid_width * grid_height
    strides = (layer, grid_width, 1)
    counts = (tile_count // layer, grid_height, grid_width)
    position = lax.axis_index(TILES)
    across = position % grid_width
    rows = queries.shape[0]
    width = hidden.shape[1]
    slots = neighbour_slots(tile_count, strides, counts)
    early = [s for s in slots if s[0] == 2]
    late = [s for s in slots if s[0] != 2]

    def flags(chosen):
        active = []
        for axis, odd, _ in chosen:
            place = position // strides[axis] % counts[axis]
            up = (place % 2 == odd).astype(jnp.int32)
            valid = jnp.where(up == 1, place + 1 < counts[axis], place >= 1)
            active.append((valid & (pattern[0, 2 * axis + up] == 1)).astype(jnp.int32))
        return jnp.stack(active)

    early_active, late_active = flags(early), flags(late)
    far_lane, near_lane = Lane(), Lane()

    shard, share = out_weight.shape[0], width // groups
    line = out_weight[:, :share]
    for g in range(1, groups):
        line = jnp.where(lax.axis_index("groups") == g, out_weight[:, g * share : (g + 1) * share], line)
    line = lax.optimization_barrier(line)[None]
    line_flips = [0]
    flip = outer // 2
    while flip > 2:
        line = jnp.concatenate([line, flipped(line, "outer", flip)])
        line_flips += [f ^ flip for f in line_flips]
        flip //= 2
    far = far_lane(swap("outer", 2), line)
    near = near_lane(swap("outer", 1), line)
    last = swap("outer", 1)(far)

    firsts = [sum(CHUNKS[:i]) for i in range(len(CHUNKS))]
    chunks = [
        jnp.concatenate([x[:, f * HEAD_DIM : (f + n) * HEAD_DIM] for x in (keys, values)], axis=1)
        for f, n in zip(firsts, CHUNKS)
    ]
    block = rows // grid_width
    lines = after(control, line).reshape(block // TILE_W, grid_width, TILE_W, width)
    control_sent = [
        lax.dynamic_index_in_dim(lines, across ^ d, 1, keepdims=False).reshape(block, width) for d in range(grid_width)
    ]
    control_parts = list(control_sent)
    early_near = [[None, None] for _ in early]
    waits = (line,)
    for i, x in enumerate((keys, values)):
        sent = []
        for slot in range(1, len(early)):
            early_near[slot][i] = lax.ppermute(after(x, *waits), TILES, early[slot][2])
            sent.append(early_near[slot][i])
        for d in range(2 + i, grid_width, 2):
            control_parts[d] = swap(TILES, d)(after(control_sent[d], *waits))
            sent.append(control_parts[d])
        waits = (far, near, *sent)
    control_parts[1] = swap(TILES, 1)(control_sent[1])
    for i, x in enumerate((keys, values)):
        early_near[0][i] = lax.ppermute(x, TILES, early[0][2])
    state = attend(early_active, queries, [keys, values] + [x for kv in early_near for x in kv])

    steps = (line, far, near, last)
    weight = [lax.all_gather(after(jnp.concatenate(steps), *sent), ("groups", "pair", "core"))]
    n = len(line_flips)
    moves = [
        (0, ((g * pair + p) * cores + c, i * n + j), (g, f ^ at, p, c))
        for g in range(groups)
        for p in range(pair)
        for c in range(cores)
        for i, at in enumerate((0, 2, 1, 3))
        for j, f in enumerate(line_flips)
    ]

    late_near = []
    for chunk in chunks:
        lanes = (far_lane, near_lane)
        late_near.append([lanes[i % 2](route_of(route), chunk) for i, (_, _, route) in enumerate(late)])
    ready = [close(late_active, queries, state, late_near[i], firsts[i]) for i in range(len(CHUNKS) - 1)]
    if block % 16:
        control_parts = [
            jnp.take(
                jnp.stack(control_parts), jnp.arange(grid_width, dtype=jnp.int32) ^ across, axis=0
            ).reshape(rows, width)
        ]
    place = jnp.stack([lax.axis_index(a) for a in ("groups",) + TILES] + [across]).astype(jnp.int32)
    if shard % 16:
        weight, moves = [in_order(weight, moves, place, (groups, outer, pair, cores))], [(0, None, None)]
    return finish(
        place,
        late_active,
        queries,
        state,
        late_near[-1],
        ready,
        weight,
        control_parts,
        hidden,
        tuple(moves),
    )


def in_order(weight, moves, place, sizes):
    blocks = {at: weight[piece][index] for piece, index, at in moves}
    whole = jnp.stack([blocks[at] for at in sorted(blocks)])
    shard, columns = whole.shape[1:]
    whole = whole.reshape(sizes + (shard, columns))
    whole = jnp.take(whole, jnp.arange(sizes[1], dtype=jnp.int32) ^ place[1], axis=1)
    return whole.reshape(sizes[0], -1, columns)


def solution(mesh):
    groups = mesh.shape["groups"]
    tiles = mesh.shape["tiles"]
    split = Mesh(mesh.devices.reshape(groups, tiles // 4, 2, 2), ("groups",) + TILES)
    rows = P(("groups",) + TILES, None)
    placed = (rows, rows, rows, rows, rows, P(TILES, None), rows)
    return jax.shard_map(
        on_device,
        mesh=split,
        in_specs=placed,
        out_specs=rows,
        check_vma=False,
    )
```

```python
import functools
import math

import jax
import jax.numpy as jnp
from jax import lax
from jax.experimental import pallas as pl
from jax.experimental.pallas import tpu as pltpu
from jax.sharding import Mesh
from jax.sharding import PartitionSpec as P

HEAD_DIM = 128
TILE_W = 8
CHUNKS = (6, 6)
SCALE = HEAD_DIM**-0.5 * math.log2(math.e)
TILES = ("outer", "pair", "core")
VMEM_LIMIT = 60 * 1024 * 1024
SMEM = pl.BlockSpec(memory_space=pltpu.SMEM)
ANY = pl.BlockSpec(memory_space=pl.ANY)


def after(x, *others):
    return lax.optimization_barrier((x, *others))[0] if others else x


def head_part(q, k, v):
    scores = lax.dot_general(q, k, (((1,), (1,)), ((), ())), preferred_element_type=jnp.float32)
    peak = jnp.max(scores, axis=1, keepdims=True)
    weights = jnp.exp2((scores - peak) * SCALE).astype(jnp.bfloat16)
    ones = jnp.ones((v.shape[0], HEAD_DIM), jnp.bfloat16)
    both = jnp.dot(weights, jnp.concatenate([v, ones], axis=1), preferred_element_type=jnp.float32)
    return both[:, :HEAD_DIM], both[:, HEAD_DIM:], jnp.broadcast_to(peak, v.shape)


def merge(old, new):
    part, total, peak = old
    part_new, total_new, peak_new = new
    top = jnp.maximum(peak, peak_new)
    f_old = jnp.exp2((peak - top) * SCALE)
    f_new = jnp.exp2((peak_new - top) * SCALE)
    return f_old * part + f_new * part_new, f_old * total + f_new * total_new, top


def columns_of(h):
    return pl.ds(h * HEAD_DIM, HEAD_DIM)


def fold(state, active, q, k, v):
    @pl.when(active == 1)
    def _():
        for h in range(q.shape[1] // HEAD_DIM):
            at = columns_of(h)
            new = head_part(q[:, at], k[:, at], v[:, at])
            for r, x in zip(state, merge(tuple(r[:, at] for r in state), new)):
                r[:, at] = x


class Fetch:
    def __init__(self, sems):
        self.sems, self.count = sems, 0

    def __call__(self, source, target):
        copy = pltpu.make_async_copy(source, target, self.sems.at[self.count])
        self.count += 1
        copy.start()
        return copy


def attend_kernel(slots, active, q, *refs):
    kv, (part, stats), scratch = refs[: 2 * slots + 2], refs[2 * slots + 2 : 2 * slots + 4], refs[2 * slots + 4 :]
    q_v, kv_v, (part_v, total_v, peak_v, stats_v, sems) = scratch[0], scratch[1 : 2 * slots + 3], scratch[2 * slots + 3 :]
    fetch = Fetch(sems)
    copies = [fetch(source, target) for source, target in zip((q, *kv), (q_v, *kv_v))]
    for copy in copies[:3]:
        copy.wait()
    state = (part_v, total_v, peak_v)
    heads = q_v.shape[1] // HEAD_DIM
    for h in range(heads):
        at = columns_of(h)
        for r, x in zip(state, head_part(q_v[:, at], kv_v[0][:, at], kv_v[1][:, at])):
            r[:, at] = x
    for slot in range(slots):
        for copy in copies[3 + 2 * slot : 5 + 2 * slot]:
            copy.wait()
        fold(state, active[slot], q_v, kv_v[2 * slot + 2], kv_v[2 * slot + 3])
    lane = lax.broadcasted_iota(jnp.int32, stats_v.shape, 1)
    packed = jnp.zeros(stats_v.shape, jnp.float32)
    for h in range(heads):
        packed = jnp.where(lane == h, total_v[:, columns_of(h)], packed)
        packed = jnp.where(lane == HEAD_DIM // 2 + h, peak_v[:, columns_of(h)], packed)
    stats_v[...] = packed
    copies = [fetch(part_v, part), fetch(stats_v, stats)]
    for copy in copies:
        copy.wait()


def attend(active, q, kv):
    rows, columns = q.shape
    slots = len(kv) // 2 - 1
    return pl.pallas_call(
        functools.partial(attend_kernel, slots),
        out_shape=[
            jax.ShapeDtypeStruct((rows, columns), jnp.float32),
            jax.ShapeDtypeStruct((rows, HEAD_DIM), jnp.float32),
        ],
        in_specs=[SMEM] + [ANY] * (1 + len(kv)),
        out_specs=[ANY] * 2,
        scratch_shapes=[pltpu.VMEM((rows, columns), jnp.bfloat16)] * (1 + len(kv))
        + [pltpu.VMEM((rows, columns), jnp.float32)] * 3
        + [pltpu.VMEM((rows, HEAD_DIM), jnp.float32), pltpu.SemaphoreType.DMA((3 + len(kv),))],
        compiler_params=pltpu.CompilerParams(vmem_limit_bytes=VMEM_LIMIT),
        cost_estimate=pl.CostEstimate(
            flops=(1 + slots) * 6 * rows * rows * columns,
            bytes_accessed=rows * columns * (10 + 4 * slots),
            transcendentals=0,
        ),
        name="attend",
    )(active, q, *kv)


def close_heads(fetch, first, active, q, part, stats, near, q_v, near_v, state, stats_v, out, out_at):
    columns = state[0].shape[1]
    copies = [
        fetch(q.at[:, pl.ds(first * HEAD_DIM, columns)], q_v),
        fetch(part.at[:, pl.ds(first * HEAD_DIM, columns)], state[0]),
        fetch(stats, stats_v),
    ] + [fetch(source, target) for source, target in zip(near, near_v)]
    for copy in copies[:3]:
        copy.wait()
    stats_now = stats_v[...]
    for h in range(columns // HEAD_DIM):
        for r, lane in zip(state[1:], (first + h, HEAD_DIM // 2 + first + h)):
            r[:, columns_of(h)] = jnp.broadcast_to(stats_now[:, lane : lane + 1], stats_now.shape)
    for slot, kv in enumerate(near_v):
        copies[3 + slot].wait()
        fold(state, active[slot], q_v, kv.at[:, pl.ds(0, columns)], kv.at[:, pl.ds(columns, columns)])
    out[:, out_at] = (state[0][...] / state[1][...]).astype(jnp.bfloat16)


def close_scratch(rows, columns, slots):
    return (
        [pltpu.VMEM((rows, columns), jnp.bfloat16)]
        + [pltpu.VMEM((rows, 2 * columns), jnp.bfloat16)] * slots
        + [pltpu.VMEM((rows, columns), jnp.float32)] * 3
        + [pltpu.VMEM((rows, HEAD_DIM), jnp.float32), pltpu.SemaphoreType.DMA((4 + slots,))]
    )


def close_kernel(first, slots, active, q, part, stats, *refs):
    near, out = refs[:slots], refs[slots]
    q_v, near_v, (*state, stats_v, sems, out_v) = refs[slots + 1], refs[slots + 2 : 2 * slots + 2], refs[2 * slots + 2 :]
    fetch = Fetch(sems)
    close_heads(fetch, first, active, q, part, stats, near, q_v, near_v, state, stats_v, out_v, slice(None))
    fetch(out_v, out).wait()


def close(active, q, state, near, first):
    rows, columns = q.shape[0], near[0].shape[1] // 2
    return pl.pallas_call(
        functools.partial(close_kernel, first, len(near)),
        out_shape=jax.ShapeDtypeStruct((rows, columns), jnp.bfloat16),
        in_specs=[SMEM] + [ANY] * (3 + len(near)),
        out_specs=ANY,
        scratch_shapes=close_scratch(rows, columns, len(near)) + [pltpu.VMEM((rows, columns), jnp.bfloat16)],
        compiler_params=pltpu.CompilerParams(vmem_limit_bytes=VMEM_LIMIT),
        cost_estimate=pl.CostEstimate(
            flops=len(near) * 6 * rows * rows * columns,
            bytes_accessed=rows * columns * (4 * len(near) + 8),
            transcendentals=0,
        ),
        name="close",
    )(active, q, *state, *near)


def finish_kernel(counts, moves, control_rows, place, hidden, *refs):
    parts = []
    for count in counts:
        parts.append(refs[:count])
        refs = refs[count:]
    ready, weight, control = parts
    out, attention, held, hidden_v, control_v, out_v, sems = refs
    blocks = len(control)
    fetch = Fetch(sems)
    fetched, residual = [], []
    done = 0
    for block in ready:
        residual.append(fetch(block, attention.at[:, pl.ds(done, block.shape[1])]))
        done += block.shape[1]
    for piece, index, at in moves:
        source = weight[piece] if at is None else weight[piece].at[index]
        if at is None:
            target = held
        else:
            flip, group, outer, pair, core = at
            count = source.shape[0]
            outer = place[1] ^ outer
            if flip:
                group, pair, core = place[0] ^ group, place[2] ^ pair, place[3] ^ core
            start = pl.multiple_of(((outer * 2 + pair) * 2 + core) * count, count)
            target = held.at[group, pl.ds(start, count), :]
        fetched.append(fetch(source, target))
    residual.append(fetch(hidden, hidden_v))
    for d in range(blocks):
        start = pl.multiple_of((place[4] ^ d) * control_rows, control_rows) if blocks > 1 else 0
        residual.append(fetch(control[d], control_v.at[pl.ds(start, control_rows), :]))
    for copy in residual:
        copy.wait()
    groups, _, columns = held.shape
    step = 512 if columns % 512 == 0 else columns
    stores = []
    for group in range(groups):
        for copy, (_, _, at) in zip(fetched, moves):
            if group == (0 if at is None or at[0] else at[1]):
                copy.wait()
        for j in range(columns // step):
            at = pl.ds(group * columns + j * step, step)
            projected = jnp.dot(
                attention[...], held[group, :, pl.ds(j * step, step)], preferred_element_type=jnp.float32
            )
            out_v[:, at] = (
                hidden_v[:, at].astype(jnp.float32) + projected + control_v[:, at].astype(jnp.float32)
            ).astype(jnp.bfloat16)
            stores.append(fetch(out_v.at[:, at], out.at[:, at]))
    for copy in stores:
        copy.wait()


def finish(place, ready, weight, control, hidden, moves):
    rows, width = hidden.shape
    inner = sum(x.shape[1] for x in ready)
    groups = lax.axis_size("groups")
    control_rows = control[0].shape[0]
    share = width // groups
    lists = (ready, weight, control)
    counts = tuple(len(x) for x in lists)
    step = 512 if share % 512 == 0 else share
    return pl.pallas_call(
        functools.partial(finish_kernel, counts, moves, control_rows),
        out_shape=jax.ShapeDtypeStruct((rows, width), jnp.bfloat16),
        in_specs=[SMEM] + [ANY] * (1 + sum(counts)),
        out_specs=ANY,
        scratch_shapes=[
            pltpu.VMEM((rows, inner), jnp.bfloat16),
            pltpu.VMEM((groups, inner, share), jnp.bfloat16),
            pltpu.VMEM((rows, width), jnp.bfloat16),
            pltpu.VMEM((rows, width), jnp.bfloat16),
            pltpu.VMEM((rows, width), jnp.bfloat16),
            pltpu.SemaphoreType.DMA((len(ready) + len(moves) + 1 + len(control) + width // step,)),
        ],
        compiler_params=pltpu.CompilerParams(vmem_limit_bytes=VMEM_LIMIT),
        cost_estimate=pl.CostEstimate(
            flops=2 * rows * inner * width, bytes_accessed=2 * inner * width + 6 * rows * width, transcendentals=0
        ),
        name="finish",
    )(place, hidden, *ready, *weight, *control)


def flipped(block, axis, flip):
    return lax.ppermute(block, axis, [(i, i ^ flip) for i in range(lax.axis_size(axis))])


class Lane:
    def __init__(self):
        self.last = ()

    def __call__(self, send, block, *others):
        self.last = (send(after(block, *self.last, *others)),)
        return self.last[0]


def swap(axis, flip):
    return lambda block: flipped(block, axis, flip)


def route_of(route):
    return lambda block: lax.ppermute(block, TILES, route)


def neighbour_slots(tile_count, strides, counts):
    slots = []
    for axis, (stride, count) in enumerate(zip(strides, counts)):
        for odd in range(2):
            route = []
            for t in range(tile_count):
                place = t // stride % count
                if place % 2 == odd and place + 1 < count:
                    route += [(t, t + stride), (t + stride, t)]
            if route:
                slots.append((axis, odd, route))
    return slots


def on_device(hidden, queries, keys, values, control, out_weight, pattern):
    groups = lax.axis_size("groups")
    outer, pair, cores = (lax.axis_size(a) for a in TILES)
    tile_count = outer * pair * cores
    grid_width = min(8, tile_count // 4)
    grid_height = min(4, tile_count // 8)
    layer = grid_width * grid_height
    strides = (layer, grid_width, 1)
    counts = (tile_count // layer, grid_height, grid_width)
    position = lax.axis_index(TILES)
    across = position % grid_width
    rows = queries.shape[0]
    width = hidden.shape[1]
    slots = neighbour_slots(tile_count, strides, counts)
    early = [s for s in slots if s[0] == 2]
    late = [s for s in slots if s[0] != 2]

    def flags(chosen):
        active = []
        for axis, odd, _ in chosen:
            place = position // strides[axis] % counts[axis]
            up = (place % 2 == odd).astype(jnp.int32)
            valid = jnp.where(up == 1, place + 1 < counts[axis], place >= 1)
            active.append((valid & (pattern[0, 2 * axis + up] == 1)).astype(jnp.int32))
        return jnp.stack(active)

    early_active, late_active = flags(early), flags(late)
    far_lane, near_lane = Lane(), Lane()

    shard, share = out_weight.shape[0], width // groups
    line = out_weight[:, :share]
    for g in range(1, groups):
        line = jnp.where(lax.axis_index("groups") == g, out_weight[:, g * share : (g + 1) * share], line)
    line = lax.optimization_barrier(line)[None]
    line_flips = [0]
    flip = outer // 2
    while flip > 2:
        line = jnp.concatenate([line, flipped(line, "outer", flip)])
        line_flips += [f ^ flip for f in line_flips]
        flip //= 2
    far = far_lane(swap("outer", 2), line)
    near = near_lane(swap("outer", 1), line)
    last = swap("outer", 1)(after(far, near))

    firsts = [sum(CHUNKS[:i]) for i in range(len(CHUNKS))]
    chunks = [
        jnp.concatenate([x[:, f * HEAD_DIM : (f + n) * HEAD_DIM] for x in (keys, values)], axis=1)
        for f, n in zip(firsts, CHUNKS)
    ]
    block = rows // grid_width
    lines = after(control, line).reshape(block // TILE_W, grid_width, TILE_W, width)
    control_sent = [
        lax.dynamic_index_in_dim(lines, across ^ d, 1, keepdims=False).reshape(block, width) for d in range(grid_width)
    ]
    control_parts = [control_sent[0]] + [None] * (grid_width - 1)
    early_x = []
    for d in range(2, grid_width - 1):
        control_parts[d] = swap(TILES, d)(after(control_sent[d], line))
        early_x.append(control_parts[d])
    control_parts[-1] = swap(TILES, grid_width - 1)(after(control_sent[-1], *early_x))
    control_parts[1] = swap(TILES, 1)(control_sent[1])
    plane = jnp.concatenate([line, swap("pair", 1)(line)])
    held = [plane, swap("groups", 1)(plane)]
    crossed = [swap("core", 1)(x) for x in held]
    early_near = [[lax.ppermute(x, TILES, route) for x in (keys, values)] for _, _, route in early]
    state = attend(early_active, queries, [keys, values] + [x for kv in early_near for x in kv])

    steps = after(jnp.concatenate([far, near, last]), control_parts[-1], held[1])
    weight = [lax.all_gather(steps, ("groups", "pair", "core"))]
    n = len(line_flips)
    moves = [
        (0, ((g * pair + p) * cores + c, i * n + j), (False, g, f ^ at, p, c))
        for g in range(groups)
        for p in range(pair)
        for c in range(cores)
        for i, at in enumerate((2, 1, 3))
        for j, f in enumerate(line_flips)
    ]
    for group_flip in range(2):
        for core_flip, pieces in enumerate((held, crossed)):
            moves += [
                (len(weight), (p * n + j,), (True, group_flip, f, p, core_flip))
                for p in range(pair)
                for j, f in enumerate(line_flips)
            ]
            weight.append(pieces[group_flip])

    late_near = []
    for chunk in chunks:
        lanes = (far_lane, near_lane)
        late_near.append([lanes[i % 2](route_of(route), chunk) for i, (_, _, route) in enumerate(late)])
    ready = [close(late_active, queries, state, late_near[i], firsts[i]) for i in range(len(CHUNKS))]
    if block % 16:
        control_parts = [
            jnp.take(
                jnp.stack(control_parts), jnp.arange(grid_width, dtype=jnp.int32) ^ across, axis=0
            ).reshape(rows, width)
        ]
    place = jnp.stack([lax.axis_index(a) for a in ("groups",) + TILES] + [across]).astype(jnp.int32)
    if shard % 16:
        weight, moves = [in_order(weight, moves, place, (groups, outer, pair, cores))], [(0, None, None)]
    return finish(place, ready, weight, control_parts, hidden, tuple(moves))


def in_order(weight, moves, place, sizes):
    groups, outer, pair, cores = sizes
    shard, columns = weight[0].shape[-2:]
    gathered = weight[0].reshape(groups, pair, cores, -1, shard, columns)
    for axis, at in enumerate((0, 2, 3)):
        gathered = jnp.take(gathered, jnp.arange(sizes[at], dtype=jnp.int32) ^ place[at], axis=axis)
    weight = [gathered.reshape(weight[0].shape)] + weight[1:]
    blocks = {at[1:]: weight[piece][index] for piece, index, at in moves}
    whole = jnp.stack([blocks[at] for at in sorted(blocks)]).reshape(sizes + (shard, columns))
    for axis, size in enumerate(sizes):
        whole = jnp.take(whole, jnp.arange(size, dtype=jnp.int32) ^ place[axis], axis=axis)
    return whole.reshape(groups, -1, columns)


def solution(mesh):
    groups = mesh.shape["groups"]
    tiles = mesh.shape["tiles"]
    split = Mesh(mesh.devices.reshape(groups, tiles // 4, 2, 2), ("groups",) + TILES)
    rows = P(("groups",) + TILES, None)
    placed = (rows, rows, rows, rows, rows, P(TILES, None), rows)
    return jax.shard_map(
        on_device,
        mesh=split,
        in_specs=placed,
        out_specs=rows,
        check_vma=False,
    )
```

```python
import functools
import math

import jax
import jax.numpy as jnp
from jax import lax
from jax.experimental import pallas as pl
from jax.experimental.pallas import tpu as pltpu
from jax.sharding import Mesh
from jax.sharding import PartitionSpec as P

HEAD_DIM = 128
TILE_W = 8
CHUNKS = (6, 6)
SCALE = HEAD_DIM**-0.5 * math.log2(math.e)
TILES = ("outer", "pair", "core")
VMEM_LIMIT = 60 * 1024 * 1024
SMEM = pl.BlockSpec(memory_space=pltpu.SMEM)
ANY = pl.BlockSpec(memory_space=pl.ANY)


def after(x, *others):
    return lax.optimization_barrier((x, *others))[0] if others else x


def head_part(q, k, v):
    scores = lax.dot_general(q, k, (((1,), (1,)), ((), ())), preferred_element_type=jnp.float32)
    peak = jnp.max(scores, axis=1, keepdims=True)
    weights = jnp.exp2((scores - peak) * SCALE).astype(jnp.bfloat16)
    ones = jnp.ones((v.shape[0], HEAD_DIM), jnp.bfloat16)
    both = jnp.dot(weights, jnp.concatenate([v, ones], axis=1), preferred_element_type=jnp.float32)
    return both[:, :HEAD_DIM], both[:, HEAD_DIM:], jnp.broadcast_to(peak, v.shape)


def merge(old, new):
    part, total, peak = old
    part_new, total_new, peak_new = new
    top = jnp.maximum(peak, peak_new)
    f_old = jnp.exp2((peak - top) * SCALE)
    f_new = jnp.exp2((peak_new - top) * SCALE)
    return f_old * part + f_new * part_new, f_old * total + f_new * total_new, top


def columns_of(h):
    return pl.ds(h * HEAD_DIM, HEAD_DIM)


def fold(state, active, q, k, v):
    @pl.when(active == 1)
    def _():
        for h in range(q.shape[1] // HEAD_DIM):
            at = columns_of(h)
            new = head_part(q[:, at], k[:, at], v[:, at])
            for r, x in zip(state, merge(tuple(r[:, at] for r in state), new)):
                r[:, at] = x


class Fetch:
    def __init__(self, sems):
        self.sems, self.count = sems, 0

    def later(self, source, target):
        self.count += 1
        return pltpu.make_async_copy(source, target, self.sems.at[self.count - 1])

    def __call__(self, source, target):
        copy = self.later(source, target)
        copy.start()
        return copy


def attend_kernel(slots, active, q, *refs):
    kv, (part, stats), scratch = refs[: 2 * slots + 2], refs[2 * slots + 2 : 2 * slots + 4], refs[2 * slots + 4 :]
    q_v, kv_v, (part_v, total_v, peak_v, stats_v, sems) = scratch[0], scratch[1 : 2 * slots + 3], scratch[2 * slots + 3 :]
    fetch = Fetch(sems)
    copies = [fetch(source, target) for source, target in zip((q, *kv), (q_v, *kv_v))]
    for copy in copies[:3]:
        copy.wait()
    state = (part_v, total_v, peak_v)
    heads = q_v.shape[1] // HEAD_DIM
    for h in range(heads):
        at = columns_of(h)
        for r, x in zip(state, head_part(q_v[:, at], kv_v[0][:, at], kv_v[1][:, at])):
            r[:, at] = x
    for slot in range(slots):
        for copy in copies[3 + 2 * slot : 5 + 2 * slot]:
            copy.wait()
        fold(state, active[slot], q_v, kv_v[2 * slot + 2], kv_v[2 * slot + 3])
    lane = lax.broadcasted_iota(jnp.int32, stats_v.shape, 1)
    packed = jnp.zeros(stats_v.shape, jnp.float32)
    for h in range(heads):
        packed = jnp.where(lane == h, total_v[:, columns_of(h)], packed)
        packed = jnp.where(lane == HEAD_DIM // 2 + h, peak_v[:, columns_of(h)], packed)
    stats_v[...] = packed
    copies = [fetch(part_v, part), fetch(stats_v, stats)]
    for copy in copies:
        copy.wait()


def attend(active, q, kv):
    rows, columns = q.shape
    slots = len(kv) // 2 - 1
    return pl.pallas_call(
        functools.partial(attend_kernel, slots),
        out_shape=[
            jax.ShapeDtypeStruct((rows, columns), jnp.float32),
            jax.ShapeDtypeStruct((rows, HEAD_DIM), jnp.float32),
        ],
        in_specs=[SMEM] + [ANY] * (1 + len(kv)),
        out_specs=[ANY] * 2,
        scratch_shapes=[pltpu.VMEM((rows, columns), jnp.bfloat16)] * (1 + len(kv))
        + [pltpu.VMEM((rows, columns), jnp.float32)] * 3
        + [pltpu.VMEM((rows, HEAD_DIM), jnp.float32), pltpu.SemaphoreType.DMA((3 + len(kv),))],
        compiler_params=pltpu.CompilerParams(vmem_limit_bytes=VMEM_LIMIT),
        cost_estimate=pl.CostEstimate(
            flops=(1 + slots) * 6 * rows * rows * columns,
            bytes_accessed=rows * columns * (10 + 4 * slots),
            transcendentals=0,
        ),
        name="attend",
    )(active, q, *kv)


def close_open(fetch, first, q, part, stats, near, q_v, near_v, state, stats_v):
    columns = state[0].shape[1]
    at = pl.ds(first * HEAD_DIM, columns)
    return [
        fetch(q.at[:, at], q_v),
        fetch(part.at[:, at], state[0]),
        fetch(stats, stats_v),
    ] + [fetch(source, target) for source, target in zip(near, near_v)]


def close_heads(copies, first, active, q_v, near_v, state, stats_v, out):
    columns = state[0].shape[1]
    for copy in copies[:3]:
        copy.wait()
    stats_now = stats_v[...]
    for h in range(columns // HEAD_DIM):
        for r, lane in zip(state[1:], (first + h, HEAD_DIM // 2 + first + h)):
            r[:, columns_of(h)] = jnp.broadcast_to(stats_now[:, lane : lane + 1], stats_now.shape)
    for slot, kv in enumerate(near_v):
        copies[3 + slot].wait()
        fold(state, active[slot], q_v, kv.at[:, pl.ds(0, columns)], kv.at[:, pl.ds(columns, columns)])
    out[...] = (state[0][...] / state[1][...]).astype(jnp.bfloat16)


def close_scratch(rows, columns, slots):
    return (
        [pltpu.VMEM((rows, columns), jnp.bfloat16)]
        + [pltpu.VMEM((rows, 2 * columns), jnp.bfloat16)] * slots
        + [pltpu.VMEM((rows, columns), jnp.float32)] * 3
        + [pltpu.VMEM((rows, HEAD_DIM), jnp.float32), pltpu.SemaphoreType.DMA((4 + slots,))]
    )


def close_kernel(first, slots, active, q, part, stats, *refs):
    near, out = refs[:slots], refs[slots]
    q_v, near_v, (*state, stats_v, sems, out_v) = refs[slots + 1], refs[slots + 2 : 2 * slots + 2], refs[2 * slots + 2 :]
    fetch = Fetch(sems)
    opened = close_open(fetch, first, q, part, stats, near, q_v, near_v, state, stats_v)
    close_heads(opened, first, active, q_v, near_v, state, stats_v, out_v)
    fetch(out_v, out).wait()


def close(active, q, state, near, first):
    rows, columns = q.shape[0], near[0].shape[1] // 2
    return pl.pallas_call(
        functools.partial(close_kernel, first, len(near)),
        out_shape=jax.ShapeDtypeStruct((rows, columns), jnp.bfloat16),
        in_specs=[SMEM] + [ANY] * (3 + len(near)),
        out_specs=ANY,
        scratch_shapes=close_scratch(rows, columns, len(near)) + [pltpu.VMEM((rows, columns), jnp.bfloat16)],
        compiler_params=pltpu.CompilerParams(vmem_limit_bytes=VMEM_LIMIT),
        cost_estimate=pl.CostEstimate(
            flops=len(near) * 6 * rows * rows * columns,
            bytes_accessed=rows * columns * (4 * len(near) + 8),
            transcendentals=0,
        ),
        name="close",
    )(active, q, *state, *near)


def fetch_weight(fetch, moves, place, weight, held, low, high):
    copies = []
    for piece, index, at in moves:
        if at is None:
            copies.append((True, 0, fetch(weight[piece], held)))
            continue
        source = weight[piece].at[index]
        flip, group, outer, pair, core = at
        known = None if flip else group
        count = source.shape[0]
        outer = place[1] ^ outer
        if flip:
            group, pair, core = place[0] ^ group, place[2] ^ pair, place[3] ^ core
        start = pl.multiple_of(((outer * 2 + pair) * 2 + core) * count, count)
        needed = (start < high) & (start + count > low)
        copy = fetch.later(source, held.at[group, pl.ds(start, count), :])
        pl.when(needed)(copy.start)
        copies.append((needed, 0 if known is None else known, copy))
    return copies


def project(copies, attention, held, low, out, add):
    groups, _, columns = held.shape
    step = 512 if columns % 512 == 0 else columns
    for group in range(groups):
        for needed, at, copy in copies:
            if at == group:
                if needed is True:
                    copy.wait()
                else:
                    pl.when(needed)(copy.wait)
        for j in range(columns // step):
            at = pl.ds(group * columns + j * step, step)
            projected = jnp.dot(
                attention[...],
                held[group, pl.ds(low, attention.shape[1]), pl.ds(j * step, step)],
                preferred_element_type=jnp.float32,
            )
            out(at, add(at) + projected)


def begin_kernel(counts, moves, control_rows, place, hidden, ready, *refs):
    weight, control = refs[: counts[0]], refs[counts[0] : sum(counts)]
    out, attention, held, hidden_v, control_v, out_v, sems = refs[sum(counts) :]
    fetch = Fetch(sems)
    residual = [fetch(ready, attention), fetch(hidden, hidden_v)]
    copies = fetch_weight(fetch, moves, place, weight, held, 0, ready.shape[1])
    for d, block in enumerate(control):
        start = pl.multiple_of((place[4] ^ d) * control_rows, control_rows) if len(control) > 1 else 0
        residual.append(fetch(block, control_v.at[pl.ds(start, control_rows), :]))
    for copy in residual:
        copy.wait()
    stores = []

    def store(at, x):
        out_v[:, at] = x
        stores.append(fetch(out_v.at[:, at], out.at[:, at]))

    project(
        copies,
        attention,
        held,
        0,
        store,
        lambda at: hidden_v[:, at].astype(jnp.float32) + control_v[:, at].astype(jnp.float32),
    )
    for copy in stores:
        copy.wait()


def finish_kernel(slots, pieces, moves, first, place, active, q, part, stats, so_far, *refs):
    near, weight, out, refs = refs[:slots], refs[slots : slots + pieces], refs[slots + pieces], refs[slots + pieces + 1 :]
    q_v, near_v, (*state, stats_v, sems, attention, held, sum_v, out_v, late_sems) = (
        refs[0],
        refs[1 : slots + 1],
        refs[slots + 1 :],
    )
    fetch, late_fetch = Fetch(sems), Fetch(late_sems)
    low = first * HEAD_DIM
    opened = close_open(fetch, first, q, part, stats, near, q_v, near_v, state, stats_v)
    copies = fetch_weight(late_fetch, moves, place, weight, held, low, low + q_v.shape[1])
    so_far_copy = late_fetch(so_far, sum_v)
    close_heads(opened, first, active, q_v, near_v, state, stats_v, attention)
    so_far_copy.wait()
    stores = []

    def store(at, x):
        out_v[:, at] = x.astype(jnp.bfloat16)
        stores.append(late_fetch(out_v.at[:, at], out.at[:, at]))

    project(copies, attention, held, low, store, lambda at: sum_v[:, at])
    for copy in stores:
        copy.wait()


def project_scratch(rows, columns, groups, inner, width, dtype, copies):
    share = width // groups
    return [
        pltpu.VMEM((rows, columns), jnp.bfloat16),
        pltpu.VMEM((groups, inner, share), jnp.bfloat16),
    ], [
        pltpu.VMEM((rows, width), dtype),
        pltpu.SemaphoreType.DMA((copies + width // (512 if share % 512 == 0 else share),)),
    ]


def begin(place, ready, weight, control, hidden, moves, inner):
    rows, width = hidden.shape
    columns = ready.shape[1]
    before, behind = project_scratch(
        rows, columns, lax.axis_size("groups"), inner, width, jnp.float32, 2 + len(moves) + len(control)
    )
    return pl.pallas_call(
        functools.partial(begin_kernel, (len(weight), len(control)), moves, control[0].shape[0]),
        out_shape=jax.ShapeDtypeStruct((rows, width), jnp.float32),
        in_specs=[SMEM] + [ANY] * (2 + len(weight) + len(control)),
        out_specs=ANY,
        scratch_shapes=before + [pltpu.VMEM((rows, width), jnp.bfloat16)] * 2 + behind,
        compiler_params=pltpu.CompilerParams(vmem_limit_bytes=VMEM_LIMIT),
        cost_estimate=pl.CostEstimate(
            flops=2 * rows * columns * width, bytes_accessed=2 * columns * width + 8 * rows * width, transcendentals=0
        ),
        name="begin",
    )(place, hidden, ready, *weight, *control)


def finish(place, active, q, state, near, first, so_far, weight, moves):
    rows, inner = q.shape
    width = so_far.shape[1]
    columns = near[0].shape[1] // 2
    before, behind = project_scratch(
        rows, columns, lax.axis_size("groups"), inner, width, jnp.bfloat16, 1 + len(moves)
    )
    return pl.pallas_call(
        functools.partial(finish_kernel, len(near), len(weight), moves, first),
        out_shape=jax.ShapeDtypeStruct((rows, width), jnp.bfloat16),
        in_specs=[SMEM] * 2 + [ANY] * (4 + len(near) + len(weight)),
        out_specs=ANY,
        scratch_shapes=close_scratch(rows, columns, len(near))
        + before
        + [pltpu.VMEM((rows, width), jnp.float32)]
        + behind,
        compiler_params=pltpu.CompilerParams(vmem_limit_bytes=VMEM_LIMIT),
        cost_estimate=pl.CostEstimate(
            flops=2 * rows * columns * width, bytes_accessed=2 * columns * width + 6 * rows * width, transcendentals=0
        ),
        name="finish",
    )(place, active, q, *state, so_far, *near, *weight)


def flipped(block, axis, flip):
    return lax.ppermute(block, axis, [(i, i ^ flip) for i in range(lax.axis_size(axis))])


class Lane:
    def __init__(self):
        self.last = ()

    def __call__(self, send, block, *others):
        self.last = (send(after(block, *self.last, *others)),)
        return self.last[0]


def swap(axis, flip):
    return lambda block: flipped(block, axis, flip)


def route_of(route):
    return lambda block: lax.ppermute(block, TILES, route)


def neighbour_slots(tile_count, strides, counts):
    slots = []
    for axis, (stride, count) in enumerate(zip(strides, counts)):
        for odd in range(2):
            route = []
            for t in range(tile_count):
                place = t // stride % count
                if place % 2 == odd and place + 1 < count:
                    route += [(t, t + stride), (t + stride, t)]
            if route:
                slots.append((axis, odd, route))
    return slots


def on_device(hidden, queries, keys, values, control, out_weight, pattern):
    groups = lax.axis_size("groups")
    outer, pair, cores = (lax.axis_size(a) for a in TILES)
    tile_count = outer * pair * cores
    grid_width = min(8, tile_count // 4)
    grid_height = min(4, tile_count // 8)
    layer = grid_width * grid_height
    strides = (layer, grid_width, 1)
    counts = (tile_count // layer, grid_height, grid_width)
    position = lax.axis_index(TILES)
    across = position % grid_width
    rows = queries.shape[0]
    width = hidden.shape[1]
    slots = neighbour_slots(tile_count, strides, counts)
    early = [s for s in slots if s[0] == 2]
    late = [s for s in slots if s[0] != 2]

    def flags(chosen):
        active = []
        for axis, odd, _ in chosen:
            place = position // strides[axis] % counts[axis]
            up = (place % 2 == odd).astype(jnp.int32)
            valid = jnp.where(up == 1, place + 1 < counts[axis], place >= 1)
            active.append((valid & (pattern[0, 2 * axis + up] == 1)).astype(jnp.int32))
        return jnp.stack(active)

    early_active, late_active = flags(early), flags(late)
    far_lane, near_lane = Lane(), Lane()

    shard, share = out_weight.shape[0], width // groups
    line = out_weight[:, :share]
    for g in range(1, groups):
        line = jnp.where(lax.axis_index("groups") == g, out_weight[:, g * share : (g + 1) * share], line)
    line = lax.optimization_barrier(line)[None]
    line_flips = [0]
    flip = outer // 2
    while flip > 2:
        line = jnp.concatenate([line, flipped(line, "outer", flip)])
        line_flips += [f ^ flip for f in line_flips]
        flip //= 2
    far = far_lane(swap("outer", 2), line)
    near = near_lane(swap("outer", 1), line)

    firsts = [sum(CHUNKS[:i]) for i in range(len(CHUNKS))]
    chunks = [
        jnp.concatenate([x[:, f * HEAD_DIM : (f + n) * HEAD_DIM] for x in (keys, values)], axis=1)
        for f, n in zip(firsts, CHUNKS)
    ]
    chunks = lax.optimization_barrier(chunks)
    block = rows // grid_width
    lines = after(control, line).reshape(block // TILE_W, grid_width, TILE_W, width)
    control_sent = [
        lax.dynamic_index_in_dim(lines, across ^ d, 1, keepdims=False).reshape(block, width) for d in range(grid_width)
    ]
    control_parts = [control_sent[0]] + [None] * (grid_width - 1)
    beside = swap("pair", 1)(line)
    for d in range(2, grid_width):
        control_parts[d] = swap(TILES, d)(after(control_sent[d], line if d < grid_width - 1 else beside))
    control_parts[1] = swap(TILES, 1)(control_sent[1])
    plane = jnp.concatenate([line, beside])
    last = swap("outer", 1)(after(far, near, *control_parts[2:-1]))
    held = [plane, swap("groups", 1)(plane)]
    crossed = [swap("core", 1)(x) for x in held]
    early_near = [[lax.ppermute(x, TILES, route) for x in (keys, values)] for _, _, route in early]
    state = attend(early_active, queries, [keys, values] + [x for kv in early_near for x in kv])

    steps = after(jnp.concatenate([far, near, last]), *control_parts[2:], held[1])
    weight = [lax.all_gather(steps, ("groups", "pair", "core"))]
    n = len(line_flips)
    moves = [
        (0, ((g * pair + p) * cores + c, i * n + j), (False, g, f ^ at, p, c))
        for g in range(groups)
        for p in range(pair)
        for c in range(cores)
        for i, at in enumerate((2, 1, 3))
        for j, f in enumerate(line_flips)
    ]
    for group_flip in range(2):
        for core_flip, pieces in enumerate((held, crossed)):
            moves += [
                (len(weight), (p * n + j,), (True, group_flip, f, p, core_flip))
                for p in range(pair)
                for j, f in enumerate(line_flips)
            ]
            weight.append(pieces[group_flip])

    late_near = []
    for chunk in chunks:
        lanes = (far_lane, near_lane)
        late_near.append([lanes[i % 2](route_of(route), chunk) for i, (_, _, route) in enumerate(late)])
    ready = [close(late_active, queries, state, late_near[i], firsts[i]) for i in range(len(CHUNKS) - 1)]
    ready = ready[0] if len(ready) == 1 else jnp.concatenate(ready, axis=1)
    if block % 16:
        control_parts = [
            jnp.take(
                jnp.stack(control_parts), jnp.arange(grid_width, dtype=jnp.int32) ^ across, axis=0
            ).reshape(rows, width)
        ]
    place = jnp.stack([lax.axis_index(a) for a in ("groups",) + TILES] + [across]).astype(jnp.int32)
    if shard % 16:
        weight, moves = [in_order(weight, moves, place, (groups, outer, pair, cores))], [(0, None, None)]
    moves = tuple(moves)
    so_far = begin(place, ready, weight, control_parts, hidden, moves, queries.shape[1])
    return finish(place, late_active, queries, state, late_near[-1], firsts[-1], so_far, weight, moves)


def in_order(weight, moves, place, sizes):
    groups, outer, pair, cores = sizes
    shard, columns = weight[0].shape[-2:]
    gathered = weight[0].reshape(groups, pair, cores, -1, shard, columns)
    for axis, at in enumerate((0, 2, 3)):
        gathered = jnp.take(gathered, jnp.arange(sizes[at], dtype=jnp.int32) ^ place[at], axis=axis)
    weight = [gathered.reshape(weight[0].shape)] + weight[1:]
    blocks = {at[1:]: weight[piece][index] for piece, index, at in moves}
    whole = jnp.stack([blocks[at] for at in sorted(blocks)]).reshape(sizes + (shard, columns))
    for axis, size in enumerate(sizes):
        whole = jnp.take(whole, jnp.arange(size, dtype=jnp.int32) ^ place[axis], axis=axis)
    return whole.reshape(groups, -1, columns)


def solution(mesh):
    groups = mesh.shape["groups"]
    tiles = mesh.shape["tiles"]
    split = Mesh(mesh.devices.reshape(groups, tiles // 4, 2, 2), ("groups",) + TILES)
    rows = P(("groups",) + TILES, None)
    placed = (rows, rows, rows, rows, rows, P(TILES, None), rows)
    return jax.shard_map(
        on_device,
        mesh=split,
        in_specs=placed,
        out_specs=rows,
        check_vma=False,
    )
```

```python
import functools
import math

import jax
import jax.numpy as jnp
from jax import lax
from jax.experimental import pallas as pl
from jax.experimental.pallas import tpu as pltpu
from jax.sharding import Mesh
from jax.sharding import PartitionSpec as P

HEAD_DIM = 128
TILE_W = 8
CHUNKS = (6, 6)
SCALE = HEAD_DIM**-0.5 * math.log2(math.e)
TILES = ("outer", "pair", "core")
PLACE = 5
VMEM_LIMIT = 60 * 1024 * 1024
SMEM = pl.BlockSpec(memory_space=pltpu.SMEM)
ANY = pl.BlockSpec(memory_space=pl.ANY)


def after(x, *others):
    return lax.optimization_barrier((x, *others))[0] if others else x


def head_part(q, k, v):
    scores = lax.dot_general(q, k, (((1,), (1,)), ((), ())), preferred_element_type=jnp.float32)
    peak = jnp.max(scores, axis=1, keepdims=True)
    weights = jnp.exp2((scores - peak) * SCALE).astype(jnp.bfloat16)
    ones = jnp.ones((v.shape[0], HEAD_DIM), jnp.bfloat16)
    both = jnp.dot(weights, jnp.concatenate([v, ones], axis=1), preferred_element_type=jnp.float32)
    return both[:, :HEAD_DIM], both[:, HEAD_DIM:], jnp.broadcast_to(peak, v.shape)


def merge(old, new):
    part, total, peak = old
    part_new, total_new, peak_new = new
    top = jnp.maximum(peak, peak_new)
    f_old = jnp.exp2((peak - top) * SCALE)
    f_new = jnp.exp2((peak_new - top) * SCALE)
    return f_old * part + f_new * part_new, f_old * total + f_new * total_new, top


def columns_of(h):
    return pl.ds(h * HEAD_DIM, HEAD_DIM)


def fold(state, active, q, k, v):
    @pl.when(active == 1)
    def _():
        for h in range(q.shape[1] // HEAD_DIM):
            at = columns_of(h)
            new = head_part(q[:, at], k[:, at], v[:, at])
            for r, x in zip(state, merge(tuple(r[:, at] for r in state), new)):
                r[:, at] = x


class Fetch:
    def __init__(self, sems):
        self.sems, self.count = sems, 0

    def later(self, source, target):
        self.count += 1
        return pltpu.make_async_copy(source, target, self.sems.at[self.count - 1])

    def __call__(self, source, target):
        copy = self.later(source, target)
        copy.start()
        return copy


def attend_kernel(slots, info, q, *refs):
    kv, (part, stats), scratch = refs[: 2 * slots + 2], refs[2 * slots + 2 : 2 * slots + 4], refs[2 * slots + 4 :]
    q_v, kv_v, (part_v, total_v, peak_v, stats_v, sems) = scratch[0], scratch[1 : 2 * slots + 3], scratch[2 * slots + 3 :]
    fetch = Fetch(sems)
    copies = [fetch(source, target) for source, target in zip((q, *kv), (q_v, *kv_v))]
    for copy in copies[:3]:
        copy.wait()
    state = (part_v, total_v, peak_v)
    heads = q_v.shape[1] // HEAD_DIM
    for h in range(heads):
        at = columns_of(h)
        for r, x in zip(state, head_part(q_v[:, at], kv_v[0][:, at], kv_v[1][:, at])):
            r[:, at] = x
    for slot in range(slots):
        for copy in copies[3 + 2 * slot : 5 + 2 * slot]:
            copy.wait()
        fold(state, info[PLACE + slot], q_v, kv_v[2 * slot + 2], kv_v[2 * slot + 3])
    lane = lax.broadcasted_iota(jnp.int32, stats_v.shape, 1)
    packed = jnp.zeros(stats_v.shape, jnp.float32)
    for h in range(heads):
        packed = jnp.where(lane == h, total_v[:, columns_of(h)], packed)
        packed = jnp.where(lane == HEAD_DIM // 2 + h, peak_v[:, columns_of(h)], packed)
    stats_v[...] = packed
    copies = [fetch(part_v, part), fetch(stats_v, stats)]
    for copy in copies:
        copy.wait()


def attend(info, q, kv):
    rows, columns = q.shape
    slots = len(kv) // 2 - 1
    return pl.pallas_call(
        functools.partial(attend_kernel, slots),
        out_shape=[
            jax.ShapeDtypeStruct((rows, columns), jnp.float32),
            jax.ShapeDtypeStruct((rows, HEAD_DIM), jnp.float32),
        ],
        in_specs=[SMEM] + [ANY] * (1 + len(kv)),
        out_specs=[ANY] * 2,
        scratch_shapes=[pltpu.VMEM((rows, columns), jnp.bfloat16)] * (1 + len(kv))
        + [pltpu.VMEM((rows, columns), jnp.float32)] * 3
        + [pltpu.VMEM((rows, HEAD_DIM), jnp.float32), pltpu.SemaphoreType.DMA((3 + len(kv),))],
        compiler_params=pltpu.CompilerParams(vmem_limit_bytes=VMEM_LIMIT),
        cost_estimate=pl.CostEstimate(
            flops=(1 + slots) * 6 * rows * rows * columns,
            bytes_accessed=rows * columns * (10 + 4 * slots),
            transcendentals=0,
        ),
        name="attend",
    )(info, q, *kv)


def close_open(fetch, first, q, part, stats, near, q_v, near_v, state, stats_v):
    columns = state[0].shape[1]
    at = pl.ds(first * HEAD_DIM, columns)
    return [
        fetch(q.at[:, at], q_v),
        fetch(part.at[:, at], state[0]),
        fetch(stats, stats_v),
    ] + [fetch(source, target) for source, target in zip(near, near_v)]


def close_heads(copies, first, info, q_v, near_v, state, stats_v, out):
    columns = state[0].shape[1]
    for copy in copies[:3]:
        copy.wait()
    stats_now = stats_v[...]
    for h in range(columns // HEAD_DIM):
        for r, lane in zip(state[1:], (first + h, HEAD_DIM // 2 + first + h)):
            r[:, columns_of(h)] = jnp.broadcast_to(stats_now[:, lane : lane + 1], stats_now.shape)
    for slot, kv in enumerate(near_v):
        copies[3 + slot].wait()
        fold(state, info[info.shape[0] - len(near_v) + slot], q_v, kv.at[:, pl.ds(0, columns)], kv.at[:, pl.ds(columns, columns)])
    out[...] = (state[0][...] / state[1][...]).astype(jnp.bfloat16)


def close_scratch(rows, columns, slots):
    return (
        [pltpu.VMEM((rows, columns), jnp.bfloat16)]
        + [pltpu.VMEM((rows, 2 * columns), jnp.bfloat16)] * slots
        + [pltpu.VMEM((rows, columns), jnp.float32)] * 3
        + [pltpu.VMEM((rows, HEAD_DIM), jnp.float32), pltpu.SemaphoreType.DMA((4 + slots,))]
    )


def close_kernel(first, slots, info, q, part, stats, *refs):
    near, out = refs[:slots], refs[slots]
    q_v, near_v, (*state, stats_v, sems, out_v) = refs[slots + 1], refs[slots + 2 : 2 * slots + 2], refs[2 * slots + 2 :]
    fetch = Fetch(sems)
    opened = close_open(fetch, first, q, part, stats, near, q_v, near_v, state, stats_v)
    close_heads(opened, first, info, q_v, near_v, state, stats_v, out_v)
    fetch(out_v, out).wait()


def close(info, q, state, near, first):
    rows, columns = q.shape[0], near[0].shape[1] // 2
    return pl.pallas_call(
        functools.partial(close_kernel, first, len(near)),
        out_shape=jax.ShapeDtypeStruct((rows, columns), jnp.bfloat16),
        in_specs=[SMEM] + [ANY] * (3 + len(near)),
        out_specs=ANY,
        scratch_shapes=close_scratch(rows, columns, len(near)) + [pltpu.VMEM((rows, columns), jnp.bfloat16)],
        compiler_params=pltpu.CompilerParams(vmem_limit_bytes=VMEM_LIMIT),
        cost_estimate=pl.CostEstimate(
            flops=len(near) * 6 * rows * rows * columns,
            bytes_accessed=rows * columns * (4 * len(near) + 8),
            transcendentals=0,
        ),
        name="close",
    )(info, q, *state, *near)


def fetch_weight(fetch, moves, place, weight, held, low, high):
    copies = []
    for piece, index, at in moves:
        if at is None:
            copies.append((True, 0, fetch(weight[piece], held)))
            continue
        source = weight[piece].at[index]
        flip, group, outer, pair, core = at
        known = None if flip else group
        count = source.shape[0]
        outer = place[1] ^ outer
        if flip:
            group, pair, core = place[0] ^ group, place[2] ^ pair, place[3] ^ core
        start = pl.multiple_of(((outer * 2 + pair) * 2 + core) * count, count)
        needed = (start < high) & (start + count > low)
        copy = fetch.later(source, held.at[group, pl.ds(start, count), :])
        pl.when(needed)(copy.start)
        copies.append((needed, 0 if known is None else known, copy))
    return copies


def project(copies, attention, held, low, out, add):
    groups, _, columns = held.shape
    step = 512 if columns % 512 == 0 else columns
    for group in range(groups):
        for needed, at, copy in copies:
            if at == group:
                if needed is True:
                    copy.wait()
                else:
                    pl.when(needed)(copy.wait)
        for j in range(columns // step):
            at = pl.ds(group * columns + j * step, step)
            projected = jnp.dot(
                attention[...],
                held[group, pl.ds(low, attention.shape[1]), pl.ds(j * step, step)],
                preferred_element_type=jnp.float32,
            )
            out(at, add(at) + projected)


def begin_kernel(counts, moves, control_rows, place, hidden, ready, *refs):
    weight, control = refs[: counts[0]], refs[counts[0] : sum(counts)]
    out, attention, held, hidden_v, control_v, out_v, sems = refs[sum(counts) :]
    fetch = Fetch(sems)
    residual = [fetch(ready, attention), fetch(hidden, hidden_v)]
    copies = fetch_weight(fetch, moves, place, weight, held, 0, ready.shape[1])
    for d, block in enumerate(control):
        start = pl.multiple_of((place[4] ^ d) * control_rows, control_rows) if len(control) > 1 else 0
        residual.append(fetch(block, control_v.at[pl.ds(start, control_rows), :]))
    for copy in residual:
        copy.wait()
    stores = []

    def store(at, x):
        out_v[:, at] = x
        stores.append(fetch(out_v.at[:, at], out.at[:, at]))

    project(
        copies,
        attention,
        held,
        0,
        store,
        lambda at: hidden_v[:, at].astype(jnp.float32) + control_v[:, at].astype(jnp.float32),
    )
    for copy in stores:
        copy.wait()


def finish_kernel(slots, pieces, moves, first, info, q, part, stats, so_far, *refs):
    near, weight, out, refs = refs[:slots], refs[slots : slots + pieces], refs[slots + pieces], refs[slots + pieces + 1 :]
    q_v, near_v, (*state, stats_v, sems, attention, held, sum_v, out_v, late_sems) = (
        refs[0],
        refs[1 : slots + 1],
        refs[slots + 1 :],
    )
    fetch, late_fetch = Fetch(sems), Fetch(late_sems)
    low = first * HEAD_DIM
    opened = close_open(fetch, first, q, part, stats, near, q_v, near_v, state, stats_v)
    copies = fetch_weight(late_fetch, moves, info, weight, held, low, low + q_v.shape[1])
    so_far_copy = late_fetch(so_far, sum_v)
    close_heads(opened, first, info, q_v, near_v, state, stats_v, attention)
    so_far_copy.wait()
    stores = []

    def store(at, x):
        out_v[:, at] = x.astype(jnp.bfloat16)
        stores.append(late_fetch(out_v.at[:, at], out.at[:, at]))

    project(copies, attention, held, low, store, lambda at: sum_v[:, at])
    for copy in stores:
        copy.wait()


def project_scratch(rows, columns, groups, inner, width, dtype, copies):
    share = width // groups
    return [
        pltpu.VMEM((rows, columns), jnp.bfloat16),
        pltpu.VMEM((groups, inner, share), jnp.bfloat16),
    ], [
        pltpu.VMEM((rows, width), dtype),
        pltpu.SemaphoreType.DMA((copies + width // (512 if share % 512 == 0 else share),)),
    ]


def begin(info, ready, weight, control, hidden, moves, inner):
    rows, width = hidden.shape
    columns = ready.shape[1]
    before, behind = project_scratch(
        rows, columns, lax.axis_size("groups"), inner, width, jnp.float32, 2 + len(moves) + len(control)
    )
    return pl.pallas_call(
        functools.partial(begin_kernel, (len(weight), len(control)), moves, control[0].shape[0]),
        out_shape=jax.ShapeDtypeStruct((rows, width), jnp.float32),
        in_specs=[SMEM] + [ANY] * (2 + len(weight) + len(control)),
        out_specs=ANY,
        scratch_shapes=before + [pltpu.VMEM((rows, width), jnp.bfloat16)] * 2 + behind,
        compiler_params=pltpu.CompilerParams(vmem_limit_bytes=VMEM_LIMIT),
        cost_estimate=pl.CostEstimate(
            flops=2 * rows * columns * width, bytes_accessed=2 * columns * width + 8 * rows * width, transcendentals=0
        ),
        name="begin",
    )(info, hidden, ready, *weight, *control)


def finish(info, q, state, near, first, so_far, weight, moves):
    rows, inner = q.shape
    width = so_far.shape[1]
    columns = near[0].shape[1] // 2
    before, behind = project_scratch(
        rows, columns, lax.axis_size("groups"), inner, width, jnp.bfloat16, 1 + len(moves)
    )
    return pl.pallas_call(
        functools.partial(finish_kernel, len(near), len(weight), moves, first),
        out_shape=jax.ShapeDtypeStruct((rows, width), jnp.bfloat16),
        in_specs=[SMEM] + [ANY] * (4 + len(near) + len(weight)),
        out_specs=ANY,
        scratch_shapes=close_scratch(rows, columns, len(near))
        + before
        + [pltpu.VMEM((rows, width), jnp.float32)]
        + behind,
        compiler_params=pltpu.CompilerParams(vmem_limit_bytes=VMEM_LIMIT),
        cost_estimate=pl.CostEstimate(
            flops=2 * rows * columns * width, bytes_accessed=2 * columns * width + 6 * rows * width, transcendentals=0
        ),
        name="finish",
    )(info, q, *state, so_far, *near, *weight)


def flipped(block, axis, flip):
    return lax.ppermute(block, axis, [(i, i ^ flip) for i in range(lax.axis_size(axis))])


class Lane:
    def __init__(self):
        self.last = ()

    def __call__(self, send, block, *others):
        self.last = (send(after(block, *self.last, *others)),)
        return self.last[0]


def swap(axis, flip):
    return lambda block: flipped(block, axis, flip)


def route_of(route):
    return lambda block: lax.ppermute(block, TILES, route)


def neighbour_slots(tile_count, strides, counts):
    slots = []
    for axis, (stride, count) in enumerate(zip(strides, counts)):
        for odd in range(2):
            route = []
            for t in range(tile_count):
                place = t // stride % count
                if place % 2 == odd and place + 1 < count:
                    route += [(t, t + stride), (t + stride, t)]
            if route:
                slots.append((axis, odd, route))
    return slots


def on_device(hidden, queries, keys, values, control, out_weight, pattern):
    groups = lax.axis_size("groups")
    outer, pair, cores = (lax.axis_size(a) for a in TILES)
    tile_count = outer * pair * cores
    grid_width = min(8, tile_count // 4)
    grid_height = min(4, tile_count // 8)
    layer = grid_width * grid_height
    strides = (layer, grid_width, 1)
    counts = (tile_count // layer, grid_height, grid_width)
    position = lax.axis_index(TILES)
    across = position % grid_width
    rows = queries.shape[0]
    width = hidden.shape[1]
    slots = neighbour_slots(tile_count, strides, counts)
    early = [s for s in slots if s[0] == 2]
    late = [s for s in slots if s[0] != 2]

    info = [lax.axis_index(a) for a in ("groups",) + TILES] + [across]
    for axis, odd, _ in early + late:
        place = position // strides[axis] % counts[axis]
        down = jnp.where(place >= 1, pattern[0, 2 * axis], 0)
        up = jnp.where(place + 1 < counts[axis], pattern[0, 2 * axis + 1], 0)
        info.append(jnp.where(place % 2 == odd, up, down))
    info = jnp.stack([x.astype(jnp.int32) for x in info])
    far_lane, near_lane = Lane(), Lane()

    shard, share = out_weight.shape[0], width // groups
    line = out_weight[:, :share]
    for g in range(1, groups):
        line = jnp.where(lax.axis_index("groups") == g, out_weight[:, g * share : (g + 1) * share], line)
    line = lax.optimization_barrier(line)[None]
    line_flips = [0]
    flip = outer // 2
    while flip > 2:
        line = jnp.concatenate([line, flipped(line, "outer", flip)])
        line_flips += [f ^ flip for f in line_flips]
        flip //= 2
    far = far_lane(swap("outer", 2), line)
    near = near_lane(swap("outer", 1), line)

    firsts = [sum(CHUNKS[:i]) for i in range(len(CHUNKS))]
    chunks = [
        jnp.concatenate([x[:, f * HEAD_DIM : (f + n) * HEAD_DIM] for x in (keys, values)], axis=1)
        for f, n in zip(firsts, CHUNKS)
    ]
    chunks, info = lax.optimization_barrier((chunks, info))
    block = rows // grid_width
    lines = after(control, line).reshape(block // TILE_W, grid_width, TILE_W, width)
    control_sent = [
        lax.dynamic_index_in_dim(lines, across ^ d, 1, keepdims=False).reshape(block, width) for d in range(grid_width)
    ]
    control_parts = [control_sent[0]] + [None] * (grid_width - 1)
    beside = swap("pair", 1)(line)
    early_near = [[None, None] for _ in early]
    for slot in range(1, len(early)):
        early_near[slot][0] = lax.ppermute(after(keys, beside), TILES, early[slot][2])
        early_near[slot][1] = lax.ppermute(after(values, early_near[slot][0]), TILES, early[slot][2])
    for i, x in enumerate((keys, values)):
        early_near[0][i] = lax.ppermute(x, TILES, early[0][2])
    for d in range(2, grid_width - 1):
        control_parts[d] = swap(TILES, d)(after(control_sent[d], line))
    control_parts[1] = swap(TILES, 1)(control_sent[1])
    plane = jnp.concatenate([line, beside])
    last = swap("outer", 1)(after(far, near, *control_parts[2:-1], *chunks, info))
    held = [plane, swap("groups", 1)(plane)]
    crossed = [swap("core", 1)(x) for x in held]
    state = attend(info, queries, [keys, values] + [x for kv in early_near for x in kv])

    steps = after(jnp.concatenate([far, near, last]), *[kv[0] for kv in early_near[1:]], held[1])
    weight = [lax.all_gather(steps, ("groups", "pair", "core"))]
    n = len(line_flips)
    moves = [
        (0, ((g * pair + p) * cores + c, i * n + j), (False, g, f ^ at, p, c))
        for g in range(groups)
        for p in range(pair)
        for c in range(cores)
        for i, at in enumerate((2, 1, 3))
        for j, f in enumerate(line_flips)
    ]
    for group_flip in range(2):
        for core_flip, pieces in enumerate((held, crossed)):
            moves += [
                (len(weight), (p * n + j,), (True, group_flip, f, p, core_flip))
                for p in range(pair)
                for j, f in enumerate(line_flips)
            ]
            weight.append(pieces[group_flip])

    late_near = []
    for chunk in chunks:
        lanes = (far_lane, near_lane)
        late_near.append([lanes[i % 2](route_of(route), chunk) for i, (_, _, route) in enumerate(late)])
    control_parts[-1] = swap(TILES, grid_width - 1)(after(control_sent[-1], *late_near[0]))
    ready = [close(info, queries, state, late_near[i], firsts[i]) for i in range(len(CHUNKS) - 1)]
    ready = ready[0] if len(ready) == 1 else jnp.concatenate(ready, axis=1)
    if block % 16:
        control_parts = [
            jnp.take(
                jnp.stack(control_parts), jnp.arange(grid_width, dtype=jnp.int32) ^ across, axis=0
            ).reshape(rows, width)
        ]
    if shard % 16:
        weight, moves = [in_order(weight, moves, info, (groups, outer, pair, cores))], [(0, None, None)]
    moves = tuple(moves)
    so_far = begin(info, ready, weight, control_parts, hidden, moves, queries.shape[1])
    return finish(info, queries, state, late_near[-1], firsts[-1], so_far, weight, moves)


def in_order(weight, moves, place, sizes):
    groups, outer, pair, cores = sizes
    shard, columns = weight[0].shape[-2:]
    gathered = weight[0].reshape(groups, pair, cores, -1, shard, columns)
    for axis, at in enumerate((0, 2, 3)):
        gathered = jnp.take(gathered, jnp.arange(sizes[at], dtype=jnp.int32) ^ place[at], axis=axis)
    weight = [gathered.reshape(weight[0].shape)] + weight[1:]
    blocks = {at[1:]: weight[piece][index] for piece, index, at in moves}
    whole = jnp.stack([blocks[at] for at in sorted(blocks)]).reshape(sizes + (shard, columns))
    for axis, size in enumerate(sizes):
        whole = jnp.take(whole, jnp.arange(size, dtype=jnp.int32) ^ place[axis], axis=axis)
    return whole.reshape(groups, -1, columns)


def solution(mesh):
    groups = mesh.shape["groups"]
    tiles = mesh.shape["tiles"]
    split = Mesh(mesh.devices.reshape(groups, tiles // 4, 2, 2), ("groups",) + TILES)
    rows = P(("groups",) + TILES, None)
    placed = (rows, rows, rows, rows, rows, P(TILES, None), rows)
    return jax.shard_map(
        on_device,
        mesh=split,
        in_specs=placed,
        out_specs=rows,
        check_vma=False,
    )
```

```python
import functools
import math

import jax
import jax.numpy as jnp
from jax import lax
from jax.experimental import pallas as pl
from jax.experimental.pallas import tpu as pltpu
from jax.sharding import Mesh
from jax.sharding import PartitionSpec as P

HEAD_DIM = 128
TILE_W = 8
CHUNKS = (6, 6)
SCALE = HEAD_DIM**-0.5 * math.log2(math.e)
TILES = ("outer", "pair", "core")
VMEM_LIMIT = 60 * 1024 * 1024
SMEM = pl.BlockSpec(memory_space=pltpu.SMEM)
ANY = pl.BlockSpec(memory_space=pl.ANY)


def after(x, *others):
    return lax.optimization_barrier((x, *others))[0] if others else x


def head_part(q, k, v):
    scores = lax.dot_general(q, k, (((1,), (1,)), ((), ())), preferred_element_type=jnp.float32)
    peak = jnp.max(scores, axis=1, keepdims=True)
    weights = jnp.exp2((scores - peak) * SCALE).astype(jnp.bfloat16)
    ones = jnp.ones((v.shape[0], HEAD_DIM), jnp.bfloat16)
    both = jnp.dot(weights, jnp.concatenate([v, ones], axis=1), preferred_element_type=jnp.float32)
    return both[:, :HEAD_DIM], both[:, HEAD_DIM:], jnp.broadcast_to(peak, v.shape)


def merge(old, new):
    part, total, peak = old
    part_new, total_new, peak_new = new
    top = jnp.maximum(peak, peak_new)
    f_old = jnp.exp2((peak - top) * SCALE)
    f_new = jnp.exp2((peak_new - top) * SCALE)
    return f_old * part + f_new * part_new, f_old * total + f_new * total_new, top


def columns_of(h):
    return pl.ds(h * HEAD_DIM, HEAD_DIM)


def fold(state, active, q, k, v):
    @pl.when(active)
    def _():
        for h in range(q.shape[1] // HEAD_DIM):
            at = columns_of(h)
            new = head_part(q[:, at], k[:, at], v[:, at])
            for r, x in zip(state, merge(tuple(r[:, at] for r in state), new)):
                r[:, at] = x


class Fetch:
    def __init__(self, sems):
        self.sems, self.count = sems, 0

    def later(self, source, target):
        self.count += 1
        return pltpu.make_async_copy(source, target, self.sems.at[self.count - 1])

    def __call__(self, source, target):
        copy = self.later(source, target)
        copy.start()
        return copy


def attend_kernel(which, pattern, q, *refs):
    slots, active = len(which), in_window(pattern, which)
    kv, (part, stats), scratch = refs[: 2 * slots + 2], refs[2 * slots + 2 : 2 * slots + 4], refs[2 * slots + 4 :]
    q_v, kv_v, (part_v, total_v, peak_v, stats_v, sems) = scratch[0], scratch[1 : 2 * slots + 3], scratch[2 * slots + 3 :]
    fetch = Fetch(sems)
    copies = [fetch(source, target) for source, target in zip((q, *kv), (q_v, *kv_v))]
    for copy in copies[:3]:
        copy.wait()
    state = (part_v, total_v, peak_v)
    heads = q_v.shape[1] // HEAD_DIM
    for h in range(heads):
        at = columns_of(h)
        for r, x in zip(state, head_part(q_v[:, at], kv_v[0][:, at], kv_v[1][:, at])):
            r[:, at] = x
    for slot in range(slots):
        for copy in copies[3 + 2 * slot : 5 + 2 * slot]:
            copy.wait()
        fold(state, active[slot], q_v, kv_v[2 * slot + 2], kv_v[2 * slot + 3])
    lane = lax.broadcasted_iota(jnp.int32, stats_v.shape, 1)
    packed = jnp.zeros(stats_v.shape, jnp.float32)
    for h in range(heads):
        packed = jnp.where(lane == h, total_v[:, columns_of(h)], packed)
        packed = jnp.where(lane == HEAD_DIM // 2 + h, peak_v[:, columns_of(h)], packed)
    stats_v[...] = packed
    copies = [fetch(part_v, part), fetch(stats_v, stats)]
    for copy in copies:
        copy.wait()


def attend(which, pattern, q, kv):
    rows, columns = q.shape
    slots = len(kv) // 2 - 1
    return pl.pallas_call(
        functools.partial(attend_kernel, which),
        out_shape=[
            jax.ShapeDtypeStruct((rows, columns), jnp.float32),
            jax.ShapeDtypeStruct((rows, HEAD_DIM), jnp.float32),
        ],
        in_specs=[SMEM] + [ANY] * (1 + len(kv)),
        out_specs=[ANY] * 2,
        scratch_shapes=[pltpu.VMEM((rows, columns), jnp.bfloat16)] * (1 + len(kv))
        + [pltpu.VMEM((rows, columns), jnp.float32)] * 3
        + [pltpu.VMEM((rows, HEAD_DIM), jnp.float32), pltpu.SemaphoreType.DMA((3 + len(kv),))],
        compiler_params=pltpu.CompilerParams(vmem_limit_bytes=VMEM_LIMIT),
        cost_estimate=pl.CostEstimate(
            flops=(1 + slots) * 6 * rows * rows * columns,
            bytes_accessed=rows * columns * (10 + 4 * slots),
            transcendentals=0,
        ),
        name="attend",
    )(pattern, q, *kv)


def close_open(fetch, first, q, part, stats, near, q_v, near_v, state, stats_v):
    columns = state[0].shape[1]
    at = pl.ds(first * HEAD_DIM, columns)
    return [
        fetch(q.at[:, at], q_v),
        fetch(part.at[:, at], state[0]),
        fetch(stats, stats_v),
    ] + [fetch(source, target) for source, target in zip(near, near_v)]


def close_heads(copies, first, active, q_v, near_v, state, stats_v, out):
    columns = state[0].shape[1]
    for copy in copies[:3]:
        copy.wait()
    stats_now = stats_v[...]
    for h in range(columns // HEAD_DIM):
        for r, lane in zip(state[1:], (first + h, HEAD_DIM // 2 + first + h)):
            r[:, columns_of(h)] = jnp.broadcast_to(stats_now[:, lane : lane + 1], stats_now.shape)
    for slot, kv in enumerate(near_v):
        copies[3 + slot].wait()
        fold(state, active[slot], q_v, kv.at[:, pl.ds(0, columns)], kv.at[:, pl.ds(columns, columns)])
    out[...] = (state[0][...] / state[1][...]).astype(jnp.bfloat16)


def close_scratch(rows, columns, slots):
    return (
        [pltpu.VMEM((rows, columns), jnp.bfloat16)]
        + [pltpu.VMEM((rows, 2 * columns), jnp.bfloat16)] * slots
        + [pltpu.VMEM((rows, columns), jnp.float32)] * 3
        + [pltpu.VMEM((rows, HEAD_DIM), jnp.float32), pltpu.SemaphoreType.DMA((4 + slots,))]
    )


def close_kernel(first, which, pattern, q, part, stats, *refs):
    slots, active = len(which), in_window(pattern, which)
    near, out = refs[:slots], refs[slots]
    q_v, near_v, (*state, stats_v, sems, out_v) = refs[slots + 1], refs[slots + 2 : 2 * slots + 2], refs[2 * slots + 2 :]
    fetch = Fetch(sems)
    opened = close_open(fetch, first, q, part, stats, near, q_v, near_v, state, stats_v)
    close_heads(opened, first, active, q_v, near_v, state, stats_v, out_v)
    fetch(out_v, out).wait()


def close(which, pattern, q, state, near, first):
    rows, columns = q.shape[0], near[0].shape[1] // 2
    return pl.pallas_call(
        functools.partial(close_kernel, first, which),
        out_shape=jax.ShapeDtypeStruct((rows, columns), jnp.bfloat16),
        in_specs=[SMEM] + [ANY] * (3 + len(near)),
        out_specs=ANY,
        scratch_shapes=close_scratch(rows, columns, len(near)) + [pltpu.VMEM((rows, columns), jnp.bfloat16)],
        compiler_params=pltpu.CompilerParams(vmem_limit_bytes=VMEM_LIMIT),
        cost_estimate=pl.CostEstimate(
            flops=len(near) * 6 * rows * rows * columns,
            bytes_accessed=rows * columns * (4 * len(near) + 8),
            transcendentals=0,
        ),
        name="close",
    )(pattern, q, *state, *near)


def fetch_weight(fetch, moves, place, weight, held, low, high):
    copies = []
    for piece, index, at in moves:
        if at is None:
            copies.append((True, 0, fetch(weight[piece], held)))
            continue
        source = weight[piece].at[index]
        flip, group, outer, pair, core = at
        known = None if flip else group
        count = source.shape[0]
        outer = place[1] ^ outer
        if flip:
            group, pair, core = place[0] ^ group, place[2] ^ pair, place[3] ^ core
        start = pl.multiple_of(((outer * 2 + pair) * 2 + core) * count, count)
        needed = (start < high) & (start + count > low)
        copy = fetch.later(source, held.at[group, pl.ds(start, count), :])
        pl.when(needed)(copy.start)
        copies.append((needed, 0 if known is None else known, copy))
    return copies


def project(copies, attention, held, low, out, add):
    groups, _, columns = held.shape
    step = 512 if columns % 512 == 0 else columns
    for group in range(groups):
        for needed, at, copy in copies:
            if at == group:
                if needed is True:
                    copy.wait()
                else:
                    pl.when(needed)(copy.wait)
        for j in range(columns // step):
            at = pl.ds(group * columns + j * step, step)
            projected = jnp.dot(
                attention[...],
                held[group, pl.ds(low, attention.shape[1]), pl.ds(j * step, step)],
                preferred_element_type=jnp.float32,
            )
            out(at, add(at) + projected)


def begin_kernel(counts, moves, control_rows, hidden, ready, *refs):
    place = device_place()
    weight, control = refs[: counts[0]], refs[counts[0] : sum(counts)]
    out, attention, held, hidden_v, control_v, out_v, sems = refs[sum(counts) :]
    fetch = Fetch(sems)
    residual = [fetch(ready, attention), fetch(hidden, hidden_v)]
    copies = fetch_weight(fetch, moves, place, weight, held, 0, ready.shape[1])
    for d, block in enumerate(control):
        start = pl.multiple_of((device_column(place) ^ d) * control_rows, control_rows) if len(control) > 1 else 0
        residual.append(fetch(block, control_v.at[pl.ds(start, control_rows), :]))
    for copy in residual:
        copy.wait()
    stores = []

    def store(at, x):
        out_v[:, at] = x
        stores.append(fetch(out_v.at[:, at], out.at[:, at]))

    project(
        copies,
        attention,
        held,
        0,
        store,
        lambda at: hidden_v[:, at].astype(jnp.float32) + control_v[:, at].astype(jnp.float32),
    )
    for copy in stores:
        copy.wait()


def finish_kernel(which, pieces, moves, first, pattern, q, part, stats, so_far, *refs):
    slots, active = len(which), in_window(pattern, which)
    near, weight, out, refs = refs[:slots], refs[slots : slots + pieces], refs[slots + pieces], refs[slots + pieces + 1 :]
    q_v, near_v, (*state, stats_v, sems, attention, held, sum_v, out_v, late_sems) = (
        refs[0],
        refs[1 : slots + 1],
        refs[slots + 1 :],
    )
    fetch, late_fetch = Fetch(sems), Fetch(late_sems)
    low = first * HEAD_DIM
    opened = close_open(fetch, first, q, part, stats, near, q_v, near_v, state, stats_v)
    copies = fetch_weight(late_fetch, moves, device_place(), weight, held, low, low + q_v.shape[1])
    so_far_copy = late_fetch(so_far, sum_v)
    close_heads(opened, first, active, q_v, near_v, state, stats_v, attention)
    so_far_copy.wait()
    stores = []

    def store(at, x):
        out_v[:, at] = x.astype(jnp.bfloat16)
        stores.append(late_fetch(out_v.at[:, at], out.at[:, at]))

    project(copies, attention, held, low, store, lambda at: sum_v[:, at])
    for copy in stores:
        copy.wait()


def project_scratch(rows, columns, groups, inner, width, dtype, copies):
    share = width // groups
    return [
        pltpu.VMEM((rows, columns), jnp.bfloat16),
        pltpu.VMEM((groups, inner, share), jnp.bfloat16),
    ], [
        pltpu.VMEM((rows, width), dtype),
        pltpu.SemaphoreType.DMA((copies + width // (512 if share % 512 == 0 else share),)),
    ]


def begin(ready, weight, control, hidden, moves, inner):
    rows, width = hidden.shape
    columns = ready.shape[1]
    before, behind = project_scratch(
        rows, columns, lax.axis_size("groups"), inner, width, jnp.float32, 2 + len(moves) + len(control)
    )
    return pl.pallas_call(
        functools.partial(begin_kernel, (len(weight), len(control)), moves, control[0].shape[0]),
        out_shape=jax.ShapeDtypeStruct((rows, width), jnp.float32),
        in_specs=[ANY] * (2 + len(weight) + len(control)),
        out_specs=ANY,
        scratch_shapes=before + [pltpu.VMEM((rows, width), jnp.bfloat16)] * 2 + behind,
        compiler_params=pltpu.CompilerParams(vmem_limit_bytes=VMEM_LIMIT),
        cost_estimate=pl.CostEstimate(
            flops=2 * rows * columns * width, bytes_accessed=2 * columns * width + 8 * rows * width, transcendentals=0
        ),
        name="begin",
    )(hidden, ready, *weight, *control)


def finish(which, pattern, q, state, near, first, so_far, weight, moves):
    rows, inner = q.shape
    width = so_far.shape[1]
    columns = near[0].shape[1] // 2
    before, behind = project_scratch(
        rows, columns, lax.axis_size("groups"), inner, width, jnp.bfloat16, 1 + len(moves)
    )
    return pl.pallas_call(
        functools.partial(finish_kernel, which, len(weight), moves, first),
        out_shape=jax.ShapeDtypeStruct((rows, width), jnp.bfloat16),
        in_specs=[SMEM] + [ANY] * (4 + len(near) + len(weight)),
        out_specs=ANY,
        scratch_shapes=close_scratch(rows, columns, len(near))
        + before
        + [pltpu.VMEM((rows, width), jnp.float32)]
        + behind,
        compiler_params=pltpu.CompilerParams(vmem_limit_bytes=VMEM_LIMIT),
        cost_estimate=pl.CostEstimate(
            flops=2 * rows * columns * width, bytes_accessed=2 * columns * width + 6 * rows * width, transcendentals=0
        ),
        name="finish",
    )(pattern, q, *state, so_far, *near, *weight)


def flipped(block, axis, flip):
    return lax.ppermute(block, axis, [(i, i ^ flip) for i in range(lax.axis_size(axis))])


class Lane:
    def __init__(self):
        self.last = ()

    def __call__(self, send, block, *others):
        self.last = (send(after(block, *self.last, *others)),)
        return self.last[0]


def swap(axis, flip):
    return lambda block: flipped(block, axis, flip)


def route_of(route):
    return lambda block: lax.ppermute(block, TILES, route)


def grid_of(tile_count):
    width = min(8, tile_count // 4)
    height = min(4, tile_count // 8)
    return (width * height, width, 1), (tile_count // (width * height), height, width)


def device_place():
    return [lax.axis_index(a) for a in ("groups",) + TILES]


def device_column(place):
    _, outer, pair, core = place
    tile_count = math.prod(lax.axis_size(a) for a in TILES)
    return lax.rem((outer * 2 + pair) * 2 + core, grid_of(tile_count)[1][2])


def in_window(pattern, slots):
    _, outer, pair, core = device_place()
    strides, counts = grid_of(math.prod(lax.axis_size(a) for a in TILES))
    position = (outer * 2 + pair) * 2 + core
    active = []
    for axis, odd in slots:
        place = lax.rem(lax.div(position, strides[axis]), counts[axis])
        down = (place >= 1) & (pattern[0, 2 * axis] == 1)
        up = (place + 1 < counts[axis]) & (pattern[0, 2 * axis + 1] == 1)
        active.append(jnp.where(lax.rem(place, 2) == odd, up.astype(jnp.int32), down.astype(jnp.int32)) == 1)
    return active


def neighbour_slots(tile_count, strides, counts):
    slots = []
    for axis, (stride, count) in enumerate(zip(strides, counts)):
        for odd in range(2):
            route = []
            for t in range(tile_count):
                place = t // stride % count
                if place % 2 == odd and place + 1 < count:
                    route += [(t, t + stride), (t + stride, t)]
            if route:
                slots.append((axis, odd, route))
    return slots


def on_device(hidden, queries, keys, values, control, out_weight, pattern):
    groups = lax.axis_size("groups")
    outer, pair, cores = (lax.axis_size(a) for a in TILES)
    tile_count = outer * pair * cores
    strides, counts = grid_of(tile_count)
    grid_width = counts[2]
    across = device_column(device_place())
    rows = queries.shape[0]
    width = hidden.shape[1]
    slots = neighbour_slots(tile_count, strides, counts)
    early = [s for s in slots if s[0] == 2]
    late = [s for s in slots if s[0] != 2]

    far_lane, near_lane = Lane(), Lane()

    shard, share = out_weight.shape[0], width // groups
    line = out_weight[:, :share]
    for g in range(1, groups):
        line = jnp.where(lax.axis_index("groups") == g, out_weight[:, g * share : (g + 1) * share], line)
    line = lax.optimization_barrier(line)[None]
    line_flips = [0]
    flip = outer // 2
    while flip > 2:
        line = jnp.concatenate([line, flipped(line, "outer", flip)])
        line_flips += [f ^ flip for f in line_flips]
        flip //= 2
    far = far_lane(swap("outer", 2), line)
    near = near_lane(swap("outer", 1), line)

    firsts = [sum(CHUNKS[:i]) for i in range(len(CHUNKS))]
    chunks = [
        jnp.concatenate([x[:, f * HEAD_DIM : (f + n) * HEAD_DIM] for x in (keys, values)], axis=1)
        for f, n in zip(firsts, CHUNKS)
    ]
    chunks = lax.optimization_barrier(chunks)
    block = rows // grid_width
    lines = after(control, line).reshape(block // TILE_W, grid_width, TILE_W, width)
    control_sent = [
        lax.dynamic_index_in_dim(lines, across ^ d, 1, keepdims=False).reshape(block, width) for d in range(grid_width)
    ]
    control_parts = [control_sent[0]] + [None] * (grid_width - 1)
    beside = swap("pair", 1)(line)
    for d in range(2, grid_width):
        control_parts[d] = swap(TILES, d)(after(control_sent[d], line if d < grid_width - 1 else beside))
    control_parts[1] = swap(TILES, 1)(control_sent[1])
    plane = jnp.concatenate([line, beside])
    last = swap("outer", 1)(after(far, near, *control_parts[2:-1], *chunks))
    early_near = [[None, None] for _ in early]
    for i, x in enumerate((keys, values)):
        early_near[0][i] = lax.ppermute(x, TILES, early[0][2])
        for slot in range(1, len(early)):
            early_near[slot][i] = lax.ppermute(after(x, early_near[0][i]), TILES, early[slot][2])
    held = [plane, swap("groups", 1)(plane)]
    crossed = [swap("core", 1)(x) for x in held]
    state = attend(tuple(s[:2] for s in early), pattern, queries, [keys, values] + [x for kv in early_near for x in kv])

    steps = after(jnp.concatenate([far, near, last]), *control_parts[2:], held[1])
    weight = [lax.all_gather(steps, ("groups", "pair", "core"))]
    n = len(line_flips)
    moves = [
        (0, ((g * pair + p) * cores + c, i * n + j), (False, g, f ^ at, p, c))
        for g in range(groups)
        for p in range(pair)
        for c in range(cores)
        for i, at in enumerate((2, 1, 3))
        for j, f in enumerate(line_flips)
    ]
    for group_flip in range(2):
        for core_flip, pieces in enumerate((held, crossed)):
            moves += [
                (len(weight), (p * n + j,), (True, group_flip, f, p, core_flip))
                for p in range(pair)
                for j, f in enumerate(line_flips)
            ]
            weight.append(pieces[group_flip])

    late_near = []
    for chunk in chunks:
        lanes = (far_lane, near_lane)
        late_near.append([lanes[i % 2](route_of(route), chunk) for i, (_, _, route) in enumerate(late)])
    which = tuple(s[:2] for s in late)
    ready = [close(which, pattern, queries, state, late_near[i], firsts[i]) for i in range(len(CHUNKS) - 1)]
    ready = ready[0] if len(ready) == 1 else jnp.concatenate(ready, axis=1)
    if block % 16:
        control_parts = [
            jnp.take(
                jnp.stack(control_parts), jnp.arange(grid_width, dtype=jnp.int32) ^ across, axis=0
            ).reshape(rows, width)
        ]
    if shard % 16:
        weight, moves = [in_order(weight, moves, device_place(), (groups, outer, pair, cores))], [(0, None, None)]
    moves = tuple(moves)
    so_far = begin(ready, weight, control_parts, hidden, moves, queries.shape[1])
    return finish(which, pattern, queries, state, late_near[-1], firsts[-1], so_far, weight, moves)


def in_order(weight, moves, place, sizes):
    groups, outer, pair, cores = sizes
    shard, columns = weight[0].shape[-2:]
    gathered = weight[0].reshape(groups, pair, cores, -1, shard, columns)
    for axis, at in enumerate((0, 2, 3)):
        gathered = jnp.take(gathered, jnp.arange(sizes[at], dtype=jnp.int32) ^ place[at], axis=axis)
    weight = [gathered.reshape(weight[0].shape)] + weight[1:]
    blocks = {at[1:]: weight[piece][index] for piece, index, at in moves}
    whole = jnp.stack([blocks[at] for at in sorted(blocks)]).reshape(sizes + (shard, columns))
    for axis, size in enumerate(sizes):
        whole = jnp.take(whole, jnp.arange(size, dtype=jnp.int32) ^ place[axis], axis=axis)
    return whole.reshape(groups, -1, columns)


def solution(mesh):
    groups = mesh.shape["groups"]
    tiles = mesh.shape["tiles"]
    split = Mesh(mesh.devices.reshape(groups, tiles // 4, 2, 2), ("groups",) + TILES)
    rows = P(("groups",) + TILES, None)
    placed = (rows, rows, rows, rows, rows, P(TILES, None), rows)
    return jax.shard_map(
        on_device,
        mesh=split,
        in_specs=placed,
        out_specs=rows,
        check_vma=False,
    )
```

```python
import functools
import math

import jax
import jax.numpy as jnp
from jax import lax
from jax.experimental import pallas as pl
from jax.experimental.pallas import tpu as pltpu
from jax.sharding import Mesh
from jax.sharding import PartitionSpec as P

HEAD_DIM = 128
TILE_W = 8
CHUNKS = (7, 5)
SCALE = HEAD_DIM**-0.5 * math.log2(math.e)
TILES = ("outer", "pair", "core")
VMEM_LIMIT = 60 * 1024 * 1024
SMEM = pl.BlockSpec(memory_space=pltpu.SMEM)
ANY = pl.BlockSpec(memory_space=pl.ANY)


def after(x, *others):
    return lax.optimization_barrier((x, *others))[0] if others else x


def head_part(q, k, v):
    scores = lax.dot_general(q, k, (((1,), (1,)), ((), ())), preferred_element_type=jnp.float32)
    peak = jnp.max(scores, axis=1, keepdims=True)
    weights = jnp.exp2((scores - peak) * SCALE).astype(jnp.bfloat16)
    ones = jnp.ones((v.shape[0], HEAD_DIM), jnp.bfloat16)
    both = jnp.dot(weights, jnp.concatenate([v, ones], axis=1), preferred_element_type=jnp.float32)
    return both[:, :HEAD_DIM], both[:, HEAD_DIM:], jnp.broadcast_to(peak, v.shape)


def merge(old, new):
    part, total, peak = old
    part_new, total_new, peak_new = new
    top = jnp.maximum(peak, peak_new)
    f_old = jnp.exp2((peak - top) * SCALE)
    f_new = jnp.exp2((peak_new - top) * SCALE)
    return f_old * part + f_new * part_new, f_old * total + f_new * total_new, top


def columns_of(h):
    return pl.ds(h * HEAD_DIM, HEAD_DIM)


def fold(state, active, q, k, v):
    @pl.when(active)
    def _():
        for h in range(q.shape[1] // HEAD_DIM):
            at = columns_of(h)
            new = head_part(q[:, at], k[:, at], v[:, at])
            for r, x in zip(state, merge(tuple(r[:, at] for r in state), new)):
                r[:, at] = x


class Fetch:
    def __init__(self, sems):
        self.sems, self.count = sems, 0

    def later(self, source, target):
        self.count += 1
        return pltpu.make_async_copy(source, target, self.sems.at[self.count - 1])

    def __call__(self, source, target):
        copy = self.later(source, target)
        copy.start()
        return copy


def attend_kernel(which, pattern, q, *refs):
    slots, active = len(which), in_window(pattern, which)
    kv, (part, stats), scratch = refs[: 2 * slots + 2], refs[2 * slots + 2 : 2 * slots + 4], refs[2 * slots + 4 :]
    q_v, kv_v, (part_v, total_v, peak_v, stats_v, sems) = scratch[0], scratch[1 : 2 * slots + 3], scratch[2 * slots + 3 :]
    fetch = Fetch(sems)
    copies = [fetch(source, target) for source, target in zip((q, *kv), (q_v, *kv_v))]
    for copy in copies[:3]:
        copy.wait()
    state = (part_v, total_v, peak_v)
    heads = q_v.shape[1] // HEAD_DIM
    for h in range(heads):
        at = columns_of(h)
        for r, x in zip(state, head_part(q_v[:, at], kv_v[0][:, at], kv_v[1][:, at])):
            r[:, at] = x
    for slot in range(slots):
        for copy in copies[3 + 2 * slot : 5 + 2 * slot]:
            copy.wait()
        fold(state, active[slot], q_v, kv_v[2 * slot + 2], kv_v[2 * slot + 3])
    lane = lax.broadcasted_iota(jnp.int32, stats_v.shape, 1)
    packed = jnp.zeros(stats_v.shape, jnp.float32)
    for h in range(heads):
        packed = jnp.where(lane == h, total_v[:, columns_of(h)], packed)
        packed = jnp.where(lane == HEAD_DIM // 2 + h, peak_v[:, columns_of(h)], packed)
    stats_v[...] = packed
    copies = [fetch(part_v, part), fetch(stats_v, stats)]
    for copy in copies:
        copy.wait()


def attend(which, pattern, q, kv):
    rows, columns = q.shape
    slots = len(kv) // 2 - 1
    return pl.pallas_call(
        functools.partial(attend_kernel, which),
        out_shape=[
            jax.ShapeDtypeStruct((rows, columns), jnp.float32),
            jax.ShapeDtypeStruct((rows, HEAD_DIM), jnp.float32),
        ],
        in_specs=[SMEM] + [ANY] * (1 + len(kv)),
        out_specs=[ANY] * 2,
        scratch_shapes=[pltpu.VMEM((rows, columns), jnp.bfloat16)] * (1 + len(kv))
        + [pltpu.VMEM((rows, columns), jnp.float32)] * 3
        + [pltpu.VMEM((rows, HEAD_DIM), jnp.float32), pltpu.SemaphoreType.DMA((3 + len(kv),))],
        compiler_params=pltpu.CompilerParams(vmem_limit_bytes=VMEM_LIMIT),
        cost_estimate=pl.CostEstimate(
            flops=(1 + slots) * 6 * rows * rows * columns,
            bytes_accessed=rows * columns * (10 + 4 * slots),
            transcendentals=0,
        ),
        name="attend",
    )(pattern, q, *kv)


def close_open(fetch, first, q, part, stats, near, q_v, near_v, state, stats_v):
    columns = state[0].shape[1]
    at = pl.ds(first * HEAD_DIM, columns)
    return [
        fetch(q.at[:, at], q_v),
        fetch(part.at[:, at], state[0]),
        fetch(stats, stats_v),
    ] + [fetch(source, target) for source, target in zip(near, near_v)]


def close_heads(copies, first, active, q_v, near_v, state, stats_v, out):
    columns = state[0].shape[1]
    for copy in copies[:3]:
        copy.wait()
    stats_now = stats_v[...]
    for h in range(columns // HEAD_DIM):
        for r, lane in zip(state[1:], (first + h, HEAD_DIM // 2 + first + h)):
            r[:, columns_of(h)] = jnp.broadcast_to(stats_now[:, lane : lane + 1], stats_now.shape)
    for slot, kv in enumerate(near_v):
        copies[3 + slot].wait()
        fold(state, active[slot], q_v, kv.at[:, pl.ds(0, columns)], kv.at[:, pl.ds(columns, columns)])
    out[...] = (state[0][...] / state[1][...]).astype(jnp.bfloat16)


def close_scratch(rows, columns, slots):
    return (
        [pltpu.VMEM((rows, columns), jnp.bfloat16)]
        + [pltpu.VMEM((rows, 2 * columns), jnp.bfloat16)] * slots
        + [pltpu.VMEM((rows, columns), jnp.float32)] * 3
        + [pltpu.VMEM((rows, HEAD_DIM), jnp.float32), pltpu.SemaphoreType.DMA((4 + slots,))]
    )


def close_kernel(first, which, pattern, q, part, stats, *refs):
    slots, active = len(which), in_window(pattern, which)
    near, out = refs[:slots], refs[slots]
    q_v, near_v, (*state, stats_v, sems, out_v) = refs[slots + 1], refs[slots + 2 : 2 * slots + 2], refs[2 * slots + 2 :]
    fetch = Fetch(sems)
    opened = close_open(fetch, first, q, part, stats, near, q_v, near_v, state, stats_v)
    close_heads(opened, first, active, q_v, near_v, state, stats_v, out_v)
    fetch(out_v, out).wait()


def close(which, pattern, q, state, near, first):
    rows, columns = q.shape[0], near[0].shape[1] // 2
    return pl.pallas_call(
        functools.partial(close_kernel, first, which),
        out_shape=jax.ShapeDtypeStruct((rows, columns), jnp.bfloat16),
        in_specs=[SMEM] + [ANY] * (3 + len(near)),
        out_specs=ANY,
        scratch_shapes=close_scratch(rows, columns, len(near)) + [pltpu.VMEM((rows, columns), jnp.bfloat16)],
        compiler_params=pltpu.CompilerParams(vmem_limit_bytes=VMEM_LIMIT),
        cost_estimate=pl.CostEstimate(
            flops=len(near) * 6 * rows * rows * columns,
            bytes_accessed=rows * columns * (4 * len(near) + 8),
            transcendentals=0,
        ),
        name="close",
    )(pattern, q, *state, *near)


def fetch_weight(fetch, moves, place, weight, held, low, high):
    copies = []
    for piece, index, at in moves:
        if at is None:
            copies.append((True, 0, fetch(weight[piece], held)))
            continue
        source = weight[piece].at[index]
        flip, group, outer, pair, core = at
        known = None if flip else group
        count = source.shape[0]
        outer = place[1] ^ outer
        if flip:
            group, pair, core = place[0] ^ group, place[2] ^ pair, place[3] ^ core
        start = pl.multiple_of(((outer * 2 + pair) * 2 + core) * count, count)
        needed = (start < high) & (start + count > low)
        copy = fetch.later(source, held.at[group, pl.ds(start, count), :])
        pl.when(needed)(copy.start)
        copies.append((needed, 0 if known is None else known, copy))
    return copies


def project(copies, attention, held, low, out, add):
    groups, _, columns = held.shape
    step = 512 if columns % 512 == 0 else columns
    for group in range(groups):
        for needed, at, copy in copies:
            if at == group:
                if needed is True:
                    copy.wait()
                else:
                    pl.when(needed)(copy.wait)
        for j in range(columns // step):
            at = pl.ds(group * columns + j * step, step)
            projected = jnp.dot(
                attention[...],
                held[group, pl.ds(low, attention.shape[1]), pl.ds(j * step, step)],
                preferred_element_type=jnp.float32,
            )
            out(at, add(at) + projected)


def begin_kernel(counts, moves, control_rows, hidden, ready, *refs):
    place = device_place()
    weight, control = refs[: counts[0]], refs[counts[0] : sum(counts)]
    out, attention, held, hidden_v, control_v, out_v, sems = refs[sum(counts) :]
    fetch = Fetch(sems)
    residual = [fetch(ready, attention), fetch(hidden, hidden_v)]
    copies = fetch_weight(fetch, moves, place, weight, held, 0, ready.shape[1])
    for d, block in enumerate(control):
        start = pl.multiple_of((device_column(place) ^ d) * control_rows, control_rows) if len(control) > 1 else 0
        residual.append(fetch(block, control_v.at[pl.ds(start, control_rows), :]))
    for copy in residual:
        copy.wait()
    stores = []

    def store(at, x):
        out_v[:, at] = x
        stores.append(fetch(out_v.at[:, at], out.at[:, at]))

    project(
        copies,
        attention,
        held,
        0,
        store,
        lambda at: hidden_v[:, at].astype(jnp.float32) + control_v[:, at].astype(jnp.float32),
    )
    for copy in stores:
        copy.wait()


def finish_kernel(which, pieces, moves, first, pattern, q, part, stats, so_far, *refs):
    slots, active = len(which), in_window(pattern, which)
    near, weight, out, refs = refs[:slots], refs[slots : slots + pieces], refs[slots + pieces], refs[slots + pieces + 1 :]
    q_v, near_v, (*state, stats_v, sems, attention, held, sum_v, out_v, late_sems) = (
        refs[0],
        refs[1 : slots + 1],
        refs[slots + 1 :],
    )
    fetch, late_fetch = Fetch(sems), Fetch(late_sems)
    low = first * HEAD_DIM
    opened = close_open(fetch, first, q, part, stats, near, q_v, near_v, state, stats_v)
    copies = fetch_weight(late_fetch, moves, device_place(), weight, held, low, low + q_v.shape[1])
    so_far_copy = late_fetch(so_far, sum_v)
    close_heads(opened, first, active, q_v, near_v, state, stats_v, attention)
    so_far_copy.wait()
    stores = []

    def store(at, x):
        out_v[:, at] = x.astype(jnp.bfloat16)
        stores.append(late_fetch(out_v.at[:, at], out.at[:, at]))

    project(copies, attention, held, low, store, lambda at: sum_v[:, at])
    for copy in stores:
        copy.wait()


def project_scratch(rows, columns, groups, inner, width, dtype, copies):
    share = width // groups
    return [
        pltpu.VMEM((rows, columns), jnp.bfloat16),
        pltpu.VMEM((groups, inner, share), jnp.bfloat16),
    ], [
        pltpu.VMEM((rows, width), dtype),
        pltpu.SemaphoreType.DMA((copies + width // (512 if share % 512 == 0 else share),)),
    ]


def begin(ready, weight, control, hidden, moves, inner):
    rows, width = hidden.shape
    columns = ready.shape[1]
    before, behind = project_scratch(
        rows, columns, lax.axis_size("groups"), inner, width, jnp.float32, 2 + len(moves) + len(control)
    )
    return pl.pallas_call(
        functools.partial(begin_kernel, (len(weight), len(control)), moves, control[0].shape[0]),
        out_shape=jax.ShapeDtypeStruct((rows, width), jnp.float32),
        in_specs=[ANY] * (2 + len(weight) + len(control)),
        out_specs=ANY,
        scratch_shapes=before + [pltpu.VMEM((rows, width), jnp.bfloat16)] * 2 + behind,
        compiler_params=pltpu.CompilerParams(vmem_limit_bytes=VMEM_LIMIT),
        cost_estimate=pl.CostEstimate(
            flops=2 * rows * columns * width, bytes_accessed=2 * columns * width + 8 * rows * width, transcendentals=0
        ),
        name="begin",
    )(hidden, ready, *weight, *control)


def finish(which, pattern, q, state, near, first, so_far, weight, moves):
    rows, inner = q.shape
    width = so_far.shape[1]
    columns = near[0].shape[1] // 2
    before, behind = project_scratch(
        rows, columns, lax.axis_size("groups"), inner, width, jnp.bfloat16, 1 + len(moves)
    )
    return pl.pallas_call(
        functools.partial(finish_kernel, which, len(weight), moves, first),
        out_shape=jax.ShapeDtypeStruct((rows, width), jnp.bfloat16),
        in_specs=[SMEM] + [ANY] * (4 + len(near) + len(weight)),
        out_specs=ANY,
        scratch_shapes=close_scratch(rows, columns, len(near))
        + before
        + [pltpu.VMEM((rows, width), jnp.float32)]
        + behind,
        compiler_params=pltpu.CompilerParams(vmem_limit_bytes=VMEM_LIMIT),
        cost_estimate=pl.CostEstimate(
            flops=2 * rows * columns * width, bytes_accessed=2 * columns * width + 6 * rows * width, transcendentals=0
        ),
        name="finish",
    )(pattern, q, *state, so_far, *near, *weight)


def flipped(block, axis, flip):
    return lax.ppermute(block, axis, [(i, i ^ flip) for i in range(lax.axis_size(axis))])


class Lane:
    def __init__(self):
        self.last = ()

    def __call__(self, send, block, *others):
        self.last = (send(after(block, *self.last, *others)),)
        return self.last[0]


def swap(axis, flip):
    return lambda block: flipped(block, axis, flip)


def route_of(route):
    return lambda block: lax.ppermute(block, TILES, route)


def grid_of(tile_count):
    width = min(8, tile_count // 4)
    height = min(4, tile_count // 8)
    return (width * height, width, 1), (tile_count // (width * height), height, width)


def device_place():
    return [lax.axis_index(a) for a in ("groups",) + TILES]


def device_column(place):
    _, outer, pair, core = place
    tile_count = math.prod(lax.axis_size(a) for a in TILES)
    return lax.rem((outer * 2 + pair) * 2 + core, grid_of(tile_count)[1][2])


def in_window(pattern, slots):
    _, outer, pair, core = device_place()
    strides, counts = grid_of(math.prod(lax.axis_size(a) for a in TILES))
    position = (outer * 2 + pair) * 2 + core
    active = []
    for axis, odd in slots:
        place = lax.rem(lax.div(position, strides[axis]), counts[axis])
        down = (place >= 1) & (pattern[0, 2 * axis] == 1)
        up = (place + 1 < counts[axis]) & (pattern[0, 2 * axis + 1] == 1)
        active.append(jnp.where(lax.rem(place, 2) == odd, up.astype(jnp.int32), down.astype(jnp.int32)) == 1)
    return active


def neighbour_slots(tile_count, strides, counts):
    slots = []
    for axis, (stride, count) in enumerate(zip(strides, counts)):
        for odd in range(2):
            route = []
            for t in range(tile_count):
                place = t // stride % count
                if place % 2 == odd and place + 1 < count:
                    route += [(t, t + stride), (t + stride, t)]
            if route:
                slots.append((axis, odd, route))
    return slots


def on_device(hidden, queries, keys, values, control, out_weight, pattern):
    groups = lax.axis_size("groups")
    outer, pair, cores = (lax.axis_size(a) for a in TILES)
    tile_count = outer * pair * cores
    strides, counts = grid_of(tile_count)
    grid_width = counts[2]
    across = device_column(device_place())
    rows = queries.shape[0]
    width = hidden.shape[1]
    slots = neighbour_slots(tile_count, strides, counts)
    early = [s for s in slots if s[0] == 2]
    late = [s for s in slots if s[0] != 2]

    far_lane, near_lane = Lane(), Lane()

    shard, share = out_weight.shape[0], width // groups
    line = out_weight[:, :share]
    for g in range(1, groups):
        line = jnp.where(lax.axis_index("groups") == g, out_weight[:, g * share : (g + 1) * share], line)
    line = lax.optimization_barrier(line)[None]
    line_flips = [0]
    flip = outer // 2
    while flip > 2:
        line = jnp.concatenate([line, flipped(line, "outer", flip)])
        line_flips += [f ^ flip for f in line_flips]
        flip //= 2
    far = far_lane(swap("outer", 2), line)
    near = near_lane(swap("outer", 1), line)

    firsts = [sum(CHUNKS[:i]) for i in range(len(CHUNKS))]
    chunks = [
        jnp.concatenate([x[:, f * HEAD_DIM : (f + n) * HEAD_DIM] for x in (keys, values)], axis=1)
        for f, n in zip(firsts, CHUNKS)
    ]
    block = rows // grid_width
    lines = after(control, line).reshape(block // TILE_W, grid_width, TILE_W, width)
    control_sent = [
        lax.dynamic_index_in_dim(lines, across ^ d, 1, keepdims=False).reshape(block, width) for d in range(grid_width)
    ]
    chunks, control_sent = lax.optimization_barrier((chunks, control_sent))
    control_parts = [control_sent[0]] + [None] * (grid_width - 1)
    beside = swap("pair", 1)(line)
    plane = jnp.concatenate([line, beside])
    early_near = [[None, None]] + [
        [lax.ppermute(after(x, wait), TILES, route) for x, wait in ((keys, line), (values, plane))]
        for _, _, route in early[1:]
    ]
    held = [plane, swap("groups", 1)(plane)]
    last = swap("outer", 1)(after(far, near, *[kv[0] for kv in early_near[1:]], *chunks))
    last_x = swap("pair", 1)(after(last, held[1]))
    early_near[0][0] = lax.ppermute(keys, TILES, early[0][2])
    early_near[0][1] = lax.ppermute(after(values, early_near[0][0]), TILES, early[0][2])
    crossed = [swap("core", 1)(x) for x in held]
    plane = jnp.concatenate([last, last_x])
    held += [plane, swap("groups", 1)(plane)]
    crossed += [swap("core", 1)(x) for x in held[2:]]
    for d in range(2, grid_width):
        control_parts[d] = swap(TILES, d)(after(control_sent[d], last_x))
    state = attend(tuple(s[:2] for s in early), pattern, queries, [keys, values] + [x for kv in early_near for x in kv])

    weight = [lax.all_gather(after(jnp.concatenate([far, near]), held[1], last, *[kv[1] for kv in early_near[1:]]), ("groups", "pair", "core"))]
    n = len(line_flips)
    moves = [
        (0, ((g * pair + p) * cores + c, i * n + j), (False, g, f ^ at, p, c))
        for g in range(groups)
        for p in range(pair)
        for c in range(cores)
        for i, at in enumerate((2, 1))
        for j, f in enumerate(line_flips)
    ]
    for number, (group_flip, at) in enumerate(((0, 0), (1, 0), (0, 3), (1, 3))):
        for core_flip, pieces in enumerate((held, crossed)):
            moves += [
                (len(weight), (p * n + j,), (True, group_flip, f ^ at, p, core_flip))
                for p in range(pair)
                for j, f in enumerate(line_flips)
            ]
            weight.append(pieces[number])

    late_near = []
    for chunk in chunks:
        lanes = (far_lane, near_lane)
        waits = [early_near[0][1], *crossed[:1]] if late_near else []
        late_near.append([lanes[i % 2](route_of(route), chunk, *waits) for i, (_, _, route) in enumerate(late)])
    control_parts[1] = swap(TILES, 1)(after(control_sent[1], *late_near[0]))
    which = tuple(s[:2] for s in late)
    ready = [close(which, pattern, queries, state, late_near[i], firsts[i]) for i in range(len(CHUNKS) - 1)]
    ready = ready[0] if len(ready) == 1 else jnp.concatenate(ready, axis=1)
    if block % 16:
        control_parts = [
            jnp.take(
                jnp.stack(control_parts), jnp.arange(grid_width, dtype=jnp.int32) ^ across, axis=0
            ).reshape(rows, width)
        ]
    if shard % 16:
        weight, moves = [in_order(weight, moves, device_place(), (groups, outer, pair, cores))], [(0, None, None)]
    moves = tuple(moves)
    so_far = begin(ready, weight, control_parts, hidden, moves, queries.shape[1])
    return finish(which, pattern, queries, state, late_near[-1], firsts[-1], so_far, weight, moves)


def in_order(weight, moves, place, sizes):
    groups, outer, pair, cores = sizes
    shard, columns = weight[0].shape[-2:]
    gathered = weight[0].reshape(groups, pair, cores, -1, shard, columns)
    for axis, at in enumerate((0, 2, 3)):
        gathered = jnp.take(gathered, jnp.arange(sizes[at], dtype=jnp.int32) ^ place[at], axis=axis)
    weight = [gathered.reshape(weight[0].shape)] + weight[1:]
    blocks = {at[1:]: weight[piece][index] for piece, index, at in moves}
    whole = jnp.stack([blocks[at] for at in sorted(blocks)]).reshape(sizes + (shard, columns))
    for axis, size in enumerate(sizes):
        whole = jnp.take(whole, jnp.arange(size, dtype=jnp.int32) ^ place[axis], axis=axis)
    return whole.reshape(groups, -1, columns)


def solution(mesh):
    groups = mesh.shape["groups"]
    tiles = mesh.shape["tiles"]
    split = Mesh(mesh.devices.reshape(groups, tiles // 4, 2, 2), ("groups",) + TILES)
    rows = P(("groups",) + TILES, None)
    placed = (rows, rows, rows, rows, rows, P(TILES, None), rows)
    return jax.shard_map(
        on_device,
        mesh=split,
        in_specs=placed,
        out_specs=rows,
        check_vma=False,
    )
```

```python
import functools
import math

import jax
import jax.numpy as jnp
from jax import lax
from jax.experimental import pallas as pl
from jax.experimental.pallas import tpu as pltpu
from jax.sharding import Mesh
from jax.sharding import PartitionSpec as P

HEAD_DIM = 128
TILE_W = 8
CHUNKS = (7, 5)
SCALE = HEAD_DIM**-0.5 * math.log2(math.e)
TILES = ("outer", "pair", "core")
VMEM_LIMIT = 60 * 1024 * 1024
SMEM = pl.BlockSpec(memory_space=pltpu.SMEM)
ANY = pl.BlockSpec(memory_space=pl.ANY)


def after(x, *others):
    return lax.optimization_barrier((x, *others))[0] if others else x


def head_part(q, k, v):
    scores = lax.dot_general(q, k, (((1,), (1,)), ((), ())), preferred_element_type=jnp.float32)
    peak = jnp.max(scores, axis=1, keepdims=True)
    weights = jnp.exp2((scores - peak) * SCALE).astype(jnp.bfloat16)
    ones = jnp.ones((v.shape[0], HEAD_DIM), jnp.bfloat16)
    both = jnp.dot(weights, jnp.concatenate([v, ones], axis=1), preferred_element_type=jnp.float32)
    return both[:, :HEAD_DIM], both[:, HEAD_DIM:], jnp.broadcast_to(peak, v.shape)


def merge(old, new):
    part, total, peak = old
    part_new, total_new, peak_new = new
    top = jnp.maximum(peak, peak_new)
    f_old = jnp.exp2((peak - top) * SCALE)
    f_new = jnp.exp2((peak_new - top) * SCALE)
    return f_old * part + f_new * part_new, f_old * total + f_new * total_new, top


def columns_of(h):
    return pl.ds(h * HEAD_DIM, HEAD_DIM)


def fold(state, active, q, k, v):
    @pl.when(active)
    def _():
        for h in range(q.shape[1] // HEAD_DIM):
            at = columns_of(h)
            new = head_part(q[:, at], k[:, at], v[:, at])
            for r, x in zip(state, merge(tuple(r[:, at] for r in state), new)):
                r[:, at] = x


class Fetch:
    def __init__(self, sems):
        self.sems, self.count = sems, 0

    def later(self, source, target):
        self.count += 1
        return pltpu.make_async_copy(source, target, self.sems.at[self.count - 1])

    def __call__(self, source, target):
        copy = self.later(source, target)
        copy.start()
        return copy


def attend_kernel(which, pattern, q, *refs):
    slots, active = len(which), in_window(pattern, which)
    kv, (part, stats), scratch = refs[: 2 * slots + 2], refs[2 * slots + 2 : 2 * slots + 4], refs[2 * slots + 4 :]
    q_v, kv_v, (part_v, total_v, peak_v, stats_v, sems) = scratch[0], scratch[1 : 2 * slots + 3], scratch[2 * slots + 3 :]
    fetch = Fetch(sems)
    copies = [fetch(source, target) for source, target in zip((q, *kv), (q_v, *kv_v))]
    for copy in copies[:3]:
        copy.wait()
    state = (part_v, total_v, peak_v)
    heads = q_v.shape[1] // HEAD_DIM
    for h in range(heads):
        at = columns_of(h)
        for r, x in zip(state, head_part(q_v[:, at], kv_v[0][:, at], kv_v[1][:, at])):
            r[:, at] = x
    for slot in range(slots):
        for copy in copies[3 + 2 * slot : 5 + 2 * slot]:
            copy.wait()
        fold(state, active[slot], q_v, kv_v[2 * slot + 2], kv_v[2 * slot + 3])
    lane = lax.broadcasted_iota(jnp.int32, stats_v.shape, 1)
    packed = jnp.zeros(stats_v.shape, jnp.float32)
    for h in range(heads):
        packed = jnp.where(lane == h, total_v[:, columns_of(h)], packed)
        packed = jnp.where(lane == HEAD_DIM // 2 + h, peak_v[:, columns_of(h)], packed)
    stats_v[...] = packed
    copies = [fetch(part_v, part), fetch(stats_v, stats)]
    for copy in copies:
        copy.wait()


def attend(which, pattern, q, kv):
    rows, columns = q.shape
    slots = len(kv) // 2 - 1
    return pl.pallas_call(
        functools.partial(attend_kernel, which),
        out_shape=[
            jax.ShapeDtypeStruct((rows, columns), jnp.float32),
            jax.ShapeDtypeStruct((rows, HEAD_DIM), jnp.float32),
        ],
        in_specs=[SMEM] + [ANY] * (1 + len(kv)),
        out_specs=[ANY] * 2,
        scratch_shapes=[pltpu.VMEM((rows, columns), jnp.bfloat16)] * (1 + len(kv))
        + [pltpu.VMEM((rows, columns), jnp.float32)] * 3
        + [pltpu.VMEM((rows, HEAD_DIM), jnp.float32), pltpu.SemaphoreType.DMA((3 + len(kv),))],
        compiler_params=pltpu.CompilerParams(vmem_limit_bytes=VMEM_LIMIT),
        cost_estimate=pl.CostEstimate(
            flops=(1 + slots) * 6 * rows * rows * columns,
            bytes_accessed=rows * columns * (10 + 4 * slots),
            transcendentals=0,
        ),
        name="attend",
    )(pattern, q, *kv)


def close_open(fetch, first, q, part, stats, near, q_v, near_v, state, stats_v):
    columns = state[0].shape[1]
    at = pl.ds(first * HEAD_DIM, columns)
    return [
        fetch(q.at[:, at], q_v),
        fetch(part.at[:, at], state[0]),
        fetch(stats, stats_v),
    ] + [fetch(source, target) for source, target in zip(near, near_v)]


def close_heads(copies, first, active, q_v, near_v, state, stats_v, out):
    columns = state[0].shape[1]
    for copy in copies[:3]:
        copy.wait()
    stats_now = stats_v[...]
    for h in range(columns // HEAD_DIM):
        for r, lane in zip(state[1:], (first + h, HEAD_DIM // 2 + first + h)):
            r[:, columns_of(h)] = jnp.broadcast_to(stats_now[:, lane : lane + 1], stats_now.shape)
    for slot, kv in enumerate(near_v):
        copies[3 + slot].wait()
        fold(state, active[slot], q_v, kv.at[:, pl.ds(0, columns)], kv.at[:, pl.ds(columns, columns)])
    out[...] = (state[0][...] / state[1][...]).astype(jnp.bfloat16)


def close_scratch(rows, columns, slots):
    return (
        [pltpu.VMEM((rows, columns), jnp.bfloat16)]
        + [pltpu.VMEM((rows, 2 * columns), jnp.bfloat16)] * slots
        + [pltpu.VMEM((rows, columns), jnp.float32)] * 3
        + [pltpu.VMEM((rows, HEAD_DIM), jnp.float32), pltpu.SemaphoreType.DMA((4 + slots,))]
    )


def close_kernel(first, which, pattern, q, part, stats, *refs):
    slots, active = len(which), in_window(pattern, which)
    near, out = refs[:slots], refs[slots]
    q_v, near_v, (*state, stats_v, sems, out_v) = refs[slots + 1], refs[slots + 2 : 2 * slots + 2], refs[2 * slots + 2 :]
    fetch = Fetch(sems)
    opened = close_open(fetch, first, q, part, stats, near, q_v, near_v, state, stats_v)
    close_heads(opened, first, active, q_v, near_v, state, stats_v, out_v)
    fetch(out_v, out).wait()


def close(which, pattern, q, state, near, first):
    rows, columns = q.shape[0], near[0].shape[1] // 2
    return pl.pallas_call(
        functools.partial(close_kernel, first, which),
        out_shape=jax.ShapeDtypeStruct((rows, columns), jnp.bfloat16),
        in_specs=[SMEM] + [ANY] * (3 + len(near)),
        out_specs=ANY,
        scratch_shapes=close_scratch(rows, columns, len(near)) + [pltpu.VMEM((rows, columns), jnp.bfloat16)],
        compiler_params=pltpu.CompilerParams(vmem_limit_bytes=VMEM_LIMIT),
        cost_estimate=pl.CostEstimate(
            flops=len(near) * 6 * rows * rows * columns,
            bytes_accessed=rows * columns * (4 * len(near) + 8),
            transcendentals=0,
        ),
        name="close",
    )(pattern, q, *state, *near)


def fetch_weight(fetch, moves, place, weight, held, low, high):
    copies = []
    for piece, index, at in moves:
        if at is None:
            copies.append((True, 0, fetch(weight[piece], held)))
            continue
        source = weight[piece].at[index]
        flip, group, outer, pair, core = at
        known = None if flip else group
        count = source.shape[0]
        outer = place[1] ^ outer
        if flip:
            group, pair, core = place[0] ^ group, place[2] ^ pair, place[3] ^ core
        start = pl.multiple_of(((outer * 2 + pair) * 2 + core) * count, count)
        needed = (start < high) & (start + count > low)
        copy = fetch.later(source, held.at[group, pl.ds(start, count), :])
        pl.when(needed)(copy.start)
        copies.append((needed, 0 if known is None else known, copy))
    return copies


def project(copies, attention, held, low, out, add):
    groups, _, columns = held.shape
    step = 512 if columns % 512 == 0 else columns
    for group in range(groups):
        for needed, at, copy in copies:
            if at == group:
                if needed is True:
                    copy.wait()
                else:
                    pl.when(needed)(copy.wait)
        for j in range(columns // step):
            at = pl.ds(group * columns + j * step, step)
            projected = jnp.dot(
                attention[...],
                held[group, pl.ds(low, attention.shape[1]), pl.ds(j * step, step)],
                preferred_element_type=jnp.float32,
            )
            out(at, add(at) + projected)


def begin_kernel(counts, moves, control_rows, hidden, ready, *refs):
    place = device_place()
    weight, control = refs[: counts[0]], refs[counts[0] : sum(counts)]
    out, attention, held, hidden_v, control_v, out_v, sems = refs[sum(counts) :]
    fetch = Fetch(sems)
    residual = [fetch(ready, attention), fetch(hidden, hidden_v)]
    copies = fetch_weight(fetch, moves, place, weight, held, 0, ready.shape[1])
    for d, block in enumerate(control):
        start = pl.multiple_of((device_column(place) ^ d) * control_rows, control_rows) if len(control) > 1 else 0
        residual.append(fetch(block, control_v.at[pl.ds(start, control_rows), :]))
    for copy in residual:
        copy.wait()
    stores = []

    def store(at, x):
        out_v[:, at] = x
        stores.append(fetch(out_v.at[:, at], out.at[:, at]))

    project(
        copies,
        attention,
        held,
        0,
        store,
        lambda at: hidden_v[:, at].astype(jnp.float32) + control_v[:, at].astype(jnp.float32),
    )
    for copy in stores:
        copy.wait()


def finish_kernel(which, pieces, moves, first, pattern, q, part, stats, so_far, *refs):
    slots, active = len(which), in_window(pattern, which)
    near, weight, out, refs = refs[:slots], refs[slots : slots + pieces], refs[slots + pieces], refs[slots + pieces + 1 :]
    q_v, near_v, (*state, stats_v, sems, attention, held, sum_v, out_v, late_sems) = (
        refs[0],
        refs[1 : slots + 1],
        refs[slots + 1 :],
    )
    fetch, late_fetch = Fetch(sems), Fetch(late_sems)
    low = first * HEAD_DIM
    opened = close_open(fetch, first, q, part, stats, near, q_v, near_v, state, stats_v)
    copies = fetch_weight(late_fetch, moves, device_place(), weight, held, low, low + q_v.shape[1])
    so_far_copy = late_fetch(so_far, sum_v)
    close_heads(opened, first, active, q_v, near_v, state, stats_v, attention)
    so_far_copy.wait()
    stores = []

    def store(at, x):
        out_v[:, at] = x.astype(jnp.bfloat16)
        stores.append(late_fetch(out_v.at[:, at], out.at[:, at]))

    project(copies, attention, held, low, store, lambda at: sum_v[:, at])
    for copy in stores:
        copy.wait()


def project_scratch(rows, columns, groups, inner, width, dtype, copies):
    share = width // groups
    return [
        pltpu.VMEM((rows, columns), jnp.bfloat16),
        pltpu.VMEM((groups, inner, share), jnp.bfloat16),
    ], [
        pltpu.VMEM((rows, width), dtype),
        pltpu.SemaphoreType.DMA((copies + width // (512 if share % 512 == 0 else share),)),
    ]


def begin(ready, weight, control, hidden, moves, inner):
    rows, width = hidden.shape
    columns = ready.shape[1]
    before, behind = project_scratch(
        rows, columns, lax.axis_size("groups"), inner, width, jnp.float32, 2 + len(moves) + len(control)
    )
    return pl.pallas_call(
        functools.partial(begin_kernel, (len(weight), len(control)), moves, control[0].shape[0]),
        out_shape=jax.ShapeDtypeStruct((rows, width), jnp.float32),
        in_specs=[ANY] * (2 + len(weight) + len(control)),
        out_specs=ANY,
        scratch_shapes=before + [pltpu.VMEM((rows, width), jnp.bfloat16)] * 2 + behind,
        compiler_params=pltpu.CompilerParams(vmem_limit_bytes=VMEM_LIMIT),
        cost_estimate=pl.CostEstimate(
            flops=2 * rows * columns * width, bytes_accessed=2 * columns * width + 8 * rows * width, transcendentals=0
        ),
        name="begin",
    )(hidden, ready, *weight, *control)


def finish(which, pattern, q, state, near, first, so_far, weight, moves):
    rows, inner = q.shape
    width = so_far.shape[1]
    columns = near[0].shape[1] // 2
    before, behind = project_scratch(
        rows, columns, lax.axis_size("groups"), inner, width, jnp.bfloat16, 1 + len(moves)
    )
    return pl.pallas_call(
        functools.partial(finish_kernel, which, len(weight), moves, first),
        out_shape=jax.ShapeDtypeStruct((rows, width), jnp.bfloat16),
        in_specs=[SMEM] + [ANY] * (4 + len(near) + len(weight)),
        out_specs=ANY,
        scratch_shapes=close_scratch(rows, columns, len(near))
        + before
        + [pltpu.VMEM((rows, width), jnp.float32)]
        + behind,
        compiler_params=pltpu.CompilerParams(vmem_limit_bytes=VMEM_LIMIT),
        cost_estimate=pl.CostEstimate(
            flops=2 * rows * columns * width, bytes_accessed=2 * columns * width + 6 * rows * width, transcendentals=0
        ),
        name="finish",
    )(pattern, q, *state, so_far, *near, *weight)


def flipped(block, axis, flip):
    return lax.ppermute(block, axis, [(i, i ^ flip) for i in range(lax.axis_size(axis))])


class Lane:
    def __init__(self):
        self.last = ()

    def __call__(self, send, block, *others):
        self.last = (send(after(block, *self.last, *others)),)
        return self.last[0]


def swap(axis, flip):
    return lambda block: flipped(block, axis, flip)


def route_of(route):
    return lambda block: lax.ppermute(block, TILES, route)


def grid_of(tile_count):
    width = min(8, tile_count // 4)
    height = min(4, tile_count // 8)
    return (width * height, width, 1), (tile_count // (width * height), height, width)


def device_place():
    return [lax.axis_index(a) for a in ("groups",) + TILES]


def device_column(place):
    _, outer, pair, core = place
    tile_count = math.prod(lax.axis_size(a) for a in TILES)
    return lax.rem((outer * 2 + pair) * 2 + core, grid_of(tile_count)[1][2])


def in_window(pattern, slots):
    _, outer, pair, core = device_place()
    strides, counts = grid_of(math.prod(lax.axis_size(a) for a in TILES))
    position = (outer * 2 + pair) * 2 + core
    active = []
    for axis, odd in slots:
        place = lax.rem(lax.div(position, strides[axis]), counts[axis])
        down = (place >= 1) & (pattern[0, 2 * axis] == 1)
        up = (place + 1 < counts[axis]) & (pattern[0, 2 * axis + 1] == 1)
        active.append(jnp.where(lax.rem(place, 2) == odd, up.astype(jnp.int32), down.astype(jnp.int32)) == 1)
    return active


def neighbour_slots(tile_count, strides, counts):
    slots = []
    for axis, (stride, count) in enumerate(zip(strides, counts)):
        for odd in range(2):
            route = []
            for t in range(tile_count):
                place = t // stride % count
                if place % 2 == odd and place + 1 < count:
                    route += [(t, t + stride), (t + stride, t)]
            if route:
                slots.append((axis, odd, route))
    return slots


def on_device(hidden, queries, keys, values, control, out_weight, pattern):
    groups = lax.axis_size("groups")
    outer, pair, cores = (lax.axis_size(a) for a in TILES)
    tile_count = outer * pair * cores
    strides, counts = grid_of(tile_count)
    grid_width = counts[2]
    across = device_column(device_place())
    rows = queries.shape[0]
    width = hidden.shape[1]
    slots = neighbour_slots(tile_count, strides, counts)
    early = [s for s in slots if s[0] == 2]
    late = [s for s in slots if s[0] != 2]

    far_lane, near_lane = Lane(), Lane()

    shard, share = out_weight.shape[0], width // groups
    line = out_weight[:, :share]
    for g in range(1, groups):
        line = jnp.where(lax.axis_index("groups") == g, out_weight[:, g * share : (g + 1) * share], line)
    line = lax.optimization_barrier(line)[None]
    line_flips = [0]
    flip = outer // 2
    while flip > 2:
        line = jnp.concatenate([line, flipped(line, "outer", flip)])
        line_flips += [f ^ flip for f in line_flips]
        flip //= 2
    far = far_lane(swap("outer", 2), line)
    near = near_lane(swap("outer", 1), line)

    firsts = [sum(CHUNKS[:i]) for i in range(len(CHUNKS))]
    chunks = [
        jnp.concatenate([x[:, f * HEAD_DIM : (f + n) * HEAD_DIM] for x in (keys, values)], axis=1)
        for f, n in zip(firsts, CHUNKS)
    ]
    block = rows // grid_width
    lines = after(control, line).reshape(block // TILE_W, grid_width, TILE_W, width)
    control_sent = [
        lax.dynamic_index_in_dim(lines, across ^ d, 1, keepdims=False).reshape(block, width) for d in range(grid_width)
    ]
    chunks, control_sent = lax.optimization_barrier((chunks, control_sent))
    control_parts = [control_sent[0]] + [None] * (grid_width - 1)
    beside = swap("pair", 1)(line)
    for d in range(2, grid_width):
        control_parts[d] = swap(TILES, d)(after(control_sent[d], line if d < grid_width - 1 else beside))
    control_parts[1] = swap(TILES, 1)(control_sent[1])
    plane = jnp.concatenate([line, beside])
    last = swap("outer", 1)(after(far, near, *control_parts[2:-1], *chunks))
    near_x = swap("pair", 1)(near)
    held = []
    for both in (plane, jnp.concatenate([near, near_x])):
        held += [both, swap("groups", 1)(both)]
    early_near = [[None, None] for _ in early]
    for i, x in enumerate((keys, values)):
        early_near[0][i] = lax.ppermute(x, TILES, early[0][2])
        for slot in range(1, len(early)):
            early_near[slot][i] = lax.ppermute(after(x, early_near[0][i]), TILES, early[slot][2])
    state = attend(tuple(s[:2] for s in early), pattern, queries, [keys, values] + [x for kv in early_near for x in kv])

    late_near = []
    for chunk in chunks:
        lanes = (far_lane, near_lane)
        late_near.append([lanes[i % 2](route_of(route), chunk) for i, (_, _, route) in enumerate(late)])
    crossed = [swap("core", 1)(x) for x in held]

    gates = [*control_parts[2:], near_x, held[1]]
    weight = [lax.all_gather(after(jnp.concatenate([far, last]), *gates), ("groups", "pair", "core"))]
    n = len(line_flips)
    moves = [
        (0, ((g * pair + p) * cores + c, i * n + j), (False, g, f ^ at, p, c))
        for g in range(groups)
        for p in range(pair)
        for c in range(cores)
        for i, at in enumerate((2, 3))
        for j, f in enumerate(line_flips)
    ]
    for number, (group_flip, at) in enumerate(((0, 0), (1, 0), (0, 1), (1, 1))):
        for core_flip, pieces in enumerate((held, crossed)):
            moves += [
                (len(weight), (p * n + j,), (True, group_flip, f ^ at, p, core_flip))
                for p in range(pair)
                for j, f in enumerate(line_flips)
            ]
            weight.append(pieces[number])

    which = tuple(s[:2] for s in late)
    ready = [close(which, pattern, queries, state, late_near[i], firsts[i]) for i in range(len(CHUNKS) - 1)]
    ready = ready[0] if len(ready) == 1 else jnp.concatenate(ready, axis=1)
    if block % 16:
        control_parts = [
            jnp.take(
                jnp.stack(control_parts), jnp.arange(grid_width, dtype=jnp.int32) ^ across, axis=0
            ).reshape(rows, width)
        ]
    if shard % 16:
        weight, moves = [in_order(weight, moves, device_place(), (groups, outer, pair, cores))], [(0, None, None)]
    moves = tuple(moves)
    so_far = begin(ready, weight, control_parts, hidden, moves, queries.shape[1])
    return finish(which, pattern, queries, state, late_near[-1], firsts[-1], so_far, weight, moves)


def in_order(weight, moves, place, sizes):
    groups, outer, pair, cores = sizes
    shard, columns = weight[0].shape[-2:]
    gathered = weight[0].reshape(groups, pair, cores, -1, shard, columns)
    for axis, at in enumerate((0, 2, 3)):
        gathered = jnp.take(gathered, jnp.arange(sizes[at], dtype=jnp.int32) ^ place[at], axis=axis)
    weight = [gathered.reshape(weight[0].shape)] + weight[1:]
    blocks = {at[1:]: weight[piece][index] for piece, index, at in moves}
    whole = jnp.stack([blocks[at] for at in sorted(blocks)]).reshape(sizes + (shard, columns))
    for axis, size in enumerate(sizes):
        whole = jnp.take(whole, jnp.arange(size, dtype=jnp.int32) ^ place[axis], axis=axis)
    return whole.reshape(groups, -1, columns)


def solution(mesh):
    groups = mesh.shape["groups"]
    tiles = mesh.shape["tiles"]
    split = Mesh(mesh.devices.reshape(groups, tiles // 4, 2, 2), ("groups",) + TILES)
    rows = P(("groups",) + TILES, None)
    placed = (rows, rows, rows, rows, rows, P(TILES, None), rows)
    return jax.shard_map(
        on_device,
        mesh=split,
        in_specs=placed,
        out_specs=rows,
        check_vma=False,
    )
```

```python
import functools
import math

import jax
import jax.numpy as jnp
from jax import lax
from jax.experimental import pallas as pl
from jax.experimental.pallas import tpu as pltpu
from jax.sharding import Mesh
from jax.sharding import PartitionSpec as P

HEAD_DIM = 128
TILE_W = 8
CHUNKS = (6, 6)
SCALE = HEAD_DIM**-0.5 * math.log2(math.e)
TILES = ("outer", "pair", "core")
VMEM_LIMIT = 60 * 1024 * 1024
SMEM = pl.BlockSpec(memory_space=pltpu.SMEM)
ANY = pl.BlockSpec(memory_space=pl.ANY)


def after(x, *others):
    return lax.optimization_barrier((x, *others))[0] if others else x


def head_part(q, k, v):
    scores = lax.dot_general(q, k, (((1,), (1,)), ((), ())), preferred_element_type=jnp.float32)
    peak = jnp.max(scores, axis=1, keepdims=True)
    weights = jnp.exp2((scores - peak) * SCALE).astype(jnp.bfloat16)
    ones = jnp.ones((v.shape[0], HEAD_DIM), jnp.bfloat16)
    both = jnp.dot(weights, jnp.concatenate([v, ones], axis=1), preferred_element_type=jnp.float32)
    return both[:, :HEAD_DIM], both[:, HEAD_DIM:], jnp.broadcast_to(peak, v.shape)


def merge(old, new):
    part, total, peak = old
    part_new, total_new, peak_new = new
    top = jnp.maximum(peak, peak_new)
    f_old = jnp.exp2((peak - top) * SCALE)
    f_new = jnp.exp2((peak_new - top) * SCALE)
    return f_old * part + f_new * part_new, f_old * total + f_new * total_new, top


def columns_of(h):
    return pl.ds(h * HEAD_DIM, HEAD_DIM)


def fold(state, active, q, k, v):
    @pl.when(active)
    def _():
        for h in range(q.shape[1] // HEAD_DIM):
            at = columns_of(h)
            new = head_part(q[:, at], k[:, at], v[:, at])
            for r, x in zip(state, merge(tuple(r[:, at] for r in state), new)):
                r[:, at] = x


class Fetch:
    def __init__(self, sems):
        self.sems, self.count = sems, 0

    def later(self, source, target):
        self.count += 1
        return pltpu.make_async_copy(source, target, self.sems.at[self.count - 1])

    def __call__(self, source, target):
        copy = self.later(source, target)
        copy.start()
        return copy


def attend_kernel(which, pattern, q, *refs):
    slots, active = len(which), in_window(pattern, which)
    kv, (part, stats), scratch = refs[: 2 * slots + 2], refs[2 * slots + 2 : 2 * slots + 4], refs[2 * slots + 4 :]
    q_v, kv_v, (part_v, total_v, peak_v, stats_v, sems) = scratch[0], scratch[1 : 2 * slots + 3], scratch[2 * slots + 3 :]
    fetch = Fetch(sems)
    copies = [fetch(source, target) for source, target in zip((q, *kv), (q_v, *kv_v))]
    for copy in copies[:3]:
        copy.wait()
    state = (part_v, total_v, peak_v)
    heads = q_v.shape[1] // HEAD_DIM
    for h in range(heads):
        at = columns_of(h)
        for r, x in zip(state, head_part(q_v[:, at], kv_v[0][:, at], kv_v[1][:, at])):
            r[:, at] = x
    for slot in range(slots):
        for copy in copies[3 + 2 * slot : 5 + 2 * slot]:
            copy.wait()
        fold(state, active[slot], q_v, kv_v[2 * slot + 2], kv_v[2 * slot + 3])
    lane = lax.broadcasted_iota(jnp.int32, stats_v.shape, 1)
    packed = jnp.zeros(stats_v.shape, jnp.float32)
    for h in range(heads):
        packed = jnp.where(lane == h, total_v[:, columns_of(h)], packed)
        packed = jnp.where(lane == HEAD_DIM // 2 + h, peak_v[:, columns_of(h)], packed)
    stats_v[...] = packed
    copies = [fetch(part_v, part), fetch(stats_v, stats)]
    for copy in copies:
        copy.wait()


def attend(which, pattern, q, kv):
    rows, columns = q.shape
    slots = len(kv) // 2 - 1
    return pl.pallas_call(
        functools.partial(attend_kernel, which),
        out_shape=[
            jax.ShapeDtypeStruct((rows, columns), jnp.float32),
            jax.ShapeDtypeStruct((rows, HEAD_DIM), jnp.float32),
        ],
        in_specs=[SMEM] + [ANY] * (1 + len(kv)),
        out_specs=[ANY] * 2,
        scratch_shapes=[pltpu.VMEM((rows, columns), jnp.bfloat16)] * (1 + len(kv))
        + [pltpu.VMEM((rows, columns), jnp.float32)] * 3
        + [pltpu.VMEM((rows, HEAD_DIM), jnp.float32), pltpu.SemaphoreType.DMA((3 + len(kv),))],
        compiler_params=pltpu.CompilerParams(vmem_limit_bytes=VMEM_LIMIT),
        cost_estimate=pl.CostEstimate(
            flops=(1 + slots) * 6 * rows * rows * columns,
            bytes_accessed=rows * columns * (10 + 4 * slots),
            transcendentals=0,
        ),
        name="attend",
    )(pattern, q, *kv)


def close_open(fetch, first, q, part, stats, near, q_v, near_v, state, stats_v):
    columns = state[0].shape[1]
    at = pl.ds(first * HEAD_DIM, columns)
    return [
        fetch(q.at[:, at], q_v),
        fetch(part.at[:, at], state[0]),
        fetch(stats, stats_v),
    ] + [fetch(source, target) for source, target in zip(near, near_v)]


def close_heads(copies, first, active, q_v, near_v, state, stats_v, out):
    columns = state[0].shape[1]
    for copy in copies[:3]:
        copy.wait()
    stats_now = stats_v[...]
    for h in range(columns // HEAD_DIM):
        for r, lane in zip(state[1:], (first + h, HEAD_DIM // 2 + first + h)):
            r[:, columns_of(h)] = jnp.broadcast_to(stats_now[:, lane : lane + 1], stats_now.shape)
    for slot, kv in enumerate(near_v):
        copies[3 + slot].wait()
        fold(state, active[slot], q_v, kv.at[:, pl.ds(0, columns)], kv.at[:, pl.ds(columns, columns)])
    out[...] = (state[0][...] / state[1][...]).astype(jnp.bfloat16)


def close_scratch(rows, columns, slots):
    return (
        [pltpu.VMEM((rows, columns), jnp.bfloat16)]
        + [pltpu.VMEM((rows, 2 * columns), jnp.bfloat16)] * slots
        + [pltpu.VMEM((rows, columns), jnp.float32)] * 3
        + [pltpu.VMEM((rows, HEAD_DIM), jnp.float32), pltpu.SemaphoreType.DMA((4 + slots,))]
    )


def close_kernel(first, which, pattern, q, part, stats, *refs):
    slots, active = len(which), in_window(pattern, which)
    near, out = refs[:slots], refs[slots]
    q_v, near_v, (*state, stats_v, sems, out_v) = refs[slots + 1], refs[slots + 2 : 2 * slots + 2], refs[2 * slots + 2 :]
    fetch = Fetch(sems)
    opened = close_open(fetch, first, q, part, stats, near, q_v, near_v, state, stats_v)
    close_heads(opened, first, active, q_v, near_v, state, stats_v, out_v)
    fetch(out_v, out).wait()


def close(which, pattern, q, state, near, first):
    rows, columns = q.shape[0], near[0].shape[1] // 2
    return pl.pallas_call(
        functools.partial(close_kernel, first, which),
        out_shape=jax.ShapeDtypeStruct((rows, columns), jnp.bfloat16),
        in_specs=[SMEM] + [ANY] * (3 + len(near)),
        out_specs=ANY,
        scratch_shapes=close_scratch(rows, columns, len(near)) + [pltpu.VMEM((rows, columns), jnp.bfloat16)],
        compiler_params=pltpu.CompilerParams(vmem_limit_bytes=VMEM_LIMIT),
        cost_estimate=pl.CostEstimate(
            flops=len(near) * 6 * rows * rows * columns,
            bytes_accessed=rows * columns * (4 * len(near) + 8),
            transcendentals=0,
        ),
        name="close",
    )(pattern, q, *state, *near)


def fetch_weight(fetch, moves, place, weight, held, low, high):
    copies = []
    for piece, index, at in moves:
        if at is None:
            copies.append((True, 0, fetch(weight[piece], held)))
            continue
        source = weight[piece].at[index]
        flip, group, outer, pair, core = at
        known = None if flip else group
        count = source.shape[0]
        outer = place[1] ^ outer
        if flip:
            group, pair, core = place[0] ^ group, place[2] ^ pair, place[3] ^ core
        start = pl.multiple_of(((outer * 2 + pair) * 2 + core) * count, count)
        needed = (start < high) & (start + count > low)
        copy = fetch.later(source, held.at[group, pl.ds(start, count), :])
        pl.when(needed)(copy.start)
        copies.append((needed, 0 if known is None else known, copy))
    return copies


def project(copies, attention, held, low, out, add):
    groups, _, columns = held.shape
    step = 512 if columns % 512 == 0 else columns
    for group in range(groups):
        for needed, at, copy in copies:
            if at == group:
                if needed is True:
                    copy.wait()
                else:
                    pl.when(needed)(copy.wait)
        for j in range(columns // step):
            at = pl.ds(group * columns + j * step, step)
            projected = jnp.dot(
                attention[...],
                held[group, pl.ds(low, attention.shape[1]), pl.ds(j * step, step)],
                preferred_element_type=jnp.float32,
            )
            out(at, add(at) + projected)


def begin_kernel(counts, moves, control_rows, hidden, ready, *refs):
    place = device_place()
    weight, control = refs[: counts[0]], refs[counts[0] : sum(counts)]
    out, attention, held, hidden_v, control_v, out_v, sems = refs[sum(counts) :]
    fetch = Fetch(sems)
    residual = [fetch(ready, attention), fetch(hidden, hidden_v)]
    copies = fetch_weight(fetch, moves, place, weight, held, 0, ready.shape[1])
    for d, block in enumerate(control):
        start = pl.multiple_of((device_column(place) ^ d) * control_rows, control_rows) if len(control) > 1 else 0
        residual.append(fetch(block, control_v.at[pl.ds(start, control_rows), :]))
    for copy in residual:
        copy.wait()
    stores = []

    def store(at, x):
        out_v[:, at] = x
        stores.append(fetch(out_v.at[:, at], out.at[:, at]))

    project(
        copies,
        attention,
        held,
        0,
        store,
        lambda at: hidden_v[:, at].astype(jnp.float32) + control_v[:, at].astype(jnp.float32),
    )
    for copy in stores:
        copy.wait()


def finish_kernel(which, pieces, moves, first, pattern, q, part, stats, so_far, *refs):
    slots, active = len(which), in_window(pattern, which)
    near, weight, out, refs = refs[:slots], refs[slots : slots + pieces], refs[slots + pieces], refs[slots + pieces + 1 :]
    q_v, near_v, (*state, stats_v, sems, attention, held, sum_v, out_v, late_sems) = (
        refs[0],
        refs[1 : slots + 1],
        refs[slots + 1 :],
    )
    fetch, late_fetch = Fetch(sems), Fetch(late_sems)
    low = first * HEAD_DIM
    opened = close_open(fetch, first, q, part, stats, near, q_v, near_v, state, stats_v)
    copies = fetch_weight(late_fetch, moves, device_place(), weight, held, low, low + q_v.shape[1])
    so_far_copy = late_fetch(so_far, sum_v)
    close_heads(opened, first, active, q_v, near_v, state, stats_v, attention)
    so_far_copy.wait()
    stores = []

    def store(at, x):
        out_v[:, at] = x.astype(jnp.bfloat16)
        stores.append(late_fetch(out_v.at[:, at], out.at[:, at]))

    project(copies, attention, held, low, store, lambda at: sum_v[:, at])
    for copy in stores:
        copy.wait()


def project_scratch(rows, columns, groups, inner, width, dtype, copies):
    share = width // groups
    return [
        pltpu.VMEM((rows, columns), jnp.bfloat16),
        pltpu.VMEM((groups, inner, share), jnp.bfloat16),
    ], [
        pltpu.VMEM((rows, width), dtype),
        pltpu.SemaphoreType.DMA((copies + width // (512 if share % 512 == 0 else share),)),
    ]


def begin(ready, weight, control, hidden, moves, inner):
    rows, width = hidden.shape
    columns = ready.shape[1]
    before, behind = project_scratch(
        rows, columns, lax.axis_size("groups"), inner, width, jnp.float32, 2 + len(moves) + len(control)
    )
    return pl.pallas_call(
        functools.partial(begin_kernel, (len(weight), len(control)), moves, control[0].shape[0]),
        out_shape=jax.ShapeDtypeStruct((rows, width), jnp.float32),
        in_specs=[ANY] * (2 + len(weight) + len(control)),
        out_specs=ANY,
        scratch_shapes=before + [pltpu.VMEM((rows, width), jnp.bfloat16)] * 2 + behind,
        compiler_params=pltpu.CompilerParams(vmem_limit_bytes=VMEM_LIMIT),
        cost_estimate=pl.CostEstimate(
            flops=2 * rows * columns * width, bytes_accessed=2 * columns * width + 8 * rows * width, transcendentals=0
        ),
        name="begin",
    )(hidden, ready, *weight, *control)


def finish(which, pattern, q, state, near, first, so_far, weight, moves):
    rows, inner = q.shape
    width = so_far.shape[1]
    columns = near[0].shape[1] // 2
    before, behind = project_scratch(
        rows, columns, lax.axis_size("groups"), inner, width, jnp.bfloat16, 1 + len(moves)
    )
    return pl.pallas_call(
        functools.partial(finish_kernel, which, len(weight), moves, first),
        out_shape=jax.ShapeDtypeStruct((rows, width), jnp.bfloat16),
        in_specs=[SMEM] + [ANY] * (4 + len(near) + len(weight)),
        out_specs=ANY,
        scratch_shapes=close_scratch(rows, columns, len(near))
        + before
        + [pltpu.VMEM((rows, width), jnp.float32)]
        + behind,
        compiler_params=pltpu.CompilerParams(vmem_limit_bytes=VMEM_LIMIT),
        cost_estimate=pl.CostEstimate(
            flops=2 * rows * columns * width, bytes_accessed=2 * columns * width + 6 * rows * width, transcendentals=0
        ),
        name="finish",
    )(pattern, q, *state, so_far, *near, *weight)


def flipped(block, axis, flip):
    return lax.ppermute(block, axis, [(i, i ^ flip) for i in range(lax.axis_size(axis))])


class Lane:
    def __init__(self):
        self.last = ()

    def __call__(self, send, block, *others):
        self.last = (send(after(block, *self.last, *others)),)
        return self.last[0]


def swap(axis, flip):
    return lambda block: flipped(block, axis, flip)


def route_of(route):
    return lambda block: lax.ppermute(block, TILES, route)


def grid_of(tile_count):
    width = min(8, tile_count // 4)
    height = min(4, tile_count // 8)
    return (width * height, width, 1), (tile_count // (width * height), height, width)


def device_place():
    return [lax.axis_index(a) for a in ("groups",) + TILES]


def device_column(place):
    _, outer, pair, core = place
    tile_count = math.prod(lax.axis_size(a) for a in TILES)
    return lax.rem((outer * 2 + pair) * 2 + core, grid_of(tile_count)[1][2])


def in_window(pattern, slots):
    _, outer, pair, core = device_place()
    strides, counts = grid_of(math.prod(lax.axis_size(a) for a in TILES))
    position = (outer * 2 + pair) * 2 + core
    active = []
    for axis, odd in slots:
        place = lax.rem(lax.div(position, strides[axis]), counts[axis])
        down = (place >= 1) & (pattern[0, 2 * axis] == 1)
        up = (place + 1 < counts[axis]) & (pattern[0, 2 * axis + 1] == 1)
        active.append(jnp.where(lax.rem(place, 2) == odd, up.astype(jnp.int32), down.astype(jnp.int32)) == 1)
    return active


def neighbour_slots(tile_count, strides, counts):
    slots = []
    for axis, (stride, count) in enumerate(zip(strides, counts)):
        for odd in range(2):
            route = []
            for t in range(tile_count):
                place = t // stride % count
                if place % 2 == odd and place + 1 < count:
                    route += [(t, t + stride), (t + stride, t)]
            if route:
                slots.append((axis, odd, route))
    return slots


def on_device(hidden, queries, keys, values, control, out_weight, pattern):
    groups = lax.axis_size("groups")
    outer, pair, cores = (lax.axis_size(a) for a in TILES)
    tile_count = outer * pair * cores
    strides, counts = grid_of(tile_count)
    grid_width = counts[2]
    across = device_column(device_place())
    rows = queries.shape[0]
    width = hidden.shape[1]
    slots = neighbour_slots(tile_count, strides, counts)
    early = [s for s in slots if s[0] == 2]
    late = [s for s in slots if s[0] != 2]

    far_lane, near_lane = Lane(), Lane()

    shard, share = out_weight.shape[0], width // groups
    line = out_weight[:, :share]
    for g in range(1, groups):
        line = jnp.where(lax.axis_index("groups") == g, out_weight[:, g * share : (g + 1) * share], line)
    line = lax.optimization_barrier(line)[None]
    line_flips = [0]
    flip = outer // 2
    while flip > 2:
        line = jnp.concatenate([line, flipped(line, "outer", flip)])
        line_flips += [f ^ flip for f in line_flips]
        flip //= 2
    far = far_lane(swap("outer", 2), line)
    near = near_lane(swap("outer", 1), line)

    firsts = [sum(CHUNKS[:i]) for i in range(len(CHUNKS))]
    chunks = [
        jnp.concatenate([x[:, f * HEAD_DIM : (f + n) * HEAD_DIM] for x in (keys, values)], axis=1)
        for f, n in zip(firsts, CHUNKS)
    ]
    block = rows // grid_width
    lines = after(control, line).reshape(block // TILE_W, grid_width, TILE_W, width)
    control_sent = [
        lax.dynamic_index_in_dim(lines, across ^ d, 1, keepdims=False).reshape(block, width) for d in range(grid_width)
    ]
    chunks, control_sent = lax.optimization_barrier((chunks, control_sent))
    control_parts = [control_sent[0]] + [None] * (grid_width - 1)
    beside = swap("pair", 1)(line)
    for d in range(2, grid_width - 1):
        control_parts[d] = swap(TILES, d)(after(control_sent[d], line))
    plane = jnp.concatenate([line, beside])
    last = swap("outer", 1)(after(far, near, *control_parts[2:-1], *chunks))
    near_x = swap("pair", 1)(near)
    held = []
    for both in (plane, jnp.concatenate([near, near_x])):
        held += [both, swap("groups", 1)(both)]
    early_near = [[None, None] for _ in early]
    for i, x in enumerate((keys, values)):
        early_near[0][i] = lax.ppermute(x, TILES, early[0][2])
        for slot in range(1, len(early)):
            early_near[slot][i] = lax.ppermute(after(x, early_near[0][i]), TILES, early[slot][2])
    state = attend(tuple(s[:2] for s in early), pattern, queries, [keys, values] + [x for kv in early_near for x in kv])

    late_near = []
    for chunk in chunks:
        lanes = (far_lane, near_lane)
        late_near.append([lanes[i % 2](route_of(route), chunk) for i, (_, _, route) in enumerate(late)])
    crossed = [swap("core", 1)(x) for x in held]
    for d in (1, grid_width - 1):
        control_parts[d] = swap(TILES, d)(after(control_sent[d], *[x for kv in early_near[1:] for x in kv]))

    gates = [*control_parts[2:-1], near_x, held[1]]
    weight = [lax.all_gather(after(jnp.concatenate([far, last]), *gates), ("groups", "pair", "core"))]
    n = len(line_flips)
    moves = [
        (0, ((g * pair + p) * cores + c, i * n + j), (False, g, f ^ at, p, c))
        for g in range(groups)
        for p in range(pair)
        for c in range(cores)
        for i, at in enumerate((2, 3))
        for j, f in enumerate(line_flips)
    ]
    for number, (group_flip, at) in enumerate(((0, 0), (1, 0), (0, 1), (1, 1))):
        for core_flip, pieces in enumerate((held, crossed)):
            moves += [
                (len(weight), (p * n + j,), (True, group_flip, f ^ at, p, core_flip))
                for p in range(pair)
                for j, f in enumerate(line_flips)
            ]
            weight.append(pieces[number])

    which = tuple(s[:2] for s in late)
    ready = [close(which, pattern, queries, state, late_near[i], firsts[i]) for i in range(len(CHUNKS) - 1)]
    ready = ready[0] if len(ready) == 1 else jnp.concatenate(ready, axis=1)
    if block % 16:
        control_parts = [
            jnp.take(
                jnp.stack(control_parts), jnp.arange(grid_width, dtype=jnp.int32) ^ across, axis=0
            ).reshape(rows, width)
        ]
    if shard % 16:
        weight, moves = [in_order(weight, moves, device_place(), (groups, outer, pair, cores))], [(0, None, None)]
    moves = tuple(moves)
    so_far = begin(ready, weight, control_parts, hidden, moves, queries.shape[1])
    return finish(which, pattern, queries, state, late_near[-1], firsts[-1], so_far, weight, moves)


def in_order(weight, moves, place, sizes):
    groups, outer, pair, cores = sizes
    shard, columns = weight[0].shape[-2:]
    gathered = weight[0].reshape(groups, pair, cores, -1, shard, columns)
    for axis, at in enumerate((0, 2, 3)):
        gathered = jnp.take(gathered, jnp.arange(sizes[at], dtype=jnp.int32) ^ place[at], axis=axis)
    weight = [gathered.reshape(weight[0].shape)] + weight[1:]
    blocks = {at[1:]: weight[piece][index] for piece, index, at in moves}
    whole = jnp.stack([blocks[at] for at in sorted(blocks)]).reshape(sizes + (shard, columns))
    for axis, size in enumerate(sizes):
        whole = jnp.take(whole, jnp.arange(size, dtype=jnp.int32) ^ place[axis], axis=axis)
    return whole.reshape(groups, -1, columns)


def solution(mesh):
    groups = mesh.shape["groups"]
    tiles = mesh.shape["tiles"]
    split = Mesh(mesh.devices.reshape(groups, tiles // 4, 2, 2), ("groups",) + TILES)
    rows = P(("groups",) + TILES, None)
    placed = (rows, rows, rows, rows, rows, P(TILES, None), rows)
    return jax.shard_map(
        on_device,
        mesh=split,
        in_specs=placed,
        out_specs=rows,
        check_vma=False,
    )
```

```python
import functools
import math

import jax
import jax.numpy as jnp
from jax import lax
from jax.experimental import pallas as pl
from jax.experimental.pallas import tpu as pltpu
from jax.sharding import Mesh
from jax.sharding import PartitionSpec as P

HEAD_DIM = 128
TILE_W = 8
CHUNKS = (6, 6)
SCALE = HEAD_DIM**-0.5 * math.log2(math.e)
TILES = ("outer", "pair", "core")
VMEM_LIMIT = 60 * 1024 * 1024
SMEM = pl.BlockSpec(memory_space=pltpu.SMEM)
ANY = pl.BlockSpec(memory_space=pl.ANY)


def after(x, *others):
    return lax.optimization_barrier((x, *others))[0] if others else x


def head_part(q, k, v):
    scores = lax.dot_general(q, k, (((1,), (1,)), ((), ())), preferred_element_type=jnp.float32)
    peak = jnp.max(scores, axis=1, keepdims=True)
    weights = jnp.exp2((scores - peak) * SCALE).astype(jnp.bfloat16)
    ones = jnp.ones((v.shape[0], HEAD_DIM), jnp.bfloat16)
    both = jnp.dot(weights, jnp.concatenate([v, ones], axis=1), preferred_element_type=jnp.float32)
    return both[:, :HEAD_DIM], both[:, HEAD_DIM:], jnp.broadcast_to(peak, v.shape)


def merge(old, new):
    part, total, peak = old
    part_new, total_new, peak_new = new
    top = jnp.maximum(peak, peak_new)
    f_old = jnp.exp2((peak - top) * SCALE)
    f_new = jnp.exp2((peak_new - top) * SCALE)
    return f_old * part + f_new * part_new, f_old * total + f_new * total_new, top


def columns_of(h):
    return pl.ds(h * HEAD_DIM, HEAD_DIM)


def fold(state, active, q, k, v):
    @pl.when(active)
    def _():
        for h in range(q.shape[1] // HEAD_DIM):
            at = columns_of(h)
            new = head_part(q[:, at], k[:, at], v[:, at])
            for r, x in zip(state, merge(tuple(r[:, at] for r in state), new)):
                r[:, at] = x


class Fetch:
    def __init__(self, sems):
        self.sems, self.count = sems, 0

    def later(self, source, target):
        self.count += 1
        return pltpu.make_async_copy(source, target, self.sems.at[self.count - 1])

    def __call__(self, source, target):
        copy = self.later(source, target)
        copy.start()
        return copy


def attend_kernel(which, pattern, q, *refs):
    slots, active = len(which), in_window(pattern, which)
    kv, (part, stats), scratch = refs[: 2 * slots + 2], refs[2 * slots + 2 : 2 * slots + 4], refs[2 * slots + 4 :]
    q_v, kv_v, (part_v, total_v, peak_v, stats_v, sems) = scratch[0], scratch[1 : 2 * slots + 3], scratch[2 * slots + 3 :]
    fetch = Fetch(sems)
    copies = [fetch(source, target) for source, target in zip((q, *kv), (q_v, *kv_v))]
    for copy in copies[:3]:
        copy.wait()
    state = (part_v, total_v, peak_v)
    heads = q_v.shape[1] // HEAD_DIM
    for h in range(heads):
        at = columns_of(h)
        for r, x in zip(state, head_part(q_v[:, at], kv_v[0][:, at], kv_v[1][:, at])):
            r[:, at] = x
    for slot in range(slots):
        for copy in copies[3 + 2 * slot : 5 + 2 * slot]:
            copy.wait()
        fold(state, active[slot], q_v, kv_v[2 * slot + 2], kv_v[2 * slot + 3])
    lane = lax.broadcasted_iota(jnp.int32, stats_v.shape, 1)
    packed = jnp.zeros(stats_v.shape, jnp.float32)
    for h in range(heads):
        packed = jnp.where(lane == h, total_v[:, columns_of(h)], packed)
        packed = jnp.where(lane == HEAD_DIM // 2 + h, peak_v[:, columns_of(h)], packed)
    stats_v[...] = packed
    copies = [fetch(part_v, part), fetch(stats_v, stats)]
    for copy in copies:
        copy.wait()


def attend(which, pattern, q, kv):
    rows, columns = q.shape
    slots = len(kv) // 2 - 1
    return pl.pallas_call(
        functools.partial(attend_kernel, which),
        out_shape=[
            jax.ShapeDtypeStruct((rows, columns), jnp.float32),
            jax.ShapeDtypeStruct((rows, HEAD_DIM), jnp.float32),
        ],
        in_specs=[SMEM] + [ANY] * (1 + len(kv)),
        out_specs=[ANY] * 2,
        scratch_shapes=[pltpu.VMEM((rows, columns), jnp.bfloat16)] * (1 + len(kv))
        + [pltpu.VMEM((rows, columns), jnp.float32)] * 3
        + [pltpu.VMEM((rows, HEAD_DIM), jnp.float32), pltpu.SemaphoreType.DMA((3 + len(kv),))],
        compiler_params=pltpu.CompilerParams(vmem_limit_bytes=VMEM_LIMIT),
        cost_estimate=pl.CostEstimate(
            flops=(1 + slots) * 6 * rows * rows * columns,
            bytes_accessed=rows * columns * (10 + 4 * slots),
            transcendentals=0,
        ),
        name="attend",
    )(pattern, q, *kv)


def close_open(fetch, first, q, part, stats, near, q_v, near_v, state, stats_v):
    columns = state[0].shape[1]
    at = pl.ds(first * HEAD_DIM, columns)
    return [
        fetch(q.at[:, at], q_v),
        fetch(part.at[:, at], state[0]),
        fetch(stats, stats_v),
    ] + [fetch(source, target) for source, target in zip(near, near_v)]


def close_heads(copies, first, active, q_v, near_v, state, stats_v, out):
    columns = state[0].shape[1]
    for copy in copies[:3]:
        copy.wait()
    stats_now = stats_v[...]
    for h in range(columns // HEAD_DIM):
        for r, lane in zip(state[1:], (first + h, HEAD_DIM // 2 + first + h)):
            r[:, columns_of(h)] = jnp.broadcast_to(stats_now[:, lane : lane + 1], stats_now.shape)
    for slot, kv in enumerate(near_v):
        copies[3 + slot].wait()
        fold(state, active[slot], q_v, kv.at[:, pl.ds(0, columns)], kv.at[:, pl.ds(columns, columns)])
    out[...] = (state[0][...] / state[1][...]).astype(jnp.bfloat16)


def close_scratch(rows, columns, slots):
    return (
        [pltpu.VMEM((rows, columns), jnp.bfloat16)]
        + [pltpu.VMEM((rows, 2 * columns), jnp.bfloat16)] * slots
        + [pltpu.VMEM((rows, columns), jnp.float32)] * 3
        + [pltpu.VMEM((rows, HEAD_DIM), jnp.float32), pltpu.SemaphoreType.DMA((4 + slots,))]
    )


def close_kernel(first, which, pattern, q, part, stats, *refs):
    slots, active = len(which), in_window(pattern, which)
    near, out = refs[:slots], refs[slots]
    q_v, near_v, (*state, stats_v, sems, out_v) = refs[slots + 1], refs[slots + 2 : 2 * slots + 2], refs[2 * slots + 2 :]
    fetch = Fetch(sems)
    opened = close_open(fetch, first, q, part, stats, near, q_v, near_v, state, stats_v)
    close_heads(opened, first, active, q_v, near_v, state, stats_v, out_v)
    fetch(out_v, out).wait()


def close(which, pattern, q, state, near, first):
    rows, columns = q.shape[0], near[0].shape[1] // 2
    return pl.pallas_call(
        functools.partial(close_kernel, first, which),
        out_shape=jax.ShapeDtypeStruct((rows, columns), jnp.bfloat16),
        in_specs=[SMEM] + [ANY] * (3 + len(near)),
        out_specs=ANY,
        scratch_shapes=close_scratch(rows, columns, len(near)) + [pltpu.VMEM((rows, columns), jnp.bfloat16)],
        compiler_params=pltpu.CompilerParams(vmem_limit_bytes=VMEM_LIMIT),
        cost_estimate=pl.CostEstimate(
            flops=len(near) * 6 * rows * rows * columns,
            bytes_accessed=rows * columns * (4 * len(near) + 8),
            transcendentals=0,
        ),
        name="close",
    )(pattern, q, *state, *near)


def fetch_weight(fetch, moves, place, weight, held, low, high):
    copies = []
    for piece, index, at in moves:
        if at is None:
            copies.append((True, 0, fetch(weight[piece], held)))
            continue
        source = weight[piece].at[index]
        flip, group, outer, pair, core = at
        known = None if flip else group
        count = source.shape[0]
        outer = place[1] ^ outer
        if flip:
            group, pair, core = place[0] ^ group, place[2] ^ pair, place[3] ^ core
        start = pl.multiple_of(((outer * 2 + pair) * 2 + core) * count, count)
        needed = (start < high) & (start + count > low)
        copy = fetch.later(source, held.at[group, pl.ds(start, count), :])
        pl.when(needed)(copy.start)
        copies.append((needed, 0 if known is None else known, copy))
    return copies


def project(copies, attention, held, low, out, add):
    groups, _, columns = held.shape
    step = 512 if columns % 512 == 0 else columns
    for group in range(groups):
        for needed, at, copy in copies:
            if at == group:
                if needed is True:
                    copy.wait()
                else:
                    pl.when(needed)(copy.wait)
        for j in range(columns // step):
            at = pl.ds(group * columns + j * step, step)
            projected = jnp.dot(
                attention[...],
                held[group, pl.ds(low, attention.shape[1]), pl.ds(j * step, step)],
                preferred_element_type=jnp.float32,
            )
            out(at, add(at) + projected)


def begin_kernel(counts, moves, control_rows, hidden, ready, *refs):
    place = device_place()
    weight, control = refs[: counts[0]], refs[counts[0] : sum(counts)]
    out, attention, held, hidden_v, control_v, out_v, sems = refs[sum(counts) :]
    fetch = Fetch(sems)
    residual = [fetch(ready, attention), fetch(hidden, hidden_v)]
    copies = fetch_weight(fetch, moves, place, weight, held, 0, ready.shape[1])
    for d, block in enumerate(control):
        start = pl.multiple_of((device_column(place) ^ d) * control_rows, control_rows) if len(control) > 1 else 0
        residual.append(fetch(block, control_v.at[pl.ds(start, control_rows), :]))
    for copy in residual:
        copy.wait()
    stores = []

    def store(at, x):
        out_v[:, at] = x
        stores.append(fetch(out_v.at[:, at], out.at[:, at]))

    project(
        copies,
        attention,
        held,
        0,
        store,
        lambda at: hidden_v[:, at].astype(jnp.float32) + control_v[:, at].astype(jnp.float32),
    )
    for copy in stores:
        copy.wait()


def finish_kernel(which, pieces, moves, first, pattern, q, part, stats, so_far, *refs):
    slots, active = len(which), in_window(pattern, which)
    near, weight, out, refs = refs[:slots], refs[slots : slots + pieces], refs[slots + pieces], refs[slots + pieces + 1 :]
    q_v, near_v, (*state, stats_v, sems, attention, held, sum_v, out_v, late_sems) = (
        refs[0],
        refs[1 : slots + 1],
        refs[slots + 1 :],
    )
    fetch, late_fetch = Fetch(sems), Fetch(late_sems)
    low = first * HEAD_DIM
    opened = close_open(fetch, first, q, part, stats, near, q_v, near_v, state, stats_v)
    copies = fetch_weight(late_fetch, moves, device_place(), weight, held, low, low + q_v.shape[1])
    so_far_copy = late_fetch(so_far, sum_v)
    close_heads(opened, first, active, q_v, near_v, state, stats_v, attention)
    so_far_copy.wait()
    stores = []

    def store(at, x):
        out_v[:, at] = x.astype(jnp.bfloat16)
        stores.append(late_fetch(out_v.at[:, at], out.at[:, at]))

    project(copies, attention, held, low, store, lambda at: sum_v[:, at])
    for copy in stores:
        copy.wait()


def project_scratch(rows, columns, groups, inner, width, dtype, copies):
    share = width // groups
    return [
        pltpu.VMEM((rows, columns), jnp.bfloat16),
        pltpu.VMEM((groups, inner, share), jnp.bfloat16),
    ], [
        pltpu.VMEM((rows, width), dtype),
        pltpu.SemaphoreType.DMA((copies + width // (512 if share % 512 == 0 else share),)),
    ]


def begin(ready, weight, control, hidden, moves, inner):
    rows, width = hidden.shape
    columns = ready.shape[1]
    before, behind = project_scratch(
        rows, columns, lax.axis_size("groups"), inner, width, jnp.float32, 2 + len(moves) + len(control)
    )
    return pl.pallas_call(
        functools.partial(begin_kernel, (len(weight), len(control)), moves, control[0].shape[0]),
        out_shape=jax.ShapeDtypeStruct((rows, width), jnp.float32),
        in_specs=[ANY] * (2 + len(weight) + len(control)),
        out_specs=ANY,
        scratch_shapes=before + [pltpu.VMEM((rows, width), jnp.bfloat16)] * 2 + behind,
        compiler_params=pltpu.CompilerParams(vmem_limit_bytes=VMEM_LIMIT),
        cost_estimate=pl.CostEstimate(
            flops=2 * rows * columns * width, bytes_accessed=2 * columns * width + 8 * rows * width, transcendentals=0
        ),
        name="begin",
    )(hidden, ready, *weight, *control)


def finish(which, pattern, q, state, near, first, so_far, weight, moves):
    rows, inner = q.shape
    width = so_far.shape[1]
    columns = near[0].shape[1] // 2
    before, behind = project_scratch(
        rows, columns, lax.axis_size("groups"), inner, width, jnp.bfloat16, 1 + len(moves)
    )
    return pl.pallas_call(
        functools.partial(finish_kernel, which, len(weight), moves, first),
        out_shape=jax.ShapeDtypeStruct((rows, width), jnp.bfloat16),
        in_specs=[SMEM] + [ANY] * (4 + len(near) + len(weight)),
        out_specs=ANY,
        scratch_shapes=close_scratch(rows, columns, len(near))
        + before
        + [pltpu.VMEM((rows, width), jnp.float32)]
        + behind,
        compiler_params=pltpu.CompilerParams(vmem_limit_bytes=VMEM_LIMIT),
        cost_estimate=pl.CostEstimate(
            flops=2 * rows * columns * width, bytes_accessed=2 * columns * width + 6 * rows * width, transcendentals=0
        ),
        name="finish",
    )(pattern, q, *state, so_far, *near, *weight)


def flipped(block, axis, flip):
    return lax.ppermute(block, axis, [(i, i ^ flip) for i in range(lax.axis_size(axis))])


class Lane:
    def __init__(self):
        self.last = ()

    def __call__(self, send, block, *others):
        self.last = (send(after(block, *self.last, *others)),)
        return self.last[0]


def swap(axis, flip):
    return lambda block: flipped(block, axis, flip)


def route_of(route):
    return lambda block: lax.ppermute(block, TILES, route)


def grid_of(tile_count):
    width = min(8, tile_count // 4)
    height = min(4, tile_count // 8)
    return (width * height, width, 1), (tile_count // (width * height), height, width)


def device_place():
    return [lax.axis_index(a) for a in ("groups",) + TILES]


def device_column(place):
    _, outer, pair, core = place
    tile_count = math.prod(lax.axis_size(a) for a in TILES)
    return lax.rem((outer * 2 + pair) * 2 + core, grid_of(tile_count)[1][2])


def in_window(pattern, slots):
    _, outer, pair, core = device_place()
    strides, counts = grid_of(math.prod(lax.axis_size(a) for a in TILES))
    position = (outer * 2 + pair) * 2 + core
    active = []
    for axis, odd in slots:
        place = lax.rem(lax.div(position, strides[axis]), counts[axis])
        down = (place >= 1) & (pattern[0, 2 * axis] == 1)
        up = (place + 1 < counts[axis]) & (pattern[0, 2 * axis + 1] == 1)
        active.append(jnp.where(lax.rem(place, 2) == odd, up.astype(jnp.int32), down.astype(jnp.int32)) == 1)
    return active


def neighbour_slots(tile_count, strides, counts):
    slots = []
    for axis, (stride, count) in enumerate(zip(strides, counts)):
        for odd in range(2):
            route = []
            for t in range(tile_count):
                place = t // stride % count
                if place % 2 == odd and place + 1 < count:
                    route += [(t, t + stride), (t + stride, t)]
            if route:
                slots.append((axis, odd, route))
    return slots


def on_device(hidden, queries, keys, values, control, out_weight, pattern):
    groups = lax.axis_size("groups")
    outer, pair, cores = (lax.axis_size(a) for a in TILES)
    tile_count = outer * pair * cores
    strides, counts = grid_of(tile_count)
    grid_width = counts[2]
    across = device_column(device_place())
    rows = queries.shape[0]
    width = hidden.shape[1]
    slots = neighbour_slots(tile_count, strides, counts)
    early = [s for s in slots if s[0] == 2]
    late = [s for s in slots if s[0] != 2]

    far_lane, near_lane = Lane(), Lane()

    shard, share = out_weight.shape[0], width // groups
    line = out_weight[:, :share]
    for g in range(1, groups):
        line = jnp.where(lax.axis_index("groups") == g, out_weight[:, g * share : (g + 1) * share], line)
    line = lax.optimization_barrier(line)[None]
    line_flips = [0]
    flip = outer // 2
    while flip > 2:
        line = jnp.concatenate([line, flipped(line, "outer", flip)])
        line_flips += [f ^ flip for f in line_flips]
        flip //= 2
    far = far_lane(swap("outer", 2), line)
    near = near_lane(swap("outer", 1), line)

    firsts = [sum(CHUNKS[:i]) for i in range(len(CHUNKS))]
    chunks = [
        jnp.concatenate([x[:, f * HEAD_DIM : (f + n) * HEAD_DIM] for x in (keys, values)], axis=1)
        for f, n in zip(firsts, CHUNKS)
    ]
    block = rows // grid_width
    lines = after(control, line).reshape(block // TILE_W, grid_width, TILE_W, width)
    control_sent = [
        lax.dynamic_index_in_dim(lines, across ^ d, 1, keepdims=False).reshape(block, width) for d in range(grid_width)
    ]
    chunks, control_sent = lax.optimization_barrier((chunks, control_sent))
    control_parts = [control_sent[0]] + [None] * (grid_width - 1)
    beside = swap("pair", 1)(line)
    for d in range(2, grid_width - 1):
        control_parts[d] = swap(TILES, d)(after(control_sent[d], line))
    plane = jnp.concatenate([line, beside])
    last = swap("outer", 1)(after(far, near, *control_parts[2:-1], *chunks))
    near_x = swap("pair", 1)(after(near, beside))
    held = []
    for both in (plane, jnp.concatenate([near, near_x])):
        held += [both, swap("groups", 1)(both)]
    early_near = [[None, None] for _ in early]
    for i, x in enumerate((keys, values)):
        early_near[0][i] = lax.ppermute(x, TILES, early[0][2])
        for slot in range(1, len(early)):
            early_near[slot][i] = lax.ppermute(after(x, early_near[0][i], held[1]), TILES, early[slot][2])
    state = attend(tuple(s[:2] for s in early), pattern, queries, [keys, values] + [x for kv in early_near for x in kv])

    late_near = []
    for chunk in chunks:
        lanes = (far_lane, near_lane)
        late_near.append([lanes[i % 2](route_of(route), chunk) for i, (_, _, route) in enumerate(late)])
    crossed = [swap("core", 1)(x) for x in held]
    for d in (1, grid_width - 1):
        control_parts[d] = swap(TILES, d)(after(control_sent[d], *[x for kv in early_near[1:] for x in kv]))

    gates = [*control_parts[2:-1], near_x]
    weight = [lax.all_gather(after(jnp.concatenate([far, last]), *gates), ("groups", "pair", "core"))]
    n = len(line_flips)
    moves = [
        (0, ((g * pair + p) * cores + c, i * n + j), (False, g, f ^ at, p, c))
        for g in range(groups)
        for p in range(pair)
        for c in range(cores)
        for i, at in enumerate((2, 3))
        for j, f in enumerate(line_flips)
    ]
    for number, (group_flip, at) in enumerate(((0, 0), (1, 0), (0, 1), (1, 1))):
        for core_flip, pieces in enumerate((held, crossed)):
            moves += [
                (len(weight), (p * n + j,), (True, group_flip, f ^ at, p, core_flip))
                for p in range(pair)
                for j, f in enumerate(line_flips)
            ]
            weight.append(pieces[number])

    which = tuple(s[:2] for s in late)
    ready = [close(which, pattern, queries, state, late_near[i], firsts[i]) for i in range(len(CHUNKS) - 1)]
    ready = ready[0] if len(ready) == 1 else jnp.concatenate(ready, axis=1)
    if block % 16:
        control_parts = [
            jnp.take(
                jnp.stack(control_parts), jnp.arange(grid_width, dtype=jnp.int32) ^ across, axis=0
            ).reshape(rows, width)
        ]
    if shard % 16:
        weight, moves = [in_order(weight, moves, device_place(), (groups, outer, pair, cores))], [(0, None, None)]
    moves = tuple(moves)
    so_far = begin(ready, weight, control_parts, hidden, moves, queries.shape[1])
    return finish(which, pattern, queries, state, late_near[-1], firsts[-1], so_far, weight, moves)


def in_order(weight, moves, place, sizes):
    groups, outer, pair, cores = sizes
    shard, columns = weight[0].shape[-2:]
    gathered = weight[0].reshape(groups, pair, cores, -1, shard, columns)
    for axis, at in enumerate((0, 2, 3)):
        gathered = jnp.take(gathered, jnp.arange(sizes[at], dtype=jnp.int32) ^ place[at], axis=axis)
    weight = [gathered.reshape(weight[0].shape)] + weight[1:]
    blocks = {at[1:]: weight[piece][index] for piece, index, at in moves}
    whole = jnp.stack([blocks[at] for at in sorted(blocks)]).reshape(sizes + (shard, columns))
    for axis, size in enumerate(sizes):
        whole = jnp.take(whole, jnp.arange(size, dtype=jnp.int32) ^ place[axis], axis=axis)
    return whole.reshape(groups, -1, columns)


def solution(mesh):
    groups = mesh.shape["groups"]
    tiles = mesh.shape["tiles"]
    split = Mesh(mesh.devices.reshape(groups, tiles // 4, 2, 2), ("groups",) + TILES)
    rows = P(("groups",) + TILES, None)
    placed = (rows, rows, rows, rows, rows, P(TILES, None), rows)
    return jax.shard_map(
        on_device,
        mesh=split,
        in_specs=placed,
        out_specs=rows,
        check_vma=False,
    )
```

```python
import functools
import math

import jax
import jax.numpy as jnp
from jax import lax
from jax.experimental import pallas as pl
from jax.experimental.pallas import tpu as pltpu
from jax.sharding import Mesh
from jax.sharding import PartitionSpec as P

HEAD_DIM = 128
TILE_W = 8
CHUNKS = (6, 6)
SCALE = HEAD_DIM**-0.5 * math.log2(math.e)
TILES = ("outer", "pair", "core")
VMEM_LIMIT = 60 * 1024 * 1024
SMEM = pl.BlockSpec(memory_space=pltpu.SMEM)
ANY = pl.BlockSpec(memory_space=pl.ANY)


def after(x, *others):
    return lax.optimization_barrier((x, *others))[0] if others else x


def head_part(q, k, v):
    scores = lax.dot_general(q, k, (((1,), (1,)), ((), ())), preferred_element_type=jnp.float32)
    peak = jnp.max(scores, axis=1, keepdims=True)
    weights = jnp.exp2((scores - peak) * SCALE).astype(jnp.bfloat16)
    ones = jnp.ones((v.shape[0], HEAD_DIM), jnp.bfloat16)
    both = jnp.dot(weights, jnp.concatenate([v, ones], axis=1), preferred_element_type=jnp.float32)
    return both[:, :HEAD_DIM], both[:, HEAD_DIM:], jnp.broadcast_to(peak, v.shape)


def merge(old, new):
    part, total, peak = old
    part_new, total_new, peak_new = new
    top = jnp.maximum(peak, peak_new)
    f_old = jnp.exp2((peak - top) * SCALE)
    f_new = jnp.exp2((peak_new - top) * SCALE)
    return f_old * part + f_new * part_new, f_old * total + f_new * total_new, top


def columns_of(h):
    return pl.ds(h * HEAD_DIM, HEAD_DIM)


def fold(state, active, q, k, v):
    @pl.when(active)
    def _():
        for h in range(q.shape[1] // HEAD_DIM):
            at = columns_of(h)
            new = head_part(q[:, at], k[:, at], v[:, at])
            for r, x in zip(state, merge(tuple(r[:, at] for r in state), new)):
                r[:, at] = x


class Fetch:
    def __init__(self, sems):
        self.sems, self.count = sems, 0

    def later(self, source, target):
        self.count += 1
        return pltpu.make_async_copy(source, target, self.sems.at[self.count - 1])

    def __call__(self, source, target):
        copy = self.later(source, target)
        copy.start()
        return copy


def attend_kernel(which, pattern, q, *refs):
    slots, active = len(which), in_window(pattern, which)
    kv, (part, stats), scratch = refs[: 2 * slots + 2], refs[2 * slots + 2 : 2 * slots + 4], refs[2 * slots + 4 :]
    q_v, kv_v, (part_v, total_v, peak_v, stats_v, sems) = scratch[0], scratch[1 : 2 * slots + 3], scratch[2 * slots + 3 :]
    fetch = Fetch(sems)
    copies = [fetch(source, target) for source, target in zip((q, *kv), (q_v, *kv_v))]
    for copy in copies[:3]:
        copy.wait()
    state = (part_v, total_v, peak_v)
    heads = q_v.shape[1] // HEAD_DIM
    for h in range(heads):
        at = columns_of(h)
        for r, x in zip(state, head_part(q_v[:, at], kv_v[0][:, at], kv_v[1][:, at])):
            r[:, at] = x
    for slot in range(slots):
        for copy in copies[3 + 2 * slot : 5 + 2 * slot]:
            copy.wait()
        fold(state, active[slot], q_v, kv_v[2 * slot + 2], kv_v[2 * slot + 3])
    lane = lax.broadcasted_iota(jnp.int32, stats_v.shape, 1)
    packed = jnp.zeros(stats_v.shape, jnp.float32)
    for h in range(heads):
        packed = jnp.where(lane == h, total_v[:, columns_of(h)], packed)
        packed = jnp.where(lane == HEAD_DIM // 2 + h, peak_v[:, columns_of(h)], packed)
    stats_v[...] = packed
    copies = [fetch(part_v, part), fetch(stats_v, stats)]
    for copy in copies:
        copy.wait()


def attend(which, pattern, q, kv):
    rows, columns = q.shape
    slots = len(kv) // 2 - 1
    return pl.pallas_call(
        functools.partial(attend_kernel, which),
        out_shape=[
            jax.ShapeDtypeStruct((rows, columns), jnp.float32),
            jax.ShapeDtypeStruct((rows, HEAD_DIM), jnp.float32),
        ],
        in_specs=[SMEM] + [ANY] * (1 + len(kv)),
        out_specs=[ANY] * 2,
        scratch_shapes=[pltpu.VMEM((rows, columns), jnp.bfloat16)] * (1 + len(kv))
        + [pltpu.VMEM((rows, columns), jnp.float32)] * 3
        + [pltpu.VMEM((rows, HEAD_DIM), jnp.float32), pltpu.SemaphoreType.DMA((3 + len(kv),))],
        compiler_params=pltpu.CompilerParams(vmem_limit_bytes=VMEM_LIMIT),
        cost_estimate=pl.CostEstimate(
            flops=(1 + slots) * 6 * rows * rows * columns,
            bytes_accessed=rows * columns * (10 + 4 * slots),
            transcendentals=0,
        ),
        name="attend",
    )(pattern, q, *kv)


def close_open(fetch, first, q, part, stats, near, q_v, near_v, state, stats_v):
    columns = state[0].shape[1]
    at = pl.ds(first * HEAD_DIM, columns)
    return [
        fetch(q.at[:, at], q_v),
        fetch(part.at[:, at], state[0]),
        fetch(stats, stats_v),
    ] + [fetch(source, target) for source, target in zip(near, near_v)]


def close_heads(copies, first, active, q_v, near_v, state, stats_v, out):
    part_v = state[0]
    columns = part_v.shape[1]
    for copy in copies:
        copy.wait()
    stats_now = stats_v[...]
    for h in range(columns // HEAD_DIM):
        at = columns_of(h)
        total, peak = (
            jnp.broadcast_to(stats_now[:, lane : lane + 1], stats_now.shape)
            for lane in (first + h, HEAD_DIM // 2 + first + h)
        )
        terms = [(part_v[:, at], total, peak)]
        for slot, kv in enumerate(near_v):
            part, total, peak = head_part(q_v[:, at], kv[:, at], kv[:, pl.ds(columns + h * HEAD_DIM, HEAD_DIM)])
            terms.append((part, total, jnp.where(active[slot], peak, -1e30)))
        top = functools.reduce(jnp.maximum, [peak for _, _, peak in terms])
        factors = [jnp.exp2((peak - top) * SCALE) for _, _, peak in terms]
        numerator = sum(f * part for f, (part, _, _) in zip(factors, terms))
        denominator = sum(f * total for f, (_, total, _) in zip(factors, terms))
        out[:, at] = (numerator / denominator).astype(jnp.bfloat16)


def close_scratch(rows, columns, slots):
    return (
        [pltpu.VMEM((rows, columns), jnp.bfloat16)]
        + [pltpu.VMEM((rows, 2 * columns), jnp.bfloat16)] * slots
        + [pltpu.VMEM((rows, columns), jnp.float32)]
        + [pltpu.VMEM((rows, HEAD_DIM), jnp.float32), pltpu.SemaphoreType.DMA((4 + slots,))]
    )


def close_kernel(first, which, pattern, q, part, stats, *refs):
    slots, active = len(which), in_window(pattern, which)
    near, out = refs[:slots], refs[slots]
    q_v, near_v, (*state, stats_v, sems, out_v) = refs[slots + 1], refs[slots + 2 : 2 * slots + 2], refs[2 * slots + 2 :]
    fetch = Fetch(sems)
    opened = close_open(fetch, first, q, part, stats, near, q_v, near_v, state, stats_v)
    close_heads(opened, first, active, q_v, near_v, state, stats_v, out_v)
    fetch(out_v, out).wait()


def close(which, pattern, q, state, near, first):
    rows, columns = q.shape[0], near[0].shape[1] // 2
    return pl.pallas_call(
        functools.partial(close_kernel, first, which),
        out_shape=jax.ShapeDtypeStruct((rows, columns), jnp.bfloat16),
        in_specs=[SMEM] + [ANY] * (3 + len(near)),
        out_specs=ANY,
        scratch_shapes=close_scratch(rows, columns, len(near)) + [pltpu.VMEM((rows, columns), jnp.bfloat16)],
        compiler_params=pltpu.CompilerParams(vmem_limit_bytes=VMEM_LIMIT),
        cost_estimate=pl.CostEstimate(
            flops=len(near) * 6 * rows * rows * columns,
            bytes_accessed=rows * columns * (4 * len(near) + 8),
            transcendentals=0,
        ),
        name="close",
    )(pattern, q, *state, *near)


def fetch_weight(fetch, moves, place, weight, held, low, high):
    copies = []
    for piece, index, at in moves:
        if at is None:
            copies.append((True, 0, fetch(weight[piece], held)))
            continue
        source = weight[piece].at[index]
        flip, group, outer, pair, core = at
        known = None if flip else group
        count = source.shape[0]
        outer = place[1] ^ outer
        if flip:
            group, pair, core = place[0] ^ group, place[2] ^ pair, place[3] ^ core
        start = pl.multiple_of(((outer * 2 + pair) * 2 + core) * count, count)
        needed = (start < high) & (start + count > low)
        copy = fetch.later(source, held.at[group, pl.ds(start, count), :])
        pl.when(needed)(copy.start)
        copies.append((needed, 0 if known is None else known, copy))
    return copies


def project(copies, attention, held, low, out, add):
    groups, _, columns = held.shape
    step = 512 if columns % 512 == 0 else columns
    for group in range(groups):
        for needed, at, copy in copies:
            if at == group:
                if needed is True:
                    copy.wait()
                else:
                    pl.when(needed)(copy.wait)
        for j in range(columns // step):
            at = pl.ds(group * columns + j * step, step)
            projected = jnp.dot(
                attention[...],
                held[group, pl.ds(low, attention.shape[1]), pl.ds(j * step, step)],
                preferred_element_type=jnp.float32,
            )
            out(at, add(at) + projected)


def begin_kernel(counts, moves, control_rows, hidden, ready, *refs):
    place = device_place()
    weight, control = refs[: counts[0]], refs[counts[0] : sum(counts)]
    out, attention, held, hidden_v, control_v, out_v, sems = refs[sum(counts) :]
    fetch = Fetch(sems)
    residual = [fetch(ready, attention), fetch(hidden, hidden_v)]
    copies = fetch_weight(fetch, moves, place, weight, held, 0, ready.shape[1])
    for d, block in enumerate(control):
        start = pl.multiple_of((device_column(place) ^ d) * control_rows, control_rows) if len(control) > 1 else 0
        residual.append(fetch(block, control_v.at[pl.ds(start, control_rows), :]))
    for copy in residual:
        copy.wait()
    stores = []

    def store(at, x):
        out_v[:, at] = x
        stores.append(fetch(out_v.at[:, at], out.at[:, at]))

    project(
        copies,
        attention,
        held,
        0,
        store,
        lambda at: hidden_v[:, at].astype(jnp.float32) + control_v[:, at].astype(jnp.float32),
    )
    for copy in stores:
        copy.wait()


def finish_kernel(which, pieces, moves, first, pattern, q, part, stats, so_far, *refs):
    slots, active = len(which), in_window(pattern, which)
    near, weight, out, refs = refs[:slots], refs[slots : slots + pieces], refs[slots + pieces], refs[slots + pieces + 1 :]
    q_v, near_v, (*state, stats_v, sems, attention, held, sum_v, out_v, late_sems) = (
        refs[0],
        refs[1 : slots + 1],
        refs[slots + 1 :],
    )
    fetch, late_fetch = Fetch(sems), Fetch(late_sems)
    low = first * HEAD_DIM
    opened = close_open(fetch, first, q, part, stats, near, q_v, near_v, state, stats_v)
    copies = fetch_weight(late_fetch, moves, device_place(), weight, held, low, low + q_v.shape[1])
    so_far_copy = late_fetch(so_far, sum_v)
    close_heads(opened, first, active, q_v, near_v, state, stats_v, attention)
    so_far_copy.wait()
    stores = []

    def store(at, x):
        out_v[:, at] = x.astype(jnp.bfloat16)
        stores.append(late_fetch(out_v.at[:, at], out.at[:, at]))

    project(copies, attention, held, low, store, lambda at: sum_v[:, at])
    for copy in stores:
        copy.wait()


def project_scratch(rows, columns, groups, inner, width, dtype, copies):
    share = width // groups
    return [
        pltpu.VMEM((rows, columns), jnp.bfloat16),
        pltpu.VMEM((groups, inner, share), jnp.bfloat16),
    ], [
        pltpu.VMEM((rows, width), dtype),
        pltpu.SemaphoreType.DMA((copies + width // (512 if share % 512 == 0 else share),)),
    ]


def begin(ready, weight, control, hidden, moves, inner):
    rows, width = hidden.shape
    columns = ready.shape[1]
    before, behind = project_scratch(
        rows, columns, lax.axis_size("groups"), inner, width, jnp.float32, 2 + len(moves) + len(control)
    )
    return pl.pallas_call(
        functools.partial(begin_kernel, (len(weight), len(control)), moves, control[0].shape[0]),
        out_shape=jax.ShapeDtypeStruct((rows, width), jnp.float32),
        in_specs=[ANY] * (2 + len(weight) + len(control)),
        out_specs=ANY,
        scratch_shapes=before + [pltpu.VMEM((rows, width), jnp.bfloat16)] * 2 + behind,
        compiler_params=pltpu.CompilerParams(vmem_limit_bytes=VMEM_LIMIT),
        cost_estimate=pl.CostEstimate(
            flops=2 * rows * columns * width, bytes_accessed=2 * columns * width + 8 * rows * width, transcendentals=0
        ),
        name="begin",
    )(hidden, ready, *weight, *control)


def finish(which, pattern, q, state, near, first, so_far, weight, moves):
    rows, inner = q.shape
    width = so_far.shape[1]
    columns = near[0].shape[1] // 2
    before, behind = project_scratch(
        rows, columns, lax.axis_size("groups"), inner, width, jnp.bfloat16, 1 + len(moves)
    )
    return pl.pallas_call(
        functools.partial(finish_kernel, which, len(weight), moves, first),
        out_shape=jax.ShapeDtypeStruct((rows, width), jnp.bfloat16),
        in_specs=[SMEM] + [ANY] * (4 + len(near) + len(weight)),
        out_specs=ANY,
        scratch_shapes=close_scratch(rows, columns, len(near))
        + before
        + [pltpu.VMEM((rows, width), jnp.float32)]
        + behind,
        compiler_params=pltpu.CompilerParams(vmem_limit_bytes=VMEM_LIMIT),
        cost_estimate=pl.CostEstimate(
            flops=2 * rows * columns * width, bytes_accessed=2 * columns * width + 6 * rows * width, transcendentals=0
        ),
        name="finish",
    )(pattern, q, *state, so_far, *near, *weight)


def flipped(block, axis, flip):
    return lax.ppermute(block, axis, [(i, i ^ flip) for i in range(lax.axis_size(axis))])


class Lane:
    def __init__(self):
        self.last = ()

    def __call__(self, send, block, *others):
        self.last = (send(after(block, *self.last, *others)),)
        return self.last[0]


def swap(axis, flip):
    return lambda block: flipped(block, axis, flip)


def route_of(route):
    return lambda block: lax.ppermute(block, TILES, route)


def grid_of(tile_count):
    width = min(8, tile_count // 4)
    height = min(4, tile_count // 8)
    return (width * height, width, 1), (tile_count // (width * height), height, width)


def device_place():
    return [lax.axis_index(a) for a in ("groups",) + TILES]


def device_column(place):
    _, outer, pair, core = place
    tile_count = math.prod(lax.axis_size(a) for a in TILES)
    return lax.rem((outer * 2 + pair) * 2 + core, grid_of(tile_count)[1][2])


def in_window(pattern, slots):
    _, outer, pair, core = device_place()
    strides, counts = grid_of(math.prod(lax.axis_size(a) for a in TILES))
    position = (outer * 2 + pair) * 2 + core
    active = []
    for axis, odd in slots:
        place = lax.rem(lax.div(position, strides[axis]), counts[axis])
        down = (place >= 1) & (pattern[0, 2 * axis] == 1)
        up = (place + 1 < counts[axis]) & (pattern[0, 2 * axis + 1] == 1)
        active.append(jnp.where(lax.rem(place, 2) == odd, up.astype(jnp.int32), down.astype(jnp.int32)) == 1)
    return active


def neighbour_slots(tile_count, strides, counts):
    slots = []
    for axis, (stride, count) in enumerate(zip(strides, counts)):
        for odd in range(2):
            route = []
            for t in range(tile_count):
                place = t // stride % count
                if place % 2 == odd and place + 1 < count:
                    route += [(t, t + stride), (t + stride, t)]
            if route:
                slots.append((axis, odd, route))
    return slots


def on_device(hidden, queries, keys, values, control, out_weight, pattern):
    groups = lax.axis_size("groups")
    outer, pair, cores = (lax.axis_size(a) for a in TILES)
    tile_count = outer * pair * cores
    strides, counts = grid_of(tile_count)
    grid_width = counts[2]
    across = device_column(device_place())
    rows = queries.shape[0]
    width = hidden.shape[1]
    slots = neighbour_slots(tile_count, strides, counts)
    early = [s for s in slots if s[0] == 2]
    late = [s for s in slots if s[0] != 2]

    far_lane, near_lane = Lane(), Lane()

    shard, share = out_weight.shape[0], width // groups
    line = out_weight[:, :share]
    for g in range(1, groups):
        line = jnp.where(lax.axis_index("groups") == g, out_weight[:, g * share : (g + 1) * share], line)
    line = lax.optimization_barrier(line)[None]
    line_flips = [0]
    flip = outer // 2
    while flip > 2:
        line = jnp.concatenate([line, flipped(line, "outer", flip)])
        line_flips += [f ^ flip for f in line_flips]
        flip //= 2
    far = far_lane(swap("outer", 2), line)
    near = near_lane(swap("outer", 1), line)

    firsts = [sum(CHUNKS[:i]) for i in range(len(CHUNKS))]
    chunks = [
        jnp.concatenate([x[:, f * HEAD_DIM : (f + n) * HEAD_DIM] for x in (keys, values)], axis=1)
        for f, n in zip(firsts, CHUNKS)
    ]
    block = rows // grid_width
    lines = after(control, line).reshape(block // TILE_W, grid_width, TILE_W, width)
    control_sent = [
        lax.dynamic_index_in_dim(lines, across ^ d, 1, keepdims=False).reshape(block, width) for d in range(grid_width)
    ]
    chunks, control_sent = lax.optimization_barrier((chunks, control_sent))
    control_parts = [control_sent[0]] + [None] * (grid_width - 1)
    beside = swap("pair", 1)(line)
    for d in range(2, grid_width - 1):
        control_parts[d] = swap(TILES, d)(after(control_sent[d], line))
    plane = jnp.concatenate([line, beside])
    last = swap("outer", 1)(after(far, near, *control_parts[2:-1], *chunks))
    near_x = swap("pair", 1)(near)
    held = []
    for both in (plane, jnp.concatenate([near, near_x])):
        held += [both, swap("groups", 1)(both)]
    early_near = [[None, None] for _ in early]
    for i, x in enumerate((keys, values)):
        early_near[0][i] = lax.ppermute(x, TILES, early[0][2])
        for slot in range(1, len(early)):
            early_near[slot][i] = lax.ppermute(after(x, early_near[0][i]), TILES, early[slot][2])
    state = attend(tuple(s[:2] for s in early), pattern, queries, [keys, values] + [x for kv in early_near for x in kv])

    late_near = []
    for chunk in chunks:
        lanes = (far_lane, near_lane)
        late_near.append([lanes[i % 2](route_of(route), chunk) for i, (_, _, route) in enumerate(late)])
    crossed = [swap("core", 1)(x) for x in held]
    for d in (1, grid_width - 1):
        control_parts[d] = swap(TILES, d)(after(control_sent[d], *[x for kv in early_near[1:] for x in kv]))

    gates = [*control_parts[2:-1], near_x, held[1]]
    weight = [lax.all_gather(after(jnp.concatenate([far, last]), *gates), ("groups", "pair", "core"))]
    n = len(line_flips)
    moves = [
        (0, ((g * pair + p) * cores + c, i * n + j), (False, g, f ^ at, p, c))
        for g in range(groups)
        for p in range(pair)
        for c in range(cores)
        for i, at in enumerate((2, 3))
        for j, f in enumerate(line_flips)
    ]
    for number, (group_flip, at) in enumerate(((0, 0), (1, 0), (0, 1), (1, 1))):
        for core_flip, pieces in enumerate((held, crossed)):
            moves += [
                (len(weight), (p * n + j,), (True, group_flip, f ^ at, p, core_flip))
                for p in range(pair)
                for j, f in enumerate(line_flips)
            ]
            weight.append(pieces[number])

    which = tuple(s[:2] for s in late)
    ready = [close(which, pattern, queries, state, late_near[i], firsts[i]) for i in range(len(CHUNKS) - 1)]
    ready = ready[0] if len(ready) == 1 else jnp.concatenate(ready, axis=1)
    if block % 16:
        control_parts = [
            jnp.take(
                jnp.stack(control_parts), jnp.arange(grid_width, dtype=jnp.int32) ^ across, axis=0
            ).reshape(rows, width)
        ]
    if shard % 16:
        weight, moves = [in_order(weight, moves, device_place(), (groups, outer, pair, cores))], [(0, None, None)]
    moves = tuple(moves)
    so_far = begin(ready, weight, control_parts, hidden, moves, queries.shape[1])
    return finish(which, pattern, queries, state, late_near[-1], firsts[-1], so_far, weight, moves)


def in_order(weight, moves, place, sizes):
    groups, outer, pair, cores = sizes
    shard, columns = weight[0].shape[-2:]
    gathered = weight[0].reshape(groups, pair, cores, -1, shard, columns)
    for axis, at in enumerate((0, 2, 3)):
        gathered = jnp.take(gathered, jnp.arange(sizes[at], dtype=jnp.int32) ^ place[at], axis=axis)
    weight = [gathered.reshape(weight[0].shape)] + weight[1:]
    blocks = {at[1:]: weight[piece][index] for piece, index, at in moves}
    whole = jnp.stack([blocks[at] for at in sorted(blocks)]).reshape(sizes + (shard, columns))
    for axis, size in enumerate(sizes):
        whole = jnp.take(whole, jnp.arange(size, dtype=jnp.int32) ^ place[axis], axis=axis)
    return whole.reshape(groups, -1, columns)


def solution(mesh):
    groups = mesh.shape["groups"]
    tiles = mesh.shape["tiles"]
    split = Mesh(mesh.devices.reshape(groups, tiles // 4, 2, 2), ("groups",) + TILES)
    rows = P(("groups",) + TILES, None)
    placed = (rows, rows, rows, rows, rows, P(TILES, None), rows)
    return jax.shard_map(
        on_device,
        mesh=split,
        in_specs=placed,
        out_specs=rows,
        check_vma=False,
    )
```

```python
import functools
import math

import jax
import jax.numpy as jnp
from jax import lax
from jax.experimental import pallas as pl
from jax.experimental.pallas import tpu as pltpu
from jax.sharding import Mesh
from jax.sharding import PartitionSpec as P

HEAD_DIM = 128
TILE_W = 8
CHUNKS = (6, 6)
SCALE = HEAD_DIM**-0.5 * math.log2(math.e)
TILES = ("outer", "pair", "core")
VMEM_LIMIT = 60 * 1024 * 1024
SMEM = pl.BlockSpec(memory_space=pltpu.SMEM)
ANY = pl.BlockSpec(memory_space=pl.ANY)


def after(x, *others):
    return lax.optimization_barrier((x, *others))[0] if others else x


def head_part(q, k, v):
    scores = lax.dot_general(q, k, (((1,), (1,)), ((), ())), preferred_element_type=jnp.float32)
    peak = jnp.max(scores, axis=1, keepdims=True)
    weights = jnp.exp2((scores - peak) * SCALE).astype(jnp.bfloat16)
    ones = jnp.ones((v.shape[0], HEAD_DIM), jnp.bfloat16)
    both = jnp.dot(weights, jnp.concatenate([v, ones], axis=1), preferred_element_type=jnp.float32)
    return both[:, :HEAD_DIM], both[:, HEAD_DIM:], jnp.broadcast_to(peak, v.shape)


def merge(old, new):
    part, total, peak = old
    part_new, total_new, peak_new = new
    top = jnp.maximum(peak, peak_new)
    f_old = jnp.exp2((peak - top) * SCALE)
    f_new = jnp.exp2((peak_new - top) * SCALE)
    return f_old * part + f_new * part_new, f_old * total + f_new * total_new, top


def columns_of(h):
    return pl.ds(h * HEAD_DIM, HEAD_DIM)


def fold(state, active, q, k, v):
    @pl.when(active)
    def _():
        for h in range(q.shape[1] // HEAD_DIM):
            at = columns_of(h)
            new = head_part(q[:, at], k[:, at], v[:, at])
            for r, x in zip(state, merge(tuple(r[:, at] for r in state), new)):
                r[:, at] = x


class Fetch:
    def __init__(self, sems):
        self.sems, self.count = sems, 0

    def later(self, source, target):
        self.count += 1
        return pltpu.make_async_copy(source, target, self.sems.at[self.count - 1])

    def __call__(self, source, target):
        copy = self.later(source, target)
        copy.start()
        return copy


def attend_kernel(which, pattern, q, *refs):
    slots, active = len(which), in_window(pattern, which)
    kv, (part, stats), scratch = refs[: 2 * slots + 2], refs[2 * slots + 2 : 2 * slots + 4], refs[2 * slots + 4 :]
    q_v, kv_v, (part_v, total_v, peak_v, stats_v, sems) = scratch[0], scratch[1 : 2 * slots + 3], scratch[2 * slots + 3 :]
    fetch = Fetch(sems)
    copies = [fetch(source, target) for source, target in zip((q, *kv), (q_v, *kv_v))]
    for copy in copies[:3]:
        copy.wait()
    state = (part_v, total_v, peak_v)
    heads = q_v.shape[1] // HEAD_DIM
    for h in range(heads):
        at = columns_of(h)
        for r, x in zip(state, head_part(q_v[:, at], kv_v[0][:, at], kv_v[1][:, at])):
            r[:, at] = x
    for slot in range(slots):
        for copy in copies[3 + 2 * slot : 5 + 2 * slot]:
            copy.wait()
        fold(state, active[slot], q_v, kv_v[2 * slot + 2], kv_v[2 * slot + 3])
    lane = lax.broadcasted_iota(jnp.int32, stats_v.shape, 1)
    packed = jnp.zeros(stats_v.shape, jnp.float32)
    for h in range(heads):
        packed = jnp.where(lane == h, total_v[:, columns_of(h)], packed)
        packed = jnp.where(lane == HEAD_DIM // 2 + h, peak_v[:, columns_of(h)], packed)
    stats_v[...] = packed
    copies = [fetch(part_v, part), fetch(stats_v, stats)]
    for copy in copies:
        copy.wait()


def attend(which, pattern, q, kv):
    rows, columns = q.shape
    slots = len(kv) // 2 - 1
    return pl.pallas_call(
        functools.partial(attend_kernel, which),
        out_shape=[
            jax.ShapeDtypeStruct((rows, columns), jnp.float32),
            jax.ShapeDtypeStruct((rows, HEAD_DIM), jnp.float32),
        ],
        in_specs=[SMEM] + [ANY] * (1 + len(kv)),
        out_specs=[ANY] * 2,
        scratch_shapes=[pltpu.VMEM((rows, columns), jnp.bfloat16)] * (1 + len(kv))
        + [pltpu.VMEM((rows, columns), jnp.float32)] * 3
        + [pltpu.VMEM((rows, HEAD_DIM), jnp.float32), pltpu.SemaphoreType.DMA((3 + len(kv),))],
        compiler_params=pltpu.CompilerParams(vmem_limit_bytes=VMEM_LIMIT),
        cost_estimate=pl.CostEstimate(
            flops=(1 + slots) * 6 * rows * rows * columns,
            bytes_accessed=rows * columns * (10 + 4 * slots),
            transcendentals=0,
        ),
        name="attend",
    )(pattern, q, *kv)


def close_open(fetch, first, q, part, stats, near, q_v, near_v, state, stats_v):
    columns = state[0].shape[1]
    at = pl.ds(first * HEAD_DIM, columns)
    return [
        fetch(q.at[:, at], q_v),
        fetch(part.at[:, at], state[0]),
        fetch(stats, stats_v),
    ] + [fetch(source, target) for source, target in zip(near, near_v)]


def close_heads(copies, first, active, q_v, near_v, state, stats_v, out):
    part_v = state[0]
    columns = part_v.shape[1]
    for copy in copies:
        copy.wait()
    stats_now = stats_v[...]
    for h in range(columns // HEAD_DIM):
        at = columns_of(h)
        total, peak = (
            jnp.broadcast_to(stats_now[:, lane : lane + 1], stats_now.shape)
            for lane in (first + h, HEAD_DIM // 2 + first + h)
        )
        terms = [(part_v[:, at], total, peak)]
        for slot, kv in enumerate(near_v):
            part, total, peak = head_part(q_v[:, at], kv[:, at], kv[:, pl.ds(columns + h * HEAD_DIM, HEAD_DIM)])
            terms.append((part, total, jnp.where(active[slot], peak, -1e30)))
        top = functools.reduce(jnp.maximum, [peak for _, _, peak in terms])
        factors = [jnp.exp2((peak - top) * SCALE) for _, _, peak in terms]
        numerator = sum(f * part for f, (part, _, _) in zip(factors, terms))
        denominator = sum(f * total for f, (_, total, _) in zip(factors, terms))
        out[:, at] = (numerator / denominator).astype(jnp.bfloat16)


def close_scratch(rows, columns, slots):
    return (
        [pltpu.VMEM((rows, columns), jnp.bfloat16)]
        + [pltpu.VMEM((rows, 2 * columns), jnp.bfloat16)] * slots
        + [pltpu.VMEM((rows, columns), jnp.float32)]
        + [pltpu.VMEM((rows, HEAD_DIM), jnp.float32), pltpu.SemaphoreType.DMA((4 + slots,))]
    )


def close_kernel(first, which, pattern, q, part, stats, *refs):
    slots, active = len(which), in_window(pattern, which)
    near, out = refs[:slots], refs[slots]
    q_v, near_v, (*state, stats_v, sems, out_v) = refs[slots + 1], refs[slots + 2 : 2 * slots + 2], refs[2 * slots + 2 :]
    fetch = Fetch(sems)
    opened = close_open(fetch, first, q, part, stats, near, q_v, near_v, state, stats_v)
    close_heads(opened, first, active, q_v, near_v, state, stats_v, out_v)
    fetch(out_v, out).wait()


def close(which, pattern, q, state, near, first):
    rows, columns = q.shape[0], near[0].shape[1] // 2
    return pl.pallas_call(
        functools.partial(close_kernel, first, which),
        out_shape=jax.ShapeDtypeStruct((rows, columns), jnp.bfloat16),
        in_specs=[SMEM] + [ANY] * (3 + len(near)),
        out_specs=ANY,
        scratch_shapes=close_scratch(rows, columns, len(near)) + [pltpu.VMEM((rows, columns), jnp.bfloat16)],
        compiler_params=pltpu.CompilerParams(vmem_limit_bytes=VMEM_LIMIT),
        cost_estimate=pl.CostEstimate(
            flops=len(near) * 6 * rows * rows * columns,
            bytes_accessed=rows * columns * (4 * len(near) + 8),
            transcendentals=0,
        ),
        name="close",
    )(pattern, q, *state, *near)


def fetch_weight(fetch, moves, place, weight, held, low, high):
    if moves[0][2] is None:
        return [(True, 0, [fetch(weight[piece], held)]) for piece, _, _ in moves]
    starts = []
    for outer_flip in sorted({at[2] for _, _, at in moves}):
        blocks = [move for move in moves if move[2][2] == outer_flip]
        count = weight[0].shape[-2]
        span = len(blocks) // held.shape[0] * count
        outer = place[1] ^ outer_flip
        needed = (outer * span < high) & ((outer + 1) * span > low)
        copies = {}
        for piece, index, (flip, group, _, pair, core) in blocks:
            known = 0 if flip else group
            if flip:
                group, pair, core = place[0] ^ group, place[2] ^ pair, place[3] ^ core
            start = pl.multiple_of(((outer * 2 + pair) * 2 + core) * count, count)
            copy = fetch.later(weight[piece].at[index], held.at[group, pl.ds(start, count), :])
            copies.setdefault(known, []).append(copy)

        @pl.when(needed)
        def _():
            for each in copies.values():
                for copy in each:
                    copy.start()

        starts += [(needed, known, each) for known, each in copies.items()]
    return starts


def project(copies, attention, held, low, out, add):
    groups, _, columns = held.shape
    step = 512 if columns % 512 == 0 else columns
    for group in range(groups):
        for needed, at, each in copies:
            if at == group:

                @pl.when(needed)
                def _():
                    for copy in each:
                        copy.wait()
        for j in range(columns // step):
            at = pl.ds(group * columns + j * step, step)
            projected = jnp.dot(
                attention[...],
                held[group, pl.ds(low, attention.shape[1]), pl.ds(j * step, step)],
                preferred_element_type=jnp.float32,
            )
            out(at, add(at) + projected)


def begin_kernel(counts, moves, control_rows, hidden, ready, *refs):
    place = device_place()
    weight, control = refs[: counts[0]], refs[counts[0] : sum(counts)]
    out, attention, held, hidden_v, control_v, out_v, sems = refs[sum(counts) :]
    fetch = Fetch(sems)
    residual = [fetch(ready, attention), fetch(hidden, hidden_v)]
    copies = fetch_weight(fetch, moves, place, weight, held, 0, ready.shape[1])
    for d, block in enumerate(control):
        start = pl.multiple_of((device_column(place) ^ d) * control_rows, control_rows) if len(control) > 1 else 0
        residual.append(fetch(block, control_v.at[pl.ds(start, control_rows), :]))
    for copy in residual:
        copy.wait()
    stores = []

    def store(at, x):
        out_v[:, at] = x
        stores.append(fetch(out_v.at[:, at], out.at[:, at]))

    project(
        copies,
        attention,
        held,
        0,
        store,
        lambda at: hidden_v[:, at].astype(jnp.float32) + control_v[:, at].astype(jnp.float32),
    )
    for copy in stores:
        copy.wait()


def finish_kernel(which, pieces, moves, first, pattern, q, part, stats, so_far, *refs):
    slots, active = len(which), in_window(pattern, which)
    near, weight, out, refs = refs[:slots], refs[slots : slots + pieces], refs[slots + pieces], refs[slots + pieces + 1 :]
    q_v, near_v, (*state, stats_v, sems, attention, held, sum_v, out_v, late_sems) = (
        refs[0],
        refs[1 : slots + 1],
        refs[slots + 1 :],
    )
    fetch, late_fetch = Fetch(sems), Fetch(late_sems)
    low = first * HEAD_DIM
    opened = close_open(fetch, first, q, part, stats, near, q_v, near_v, state, stats_v)
    copies = fetch_weight(late_fetch, moves, device_place(), weight, held, low, low + q_v.shape[1])
    so_far_copy = late_fetch(so_far, sum_v)
    close_heads(opened, first, active, q_v, near_v, state, stats_v, attention)
    so_far_copy.wait()
    stores = []

    def store(at, x):
        out_v[:, at] = x.astype(jnp.bfloat16)
        stores.append(late_fetch(out_v.at[:, at], out.at[:, at]))

    project(copies, attention, held, low, store, lambda at: sum_v[:, at])
    for copy in stores:
        copy.wait()


def project_scratch(rows, columns, groups, inner, width, dtype, copies):
    share = width // groups
    return [
        pltpu.VMEM((rows, columns), jnp.bfloat16),
        pltpu.VMEM((groups, inner, share), jnp.bfloat16),
    ], [
        pltpu.VMEM((rows, width), dtype),
        pltpu.SemaphoreType.DMA((copies + width // (512 if share % 512 == 0 else share),)),
    ]


def begin(ready, weight, control, hidden, moves, inner):
    rows, width = hidden.shape
    columns = ready.shape[1]
    before, behind = project_scratch(
        rows, columns, lax.axis_size("groups"), inner, width, jnp.float32, 2 + len(moves) + len(control)
    )
    return pl.pallas_call(
        functools.partial(begin_kernel, (len(weight), len(control)), moves, control[0].shape[0]),
        out_shape=jax.ShapeDtypeStruct((rows, width), jnp.float32),
        in_specs=[ANY] * (2 + len(weight) + len(control)),
        out_specs=ANY,
        scratch_shapes=before + [pltpu.VMEM((rows, width), jnp.bfloat16)] * 2 + behind,
        compiler_params=pltpu.CompilerParams(vmem_limit_bytes=VMEM_LIMIT),
        cost_estimate=pl.CostEstimate(
            flops=2 * rows * columns * width, bytes_accessed=2 * columns * width + 8 * rows * width, transcendentals=0
        ),
        name="begin",
    )(hidden, ready, *weight, *control)


def finish(which, pattern, q, state, near, first, so_far, weight, moves):
    rows, inner = q.shape
    width = so_far.shape[1]
    columns = near[0].shape[1] // 2
    before, behind = project_scratch(
        rows, columns, lax.axis_size("groups"), inner, width, jnp.bfloat16, 1 + len(moves)
    )
    return pl.pallas_call(
        functools.partial(finish_kernel, which, len(weight), moves, first),
        out_shape=jax.ShapeDtypeStruct((rows, width), jnp.bfloat16),
        in_specs=[SMEM] + [ANY] * (4 + len(near) + len(weight)),
        out_specs=ANY,
        scratch_shapes=close_scratch(rows, columns, len(near))
        + before
        + [pltpu.VMEM((rows, width), jnp.float32)]
        + behind,
        compiler_params=pltpu.CompilerParams(vmem_limit_bytes=VMEM_LIMIT),
        cost_estimate=pl.CostEstimate(
            flops=2 * rows * columns * width, bytes_accessed=2 * columns * width + 6 * rows * width, transcendentals=0
        ),
        name="finish",
    )(pattern, q, *state, so_far, *near, *weight)


def flipped(block, axis, flip):
    return lax.ppermute(block, axis, [(i, i ^ flip) for i in range(lax.axis_size(axis))])


class Lane:
    def __init__(self):
        self.last = ()

    def __call__(self, send, block, *others):
        self.last = (send(after(block, *self.last, *others)),)
        return self.last[0]


def swap(axis, flip):
    return lambda block: flipped(block, axis, flip)


def route_of(route):
    return lambda block: lax.ppermute(block, TILES, route)


def grid_of(tile_count):
    width = min(8, tile_count // 4)
    height = min(4, tile_count // 8)
    return (width * height, width, 1), (tile_count // (width * height), height, width)


def device_place():
    return [lax.axis_index(a) for a in ("groups",) + TILES]


def device_column(place):
    _, outer, pair, core = place
    tile_count = math.prod(lax.axis_size(a) for a in TILES)
    return lax.rem((outer * 2 + pair) * 2 + core, grid_of(tile_count)[1][2])


def in_window(pattern, slots):
    _, outer, pair, core = device_place()
    strides, counts = grid_of(math.prod(lax.axis_size(a) for a in TILES))
    position = (outer * 2 + pair) * 2 + core
    active = []
    for axis, odd in slots:
        place = lax.rem(lax.div(position, strides[axis]), counts[axis])
        down = (place >= 1) & (pattern[0, 2 * axis] == 1)
        up = (place + 1 < counts[axis]) & (pattern[0, 2 * axis + 1] == 1)
        active.append(jnp.where(lax.rem(place, 2) == odd, up.astype(jnp.int32), down.astype(jnp.int32)) == 1)
    return active


def neighbour_slots(tile_count, strides, counts):
    slots = []
    for axis, (stride, count) in enumerate(zip(strides, counts)):
        for odd in range(2):
            route = []
            for t in range(tile_count):
                place = t // stride % count
                if place % 2 == odd and place + 1 < count:
                    route += [(t, t + stride), (t + stride, t)]
            if route:
                slots.append((axis, odd, route))
    return slots


def on_device(hidden, queries, keys, values, control, out_weight, pattern):
    groups = lax.axis_size("groups")
    outer, pair, cores = (lax.axis_size(a) for a in TILES)
    tile_count = outer * pair * cores
    strides, counts = grid_of(tile_count)
    grid_width = counts[2]
    across = device_column(device_place())
    rows = queries.shape[0]
    width = hidden.shape[1]
    slots = neighbour_slots(tile_count, strides, counts)
    early = [s for s in slots if s[0] == 2]
    late = [s for s in slots if s[0] != 2]

    far_lane, near_lane = Lane(), Lane()

    shard, share = out_weight.shape[0], width // groups
    line = out_weight[:, :share]
    for g in range(1, groups):
        line = jnp.where(lax.axis_index("groups") == g, out_weight[:, g * share : (g + 1) * share], line)
    line = lax.optimization_barrier(line)[None]
    line_flips = [0]
    flip = outer // 2
    while flip > 2:
        line = jnp.concatenate([line, flipped(line, "outer", flip)])
        line_flips += [f ^ flip for f in line_flips]
        flip //= 2
    far = far_lane(swap("outer", 2), line)
    near = near_lane(swap("outer", 1), line)

    firsts = [sum(CHUNKS[:i]) for i in range(len(CHUNKS))]
    chunks = [
        jnp.concatenate([x[:, f * HEAD_DIM : (f + n) * HEAD_DIM] for x in (keys, values)], axis=1)
        for f, n in zip(firsts, CHUNKS)
    ]
    block = rows // grid_width
    lines = after(control, line).reshape(block // TILE_W, grid_width, TILE_W, width)
    control_sent = [
        lax.dynamic_index_in_dim(lines, across ^ d, 1, keepdims=False).reshape(block, width) for d in range(grid_width)
    ]
    chunks, control_sent = lax.optimization_barrier((chunks, control_sent))
    control_parts = [control_sent[0]] + [None] * (grid_width - 1)
    beside = swap("pair", 1)(line)
    for d in range(2, grid_width - 1):
        control_parts[d] = swap(TILES, d)(after(control_sent[d], line))
    plane = jnp.concatenate([line, beside])
    last = swap("outer", 1)(after(far, near, *control_parts[2:-1], *chunks))
    near_x = swap("pair", 1)(near)
    held = []
    for both in (plane, jnp.concatenate([near, near_x])):
        held += [both, swap("groups", 1)(both)]
    early_near = [[None, None] for _ in early]
    for i, x in enumerate((keys, values)):
        early_near[0][i] = lax.ppermute(x, TILES, early[0][2])
        for slot in range(1, len(early)):
            early_near[slot][i] = lax.ppermute(after(x, early_near[0][i]), TILES, early[slot][2])
    state = attend(tuple(s[:2] for s in early), pattern, queries, [keys, values] + [x for kv in early_near for x in kv])

    late_near = []
    for chunk in chunks:
        lanes = (far_lane, near_lane)
        late_near.append([lanes[i % 2](route_of(route), chunk) for i, (_, _, route) in enumerate(late)])
    crossed = [swap("core", 1)(x) for x in held]
    for d in (1, grid_width - 1):
        control_parts[d] = swap(TILES, d)(after(control_sent[d], *[x for kv in early_near[1:] for x in kv]))

    gates = [*control_parts[2:-1], near_x, held[1]]
    weight = [lax.all_gather(after(jnp.concatenate([far, last]), *gates), ("groups", "pair", "core"))]
    n = len(line_flips)
    moves = [
        (0, ((g * pair + p) * cores + c, i * n + j), (False, g, f ^ at, p, c))
        for g in range(groups)
        for p in range(pair)
        for c in range(cores)
        for i, at in enumerate((2, 3))
        for j, f in enumerate(line_flips)
    ]
    for number, (group_flip, at) in enumerate(((0, 0), (1, 0), (0, 1), (1, 1))):
        for core_flip, pieces in enumerate((held, crossed)):
            moves += [
                (len(weight), (p * n + j,), (True, group_flip, f ^ at, p, core_flip))
                for p in range(pair)
                for j, f in enumerate(line_flips)
            ]
            weight.append(pieces[number])

    which = tuple(s[:2] for s in late)
    ready = [close(which, pattern, queries, state, late_near[i], firsts[i]) for i in range(len(CHUNKS) - 1)]
    ready = ready[0] if len(ready) == 1 else jnp.concatenate(ready, axis=1)
    if block % 16:
        control_parts = [
            jnp.take(
                jnp.stack(control_parts), jnp.arange(grid_width, dtype=jnp.int32) ^ across, axis=0
            ).reshape(rows, width)
        ]
    if shard % 16:
        weight, moves = [in_order(weight, moves, device_place(), (groups, outer, pair, cores))], [(0, None, None)]
    moves = tuple(moves)
    so_far = begin(ready, weight, control_parts, hidden, moves, queries.shape[1])
    return finish(which, pattern, queries, state, late_near[-1], firsts[-1], so_far, weight, moves)


def in_order(weight, moves, place, sizes):
    groups, outer, pair, cores = sizes
    shard, columns = weight[0].shape[-2:]
    gathered = weight[0].reshape(groups, pair, cores, -1, shard, columns)
    for axis, at in enumerate((0, 2, 3)):
        gathered = jnp.take(gathered, jnp.arange(sizes[at], dtype=jnp.int32) ^ place[at], axis=axis)
    weight = [gathered.reshape(weight[0].shape)] + weight[1:]
    blocks = {at[1:]: weight[piece][index] for piece, index, at in moves}
    whole = jnp.stack([blocks[at] for at in sorted(blocks)]).reshape(sizes + (shard, columns))
    for axis, size in enumerate(sizes):
        whole = jnp.take(whole, jnp.arange(size, dtype=jnp.int32) ^ place[axis], axis=axis)
    return whole.reshape(groups, -1, columns)


def solution(mesh):
    groups = mesh.shape["groups"]
    tiles = mesh.shape["tiles"]
    split = Mesh(mesh.devices.reshape(groups, tiles // 4, 2, 2), ("groups",) + TILES)
    rows = P(("groups",) + TILES, None)
    placed = (rows, rows, rows, rows, rows, P(TILES, None), rows)
    return jax.shard_map(
        on_device,
        mesh=split,
        in_specs=placed,
        out_specs=rows,
        check_vma=False,
    )
```

```python
import functools
import math

import jax
import jax.numpy as jnp
from jax import lax
from jax.experimental import pallas as pl
from jax.experimental.pallas import tpu as pltpu
from jax.sharding import Mesh
from jax.sharding import PartitionSpec as P

HEAD_DIM = 128
TILE_W = 8
CHUNKS = (6, 6)
SCALE = HEAD_DIM**-0.5 * math.log2(math.e)
TILES = ("outer", "pair", "core")
VMEM_LIMIT = 60 * 1024 * 1024
SMEM = pl.BlockSpec(memory_space=pltpu.SMEM)
ANY = pl.BlockSpec(memory_space=pl.ANY)


def after(x, *others):
    return lax.optimization_barrier((x, *others))[0] if others else x


def head_part(q, k, v):
    scores = lax.dot_general(q, k, (((1,), (1,)), ((), ())), preferred_element_type=jnp.float32)
    peak = jnp.max(scores, axis=1, keepdims=True)
    weights = jnp.exp2((scores - peak) * SCALE).astype(jnp.bfloat16)
    ones = jnp.ones((v.shape[0], HEAD_DIM), jnp.bfloat16)
    both = jnp.dot(weights, jnp.concatenate([v, ones], axis=1), preferred_element_type=jnp.float32)
    return both[:, :HEAD_DIM], both[:, HEAD_DIM:], jnp.broadcast_to(peak, v.shape)


def merge(old, new):
    part, total, peak = old
    part_new, total_new, peak_new = new
    top = jnp.maximum(peak, peak_new)
    f_old = jnp.exp2((peak - top) * SCALE)
    f_new = jnp.exp2((peak_new - top) * SCALE)
    return f_old * part + f_new * part_new, f_old * total + f_new * total_new, top


def columns_of(h):
    return pl.ds(h * HEAD_DIM, HEAD_DIM)


def fold(state, active, q, k, v):
    @pl.when(active)
    def _():
        for h in range(q.shape[1] // HEAD_DIM):
            at = columns_of(h)
            new = head_part(q[:, at], k[:, at], v[:, at])
            for r, x in zip(state, merge(tuple(r[:, at] for r in state), new)):
                r[:, at] = x


class Fetch:
    def __init__(self, sems):
        self.sems, self.count = sems, 0

    def later(self, source, target):
        self.count += 1
        return pltpu.make_async_copy(source, target, self.sems.at[self.count - 1])

    def __call__(self, source, target):
        copy = self.later(source, target)
        copy.start()
        return copy


def attend_kernel(which, pattern, q, *refs):
    slots, active = len(which), in_window(pattern, which)
    kv, (part, stats), scratch = refs[: 2 * slots + 2], refs[2 * slots + 2 : 2 * slots + 4], refs[2 * slots + 4 :]
    q_v, kv_v, (part_v, total_v, peak_v, stats_v, sems) = scratch[0], scratch[1 : 2 * slots + 3], scratch[2 * slots + 3 :]
    fetch = Fetch(sems)
    copies = [fetch(source, target) for source, target in zip((q, *kv), (q_v, *kv_v))]
    for copy in copies[:3]:
        copy.wait()
    state = (part_v, total_v, peak_v)
    heads = q_v.shape[1] // HEAD_DIM
    for h in range(heads):
        at = columns_of(h)
        for r, x in zip(state, head_part(q_v[:, at], kv_v[0][:, at], kv_v[1][:, at])):
            r[:, at] = x
    for slot in range(slots):
        for copy in copies[3 + 2 * slot : 5 + 2 * slot]:
            copy.wait()
        fold(state, active[slot], q_v, kv_v[2 * slot + 2], kv_v[2 * slot + 3])
    lane = lax.broadcasted_iota(jnp.int32, stats_v.shape, 1)
    packed = jnp.zeros(stats_v.shape, jnp.float32)
    for h in range(heads):
        packed = jnp.where(lane == h, total_v[:, columns_of(h)], packed)
        packed = jnp.where(lane == HEAD_DIM // 2 + h, peak_v[:, columns_of(h)], packed)
    stats_v[...] = packed
    copies = [fetch(part_v, part), fetch(stats_v, stats)]
    for copy in copies:
        copy.wait()


def attend(which, pattern, q, kv):
    rows, columns = q.shape
    slots = len(kv) // 2 - 1
    return pl.pallas_call(
        functools.partial(attend_kernel, which),
        out_shape=[
            jax.ShapeDtypeStruct((rows, columns), jnp.float32),
            jax.ShapeDtypeStruct((rows, HEAD_DIM), jnp.float32),
        ],
        in_specs=[SMEM] + [ANY] * (1 + len(kv)),
        out_specs=[ANY] * 2,
        scratch_shapes=[pltpu.VMEM((rows, columns), jnp.bfloat16)] * (1 + len(kv))
        + [pltpu.VMEM((rows, columns), jnp.float32)] * 3
        + [pltpu.VMEM((rows, HEAD_DIM), jnp.float32), pltpu.SemaphoreType.DMA((3 + len(kv),))],
        compiler_params=pltpu.CompilerParams(vmem_limit_bytes=VMEM_LIMIT),
        cost_estimate=pl.CostEstimate(
            flops=(1 + slots) * 6 * rows * rows * columns,
            bytes_accessed=rows * columns * (10 + 4 * slots),
            transcendentals=0,
        ),
        name="attend",
    )(pattern, q, *kv)


def close_open(fetch, first, q, part, stats, near, q_v, near_v, state, stats_v):
    columns = state[0].shape[1]
    at = pl.ds(first * HEAD_DIM, columns)
    return [
        fetch(q.at[:, at], q_v),
        fetch(part.at[:, at], state[0]),
        fetch(stats, stats_v),
    ] + [fetch(source, target) for source, target in zip(near, near_v)]


def close_heads(copies, first, active, q_v, near_v, state, stats_v, out):
    part_v = state[0]
    columns = part_v.shape[1]
    for copy in copies:
        copy.wait()
    stats_now = stats_v[...]
    for h in range(columns // HEAD_DIM):
        at = columns_of(h)
        total, peak = (
            jnp.broadcast_to(stats_now[:, lane : lane + 1], stats_now.shape)
            for lane in (first + h, HEAD_DIM // 2 + first + h)
        )
        terms = [(part_v[:, at], total, peak)]
        for slot, kv in enumerate(near_v):
            part, total, peak = head_part(q_v[:, at], kv[:, at], kv[:, pl.ds(columns + h * HEAD_DIM, HEAD_DIM)])
            terms.append((part, total, jnp.where(active[slot], peak, -1e30)))
        top = functools.reduce(jnp.maximum, [peak for _, _, peak in terms])
        factors = [jnp.exp2((peak - top) * SCALE) for _, _, peak in terms]
        numerator = sum(f * part for f, (part, _, _) in zip(factors, terms))
        denominator = sum(f * total for f, (_, total, _) in zip(factors, terms))
        out[:, at] = (numerator / denominator).astype(jnp.bfloat16)


def close_scratch(rows, columns, slots):
    return (
        [pltpu.VMEM((rows, columns), jnp.bfloat16)]
        + [pltpu.VMEM((rows, 2 * columns), jnp.bfloat16)] * slots
        + [pltpu.VMEM((rows, columns), jnp.float32)]
        + [pltpu.VMEM((rows, HEAD_DIM), jnp.float32), pltpu.SemaphoreType.DMA((4 + slots,))]
    )


def close_kernel(first, which, pattern, q, part, stats, *refs):
    slots, active = len(which), in_window(pattern, which)
    near, out = refs[:slots], refs[slots]
    q_v, near_v, (*state, stats_v, sems, out_v) = refs[slots + 1], refs[slots + 2 : 2 * slots + 2], refs[2 * slots + 2 :]
    fetch = Fetch(sems)
    opened = close_open(fetch, first, q, part, stats, near, q_v, near_v, state, stats_v)
    close_heads(opened, first, active, q_v, near_v, state, stats_v, out_v)
    fetch(out_v, out).wait()


def close(which, pattern, q, state, near, first):
    rows, columns = q.shape[0], near[0].shape[1] // 2
    return pl.pallas_call(
        functools.partial(close_kernel, first, which),
        out_shape=jax.ShapeDtypeStruct((rows, columns), jnp.bfloat16),
        in_specs=[SMEM] + [ANY] * (3 + len(near)),
        out_specs=ANY,
        scratch_shapes=close_scratch(rows, columns, len(near)) + [pltpu.VMEM((rows, columns), jnp.bfloat16)],
        compiler_params=pltpu.CompilerParams(vmem_limit_bytes=VMEM_LIMIT),
        cost_estimate=pl.CostEstimate(
            flops=len(near) * 6 * rows * rows * columns,
            bytes_accessed=rows * columns * (4 * len(near) + 8),
            transcendentals=0,
        ),
        name="close",
    )(pattern, q, *state, *near)


def fetch_weight(fetch, moves, place, weight, held, low, high):
    if moves[0][2] is None:
        return [(True, 0, [fetch(weight[piece], held)]) for piece, _, _ in moves]
    starts = []
    for outer_flip in sorted({at[2] for _, _, at in moves}):
        blocks = [move for move in moves if move[2][2] == outer_flip]
        count = weight[0].shape[-2]
        span = len(blocks) // held.shape[0] * count
        outer = place[1] ^ outer_flip
        needed = (outer * span < high) & ((outer + 1) * span > low)
        copies = {}
        for piece, index, (flip, group, _, pair, core) in blocks:
            known = 0 if flip else group
            if flip:
                group, pair, core = place[0] ^ group, place[2] ^ pair, place[3] ^ core
            start = pl.multiple_of(((outer * 2 + pair) * 2 + core) * count, count)
            copy = fetch.later(weight[piece].at[index], held.at[group, pl.ds(start, count), :])
            copies.setdefault(known, []).append(copy)

        @pl.when(needed)
        def _():
            for each in copies.values():
                for copy in each:
                    copy.start()

        starts += [(needed, known, each) for known, each in copies.items()]
    return starts


def project(copies, attention, held, low, out, add):
    groups, _, columns = held.shape
    step = 512 if columns % 512 == 0 else columns
    for group in range(groups):
        for needed, at, each in copies:
            if at == group:

                @pl.when(needed)
                def _():
                    for copy in each:
                        copy.wait()
        for j in range(columns // step):
            at = pl.ds(group * columns + j * step, step)
            projected = jnp.dot(
                attention[...],
                held[group, pl.ds(low, attention.shape[1]), pl.ds(j * step, step)],
                preferred_element_type=jnp.float32,
            )
            out(at, add(at) + projected)


def begin_kernel(counts, moves, control_rows, hidden, ready, *refs):
    place = device_place()
    weight, control = refs[: counts[0]], refs[counts[0] : sum(counts)]
    out, attention, held, hidden_v, control_v, out_v, sems = refs[sum(counts) :]
    fetch = Fetch(sems)
    residual = [fetch(ready, attention), fetch(hidden, hidden_v)]
    copies = fetch_weight(fetch, moves, place, weight, held, 0, ready.shape[1])
    for d, block in enumerate(control):
        start = pl.multiple_of((device_column(place) ^ d) * control_rows, control_rows) if len(control) > 1 else 0
        residual.append(fetch(block, control_v.at[pl.ds(start, control_rows), :]))
    for copy in residual:
        copy.wait()
    stores = []

    def store(at, x):
        out_v[:, at] = x
        stores.append(fetch(out_v.at[:, at], out.at[:, at]))

    project(
        copies,
        attention,
        held,
        0,
        store,
        lambda at: hidden_v[:, at].astype(jnp.float32) + control_v[:, at].astype(jnp.float32),
    )
    for copy in stores:
        copy.wait()


def finish_kernel(which, pieces, moves, first, pattern, q, part, stats, so_far, *refs):
    slots, active = len(which), in_window(pattern, which)
    near, weight, out, refs = refs[:slots], refs[slots : slots + pieces], refs[slots + pieces], refs[slots + pieces + 1 :]
    q_v, near_v, (*state, stats_v, sems, attention, held, sum_v, out_v, late_sems) = (
        refs[0],
        refs[1 : slots + 1],
        refs[slots + 1 :],
    )
    fetch, late_fetch = Fetch(sems), Fetch(late_sems)
    low = first * HEAD_DIM
    opened = close_open(fetch, first, q, part, stats, near, q_v, near_v, state, stats_v)
    copies = fetch_weight(late_fetch, moves, device_place(), weight, held, low, low + q_v.shape[1])
    so_far_copy = late_fetch(so_far, sum_v)
    close_heads(opened, first, active, q_v, near_v, state, stats_v, attention)
    so_far_copy.wait()
    stores = []

    def store(at, x):
        out_v[:, at] = x.astype(jnp.bfloat16)
        stores.append(late_fetch(out_v.at[:, at], out.at[:, at]))

    project(copies, attention, held, low, store, lambda at: sum_v[:, at])
    for copy in stores:
        copy.wait()


def project_scratch(rows, columns, groups, inner, width, dtype, copies):
    share = width // groups
    return [
        pltpu.VMEM((rows, columns), jnp.bfloat16),
        pltpu.VMEM((groups, inner, share), jnp.bfloat16),
    ], [
        pltpu.VMEM((rows, width), dtype),
        pltpu.SemaphoreType.DMA((copies + width // (512 if share % 512 == 0 else share),)),
    ]


def begin(ready, weight, control, hidden, moves, inner):
    rows, width = hidden.shape
    columns = ready.shape[1]
    before, behind = project_scratch(
        rows, columns, lax.axis_size("groups"), inner, width, jnp.float32, 2 + len(moves) + len(control)
    )
    return pl.pallas_call(
        functools.partial(begin_kernel, (len(weight), len(control)), moves, control[0].shape[0]),
        out_shape=jax.ShapeDtypeStruct((rows, width), jnp.float32),
        in_specs=[ANY] * (2 + len(weight) + len(control)),
        out_specs=ANY,
        scratch_shapes=before + [pltpu.VMEM((rows, width), jnp.bfloat16)] * 2 + behind,
        compiler_params=pltpu.CompilerParams(vmem_limit_bytes=VMEM_LIMIT),
        cost_estimate=pl.CostEstimate(
            flops=2 * rows * columns * width, bytes_accessed=2 * columns * width + 8 * rows * width, transcendentals=0
        ),
        name="begin",
    )(hidden, ready, *weight, *control)


def finish(which, pattern, q, state, near, first, so_far, weight, moves):
    rows, inner = q.shape
    width = so_far.shape[1]
    columns = near[0].shape[1] // 2
    before, behind = project_scratch(
        rows, columns, lax.axis_size("groups"), inner, width, jnp.bfloat16, 1 + len(moves)
    )
    return pl.pallas_call(
        functools.partial(finish_kernel, which, len(weight), moves, first),
        out_shape=jax.ShapeDtypeStruct((rows, width), jnp.bfloat16),
        in_specs=[SMEM] + [ANY] * (4 + len(near) + len(weight)),
        out_specs=ANY,
        scratch_shapes=close_scratch(rows, columns, len(near))
        + before
        + [pltpu.VMEM((rows, width), jnp.float32)]
        + behind,
        compiler_params=pltpu.CompilerParams(vmem_limit_bytes=VMEM_LIMIT),
        cost_estimate=pl.CostEstimate(
            flops=2 * rows * columns * width, bytes_accessed=2 * columns * width + 6 * rows * width, transcendentals=0
        ),
        name="finish",
    )(pattern, q, *state, so_far, *near, *weight)


def flipped(block, axis, flip):
    return lax.ppermute(block, axis, [(i, i ^ flip) for i in range(lax.axis_size(axis))])


class Lane:
    def __init__(self):
        self.last = ()

    def __call__(self, send, block, *others):
        self.last = (send(after(block, *self.last, *others)),)
        return self.last[0]


def swap(axis, flip):
    return lambda block: flipped(block, axis, flip)


def route_of(route):
    return lambda block: lax.ppermute(block, TILES, route)


def grid_of(tile_count):
    width = min(8, tile_count // 4)
    height = min(4, tile_count // 8)
    return (width * height, width, 1), (tile_count // (width * height), height, width)


def device_place():
    return [lax.axis_index(a) for a in ("groups",) + TILES]


def device_column(place):
    _, outer, pair, core = place
    tile_count = math.prod(lax.axis_size(a) for a in TILES)
    return lax.rem((outer * 2 + pair) * 2 + core, grid_of(tile_count)[1][2])


def in_window(pattern, slots):
    _, outer, pair, core = device_place()
    strides, counts = grid_of(math.prod(lax.axis_size(a) for a in TILES))
    position = (outer * 2 + pair) * 2 + core
    active = []
    for axis, odd in slots:
        place = lax.rem(lax.div(position, strides[axis]), counts[axis])
        down = (place >= 1) & (pattern[0, 2 * axis] == 1)
        up = (place + 1 < counts[axis]) & (pattern[0, 2 * axis + 1] == 1)
        active.append(jnp.where(lax.rem(place, 2) == odd, up.astype(jnp.int32), down.astype(jnp.int32)) == 1)
    return active


def neighbour_slots(tile_count, strides, counts):
    slots = []
    for axis, (stride, count) in enumerate(zip(strides, counts)):
        for odd in range(2):
            route = []
            for t in range(tile_count):
                place = t // stride % count
                if place % 2 == odd and place + 1 < count:
                    route += [(t, t + stride), (t + stride, t)]
            if route:
                slots.append((axis, odd, route))
    return slots


def on_device(hidden, queries, keys, values, control, out_weight, pattern):
    groups = lax.axis_size("groups")
    outer, pair, cores = (lax.axis_size(a) for a in TILES)
    tile_count = outer * pair * cores
    strides, counts = grid_of(tile_count)
    grid_width = counts[2]
    across = device_column(device_place())
    rows = queries.shape[0]
    width = hidden.shape[1]
    slots = neighbour_slots(tile_count, strides, counts)
    early = [s for s in slots if s[0] == 2]
    late = [s for s in slots if s[0] != 2]

    far_lane, near_lane = Lane(), Lane()

    shard, share = out_weight.shape[0], width // groups
    line = out_weight[:, :share]
    for g in range(1, groups):
        line = jnp.where(lax.axis_index("groups") == g, out_weight[:, g * share : (g + 1) * share], line)
    line = lax.optimization_barrier(line)[None]
    line_flips = [0]
    flip = outer // 2
    while flip > 2:
        line = jnp.concatenate([line, flipped(line, "outer", flip)])
        line_flips += [f ^ flip for f in line_flips]
        flip //= 2
    far = far_lane(swap("outer", 2), line)
    near = near_lane(swap("outer", 1), line)

    firsts = [sum(CHUNKS[:i]) for i in range(len(CHUNKS))]
    chunks = [
        jnp.concatenate([x[:, f * HEAD_DIM : (f + n) * HEAD_DIM] for x in (keys, values)], axis=1)
        for f, n in zip(firsts, CHUNKS)
    ]
    block = rows // grid_width
    lines = after(control, line).reshape(block // TILE_W, grid_width, TILE_W, width)
    control_sent = [
        lax.dynamic_index_in_dim(lines, across ^ d, 1, keepdims=False).reshape(block, width) for d in range(grid_width)
    ]
    chunks, control_sent = lax.optimization_barrier((chunks, control_sent))
    control_parts = [control_sent[0]] + [None] * (grid_width - 1)
    beside = swap("pair", 1)(line)
    for d in range(2, grid_width - 1):
        control_parts[d] = swap(TILES, d)(after(control_sent[d], line))
    plane = jnp.concatenate([line, beside])
    last = swap("outer", 1)(after(far, near, *control_parts[2:-1], *chunks))
    near_x = swap("pair", 1)(near)
    held = []
    for both in (plane, jnp.concatenate([near, near_x])):
        held += [both, swap("groups", 1)(both)]
    early_near = [[None, None] for _ in early]
    for i, x in enumerate((keys, values)):
        early_near[0][i] = lax.ppermute(x, TILES, early[0][2])
        for slot in range(1, len(early)):
            early_near[slot][i] = lax.ppermute(after(x, early_near[0][i]), TILES, early[slot][2])
    state = attend(tuple(s[:2] for s in early), pattern, queries, [keys, values] + [x for kv in early_near for x in kv])

    late_near = []
    for chunk in chunks:
        lanes = (far_lane, near_lane)
        late_near.append([lanes[i % 2](route_of(route), chunk) for i, (_, _, route) in enumerate(late)])
    crossed = [swap("core", 1)(x) for x in held]
    for d in (1, grid_width - 1):
        control_parts[d] = swap(TILES, d)(after(control_sent[d], *[x for kv in early_near[1:] for x in kv]))

    gates = [*control_parts[2:-1], near_x, held[1], crossed[0]]
    weight = [lax.all_gather(after(jnp.concatenate([far, last]), *gates), ("groups", "pair", "core"))]
    n = len(line_flips)
    moves = [
        (0, ((g * pair + p) * cores + c, i * n + j), (False, g, f ^ at, p, c))
        for g in range(groups)
        for p in range(pair)
        for c in range(cores)
        for i, at in enumerate((2, 3))
        for j, f in enumerate(line_flips)
    ]
    for number, (group_flip, at) in enumerate(((0, 0), (1, 0), (0, 1), (1, 1))):
        for core_flip, pieces in enumerate((held, crossed)):
            moves += [
                (len(weight), (p * n + j,), (True, group_flip, f ^ at, p, core_flip))
                for p in range(pair)
                for j, f in enumerate(line_flips)
            ]
            weight.append(pieces[number])

    which = tuple(s[:2] for s in late)
    ready = [close(which, pattern, queries, state, late_near[i], firsts[i]) for i in range(len(CHUNKS) - 1)]
    ready = ready[0] if len(ready) == 1 else jnp.concatenate(ready, axis=1)
    if block % 16:
        control_parts = [
            jnp.take(
                jnp.stack(control_parts), jnp.arange(grid_width, dtype=jnp.int32) ^ across, axis=0
            ).reshape(rows, width)
        ]
    if shard % 16:
        weight, moves = [in_order(weight, moves, device_place(), (groups, outer, pair, cores))], [(0, None, None)]
    moves = tuple(moves)
    so_far = begin(ready, weight, control_parts, hidden, moves, queries.shape[1])
    return finish(which, pattern, queries, state, late_near[-1], firsts[-1], so_far, weight, moves)


def in_order(weight, moves, place, sizes):
    groups, outer, pair, cores = sizes
    shard, columns = weight[0].shape[-2:]
    gathered = weight[0].reshape(groups, pair, cores, -1, shard, columns)
    for axis, at in enumerate((0, 2, 3)):
        gathered = jnp.take(gathered, jnp.arange(sizes[at], dtype=jnp.int32) ^ place[at], axis=axis)
    weight = [gathered.reshape(weight[0].shape)] + weight[1:]
    blocks = {at[1:]: weight[piece][index] for piece, index, at in moves}
    whole = jnp.stack([blocks[at] for at in sorted(blocks)]).reshape(sizes + (shard, columns))
    for axis, size in enumerate(sizes):
        whole = jnp.take(whole, jnp.arange(size, dtype=jnp.int32) ^ place[axis], axis=axis)
    return whole.reshape(groups, -1, columns)


def solution(mesh):
    groups = mesh.shape["groups"]
    tiles = mesh.shape["tiles"]
    split = Mesh(mesh.devices.reshape(groups, tiles // 4, 2, 2), ("groups",) + TILES)
    rows = P(("groups",) + TILES, None)
    placed = (rows, rows, rows, rows, rows, P(TILES, None), rows)
    return jax.shard_map(
        on_device,
        mesh=split,
        in_specs=placed,
        out_specs=rows,
        check_vma=False,
    )
```

```python
import functools
import math

import jax
import jax.numpy as jnp
from jax import lax
from jax.experimental import pallas as pl
from jax.experimental.pallas import tpu as pltpu
from jax.sharding import Mesh
from jax.sharding import PartitionSpec as P

HEAD_DIM = 128
TILE_W = 8
CHUNKS = (6, 6)
SCALE = HEAD_DIM**-0.5 * math.log2(math.e)
TILES = ("outer", "pair", "core")
VMEM_LIMIT = 60 * 1024 * 1024
SMEM = pl.BlockSpec(memory_space=pltpu.SMEM)
ANY = pl.BlockSpec(memory_space=pl.ANY)


def after(x, *others):
    return lax.optimization_barrier((x, *others))[0] if others else x


def head_part(q, k, v):
    scores = lax.dot_general(q, k, (((1,), (1,)), ((), ())), preferred_element_type=jnp.float32)
    peak = jnp.max(scores, axis=1, keepdims=True)
    weights = jnp.exp2((scores - peak) * SCALE).astype(jnp.bfloat16)
    ones = jnp.ones((v.shape[0], HEAD_DIM), jnp.bfloat16)
    both = jnp.dot(weights, jnp.concatenate([v, ones], axis=1), preferred_element_type=jnp.float32)
    return both[:, :HEAD_DIM], both[:, HEAD_DIM:], jnp.broadcast_to(peak, v.shape)


def merge(old, new):
    part, total, peak = old
    part_new, total_new, peak_new = new
    top = jnp.maximum(peak, peak_new)
    f_old = jnp.exp2((peak - top) * SCALE)
    f_new = jnp.exp2((peak_new - top) * SCALE)
    return f_old * part + f_new * part_new, f_old * total + f_new * total_new, top


def columns_of(h):
    return pl.ds(h * HEAD_DIM, HEAD_DIM)


def fold(state, active, q, k, v):
    @pl.when(active)
    def _():
        for h in range(q.shape[1] // HEAD_DIM):
            at = columns_of(h)
            new = head_part(q[:, at], k[:, at], v[:, at])
            for r, x in zip(state, merge(tuple(r[:, at] for r in state), new)):
                r[:, at] = x


class Fetch:
    def __init__(self, sems):
        self.sems, self.count = sems, 0

    def later(self, source, target):
        self.count += 1
        return pltpu.make_async_copy(source, target, self.sems.at[self.count - 1])

    def __call__(self, source, target):
        copy = self.later(source, target)
        copy.start()
        return copy


def attend_kernel(which, pattern, q, *refs):
    slots, active = len(which), in_window(pattern, which)
    kv, (part, stats), scratch = refs[: 2 * slots + 2], refs[2 * slots + 2 : 2 * slots + 4], refs[2 * slots + 4 :]
    q_v, kv_v, (part_v, total_v, peak_v, stats_v, sems) = scratch[0], scratch[1 : 2 * slots + 3], scratch[2 * slots + 3 :]
    fetch = Fetch(sems)
    copies = [fetch(source, target) for source, target in zip((q, *kv), (q_v, *kv_v))]
    for copy in copies[:3]:
        copy.wait()
    state = (part_v, total_v, peak_v)
    heads = q_v.shape[1] // HEAD_DIM
    for h in range(heads):
        at = columns_of(h)
        for r, x in zip(state, head_part(q_v[:, at], kv_v[0][:, at], kv_v[1][:, at])):
            r[:, at] = x
    for slot in range(slots):
        for copy in copies[3 + 2 * slot : 5 + 2 * slot]:
            copy.wait()
        fold(state, active[slot], q_v, kv_v[2 * slot + 2], kv_v[2 * slot + 3])
    lane = lax.broadcasted_iota(jnp.int32, stats_v.shape, 1)
    packed = jnp.zeros(stats_v.shape, jnp.float32)
    for h in range(heads):
        packed = jnp.where(lane == h, total_v[:, columns_of(h)], packed)
        packed = jnp.where(lane == HEAD_DIM // 2 + h, peak_v[:, columns_of(h)], packed)
    stats_v[...] = packed
    copies = [fetch(part_v, part), fetch(stats_v, stats)]
    for copy in copies:
        copy.wait()


def attend(which, pattern, q, kv):
    rows, columns = q.shape
    slots = len(kv) // 2 - 1
    return pl.pallas_call(
        functools.partial(attend_kernel, which),
        out_shape=[
            jax.ShapeDtypeStruct((rows, columns), jnp.float32),
            jax.ShapeDtypeStruct((rows, HEAD_DIM), jnp.float32),
        ],
        in_specs=[SMEM] + [ANY] * (1 + len(kv)),
        out_specs=[ANY] * 2,
        scratch_shapes=[pltpu.VMEM((rows, columns), jnp.bfloat16)] * (1 + len(kv))
        + [pltpu.VMEM((rows, columns), jnp.float32)] * 3
        + [pltpu.VMEM((rows, HEAD_DIM), jnp.float32), pltpu.SemaphoreType.DMA((3 + len(kv),))],
        compiler_params=pltpu.CompilerParams(vmem_limit_bytes=VMEM_LIMIT),
        cost_estimate=pl.CostEstimate(
            flops=(1 + slots) * 6 * rows * rows * columns,
            bytes_accessed=rows * columns * (10 + 4 * slots),
            transcendentals=0,
        ),
        name="attend",
    )(pattern, q, *kv)


def close_open(fetch, first, q, part, stats, near, q_v, near_v, state, stats_v):
    columns = state[0].shape[1]
    at = pl.ds(first * HEAD_DIM, columns)
    return [
        fetch(q.at[:, at], q_v),
        fetch(part.at[:, at], state[0]),
        fetch(stats, stats_v),
    ] + [fetch(source, target) for source, target in zip(near, near_v)]


def close_heads(copies, first, active, q_v, near_v, state, stats_v, out):
    part_v = state[0]
    columns = part_v.shape[1]
    for copy in copies:
        copy.wait()
    stats_now = stats_v[...]
    for h in range(columns // HEAD_DIM):
        at = columns_of(h)
        total, peak = (
            jnp.broadcast_to(stats_now[:, lane : lane + 1], stats_now.shape)
            for lane in (first + h, HEAD_DIM // 2 + first + h)
        )
        terms = [(part_v[:, at], total, peak)]
        for slot, kv in enumerate(near_v):
            part, total, peak = head_part(q_v[:, at], kv[:, at], kv[:, pl.ds(columns + h * HEAD_DIM, HEAD_DIM)])
            terms.append((part, total, jnp.where(active[slot], peak, -1e30)))
        top = functools.reduce(jnp.maximum, [peak for _, _, peak in terms])
        factors = [jnp.exp2((peak - top) * SCALE) for _, _, peak in terms]
        numerator = sum(f * part for f, (part, _, _) in zip(factors, terms))
        denominator = sum(f * total for f, (_, total, _) in zip(factors, terms))
        out[:, at] = (numerator / denominator).astype(jnp.bfloat16)


def close_scratch(rows, columns, slots):
    return (
        [pltpu.VMEM((rows, columns), jnp.bfloat16)]
        + [pltpu.VMEM((rows, 2 * columns), jnp.bfloat16)] * slots
        + [pltpu.VMEM((rows, columns), jnp.float32)]
        + [pltpu.VMEM((rows, HEAD_DIM), jnp.float32), pltpu.SemaphoreType.DMA((4 + slots,))]
    )


def close_kernel(first, which, pattern, q, part, stats, *refs):
    slots, active = len(which), in_window(pattern, which)
    near, out = refs[:slots], refs[slots]
    q_v, near_v, (*state, stats_v, sems, out_v) = refs[slots + 1], refs[slots + 2 : 2 * slots + 2], refs[2 * slots + 2 :]
    fetch = Fetch(sems)
    opened = close_open(fetch, first, q, part, stats, near, q_v, near_v, state, stats_v)
    close_heads(opened, first, active, q_v, near_v, state, stats_v, out_v)
    fetch(out_v, out).wait()


def close(which, pattern, q, state, near, first):
    rows, columns = q.shape[0], near[0].shape[1] // 2
    return pl.pallas_call(
        functools.partial(close_kernel, first, which),
        out_shape=jax.ShapeDtypeStruct((rows, columns), jnp.bfloat16),
        in_specs=[SMEM] + [ANY] * (3 + len(near)),
        out_specs=ANY,
        scratch_shapes=close_scratch(rows, columns, len(near)) + [pltpu.VMEM((rows, columns), jnp.bfloat16)],
        compiler_params=pltpu.CompilerParams(vmem_limit_bytes=VMEM_LIMIT),
        cost_estimate=pl.CostEstimate(
            flops=len(near) * 6 * rows * rows * columns,
            bytes_accessed=rows * columns * (4 * len(near) + 8),
            transcendentals=0,
        ),
        name="close",
    )(pattern, q, *state, *near)


def fetch_weight(fetch, moves, place, weight, held, low, high):
    if moves[0][2] is None:
        return [(True, 0, [fetch(weight[piece], held)]) for piece, _, _ in moves]
    starts = []
    for outer_flip in sorted({at[2] for _, _, at in moves}):
        blocks = [move for move in moves if move[2][2] == outer_flip]
        count = weight[0].shape[-2]
        span = len(blocks) // held.shape[0] * count
        outer = place[1] ^ outer_flip
        needed = (outer * span < high) & ((outer + 1) * span > low)
        copies = {}
        for piece, index, (flip, group, _, pair, core) in blocks:
            known = 0 if flip else group
            if flip:
                group, pair, core = place[0] ^ group, place[2] ^ pair, place[3] ^ core
            start = pl.multiple_of(((outer * 2 + pair) * 2 + core) * count, count)
            copy = fetch.later(weight[piece].at[index], held.at[group, pl.ds(start, count), :])
            copies.setdefault(known, []).append(copy)

        @pl.when(needed)
        def _():
            for each in copies.values():
                for copy in each:
                    copy.start()

        starts += [(needed, known, each) for known, each in copies.items()]
    return starts


def project(copies, attention, held, low, out, add):
    groups, _, columns = held.shape
    step = columns
    for group in range(groups):
        for needed, at, each in copies:
            if at == group:

                @pl.when(needed)
                def _():
                    for copy in each:
                        copy.wait()
        for j in range(columns // step):
            at = pl.ds(group * columns + j * step, step)
            projected = jnp.dot(
                attention[...],
                held[group, pl.ds(low, attention.shape[1]), pl.ds(j * step, step)],
                preferred_element_type=jnp.float32,
            )
            out(at, add(at) + projected)


def begin_kernel(counts, moves, control_rows, hidden, ready, *refs):
    place = device_place()
    weight, control = refs[: counts[0]], refs[counts[0] : sum(counts)]
    out, attention, held, hidden_v, control_v, out_v, sems = refs[sum(counts) :]
    fetch = Fetch(sems)
    residual = [fetch(ready, attention), fetch(hidden, hidden_v)]
    copies = fetch_weight(fetch, moves, place, weight, held, 0, ready.shape[1])
    for d, block in enumerate(control):
        start = pl.multiple_of((device_column(place) ^ d) * control_rows, control_rows) if len(control) > 1 else 0
        residual.append(fetch(block, control_v.at[pl.ds(start, control_rows), :]))
    for copy in residual:
        copy.wait()
    stores = []

    def store(at, x):
        out_v[:, at] = x
        stores.append(fetch(out_v.at[:, at], out.at[:, at]))

    project(
        copies,
        attention,
        held,
        0,
        store,
        lambda at: hidden_v[:, at].astype(jnp.float32) + control_v[:, at].astype(jnp.float32),
    )
    for copy in stores:
        copy.wait()


def finish_kernel(which, pieces, moves, first, pattern, q, part, stats, so_far, *refs):
    slots, active = len(which), in_window(pattern, which)
    near, weight, out, refs = refs[:slots], refs[slots : slots + pieces], refs[slots + pieces], refs[slots + pieces + 1 :]
    q_v, near_v, (*state, stats_v, sems, attention, held, sum_v, out_v, late_sems) = (
        refs[0],
        refs[1 : slots + 1],
        refs[slots + 1 :],
    )
    fetch, late_fetch = Fetch(sems), Fetch(late_sems)
    low = first * HEAD_DIM
    opened = close_open(fetch, first, q, part, stats, near, q_v, near_v, state, stats_v)
    copies = fetch_weight(late_fetch, moves, device_place(), weight, held, low, low + q_v.shape[1])
    so_far_copy = late_fetch(so_far, sum_v)
    close_heads(opened, first, active, q_v, near_v, state, stats_v, attention)
    so_far_copy.wait()
    stores = []

    def store(at, x):
        out_v[:, at] = x.astype(jnp.bfloat16)
        stores.append(late_fetch(out_v.at[:, at], out.at[:, at]))

    project(copies, attention, held, low, store, lambda at: sum_v[:, at])
    for copy in stores:
        copy.wait()


def project_scratch(rows, columns, groups, inner, width, dtype, copies):
    share = width // groups
    return [
        pltpu.VMEM((rows, columns), jnp.bfloat16),
        pltpu.VMEM((groups, inner, share), jnp.bfloat16),
    ], [
        pltpu.VMEM((rows, width), dtype),
        pltpu.SemaphoreType.DMA((copies + width // (512 if share % 512 == 0 else share),)),
    ]


def begin(ready, weight, control, hidden, moves, inner):
    rows, width = hidden.shape
    columns = ready.shape[1]
    before, behind = project_scratch(
        rows, columns, lax.axis_size("groups"), inner, width, jnp.float32, 2 + len(moves) + len(control)
    )
    return pl.pallas_call(
        functools.partial(begin_kernel, (len(weight), len(control)), moves, control[0].shape[0]),
        out_shape=jax.ShapeDtypeStruct((rows, width), jnp.float32),
        in_specs=[ANY] * (2 + len(weight) + len(control)),
        out_specs=ANY,
        scratch_shapes=before + [pltpu.VMEM((rows, width), jnp.bfloat16)] * 2 + behind,
        compiler_params=pltpu.CompilerParams(vmem_limit_bytes=VMEM_LIMIT),
        cost_estimate=pl.CostEstimate(
            flops=2 * rows * columns * width, bytes_accessed=2 * columns * width + 8 * rows * width, transcendentals=0
        ),
        name="begin",
    )(hidden, ready, *weight, *control)


def finish(which, pattern, q, state, near, first, so_far, weight, moves):
    rows, inner = q.shape
    width = so_far.shape[1]
    columns = near[0].shape[1] // 2
    before, behind = project_scratch(
        rows, columns, lax.axis_size("groups"), inner, width, jnp.bfloat16, 1 + len(moves)
    )
    return pl.pallas_call(
        functools.partial(finish_kernel, which, len(weight), moves, first),
        out_shape=jax.ShapeDtypeStruct((rows, width), jnp.bfloat16),
        in_specs=[SMEM] + [ANY] * (4 + len(near) + len(weight)),
        out_specs=ANY,
        scratch_shapes=close_scratch(rows, columns, len(near))
        + before
        + [pltpu.VMEM((rows, width), jnp.float32)]
        + behind,
        compiler_params=pltpu.CompilerParams(vmem_limit_bytes=VMEM_LIMIT),
        cost_estimate=pl.CostEstimate(
            flops=2 * rows * columns * width, bytes_accessed=2 * columns * width + 6 * rows * width, transcendentals=0
        ),
        name="finish",
    )(pattern, q, *state, so_far, *near, *weight)


def flipped(block, axis, flip):
    return lax.ppermute(block, axis, [(i, i ^ flip) for i in range(lax.axis_size(axis))])


class Lane:
    def __init__(self):
        self.last = ()

    def __call__(self, send, block, *others):
        self.last = (send(after(block, *self.last, *others)),)
        return self.last[0]


def swap(axis, flip):
    return lambda block: flipped(block, axis, flip)


def route_of(route):
    return lambda block: lax.ppermute(block, TILES, route)


def grid_of(tile_count):
    width = min(8, tile_count // 4)
    height = min(4, tile_count // 8)
    return (width * height, width, 1), (tile_count // (width * height), height, width)


def device_place():
    return [lax.axis_index(a) for a in ("groups",) + TILES]


def device_column(place):
    _, outer, pair, core = place
    tile_count = math.prod(lax.axis_size(a) for a in TILES)
    return lax.rem((outer * 2 + pair) * 2 + core, grid_of(tile_count)[1][2])


def in_window(pattern, slots):
    _, outer, pair, core = device_place()
    strides, counts = grid_of(math.prod(lax.axis_size(a) for a in TILES))
    position = (outer * 2 + pair) * 2 + core
    active = []
    for axis, odd in slots:
        place = lax.rem(lax.div(position, strides[axis]), counts[axis])
        down = (place >= 1) & (pattern[0, 2 * axis] == 1)
        up = (place + 1 < counts[axis]) & (pattern[0, 2 * axis + 1] == 1)
        active.append(jnp.where(lax.rem(place, 2) == odd, up.astype(jnp.int32), down.astype(jnp.int32)) == 1)
    return active


def neighbour_slots(tile_count, strides, counts):
    slots = []
    for axis, (stride, count) in enumerate(zip(strides, counts)):
        for odd in range(2):
            route = []
            for t in range(tile_count):
                place = t // stride % count
                if place % 2 == odd and place + 1 < count:
                    route += [(t, t + stride), (t + stride, t)]
            if route:
                slots.append((axis, odd, route))
    return slots


def on_device(hidden, queries, keys, values, control, out_weight, pattern):
    groups = lax.axis_size("groups")
    outer, pair, cores = (lax.axis_size(a) for a in TILES)
    tile_count = outer * pair * cores
    strides, counts = grid_of(tile_count)
    grid_width = counts[2]
    across = device_column(device_place())
    rows = queries.shape[0]
    width = hidden.shape[1]
    slots = neighbour_slots(tile_count, strides, counts)
    early = [s for s in slots if s[0] == 2]
    late = [s for s in slots if s[0] != 2]

    far_lane, near_lane = Lane(), Lane()

    shard, share = out_weight.shape[0], width // groups
    line = out_weight[:, :share]
    for g in range(1, groups):
        line = jnp.where(lax.axis_index("groups") == g, out_weight[:, g * share : (g + 1) * share], line)
    line = lax.optimization_barrier(line)[None]
    line_flips = [0]
    flip = outer // 2
    while flip > 2:
        line = jnp.concatenate([line, flipped(line, "outer", flip)])
        line_flips += [f ^ flip for f in line_flips]
        flip //= 2
    far = far_lane(swap("outer", 2), line)
    near = near_lane(swap("outer", 1), line)

    firsts = [sum(CHUNKS[:i]) for i in range(len(CHUNKS))]
    chunks = [
        jnp.concatenate([x[:, f * HEAD_DIM : (f + n) * HEAD_DIM] for x in (keys, values)], axis=1)
        for f, n in zip(firsts, CHUNKS)
    ]
    block = rows // grid_width
    lines = after(control, line).reshape(block // TILE_W, grid_width, TILE_W, width)
    control_sent = [
        lax.dynamic_index_in_dim(lines, across ^ d, 1, keepdims=False).reshape(block, width) for d in range(grid_width)
    ]
    chunks, control_sent = lax.optimization_barrier((chunks, control_sent))
    control_parts = [control_sent[0]] + [None] * (grid_width - 1)
    beside = swap("pair", 1)(line)
    for d in range(2, grid_width - 1):
        control_parts[d] = swap(TILES, d)(after(control_sent[d], line))
    plane = jnp.concatenate([line, beside])
    last = swap("outer", 1)(after(far, near, *control_parts[2:-1], *chunks))
    near_x = swap("pair", 1)(near)
    held = []
    for both in (plane, jnp.concatenate([near, near_x])):
        held += [both, swap("groups", 1)(both)]
    early_near = [[None, None] for _ in early]
    for i, x in enumerate((keys, values)):
        early_near[0][i] = lax.ppermute(x, TILES, early[0][2])
        for slot in range(1, len(early)):
            early_near[slot][i] = lax.ppermute(after(x, early_near[0][i]), TILES, early[slot][2])
    state = attend(tuple(s[:2] for s in early), pattern, queries, [keys, values] + [x for kv in early_near for x in kv])

    late_near = []
    for chunk in chunks:
        lanes = (far_lane, near_lane)
        late_near.append([lanes[i % 2](route_of(route), chunk) for i, (_, _, route) in enumerate(late)])
    crossed = [swap("core", 1)(x) for x in held]
    for d in (1, grid_width - 1):
        control_parts[d] = swap(TILES, d)(after(control_sent[d], *[x for kv in early_near[1:] for x in kv]))

    gates = [*control_parts[2:-1], near_x, held[1]]
    weight = [lax.all_gather(after(jnp.concatenate([far, last]), *gates), ("groups", "pair", "core"))]
    n = len(line_flips)
    moves = [
        (0, ((g * pair + p) * cores + c, i * n + j), (False, g, f ^ at, p, c))
        for g in range(groups)
        for p in range(pair)
        for c in range(cores)
        for i, at in enumerate((2, 3))
        for j, f in enumerate(line_flips)
    ]
    for number, (group_flip, at) in enumerate(((0, 0), (1, 0), (0, 1), (1, 1))):
        for core_flip, pieces in enumerate((held, crossed)):
            moves += [
                (len(weight), (p * n + j,), (True, group_flip, f ^ at, p, core_flip))
                for p in range(pair)
                for j, f in enumerate(line_flips)
            ]
            weight.append(pieces[number])

    which = tuple(s[:2] for s in late)
    ready = [close(which, pattern, queries, state, late_near[i], firsts[i]) for i in range(len(CHUNKS) - 1)]
    ready = ready[0] if len(ready) == 1 else jnp.concatenate(ready, axis=1)
    if block % 16:
        control_parts = [
            jnp.take(
                jnp.stack(control_parts), jnp.arange(grid_width, dtype=jnp.int32) ^ across, axis=0
            ).reshape(rows, width)
        ]
    if shard % 16:
        weight, moves = [in_order(weight, moves, device_place(), (groups, outer, pair, cores))], [(0, None, None)]
    moves = tuple(moves)
    so_far = begin(ready, weight, control_parts, hidden, moves, queries.shape[1])
    return finish(which, pattern, queries, state, late_near[-1], firsts[-1], so_far, weight, moves)


def in_order(weight, moves, place, sizes):
    groups, outer, pair, cores = sizes
    shard, columns = weight[0].shape[-2:]
    gathered = weight[0].reshape(groups, pair, cores, -1, shard, columns)
    for axis, at in enumerate((0, 2, 3)):
        gathered = jnp.take(gathered, jnp.arange(sizes[at], dtype=jnp.int32) ^ place[at], axis=axis)
    weight = [gathered.reshape(weight[0].shape)] + weight[1:]
    blocks = {at[1:]: weight[piece][index] for piece, index, at in moves}
    whole = jnp.stack([blocks[at] for at in sorted(blocks)]).reshape(sizes + (shard, columns))
    for axis, size in enumerate(sizes):
        whole = jnp.take(whole, jnp.arange(size, dtype=jnp.int32) ^ place[axis], axis=axis)
    return whole.reshape(groups, -1, columns)


def solution(mesh):
    groups = mesh.shape["groups"]
    tiles = mesh.shape["tiles"]
    split = Mesh(mesh.devices.reshape(groups, tiles // 4, 2, 2), ("groups",) + TILES)
    rows = P(("groups",) + TILES, None)
    placed = (rows, rows, rows, rows, rows, P(TILES, None), rows)
    return jax.shard_map(
        on_device,
        mesh=split,
        in_specs=placed,
        out_specs=rows,
        check_vma=False,
    )
```

```python
import functools
import math

import jax
import jax.numpy as jnp
from jax import lax
from jax.experimental import pallas as pl
from jax.experimental.pallas import tpu as pltpu
from jax.sharding import Mesh
from jax.sharding import PartitionSpec as P

HEAD_DIM = 128
TILE_W = 8
CHUNKS = (6, 6)
SCALE = HEAD_DIM**-0.5 * math.log2(math.e)
TILES = ("outer", "pair", "core")
VMEM_LIMIT = 60 * 1024 * 1024
SMEM = pl.BlockSpec(memory_space=pltpu.SMEM)
ANY = pl.BlockSpec(memory_space=pl.ANY)


def after(x, *others):
    return lax.optimization_barrier((x, *others))[0] if others else x


def head_part(q, k, v):
    scores = lax.dot_general(q, k, (((1,), (1,)), ((), ())), preferred_element_type=jnp.float32)
    peak = jnp.max(scores, axis=1, keepdims=True)
    weights = jnp.exp2((scores - peak) * SCALE).astype(jnp.bfloat16)
    ones = jnp.ones((v.shape[0], HEAD_DIM), jnp.bfloat16)
    both = jnp.dot(weights, jnp.concatenate([v, ones], axis=1), preferred_element_type=jnp.float32)
    return both[:, :HEAD_DIM], both[:, HEAD_DIM:], jnp.broadcast_to(peak, v.shape)


def merge(old, new):
    part, total, peak = old
    part_new, total_new, peak_new = new
    top = jnp.maximum(peak, peak_new)
    f_old = jnp.exp2((peak - top) * SCALE)
    f_new = jnp.exp2((peak_new - top) * SCALE)
    return f_old * part + f_new * part_new, f_old * total + f_new * total_new, top


def columns_of(h):
    return pl.ds(h * HEAD_DIM, HEAD_DIM)


def fold(state, active, q, k, v):
    @pl.when(active)
    def _():
        for h in range(q.shape[1] // HEAD_DIM):
            at = columns_of(h)
            new = head_part(q[:, at], k[:, at], v[:, at])
            for r, x in zip(state, merge(tuple(r[:, at] for r in state), new)):
                r[:, at] = x


class Fetch:
    def __init__(self, sems):
        self.sems, self.count = sems, 0

    def later(self, source, target):
        self.count += 1
        return pltpu.make_async_copy(source, target, self.sems.at[self.count - 1])

    def __call__(self, source, target):
        copy = self.later(source, target)
        copy.start()
        return copy


def attend_kernel(which, pattern, q, *refs):
    slots, active = len(which), in_window(pattern, which)
    kv, (part, stats), scratch = refs[: 2 * slots + 2], refs[2 * slots + 2 : 2 * slots + 4], refs[2 * slots + 4 :]
    q_v, kv_v, (part_v, total_v, peak_v, stats_v, sems) = scratch[0], scratch[1 : 2 * slots + 3], scratch[2 * slots + 3 :]
    fetch = Fetch(sems)
    copies = [fetch(source, target) for source, target in zip((q, *kv), (q_v, *kv_v))]
    for copy in copies[:3]:
        copy.wait()
    state = (part_v, total_v, peak_v)
    heads = q_v.shape[1] // HEAD_DIM
    for h in range(heads):
        at = columns_of(h)
        for r, x in zip(state, head_part(q_v[:, at], kv_v[0][:, at], kv_v[1][:, at])):
            r[:, at] = x
    for slot in range(slots):
        for copy in copies[3 + 2 * slot : 5 + 2 * slot]:
            copy.wait()
        fold(state, active[slot], q_v, kv_v[2 * slot + 2], kv_v[2 * slot + 3])
    lane = lax.broadcasted_iota(jnp.int32, stats_v.shape, 1)
    packed = jnp.zeros(stats_v.shape, jnp.float32)
    for h in range(heads):
        packed = jnp.where(lane == h, total_v[:, columns_of(h)], packed)
        packed = jnp.where(lane == HEAD_DIM // 2 + h, peak_v[:, columns_of(h)], packed)
    stats_v[...] = packed
    copies = [fetch(part_v, part), fetch(stats_v, stats)]
    for copy in copies:
        copy.wait()


def attend(which, pattern, q, kv):
    rows, columns = q.shape
    slots = len(kv) // 2 - 1
    return pl.pallas_call(
        functools.partial(attend_kernel, which),
        out_shape=[
            jax.ShapeDtypeStruct((rows, columns), jnp.float32),
            jax.ShapeDtypeStruct((rows, HEAD_DIM), jnp.float32),
        ],
        in_specs=[SMEM] + [ANY] * (1 + len(kv)),
        out_specs=[ANY] * 2,
        scratch_shapes=[pltpu.VMEM((rows, columns), jnp.bfloat16)] * (1 + len(kv))
        + [pltpu.VMEM((rows, columns), jnp.float32)] * 3
        + [pltpu.VMEM((rows, HEAD_DIM), jnp.float32), pltpu.SemaphoreType.DMA((3 + len(kv),))],
        compiler_params=pltpu.CompilerParams(vmem_limit_bytes=VMEM_LIMIT),
        cost_estimate=pl.CostEstimate(
            flops=(1 + slots) * 6 * rows * rows * columns,
            bytes_accessed=rows * columns * (10 + 4 * slots),
            transcendentals=0,
        ),
        name="attend",
    )(pattern, q, *kv)


def close_open(fetch, first, q, part, stats, near, q_v, near_v, state, stats_v):
    columns = state[0].shape[1]
    at = pl.ds(first * HEAD_DIM, columns)
    return [
        fetch(q.at[:, at], q_v),
        fetch(part.at[:, at], state[0]),
        fetch(stats, stats_v),
    ] + [fetch(source, target) for source, target in zip(near, near_v)]


def close_heads(copies, first, active, q_v, near_v, state, stats_v, out):
    columns = state[0].shape[1]
    for copy in copies[:3]:
        copy.wait()
    stats_now = stats_v[...]
    for h in range(columns // HEAD_DIM):
        for r, lane in zip(state[1:], (first + h, HEAD_DIM // 2 + first + h)):
            r[:, columns_of(h)] = jnp.broadcast_to(stats_now[:, lane : lane + 1], stats_now.shape)
    for slot, kv in enumerate(near_v):
        copies[3 + slot].wait()
        fold(state, active[slot], q_v, kv.at[:, pl.ds(0, columns)], kv.at[:, pl.ds(columns, columns)])
    out[...] = (state[0][...] / state[1][...]).astype(jnp.bfloat16)


def close_scratch(rows, columns, slots):
    return (
        [pltpu.VMEM((rows, columns), jnp.bfloat16)]
        + [pltpu.VMEM((rows, 2 * columns), jnp.bfloat16)] * slots
        + [pltpu.VMEM((rows, columns), jnp.float32)] * 3
        + [pltpu.VMEM((rows, HEAD_DIM), jnp.float32), pltpu.SemaphoreType.DMA((4 + slots,))]
    )


def close_kernel(first, which, pattern, q, part, stats, *refs):
    slots, active = len(which), in_window(pattern, which)
    near, out = refs[:slots], refs[slots]
    q_v, near_v, (*state, stats_v, sems, out_v) = refs[slots + 1], refs[slots + 2 : 2 * slots + 2], refs[2 * slots + 2 :]
    fetch = Fetch(sems)
    opened = close_open(fetch, first, q, part, stats, near, q_v, near_v, state, stats_v)
    close_heads(opened, first, active, q_v, near_v, state, stats_v, out_v)
    fetch(out_v, out).wait()


def close(which, pattern, q, state, near, first):
    rows, columns = q.shape[0], near[0].shape[1] // 2
    return pl.pallas_call(
        functools.partial(close_kernel, first, which),
        out_shape=jax.ShapeDtypeStruct((rows, columns), jnp.bfloat16),
        in_specs=[SMEM] + [ANY] * (3 + len(near)),
        out_specs=ANY,
        scratch_shapes=close_scratch(rows, columns, len(near)) + [pltpu.VMEM((rows, columns), jnp.bfloat16)],
        compiler_params=pltpu.CompilerParams(vmem_limit_bytes=VMEM_LIMIT),
        cost_estimate=pl.CostEstimate(
            flops=len(near) * 6 * rows * rows * columns,
            bytes_accessed=rows * columns * (4 * len(near) + 8),
            transcendentals=0,
        ),
        name="close",
    )(pattern, q, *state, *near)


def fetch_weight(fetch, moves, place, weight, held, low, high):
    copies = []
    for piece, index, at in moves:
        if at is None:
            copies.append((True, 0, fetch(weight[piece], held)))
            continue
        source = weight[piece].at[index]
        flip, group, outer, pair, core = at
        known = None if flip else group
        count = source.shape[0]
        outer = place[1] ^ outer
        if flip:
            group, pair, core = place[0] ^ group, place[2] ^ pair, place[3] ^ core
        start = pl.multiple_of(((outer * 2 + pair) * 2 + core) * count, count)
        needed = (start < high) & (start + count > low)
        copy = fetch.later(source, held.at[group, pl.ds(start, count), :])
        pl.when(needed)(copy.start)
        copies.append((needed, 0 if known is None else known, copy))
    return copies


def project(copies, attention, held, low, out, add):
    groups, _, columns = held.shape
    step = 512 if columns % 512 == 0 else columns
    for group in range(groups):
        for needed, at, copy in copies:
            if at == group:
                if needed is True:
                    copy.wait()
                else:
                    pl.when(needed)(copy.wait)
        for j in range(columns // step):
            at = pl.ds(group * columns + j * step, step)
            projected = jnp.dot(
                attention[...],
                held[group, pl.ds(low, attention.shape[1]), pl.ds(j * step, step)],
                preferred_element_type=jnp.float32,
            )
            out(at, add(at) + projected)


def begin_kernel(counts, moves, control_rows, hidden, ready, *refs):
    place = device_place()
    weight, control = refs[: counts[0]], refs[counts[0] : sum(counts)]
    out, attention, held, hidden_v, control_v, out_v, sems = refs[sum(counts) :]
    fetch = Fetch(sems)
    residual = [fetch(ready, attention), fetch(hidden, hidden_v)]
    copies = fetch_weight(fetch, moves, place, weight, held, 0, ready.shape[1])
    for d, block in enumerate(control):
        start = pl.multiple_of((device_column(place) ^ d) * control_rows, control_rows) if len(control) > 1 else 0
        residual.append(fetch(block, control_v.at[pl.ds(start, control_rows), :]))
    for copy in residual:
        copy.wait()
    stores = []

    def store(at, x):
        out_v[:, at] = x
        stores.append(fetch(out_v.at[:, at], out.at[:, at]))

    project(
        copies,
        attention,
        held,
        0,
        store,
        lambda at: hidden_v[:, at].astype(jnp.float32) + control_v[:, at].astype(jnp.float32),
    )
    for copy in stores:
        copy.wait()


def finish_kernel(which, pieces, moves, first, pattern, q, part, stats, so_far, *refs):
    slots, active = len(which), in_window(pattern, which)
    near, weight, out, refs = refs[:slots], refs[slots : slots + pieces], refs[slots + pieces], refs[slots + pieces + 1 :]
    q_v, near_v, (*state, stats_v, sems, attention, held, sum_v, out_v, late_sems) = (
        refs[0],
        refs[1 : slots + 1],
        refs[slots + 1 :],
    )
    fetch, late_fetch = Fetch(sems), Fetch(late_sems)
    low = first * HEAD_DIM
    opened = close_open(fetch, first, q, part, stats, near, q_v, near_v, state, stats_v)
    copies = fetch_weight(late_fetch, moves, device_place(), weight, held, low, low + q_v.shape[1])
    so_far_copy = late_fetch(so_far, sum_v)
    close_heads(opened, first, active, q_v, near_v, state, stats_v, attention)
    so_far_copy.wait()
    stores = []

    def store(at, x):
        out_v[:, at] = x.astype(jnp.bfloat16)
        stores.append(late_fetch(out_v.at[:, at], out.at[:, at]))

    project(copies, attention, held, low, store, lambda at: sum_v[:, at])
    for copy in stores:
        copy.wait()


def project_scratch(rows, columns, groups, inner, width, dtype, copies):
    share = width // groups
    return [
        pltpu.VMEM((rows, columns), jnp.bfloat16),
        pltpu.VMEM((groups, inner, share), jnp.bfloat16),
    ], [
        pltpu.VMEM((rows, width), dtype),
        pltpu.SemaphoreType.DMA((copies + width // (512 if share % 512 == 0 else share),)),
    ]


def begin(ready, weight, control, hidden, moves, inner):
    rows, width = hidden.shape
    columns = ready.shape[1]
    before, behind = project_scratch(
        rows, columns, lax.axis_size("groups"), inner, width, jnp.float32, 2 + len(moves) + len(control)
    )
    return pl.pallas_call(
        functools.partial(begin_kernel, (len(weight), len(control)), moves, control[0].shape[0]),
        out_shape=jax.ShapeDtypeStruct((rows, width), jnp.float32),
        in_specs=[ANY] * (2 + len(weight) + len(control)),
        out_specs=ANY,
        scratch_shapes=before + [pltpu.VMEM((rows, width), jnp.bfloat16)] * 2 + behind,
        compiler_params=pltpu.CompilerParams(vmem_limit_bytes=VMEM_LIMIT),
        cost_estimate=pl.CostEstimate(
            flops=2 * rows * columns * width, bytes_accessed=2 * columns * width + 8 * rows * width, transcendentals=0
        ),
        name="begin",
    )(hidden, ready, *weight, *control)


def finish(which, pattern, q, state, near, first, so_far, weight, moves):
    rows, inner = q.shape
    width = so_far.shape[1]
    columns = near[0].shape[1] // 2
    before, behind = project_scratch(
        rows, columns, lax.axis_size("groups"), inner, width, jnp.bfloat16, 1 + len(moves)
    )
    return pl.pallas_call(
        functools.partial(finish_kernel, which, len(weight), moves, first),
        out_shape=jax.ShapeDtypeStruct((rows, width), jnp.bfloat16),
        in_specs=[SMEM] + [ANY] * (4 + len(near) + len(weight)),
        out_specs=ANY,
        scratch_shapes=close_scratch(rows, columns, len(near))
        + before
        + [pltpu.VMEM((rows, width), jnp.float32)]
        + behind,
        compiler_params=pltpu.CompilerParams(vmem_limit_bytes=VMEM_LIMIT),
        cost_estimate=pl.CostEstimate(
            flops=2 * rows * columns * width, bytes_accessed=2 * columns * width + 6 * rows * width, transcendentals=0
        ),
        name="finish",
    )(pattern, q, *state, so_far, *near, *weight)


def flipped(block, axis, flip):
    return lax.ppermute(block, axis, [(i, i ^ flip) for i in range(lax.axis_size(axis))])


class Lane:
    def __init__(self):
        self.last = ()

    def __call__(self, send, block, *others):
        self.last = (send(after(block, *self.last, *others)),)
        return self.last[0]


def swap(axis, flip):
    return lambda block: flipped(block, axis, flip)


def route_of(route):
    return lambda block: lax.ppermute(block, TILES, route)


def grid_of(tile_count):
    width = min(8, tile_count // 4)
    height = min(4, tile_count // 8)
    return (width * height, width, 1), (tile_count // (width * height), height, width)


def device_place():
    return [lax.axis_index(a) for a in ("groups",) + TILES]


def device_column(place):
    _, outer, pair, core = place
    tile_count = math.prod(lax.axis_size(a) for a in TILES)
    return lax.rem((outer * 2 + pair) * 2 + core, grid_of(tile_count)[1][2])


def in_window(pattern, slots):
    _, outer, pair, core = device_place()
    strides, counts = grid_of(math.prod(lax.axis_size(a) for a in TILES))
    position = (outer * 2 + pair) * 2 + core
    active = []
    for axis, odd in slots:
        place = lax.rem(lax.div(position, strides[axis]), counts[axis])
        down = (place >= 1) & (pattern[0, 2 * axis] == 1)
        up = (place + 1 < counts[axis]) & (pattern[0, 2 * axis + 1] == 1)
        active.append(jnp.where(lax.rem(place, 2) == odd, up.astype(jnp.int32), down.astype(jnp.int32)) == 1)
    return active


def neighbour_slots(tile_count, strides, counts):
    slots = []
    for axis, (stride, count) in enumerate(zip(strides, counts)):
        for odd in range(2):
            route = []
            for t in range(tile_count):
                place = t // stride % count
                if place % 2 == odd and place + 1 < count:
                    route += [(t, t + stride), (t + stride, t)]
            if route:
                slots.append((axis, odd, route))
    return slots


def on_device(hidden, queries, keys, values, control, out_weight, pattern):
    groups = lax.axis_size("groups")
    outer, pair, cores = (lax.axis_size(a) for a in TILES)
    tile_count = outer * pair * cores
    strides, counts = grid_of(tile_count)
    grid_width = counts[2]
    across = device_column(device_place())
    rows = queries.shape[0]
    width = hidden.shape[1]
    slots = neighbour_slots(tile_count, strides, counts)
    early = [s for s in slots if s[0] == 2]
    late = [s for s in slots if s[0] != 2]

    far_lane, near_lane = Lane(), Lane()

    shard, share = out_weight.shape[0], width // groups
    line = out_weight[:, :share]
    for g in range(1, groups):
        line = jnp.where(lax.axis_index("groups") == g, out_weight[:, g * share : (g + 1) * share], line)
    line = lax.optimization_barrier(line)[None]
    line_flips = [0]
    flip = outer // 2
    while flip > 2:
        line = jnp.concatenate([line, flipped(line, "outer", flip)])
        line_flips += [f ^ flip for f in line_flips]
        flip //= 2
    far = far_lane(swap("outer", 2), line)
    near = near_lane(swap("outer", 1), line)

    firsts = [sum(CHUNKS[:i]) for i in range(len(CHUNKS))]
    chunks = [
        jnp.concatenate([x[:, f * HEAD_DIM : (f + n) * HEAD_DIM] for x in (keys, values)], axis=1)
        for f, n in zip(firsts, CHUNKS)
    ]
    block = rows // grid_width
    lines = after(control, line).reshape(block // TILE_W, grid_width, TILE_W, width)
    control_sent = [
        lax.dynamic_index_in_dim(lines, across ^ d, 1, keepdims=False).reshape(block, width) for d in range(grid_width)
    ]
    chunks, control_sent = lax.optimization_barrier((chunks, control_sent))
    control_parts = [control_sent[0]] + [None] * (grid_width - 1)
    beside = swap("pair", 1)(line)
    for d in range(2, grid_width - 1):
        control_parts[d] = swap(TILES, d)(after(control_sent[d], line))
    plane = jnp.concatenate([line, beside])
    last = swap("outer", 1)(after(far, near, *control_parts[2:-1], *chunks))
    near_x = swap("pair", 1)(near)
    held = []
    for both in (plane, jnp.concatenate([near, near_x])):
        held += [both, swap("groups", 1)(both)]
    early_near = [[None, None] for _ in early]
    for i, x in enumerate((keys, values)):
        early_near[0][i] = lax.ppermute(x, TILES, early[0][2])
        for slot in range(1, len(early)):
            early_near[slot][i] = lax.ppermute(after(x, early_near[0][i]), TILES, early[slot][2])
    state = attend(tuple(s[:2] for s in early), pattern, queries, [keys, values] + [x for kv in early_near for x in kv])

    late_near = []
    for chunk in chunks:
        lanes = (far_lane, near_lane)
        if not late_near:
            sent = [lanes[i % 2](route_of(route), chunk) for i, (_, _, route) in enumerate(late)]
        else:
            waits = [kv[0] for kv in early_near[1:]]
            sent = [lax.ppermute(after(chunk, *waits), TILES, route) for _, _, route in late]
        late_near.append(sent)
    crossed = [swap("core", 1)(x) for x in held]
    for d in (1, grid_width - 1):
        control_parts[d] = swap(TILES, d)(after(control_sent[d], *[x for kv in early_near[1:] for x in kv]))

    gates = [*control_parts[2:-1], near_x, held[1]]
    weight = [lax.all_gather(after(jnp.concatenate([far, last]), *gates), ("groups", "pair", "core"))]
    n = len(line_flips)
    moves = [
        (0, ((g * pair + p) * cores + c, i * n + j), (False, g, f ^ at, p, c))
        for g in range(groups)
        for p in range(pair)
        for c in range(cores)
        for i, at in enumerate((2, 3))
        for j, f in enumerate(line_flips)
    ]
    for number, (group_flip, at) in enumerate(((0, 0), (1, 0), (0, 1), (1, 1))):
        for core_flip, pieces in enumerate((held, crossed)):
            moves += [
                (len(weight), (p * n + j,), (True, group_flip, f ^ at, p, core_flip))
                for p in range(pair)
                for j, f in enumerate(line_flips)
            ]
            weight.append(pieces[number])

    which = tuple(s[:2] for s in late)
    ready = [close(which, pattern, queries, state, late_near[i], firsts[i]) for i in range(len(CHUNKS) - 1)]
    ready = ready[0] if len(ready) == 1 else jnp.concatenate(ready, axis=1)
    if block % 16:
        control_parts = [
            jnp.take(
                jnp.stack(control_parts), jnp.arange(grid_width, dtype=jnp.int32) ^ across, axis=0
            ).reshape(rows, width)
        ]
    if shard % 16:
        weight, moves = [in_order(weight, moves, device_place(), (groups, outer, pair, cores))], [(0, None, None)]
    moves = tuple(moves)
    so_far = begin(ready, weight, control_parts, hidden, moves, queries.shape[1])
    return finish(which, pattern, queries, state, late_near[-1], firsts[-1], so_far, weight, moves)


def in_order(weight, moves, place, sizes):
    groups, outer, pair, cores = sizes
    shard, columns = weight[0].shape[-2:]
    gathered = weight[0].reshape(groups, pair, cores, -1, shard, columns)
    for axis, at in enumerate((0, 2, 3)):
        gathered = jnp.take(gathered, jnp.arange(sizes[at], dtype=jnp.int32) ^ place[at], axis=axis)
    weight = [gathered.reshape(weight[0].shape)] + weight[1:]
    blocks = {at[1:]: weight[piece][index] for piece, index, at in moves}
    whole = jnp.stack([blocks[at] for at in sorted(blocks)]).reshape(sizes + (shard, columns))
    for axis, size in enumerate(sizes):
        whole = jnp.take(whole, jnp.arange(size, dtype=jnp.int32) ^ place[axis], axis=axis)
    return whole.reshape(groups, -1, columns)


def solution(mesh):
    groups = mesh.shape["groups"]
    tiles = mesh.shape["tiles"]
    split = Mesh(mesh.devices.reshape(groups, tiles // 4, 2, 2), ("groups",) + TILES)
    rows = P(("groups",) + TILES, None)
    placed = (rows, rows, rows, rows, rows, P(TILES, None), rows)
    return jax.shard_map(
        on_device,
        mesh=split,
        in_specs=placed,
        out_specs=rows,
        check_vma=False,
    )
```
